32 devices in a mesh: var: 8 (over y, x, core), space: 4 (over z).
Axes of the slice: x: 2, y: 2, z: 4, core: 2. Of those that a mesh axis runs over, the one named last changes fastest.
Arguments:
- patches: bfloat16 [48, 1024, 256], P('var', 'space'), may hold values from -6 to 6
- embed_weight: bfloat16 [48, 256, 1024], P('var'), may hold values from -0.375 to 0.375
- var_embed: float32 [48, 1024], P('var'), may hold values from -3 to 3
- agg_query: float32 [1024], replicated, may hold values from -240 to 240
- agg_kv: bfloat16 [1024, 2048], replicated, may hold values from -0.1875 to 0.1875
- agg_out: bfloat16 [1024, 1024], replicated, may hold values from -0.1875 to 0.1875
- norm_gain: float32 [1024], replicated, may hold values from 0.5 to 1.5
- qkv_weight: bfloat16 [1024, 3072], P(None, 'var'), may hold values from -4 to 4
- out_weight: bfloat16 [1024, 1024], P('var'), may hold values from -0.1875 to 0.1875
- cotangent: bfloat16 [1024, 1024], P('space'), may hold values from -6 to 6
Outputs:
- grad_embed: float32 [48, 256, 1024], P('var', None, 'space')
- grad_var_embed: float32 [48, 1024], P('var', 'space')
- grad_agg_query: float32 [1024], P('space')
- grad_agg_kv: float32 [1024, 2048], P(None, 'space')
- grad_agg_out: float32 [1024, 1024], P(None, 'space')
- grad_norm_gain: float32 [1024], P('space')
- grad_qkv: float32 [1024, 3072], P('space', 'var')
- grad_out_weight: float32 [1024, 1024], P('var', 'space')
The draws below stay inside these ranges and needn't reach their ends.
All inputs are finite; a program needn't handle non-finite values.
Results may differ from the reference program's by a relative error of at most 0.019.
The reference program's roundings to bfloat16 on the way count: a program that leaves them out, or rounds other values in their place, can miss the bound.
Values may be sent and summed in bfloat16 or wider, within the bound.
No kernel may reach another device: no remote copies, remote signals or barrier semaphores. Data moves between devices by JAX's collectives and lax.ppermute only.
A program may use at most 128 MiB of HBM per device.

```python
import math
import jax
import jax.numpy as jnp
from jax import lax

D = 1024
HEADS = 16
HEAD_SIZE = 64
PIX = 256
VARS = 48
TOKENS = 1024


def draw_agg_query(key, part):
    key = jax.random.fold_in(key, 11)
    base_draw = jnp.clip(jax.random.normal(key, (HEADS, D // HEADS), jnp.float32), -6.0, 6.0)
    return base_draw.reshape(D)


def draw_qkv_weight(key, part):
    key = jax.random.fold_in(key, 23)
    base_draw = jnp.clip(jax.random.normal(key, (D, HEADS, 3, D // HEADS), jnp.float32), -6.0, 6.0) / math.sqrt(D)
    return base_draw.reshape(D, 3 * D).astype(jnp.bfloat16)


def block_scale(own_key, extent, shards, least, top_value):
    level, own = 1.0, jax.random.fold_in(own_key, 6)
    for position, blocks in shards:
        draws = jnp.exp(jax.random.uniform(jax.random.fold_in(own, position), (blocks,), jnp.float32, least / len(shards), top_value / len(shards)))
        level = level * jnp.repeat(draws, extent[position] // blocks).reshape([-1 if axis == position else 1 for axis in range(len(extent))])
    return level


def gaussian(stream_key, extent, spread, reach, cuts=(), dtype=jnp.bfloat16):
    entries = jax.random.normal(stream_key, extent, jnp.float32) * spread
    if len(cuts) > 0:
        entries = block_scale(stream_key, extent, cuts, -0.22, 0.18) * entries
    return jnp.clip(entries, min=-reach, max=reach).astype(dtype)


def setup_inputs(seed: int = 0) -> dict:
    streams_of = jax.random.split(jax.random.key(seed), 11)
    return {
        "patches": gaussian(streams_of[0], (VARS, TOKENS, PIX), 1.0, 6.0, ((0, 8), (1, 4))),
        "embed_weight": gaussian(streams_of[1], (VARS, PIX, D), PIX ** -0.5, 0.375, ((0, 8),)),
        "var_embed": gaussian(streams_of[2], (VARS, D), 0.5, 3.0, ((0, 8),), jnp.float32),
        "agg_query": draw_agg_query(jax.random.fold_in(streams_of[10], 71), 0),
        "agg_kv": gaussian(streams_of[4], (D, 2 * D), D ** -0.5, 0.1875),
        "agg_out": gaussian(streams_of[5], (D, D), D ** -0.5, 0.1875),
        "norm_gain": jnp.clip(1.0 + 0.1 * jax.random.normal(streams_of[6], (D,), jnp.float32), 0.5, 1.5),
        "qkv_weight": draw_qkv_weight(jax.random.fold_in(streams_of[10], 71), 0),
        "out_weight": gaussian(streams_of[8], (D, D), D ** -0.5, 0.1875, ((0, 8),)),
        "cotangent": gaussian(streams_of[9], (TOKENS, D), 1.0, 6.0, ((0, 4),)),
    }


EPSILON = 1e-05

def embed_one(patch_rows, embed_rows, var_offset):
    return (jnp.dot(patch_rows, embed_rows, preferred_element_type=jnp.float32) + var_offset).astype(jnp.bfloat16)

def reference(patches, embed_weight, var_embed, agg_query, agg_kv, agg_out, norm_gain, qkv_weight, out_weight, cotangent):
    score_scale = 1.0 / math.sqrt(HEAD_SIZE)
    head_query = agg_query.reshape(HEADS, HEAD_SIZE)

    def project(patch_rows, embed_rows, var_offset):
        embedded = embed_one(patch_rows, embed_rows, var_offset)
        projected = jnp.dot(embedded, agg_kv, preferred_element_type=jnp.float32)
        key_rows = projected[:, :D].reshape(TOKENS, HEADS, HEAD_SIZE)
        value_rows = projected[:, D:].reshape(TOKENS, HEADS, HEAD_SIZE)
        scores = lax.optimization_barrier(jnp.sum(key_rows * head_query, axis=-1)) * score_scale
        return (embedded, key_rows, value_rows, scores)

    def forward_step(running, per_var):
        run_max, run_sum, run_value = running
        embedded, key_rows, value_rows, scores = project(per_var[0], per_var[1], per_var[2])
        new_max = jnp.maximum(run_max, scores)
        old_factor = jnp.exp(run_max - new_max)
        new_factor = jnp.exp(scores - new_max)
        run_sum = run_sum * old_factor + new_factor
        run_value = run_value * old_factor[..., None] + new_factor[..., None] * value_rows
        return ((new_max, run_sum, run_value), None)
    start_state = (jnp.full((TOKENS, HEADS), -jnp.inf, jnp.float32), jnp.zeros((TOKENS, HEADS), jnp.float32), jnp.zeros((TOKENS, HEADS, HEAD_SIZE), jnp.float32))
    (maxima, totals, weighted), ignored = lax.scan(forward_step, start_state, (patches, embed_weight, var_embed))
    mixed_heads = weighted / totals[..., None]
    pooled = mixed_heads.reshape(TOKENS, D).astype(jnp.bfloat16)
    joined_tokens = jnp.dot(pooled, agg_out, preferred_element_type=jnp.float32).astype(jnp.bfloat16)
    joined_wide = joined_tokens.astype(jnp.float32)
    feature_mean = lax.optimization_barrier(jnp.mean(joined_wide, axis=-1, keepdims=True))
    spread_sq = lax.optimization_barrier(jnp.mean((joined_wide - feature_mean) ** 2, axis=-1, keepdims=True))
    inv_spread = lax.rsqrt(spread_sq + EPSILON)
    centred = (joined_wide - feature_mean) * inv_spread
    normed = (centred * norm_gain).astype(jnp.bfloat16)
    qkv_rows = jnp.dot(normed, qkv_weight, preferred_element_type=jnp.float32).astype(jnp.bfloat16)
    qkv_rows = qkv_rows.reshape(TOKENS, HEADS, 3, HEAD_SIZE).transpose(1, 2, 0, 3)
    d_attn = jnp.dot(cotangent, out_weight.T, preferred_element_type=jnp.float32).astype(jnp.bfloat16)
    d_attn = d_attn.reshape(TOKENS, HEADS, HEAD_SIZE).transpose(1, 0, 2)

    def head_pass(operands):
        head_qkv, head_dattn = operands
        queries = head_qkv[0]
        key_rows = head_qkv[1]
        value_rows = head_qkv[2]
        logits = jnp.dot(queries, key_rows.T, preferred_element_type=jnp.float32) * score_scale
        shifted = jnp.exp(logits - lax.optimization_barrier(jnp.max(logits, axis=-1, keepdims=True)))
        probs = shifted / lax.optimization_barrier(jnp.sum(shifted, axis=-1, keepdims=True))
        probs_b = probs.astype(jnp.bfloat16)
        attn_head = jnp.dot(probs_b, value_rows, preferred_element_type=jnp.float32).astype(jnp.bfloat16)
        dprob = jnp.dot(head_dattn, value_rows.T, preferred_element_type=jnp.float32)
        row_delta = lax.optimization_barrier(jnp.sum(probs * dprob, axis=-1, keepdims=True))
        dscore = (probs * (dprob - row_delta) * score_scale).astype(jnp.bfloat16)
        grad_q = jnp.dot(dscore, key_rows, preferred_element_type=jnp.float32)
        grad_k = jnp.dot(dscore.T, queries, preferred_element_type=jnp.float32)
        grad_v = jnp.dot(probs_b.T, head_dattn, preferred_element_type=jnp.float32)
        return (attn_head, jnp.stack([grad_q, grad_k, grad_v], axis=1).astype(jnp.bfloat16))
    attn_heads, dqkv_heads = lax.map(head_pass, (qkv_rows, d_attn))
    attn = attn_heads.transpose(1, 0, 2).reshape(TOKENS, D)
    d_qkv = dqkv_heads.transpose(1, 0, 2, 3).reshape(TOKENS, 3 * D)
    grad_out_weight = jnp.dot(attn.T, cotangent, preferred_element_type=jnp.float32)
    grad_qkv = jnp.dot(normed.T, d_qkv, preferred_element_type=jnp.float32)
    d_normed = jnp.dot(d_qkv, qkv_weight.T, preferred_element_type=jnp.float32)
    grad_norm_gain = lax.optimization_barrier(jnp.sum(d_normed * centred, axis=0))
    gained = d_normed * norm_gain
    d_joined = (cotangent.astype(jnp.float32) + (gained - lax.optimization_barrier(jnp.mean(gained, axis=-1, keepdims=True)) - centred * lax.optimization_barrier(jnp.mean(gained * centred, axis=-1, keepdims=True))) * inv_spread).astype(jnp.bfloat16)
    grad_agg_out = jnp.dot(pooled.T, d_joined, preferred_element_type=jnp.float32)
    d_pooled = jnp.dot(d_joined, agg_out.T, preferred_element_type=jnp.float32).reshape(TOKENS, HEADS, HEAD_SIZE)
    center = lax.optimization_barrier(jnp.sum(d_pooled * mixed_heads, axis=-1))

    def backward_step(running, per_var):
        grad_proj_sum, grad_query_sum = running
        embedded, key_rows, value_rows, scores = project(per_var[0], per_var[1], per_var[2])
        soft_weight = jnp.exp(scores - maxima) / totals
        dweight = lax.optimization_barrier(jnp.sum(d_pooled * value_rows, axis=-1))
        dlogit = soft_weight * (dweight - center)
        d_key = dlogit[..., None] * head_query * score_scale
        d_value = soft_weight[..., None] * d_pooled
        grad_query_sum = grad_query_sum + lax.optimization_barrier(jnp.sum(dlogit[..., None] * key_rows, axis=0)) * score_scale
        d_proj = jnp.concatenate([d_key.reshape(TOKENS, D), d_value.reshape(TOKENS, D)], axis=1).astype(jnp.bfloat16)
        grad_proj_sum = grad_proj_sum + jnp.dot(embedded.T, d_proj, preferred_element_type=jnp.float32)
        d_tokens = jnp.dot(d_proj, agg_kv.T, preferred_element_type=jnp.float32).astype(jnp.bfloat16)
        grad_embed_one = jnp.dot(per_var[0].T, d_tokens, preferred_element_type=jnp.float32)
        grad_offset = lax.optimization_barrier(jnp.sum(d_tokens.astype(jnp.float32), axis=0))
        return ((grad_proj_sum, grad_query_sum), (grad_embed_one, grad_offset))
    back_state = (jnp.zeros((D, 2 * D), jnp.float32), jnp.zeros((HEADS, HEAD_SIZE), jnp.float32))
    (grad_agg_kv, grad_query_heads), (grad_embed, grad_var_embed) = lax.scan(backward_step, back_state, (patches, embed_weight, var_embed))
    grad_agg_query = grad_query_heads.reshape(D)
    return (grad_embed, grad_var_embed, grad_agg_query, grad_agg_kv, grad_agg_out, grad_norm_gain, grad_qkv, grad_out_weight)
```

```python
import functools
import math

import jax
import jax.numpy as jnp
from jax import lax
from jax.experimental import pallas as pl
from jax.experimental.pallas import tpu as pltpu
from jax.sharding import PartitionSpec as P

HEADS = 16
LANES = 128
EPSILON = 1e-05
MIB = 1 << 20

F32 = jnp.float32
BF16 = jnp.bfloat16

NN = (((1,), (0,)), ((), ()))
NT = (((1,), (1,)), ((), ()))
TN = (((0,), (0,)), ((), ()))


def mm(a, b, dims=NN):
    return lax.dot_general(a, b, dims, preferred_element_type=F32)


def iota(shape, axis):
    return lax.broadcasted_iota(jnp.int32, shape, axis)


def parts3(x):
    hi = x.astype(BF16).astype(F32)
    rest = x - hi
    mid = rest.astype(BF16).astype(F32)
    return hi, mid, rest - mid


def pack(x, y=None):
    group = iota(x.shape, 1) >> 4
    hi, mid, lo = parts3(x)
    out = jnp.where(group == 0, hi, jnp.where(group == 1, mid, jnp.where(group == 2, lo, 0.0)))
    if y is not None:
        hi, mid, lo = parts3(y)
        out = jnp.where(group == 3, hi, jnp.where(group == 4, mid, jnp.where(group == 5, lo, out)))
    return out.astype(BF16)


def unpack(packed, first_group=0):
    row, column = iota((LANES, LANES), 0), iota((LANES, LANES), 1)
    group = row >> 4
    take = ((row & 15) == (column & 15)) & (group >= first_group) & (group < first_group + 3)
    return mm(packed, jnp.where(take, 1.0, 0.0).astype(BF16))


def spread_matrix(width, size, first=0):
    row, column = iota((LANES, width), 0), iota((LANES, width), 1)
    shift = size.bit_length() - 1
    take = ((row & 15) == ((column + first) >> shift)) & (row < 48)
    return jnp.where(take, 1.0, 0.0).astype(BF16)


def fold_matrix(width, size):
    row, column = iota((width, LANES), 0), iota((width, LANES), 1)
    shift = size.bit_length() - 1
    return jnp.where((column & 15) == (row >> shift), 1.0, 0.0).astype(BF16)


def head_sums(x, fold):
    hi, mid, lo = parts3(x)
    return mm(hi.astype(BF16), fold) + mm(mid.astype(BF16), fold) + mm(lo.astype(BF16), fold)


def call(body, out_shape, limit=32, **kw):
    return pl.pallas_call(
        body,
        out_shape=out_shape,
        compiler_params=pltpu.CompilerParams(vmem_limit_bytes=limit * MIB),
        **kw,
    )


def struct(shape, dtype):
    return jax.ShapeDtypeStruct(shape, dtype)


def cost(flops, moved):
    return pl.CostEstimate(flops=int(flops), bytes_accessed=int(moved), transcendentals=0)


SMEM = pl.BlockSpec(memory_space=pltpu.SMEM)


def xor_rows(me, source, target, count):
    block = target.shape[0] // count
    for k in range(count):
        start = pl.multiple_of((me ^ k) * block, block)
        target[k * block : (k + 1) * block, :] = source[pl.ds(start, block), :]


def swap(x, axis, k, keep=None):
    pairs = [(i, i ^ k) for i in range(lax.axis_size(axis))]
    if keep is not None:
        pairs = [pair for pair in pairs if keep(pair[1])]
    return lax.ppermute(x, axis, pairs)


def gather_direct(x, axis):
    return [x] + [swap(x, axis, k) for k in range(1, lax.axis_size(axis))]


def exchange_direct(blocks, axis):
    return [blocks[0]] + [swap(blocks[k], axis, k) for k in range(1, len(blocks))]


def gather_pairs(x, axis):
    n = lax.axis_size(axis)
    even = {k: (x if k == 0 else swap(x, axis, k)) for k in range(0, n, 2)}
    odd = {k + 1: swap(even[k], axis, 1) for k in range(0, n, 2)}
    return [even[k] if k % 2 == 0 else odd[k] for k in range(n)]


def early_body(n_var, n_space, me_ref, cot_ref, outw_ref, qkvw_ref, dattn_ref, own_ref, wperm_ref, *rest):
    cot_refs, (rows_ref, cols_ref) = rest[:n_space], rest[n_space:]
    me_v, me_s = me_ref[0], me_ref[1]
    xor_rows(me_v, cot_ref, rows_ref, n_var)
    cot = rows_ref[...]
    dattn_ref[...] = mm(cot, outw_ref[...], NT).astype(BF16)
    own_ref[...] = rows_ref[: own_ref.shape[0], :]
    width = cols_ref.shape[2]
    for c in range(n_space):
        cols_ref[c] = cot[:, c * width : (c + 1) * width]
    for k in range(n_space):
        cot_refs[k][...] = cols_ref[me_s ^ k]
    wperm_ref[...] = mm(qkvw_ref[...], head_order(qkvw_ref.shape[1])).astype(BF16)


def head_order(width, size=64):
    heads = width // (3 * size)
    row, column = iota((width, width), 0), iota((width, width), 1)
    take = jnp.zeros((width, width), jnp.bool_)
    for h in range(heads):
        for c in range(3):
            start, target = h * 3 * size + c * size, c * heads * size + h * size
            inside = (column >= target) & (column < target + size)
            take = take | (inside & ((row - start) == (column - target)))
    return jnp.where(take, 1.0, 0.0).astype(BF16)


def forward_body(
    n_var, scale, me_ref, patches_ref, embed_ref, offset_ref, query_ref, wk_ref, wv_ref,
    tokens_ref, value_ref, scores_ref, wback_ref, *rest,
):
    send_refs, (wq_ref, max_ref, sum_ref, acc_ref, rows_ref) = rest[:n_var], rest[n_var:]
    v = pl.program_id(0)
    width = wv_ref.shape[1]
    size = width // HEADS

    @pl.when(v == 0)
    def _():
        fold = fold_matrix(width, size).astype(F32)
        hi, mid, lo = parts3(query_ref[...])
        wq = jnp.zeros((width, LANES), F32)
        for part in (hi, mid, lo):
            wq = wq + mm(wk_ref[...], (part * fold).astype(BF16))
        hi, mid, lo = parts3(wq * scale)
        wq_ref[:, :LANES] = hi.astype(BF16)
        wq_ref[:, LANES : 2 * LANES] = mid.astype(BF16)
        wq_ref[:, 2 * LANES :] = lo.astype(BF16)
        group = iota((width, LANES), 1) >> 4
        back = jnp.where((group == 0) | (group == 2), hi, jnp.where(group == 1, mid, 0.0))
        wback_ref[...] = back.astype(BF16)

    xor_rows(me_ref[0], patches_ref.at[0], rows_ref, n_var)
    tokens = (mm(rows_ref[...], embed_ref[0]) + offset_ref[0]).astype(BF16)
    tokens_ref[0] = tokens
    pieces = mm(tokens, wq_ref[...])
    scores = pieces[:, :LANES] + pieces[:, LANES : 2 * LANES] + pieces[:, 2 * LANES :]
    scores_ref[0] = scores
    value = mm(tokens, wv_ref[...])
    value_ref[0] = value

    @pl.when(v == 0)
    def _():
        max_ref[...] = scores
        sum_ref[...] = jnp.ones_like(scores)
        acc_ref[...] = value

    @pl.when(v > 0)
    def _():
        spread = spread_matrix(width, size)
        new_max = jnp.maximum(max_ref[...], scores)
        old = jnp.exp(max_ref[...] - new_max)
        new = jnp.exp(scores - new_max)
        max_ref[...] = new_max
        sum_ref[...] = sum_ref[...] * old + new
        acc_ref[...] = acc_ref[...] * mm(pack(old), spread) + value * mm(pack(new), spread)

    @pl.when(v == pl.num_programs(0) - 1)
    def _():
        block = send_refs[0].shape[0]
        low = iota((block, LANES), 1) < LANES // 2
        for k in range(n_var):
            rows = slice(k * block, (k + 1) * block)
            send_refs[k][:, :width] = acc_ref[rows, :]
            send_refs[k][:, width:] = jnp.where(low, max_ref[rows, :], sum_ref[rows, :])


def pool_body(n_var, *refs):
    ins, (mixed_ref, packet_ref) = refs[:n_var], refs[n_var:]
    width = mixed_ref.shape[1]
    low = iota((mixed_ref.shape[0], LANES), 1) < LANES // 2
    maxima, sums = [], []
    for ref in ins:
        both = ref[:, width:]
        turned = pltpu.roll(both, LANES // 2, 1)
        maxima.append(jnp.where(low, both, turned))
        sums.append(jnp.where(low, turned, both))
    top = functools.reduce(jnp.maximum, maxima)
    factors = [jnp.exp(m - top) for m in maxima]
    total = sum(s * f for s, f in zip(sums, factors))
    spread = spread_matrix(width, width // HEADS)
    mixed = jnp.zeros(mixed_ref.shape, F32)
    for ref, factor in zip(ins, factors):
        mixed = mixed + ref[:, :width] * mm(pack(factor / total), spread)
    mixed_ref[...] = mixed
    packet_ref[:, :width] = mixed.astype(BF16)
    packet_ref[:, width:] = pack(top, total)


def norm_body(n_var, n_space, me_ref, *refs):
    ins = refs[:n_var]
    agg_ref, gain_ref, w_ref, pooled_ref, stats_ref, qkv_ref, centred_ref, inv_ref = refs[n_var : n_var + 8]
    normed_refs, (cols_ref,) = refs[n_var + 8 : n_var + 8 + n_space], refs[n_var + 8 + n_space :]
    width = agg_ref.shape[0]
    block = ins[0].shape[0]
    for k in range(n_var):
        pooled_ref[k * block : (k + 1) * block, :] = ins[k][:, :width]
        stats_ref[k * block : (k + 1) * block, :] = ins[k][:, width:]
    joined = mm(pooled_ref[...], agg_ref[...]).astype(BF16).astype(F32)
    mean = jnp.mean(joined, axis=-1, keepdims=True)
    spread_sq = jnp.mean((joined - mean) ** 2, axis=-1, keepdims=True)
    inv = lax.rsqrt(spread_sq + EPSILON)
    centred = (joined - mean) * inv
    normed = (centred * gain_ref[...]).astype(BF16)
    qkv_ref[...] = mm(normed, w_ref[...]).astype(BF16)
    centred_ref[...] = centred[:block, :]
    inv_ref[...] = jnp.broadcast_to(inv[:block, :], inv_ref.shape)
    cols = cols_ref.shape[2]
    for c in range(n_space):
        cols_ref[c] = normed[:, c * cols : (c + 1) * cols]
    for k in range(n_space):
        normed_refs[k][...] = cols_ref[me_ref[1] ^ k]


def attention_body(n_var, n_space, size, scale, *refs):
    qkv_refs, dattn_refs = refs[:n_space], refs[n_space : 2 * n_space]
    w_ref, attn_ref, dqkv_ref = refs[2 * n_space : 2 * n_space + 3]
    dn_refs = refs[2 * n_space + 3 : 2 * n_space + 3 + n_var]
    k_ref, v_ref, dk_ref, dv_ref = refs[2 * n_space + 3 + n_var :]
    rows, group = dattn_refs[0].shape
    heads = group // size
    for b in range(n_space):
        at = slice(b * rows, (b + 1) * rows)
        k_ref[at, :] = qkv_refs[b][:, group : 2 * group]
        v_ref[at, :] = qkv_refs[b][:, 2 * group :]
    lane_head = iota((rows, group), 1) // size if heads > 1 else None
    for b in range(n_space):
        at = slice(b * rows, (b + 1) * rows)
        queries, d_out = qkv_refs[b][:, :group], dattn_refs[b][...]
        attn = dq = None
        for h in range(heads):
            if heads > 1:
                q_h = jnp.where(lane_head == h, queries.astype(F32), 0.0).astype(BF16)
                do_h = jnp.where(lane_head == h, d_out.astype(F32), 0.0).astype(BF16)
            else:
                q_h, do_h = queries, d_out
            logits = mm(q_h, k_ref[...], NT) * scale
            shifted = jnp.exp(logits - jnp.max(logits, axis=-1, keepdims=True))
            probs = shifted * (1.0 / jnp.sum(shifted, axis=-1, keepdims=True))
            probs_b = probs.astype(BF16)
            attn_h = mm(probs_b, v_ref[...])
            dprob = mm(do_h, v_ref[...], NT)
            delta = jnp.sum(probs * dprob, axis=-1, keepdims=True)
            dscore = (probs * (dprob - delta) * scale).astype(BF16)
            dq_h = mm(dscore, k_ref[...])
            dk = mm(dscore, q_h, TN)
            dv = mm(probs_b, do_h, TN)
            if b == 0 and h == 0:
                dk_ref[...] = dk
                dv_ref[...] = dv
            else:
                dk_ref[...] += dk
                dv_ref[...] += dv
            attn = attn_h if attn is None else jnp.where(lane_head == h, attn_h, attn)
            dq = dq_h if dq is None else jnp.where(lane_head == h, dq_h, dq)
        attn_ref[at, :] = attn.astype(BF16)
        dqkv_ref[at, :group] = dq.astype(BF16)
    dqkv_ref[:, group : 2 * group] = dk_ref[...].astype(BF16)
    dqkv_ref[:, 2 * group :] = dv_ref[...].astype(BF16)
    d_normed = mm(dqkv_ref[:rows, :], w_ref[...], NT).astype(BF16)
    block = dn_refs[0].shape[0]
    for k in range(n_var):
        dn_refs[k][...] = d_normed[k * block : (k + 1) * block, :]


def head_grads_body(n_space, *refs):
    normed_refs, cot_refs = refs[:n_space], refs[n_space : 2 * n_space]
    dqkv_ref, attn_ref, gqkv_ref, gout_ref = refs[2 * n_space :]
    rows = normed_refs[0].shape[0]
    order = head_order(dqkv_ref.shape[1])
    natural = mm(dqkv_ref[...], order, NT).astype(BF16)
    gqkv, gout = 0.0, 0.0
    for b in range(n_space):
        at = slice(b * rows, (b + 1) * rows)
        gqkv = gqkv + mm(normed_refs[b][...], natural[at, :], TN)
        gout = gout + mm(attn_ref[at, :], cot_refs[b][...], TN)
    gqkv_ref[...] = gqkv
    gout_ref[...] = gout


def joined_body(n_var, *refs):
    ins = refs[:n_var]
    centred_ref, inv_ref, gain_ref, cot_ref, mixed_ref, agg_ref, packet_ref, dgain_ref = refs[n_var:]
    width = agg_ref.shape[0]
    d_normed = ins[0][...].astype(F32)
    for ref in ins[1:]:
        d_normed = d_normed + ref[...].astype(F32)
    centred = centred_ref[...]
    dgain_ref[...] = jnp.broadcast_to(jnp.sum(d_normed * centred, axis=0, keepdims=True), dgain_ref.shape)
    gained = d_normed * gain_ref[...]
    inner = (
        gained
        - jnp.mean(gained, axis=-1, keepdims=True)
        - centred * jnp.mean(gained * centred, axis=-1, keepdims=True)
    )
    d_joined = (cot_ref[...].astype(F32) + inner * inv_ref[:, :1]).astype(BF16)
    d_pooled = mm(d_joined, agg_ref[...], NT)
    center = head_sums(d_pooled * mixed_ref[...], fold_matrix(width, width // HEADS))
    packet_ref[:, :width] = d_joined
    packet_ref[:, width:] = pack(center)


def backward_body(n_var, n_space, me_ref, *refs):
    packets = refs[:n_var]
    (
        stats_ref, tokens_ref, value_ref, scores_ref, patches_ref, wv_ref, wback_ref, agg_ref,
        djoined_ref, dvalue_ref, dlogit_ref,
    ) = refs[n_var : n_var + 11]
    grad_refs = refs[n_var + 11 : n_var + 11 + n_space]
    dpool_ref, stat_ref, rows_ref, cols_ref = refs[n_var + 11 + n_space :]
    width = agg_ref.shape[0]
    size = width // HEADS

    @pl.when(pl.program_id(0) == 0)
    def _():
        block = packets[0].shape[0]
        for k in range(n_var):
            at = slice(k * block, (k + 1) * block)
            djoined_ref[at, :] = packets[k][:, :width]
            stat_ref[0, at, :] = unpack(packets[k][:, width:])
        dpool_ref[...] = mm(djoined_ref[...], agg_ref[...], NT)
        stat_ref[1] = unpack(stats_ref[...], 0)
        stat_ref[2] = 1.0 / unpack(stats_ref[...], 3)

    xor_rows(me_ref[0], patches_ref.at[0], rows_ref, n_var)
    weight = jnp.exp(scores_ref[0] - stat_ref[1]) * stat_ref[2]
    dweight = head_sums(dpool_ref[...] * value_ref[0], fold_matrix(width, size))
    dlogit = weight * (dweight - stat_ref[0])
    hi = dlogit.astype(BF16).astype(F32)
    lo = (dlogit - hi).astype(BF16)
    dlogit_ref[0, :, :LANES] = hi.astype(BF16)
    dlogit_ref[0, :, LANES:] = lo
    group = iota(dlogit.shape, 1) >> 4
    mixed = jnp.where(group < 2, hi, jnp.where(group == 2, lo.astype(F32), 0.0)).astype(BF16)
    d_value = (mm(pack(weight), spread_matrix(width, size)) * dpool_ref[...]).astype(BF16)
    dvalue_ref[0] = d_value
    d_tokens = (mm(d_value, wv_ref[...], NT) + mm(mixed, wback_ref[...], NT)).astype(BF16)
    grad = mm(rows_ref[...], d_tokens, TN).astype(BF16)
    offset = jnp.sum(d_tokens.astype(F32), axis=0, keepdims=True)
    o_hi, o_mid, o_lo = parts3(offset)
    row = iota((16, width), 0)
    extra = jnp.where(row == 0, o_hi, jnp.where(row == 1, o_mid, jnp.where(row == 2, o_lo, 0.0)))
    extra = extra.astype(BF16)
    cols = cols_ref.shape[2]
    pixels = rows_ref.shape[1]
    for c in range(n_space):
        cols_ref[c, :pixels, :] = grad[:, c * cols : (c + 1) * cols]
        cols_ref[c, pixels:, :] = extra[:, c * cols : (c + 1) * cols]
    for k in range(n_space):
        grad_refs[k][0] = cols_ref[me_ref[1] ^ k]


def value_grad_body(n_var, me_ref, tokens_ref, dvalue_ref, dlogit_ref, *refs):
    out_refs, (all_ref,) = refs[:n_var], refs[n_var:]
    width = tokens_ref.shape[2]
    flat = tokens_ref.shape[0] * tokens_ref.shape[1]
    tokens = tokens_ref[...].reshape(flat, width)
    step = 256
    for c in range(0, width, step):
        all_ref[:, c : c + step] = mm(
            tokens, dvalue_ref[:, :, c : c + step].reshape(flat, step), TN
        ).astype(BF16)
    both = mm(tokens, dlogit_ref[...].reshape(flat, 2 * LANES), TN)
    all_ref[:, width:] = pack(both[:, :LANES] + both[:, LANES:])
    block = out_refs[0].shape[0]
    for k in range(n_var):
        start = pl.multiple_of((me_ref[0] ^ k) * block, block)
        out_refs[k][...] = all_ref[pl.ds(start, block), :]


def out_grad_body(n_space, me_ref, pooled_ref, djoined_ref, dgain_ref, *refs):
    out_refs, (all_ref, cols_ref) = refs[:n_space], refs[n_space:]
    all_ref[...] = mm(pooled_ref[...], djoined_ref[...], TN)
    cols = cols_ref.shape[2]
    block = out_refs[0].shape[0] - 16
    start = pl.multiple_of(me_ref[0] * block, block)
    own = all_ref[pl.ds(start, block), :].astype(BF16)
    hi, mid, lo = parts3(dgain_ref[:1, :])
    row = iota((16, dgain_ref.shape[1]), 0)
    extra = jnp.where(row == 0, hi, jnp.where(row == 1, mid, jnp.where(row == 2, lo, 0.0)))
    extra = extra.astype(BF16)
    for c in range(n_space):
        cols_ref[c, :block, :] = own[:, c * cols : (c + 1) * cols]
        cols_ref[c, block:, :] = extra[:, c * cols : (c + 1) * cols]
    for k in range(n_space):
        out_refs[k][...] = cols_ref[me_ref[1] ^ k]


def out_sum_body(n, *refs):
    total = refs[0][...].astype(F32)
    for ref in refs[1:n]:
        total = total + ref[...].astype(F32)
    out_ref = refs[n]
    block = out_ref.shape[0] - 16
    out_ref[:block, :] = total[:block, :].astype(BF16)
    hi, mid, lo = parts3(jnp.sum(total[block:, :], axis=0, keepdims=True))
    row = iota((16, out_ref.shape[1]), 0)
    extra = jnp.where(row == 0, hi, jnp.where(row == 1, mid, jnp.where(row == 2, lo, 0.0)))
    out_ref[block:, :] = extra.astype(BF16)


def out_final_body(n, me_ref, *refs):
    ins, (grad_ref, gain_ref) = refs[:n], refs[n:]
    block = ins[0].shape[0] - 16
    gain = 0.0
    for k in range(n):
        start = pl.multiple_of((me_ref[0] ^ k) * block, block)
        grad_ref[pl.ds(start, block), :] = ins[k][:block, :].astype(F32)
        gain = gain + jnp.sum(ins[k][block:, :].astype(F32), axis=0, keepdims=True)
    gain_ref[...] = gain


def packet_sum_body(n_out, n_in, *refs):
    width = refs[0].shape[1] - LANES
    for i in range(n_out):
        ins, out = refs[i * n_in : (i + 1) * n_in], refs[n_out * n_in + i]
        out[:, :width] = sum(ref[:, :width].astype(F32) for ref in ins).astype(BF16)
        out[:, width:] = pack(sum(unpack(ref[:, width:]) for ref in ins))


def packet_split_body(n_in, n_space, me_ref, *refs):
    ins, small_ref = refs[:n_in], refs[n_in]
    out_refs, (cols_ref,) = refs[n_in + 1 : n_in + 1 + n_space], refs[n_in + 1 + n_space :]
    width = ins[0].shape[1] - LANES
    total = sum(ref[:, :width].astype(F32) for ref in ins).astype(BF16)
    small_ref[...] = pack(sum(unpack(ref[:, width:]) for ref in ins))
    half = n_space // 2
    cols = cols_ref.shape[2]
    for c in range(half):
        cols_ref[c] = total[:, c * cols : (c + 1) * cols]
    for k in range(n_space):
        out_refs[k][...] = cols_ref[jnp.maximum((me_ref[1] ^ k) - half, 0)]


def space_sum_body(n, *refs):
    small, large, (small_ref, large_ref) = refs[:n], refs[n : 2 * n], refs[2 * n :]
    small_ref[...] = pack(sum(unpack(ref[...]) for ref in small))
    large_ref[...] = sum(ref[...].astype(F32) for ref in large).astype(BF16)


def final_body(n_var, n_space, scale, me_ref, *refs):
    small, large = refs[:n_var], refs[n_var : 2 * n_var]
    query_ref, wk_ref, kv_ref, gq_ref = refs[2 * n_var :]
    me_v, me_s = me_ref[0], me_ref[1]
    half = n_space // 2
    width = wk_ref.shape[1]
    size = width // HEADS
    cols, qcols = kv_ref.shape[1], gq_ref.shape[1]
    place = pl.multiple_of(jnp.minimum(me_s, half - 1) * cols, LANES)
    spread_kv = spread_matrix(cols, size, place)
    qplace = pl.multiple_of(me_s * qcols, LANES)
    spread_q = spread_matrix(qcols, size, qplace)
    query = query_ref[:, pl.ds(place, cols)] * scale
    block = small[0].shape[0]
    total = 0.0
    for k in range(n_var):
        start = pl.multiple_of((me_v ^ k) * block, block)
        packed = small[k][...]
        key_grad = mm(packed, spread_kv) * query
        kv_ref[pl.ds(start, block), :] = jnp.where(me_s < half, key_grad, large[k][...].astype(F32))
        keys = wk_ref[pl.ds(start, block), pl.ds(qplace, qcols)].astype(F32)
        total = total + jnp.sum(mm(packed, spread_q) * keys, axis=0, keepdims=True)
    gq_ref[...] = total * scale


def shards(
    patches, embed_weight, var_embed, agg_query, agg_kv, agg_out, norm_gain, qkv_weight, out_weight, cotangent
):
    n_var, n_space = lax.axis_size("var"), lax.axis_size("space")
    count, rows, pixels = patches.shape
    width = agg_out.shape[0]
    size = width // HEADS
    scale = 1.0 / math.sqrt(size)
    block = rows // n_var
    cols = width // n_space
    group = out_weight.shape[0]
    drows = width // n_var
    positions = rows * n_space
    kv_cols = 2 * width // n_space
    me = jnp.stack([lax.axis_index("var"), lax.axis_index("space")]).astype(jnp.int32)
    gain = norm_gain.reshape(1, width)

    dattn, cot_own, w_heads, *cot_cols = call(
        functools.partial(early_body, n_var, n_space),
        [struct((rows, group), BF16), struct((block, width), BF16), struct(qkv_weight.shape, BF16)]
        + [struct((rows, cols), BF16)] * n_space,
        in_specs=[SMEM] + [pl.BlockSpec(memory_space=pltpu.VMEM)] * 3,
        scratch_shapes=[pltpu.VMEM((rows, width), BF16), pltpu.VMEM((n_space, rows, cols), BF16)],
        cost_estimate=cost(2e8, 4e6),
        name="early",
    )(me, cotangent, out_weight, qkv_weight)
    dattn_all = gather_direct(dattn, "space")
    cot_all = exchange_direct(cot_cols, "space")

    whole = lambda shape: pl.BlockSpec(shape, lambda v: (0,) * len(shape))
    each = lambda shape: pl.BlockSpec((1,) + shape, lambda v: (v,) + (0,) * len(shape))
    packet = width + LANES
    tokens, value, scores, w_back, *sends = call(
        functools.partial(forward_body, n_var, scale),
        [
            struct((count, rows, width), BF16),
            struct((count, rows, width), F32),
            struct((count, rows, LANES), F32),
            struct((width, LANES), BF16),
        ]
        + [struct((block, packet), F32)] * n_var,
        limit=48,
        grid=(count,),
        in_specs=[
            SMEM,
            each((rows, pixels)),
            each((pixels, width)),
            each((1, width)),
            whole((width, 1)),
            pl.BlockSpec((width, width), lambda v: (0, 0)),
            pl.BlockSpec((width, width), lambda v: (0, 1)),
        ],
        out_specs=[each((rows, width)), each((rows, width)), each((rows, LANES)), whole((width, LANES))]
        + [whole((block, packet))] * n_var,
        scratch_shapes=[
            pltpu.VMEM((width, 3 * LANES), BF16),
            pltpu.VMEM((rows, LANES), F32),
            pltpu.VMEM((rows, LANES), F32),
            pltpu.VMEM((rows, width), F32),
            pltpu.VMEM((rows, pixels), BF16),
        ],
        cost_estimate=cost(6e9, 2e7),
        name="forward",
    )(me, patches, embed_weight, var_embed.reshape(count, 1, width), agg_query.reshape(width, 1), agg_kv, agg_kv)

    received = exchange_direct(sends, "var")
    mixed, pooled_packet = call(
        functools.partial(pool_body, n_var),
        [struct((block, width), F32), struct((block, packet), BF16)],
        cost_estimate=cost(1e8, 3e6),
        name="pool",
    )(*received)
    pooled_packets = gather_direct(pooled_packet, "var")

    vmem = pl.BlockSpec(memory_space=pltpu.VMEM)
    pooled, stats, qkv, centred, inv, *normed_cols = call(
        functools.partial(norm_body, n_var, n_space),
        [
            struct((rows, width), BF16),
            struct((rows, LANES), BF16),
            struct((rows, 3 * group), BF16),
            struct((block, width), F32),
            struct((block, LANES), F32),
        ]
        + [struct((rows, cols), BF16)] * n_space,
        in_specs=[SMEM] + [vmem] * (n_var + 3),
        scratch_shapes=[pltpu.VMEM((n_space, rows, cols), BF16)],
        cost_estimate=cost(8e8, 5e6),
        name="norm",
    )(me, *pooled_packets, agg_out, gain, w_heads)

    qkv_all = gather_direct(qkv, "space")
    normed_all = exchange_direct(normed_cols, "space")
    attn, dqkv, *dn_blocks = call(
        functools.partial(attention_body, n_var, n_space, size, scale),
        [struct((positions, group), BF16), struct((positions, 3 * group), BF16)]
        + [struct((block, width), BF16)] * n_var,
        limit=48,
        scratch_shapes=[pltpu.VMEM((positions, group), BF16)] * 2 + [pltpu.VMEM((positions, group), F32)] * 2,
        cost_estimate=cost(6e9, 4e6),
        name="attention",
    )(*qkv_all, *dattn_all, w_heads)

    dn_all = exchange_direct(dn_blocks, "var")
    grad_qkv, grad_out = call(
        functools.partial(head_grads_body, n_space),
        [struct((cols, 3 * group), F32), struct((group, cols), F32)],
        cost_estimate=cost(1e9, 3e6),
        name="head_grads",
    )(*normed_all, *cot_all, dqkv, attn)

    joined_packet, dgain = call(
        functools.partial(joined_body, n_var),
        [struct((block, packet), BF16), struct((8, width), F32)],
        cost_estimate=cost(2e8, 3e6),
        name="joined",
    )(*dn_all, centred, inv, gain, cot_own, mixed, agg_out)
    joined_packets = gather_direct(joined_packet, "var")

    d_joined, d_value, d_logit, *embed_blocks = call(
        functools.partial(backward_body, n_var, n_space),
        [
            struct((rows, width), BF16),
            struct((count, rows, width), BF16),
            struct((count, rows, 2 * LANES), BF16),
        ]
        + [struct((count, pixels + 16, cols), BF16)] * n_space,
        limit=48,
        grid=(count,),
        in_specs=[SMEM]
        + [whole((block, packet))] * n_var
        + [
            whole((rows, LANES)),
            each((rows, width)),
            each((rows, width)),
            each((rows, LANES)),
            each((rows, pixels)),
            pl.BlockSpec((width, width), lambda v: (0, 1)),
            whole((width, LANES)),
            whole((width, width)),
        ],
        out_specs=[whole((rows, width)), each((rows, width)), each((rows, 2 * LANES))]
        + [each((pixels + 16, cols))] * n_space,
        scratch_shapes=[
            pltpu.VMEM((rows, width), F32),
            pltpu.VMEM((3, rows, LANES), F32),
            pltpu.VMEM((rows, pixels), BF16),
            pltpu.VMEM((n_space, pixels + 16, cols), BF16),
        ],
        cost_estimate=cost(8e9, 2e7),
        name="backward",
    )(me, *joined_packets, stats, tokens, value, scores, patches, agg_kv, w_back, agg_out)

    blocks, bit = list(embed_blocks), 1
    mine = [blocks[0]]
    while bit < n_space:
        arrived = {k ^ bit: swap(blocks[k], "space", bit) for k in range(n_space) if k & bit and k % bit == 0}
        mine.append(arrived[0])
        for k in arrived:
            if k:
                blocks[k] = (blocks[k].astype(F32) + arrived[k].astype(F32)).astype(BF16)
        bit *= 2
    embed_sum = sum(part.astype(F32) for part in mine)
    grad_embed = embed_sum[:, :pixels, :]
    grad_var_embed = jnp.sum(embed_sum[:, pixels:, :], axis=1)

    kv_blocks = call(
        functools.partial(value_grad_body, n_var),
        [struct((drows, packet), BF16)] * n_var,
        limit=48,
        in_specs=[SMEM] + [vmem] * 3,
        scratch_shapes=[pltpu.VMEM((width, packet), BF16)],
        cost_estimate=cost(4e9, 1e7),
        name="value_grad",
    )(me, tokens, d_value, d_logit)
    pair = [swap(kv_blocks[k], "var", 1) for k in range(1, n_var, 2)]
    halves = call(
        functools.partial(packet_sum_body, n_var // 2, 2),
        [struct((drows, packet), BF16)] * (n_var // 2),
        cost_estimate=cost(1e7, 3e6),
        name="pair_sum",
    )(*[x for k in range(n_var // 2) for x in (kv_blocks[2 * k], pair[k])])
    kv_parts = [halves[0]] + [swap(halves[k], "var", 2 * k) for k in range(1, n_var // 2)]
    small, *large = call(
        functools.partial(packet_split_body, n_var // 2, n_space),
        [struct((drows, LANES), BF16)] + [struct((drows, kv_cols), BF16)] * n_space,
        in_specs=[SMEM] + [vmem] * (n_var // 2),
        scratch_shapes=[pltpu.VMEM((n_space // 2, drows, kv_cols), BF16)],
        cost_estimate=cost(1e7, 3e6),
        name="packet_split",
    )(me, *kv_parts)
    small_all = gather_direct(small, "space")
    large_all = [large[0]] + [
        swap(large[k], "space", k, lambda target: target >= n_space // 2) for k in range(1, n_space)
    ]
    small, large = call(
        functools.partial(space_sum_body, n_space),
        [struct((drows, LANES), BF16), struct((drows, kv_cols), BF16)],
        cost_estimate=cost(1e7, 1e6),
        name="space_sum",
    )(*small_all, *large_all)

    out_blocks = call(
        functools.partial(out_grad_body, n_space),
        [struct((drows + 16, cols), BF16)] * n_space,
        in_specs=[SMEM] + [vmem] * 3,
        scratch_shapes=[pltpu.VMEM((width, width), F32), pltpu.VMEM((n_space, drows + 16, cols), BF16)],
        cost_estimate=cost(6e8, 4e6),
        name="out_grad",
    )(me, pooled, d_joined, dgain)
    out_all = exchange_direct(out_blocks, "space")
    out_part = call(
        functools.partial(out_sum_body, n_space),
        struct((drows + 16, cols), BF16),
        cost_estimate=cost(1e6, 3e5),
        name="out_sum",
    )(*out_all)
    out_parts = gather_direct(out_part, "var")
    grad_agg_out, grad_gain = call(
        functools.partial(out_final_body, n_var),
        [struct((width, cols), F32), struct((1, cols), F32)],
        in_specs=[SMEM] + [vmem] * n_var,
        cost_estimate=cost(1e6, 2e6),
        name="out_final",
    )(me, *out_parts)

    smalls, larges = gather_pairs(small, "var"), gather_pairs(large, "var")
    grad_agg_kv, grad_query = call(
        functools.partial(final_body, n_var, n_space, scale),
        [struct((width, kv_cols), F32), struct((1, cols), F32)],
        grid=(1,),
        in_specs=[SMEM] + [vmem] * (2 * n_var + 1) + [pl.BlockSpec((width, width), lambda i: (0, 0))],
        cost_estimate=cost(2e8, 5e6),
        name="final",
    )(me, *smalls, *larges, agg_query.reshape(1, width), agg_kv)

    return (
        grad_embed,
        grad_var_embed,
        grad_query.reshape(cols),
        grad_agg_kv,
        grad_agg_out,
        grad_gain.reshape(cols),
        grad_qkv,
        grad_out,
    )


def solution(mesh):
    return jax.shard_map(
        shards,
        mesh=mesh,
        in_specs=(
            P("var", "space", None),
            P("var", None, None),
            P("var", None),
            P(),
            P(),
            P(),
            P(),
            P(None, "var"),
            P("var", None),
            P("space", None),
        ),
        out_specs=(
            P("var", None, "space"),
            P("var", "space"),
            P("space"),
            P(None, "space"),
            P(None, "space"),
            P("space"),
            P("space", "var"),
            P("var", "space"),
        ),
        check_vma=False,
    )
```

```python
import functools
import math

import jax
import jax.numpy as jnp
from jax import lax
from jax.experimental import pallas as pl
from jax.experimental.pallas import tpu as pltpu
from jax.sharding import PartitionSpec as P

HEADS = 16
LANES = 128
EPSILON = 1e-05
MIB = 1 << 20

F32 = jnp.float32
BF16 = jnp.bfloat16

NN = (((1,), (0,)), ((), ()))
NT = (((1,), (1,)), ((), ()))
TN = (((0,), (0,)), ((), ()))


def mm(a, b, dims=NN):
    return lax.dot_general(a, b, dims, preferred_element_type=F32)


def iota(shape, axis):
    return lax.broadcasted_iota(jnp.int32, shape, axis)


def parts3(x):
    hi = x.astype(BF16).astype(F32)
    rest = x - hi
    mid = rest.astype(BF16).astype(F32)
    return hi, mid, rest - mid


def pack(x, y=None):
    group = iota(x.shape, 1) >> 4
    hi, mid, lo = parts3(x)
    out = jnp.where(group == 0, hi, jnp.where(group == 1, mid, jnp.where(group == 2, lo, 0.0)))
    if y is not None:
        hi, mid, lo = parts3(y)
        out = jnp.where(group == 3, hi, jnp.where(group == 4, mid, jnp.where(group == 5, lo, out)))
    return out.astype(BF16)


def unpack(packed, first_group=0):
    row, column = iota((LANES, LANES), 0), iota((LANES, LANES), 1)
    group = row >> 4
    take = ((row & 15) == (column & 15)) & (group >= first_group) & (group < first_group + 3)
    return mm(packed, jnp.where(take, 1.0, 0.0).astype(BF16))


def spread_matrix(width, size, first=0):
    row, column = iota((LANES, width), 0), iota((LANES, width), 1)
    shift = size.bit_length() - 1
    take = ((row & 15) == ((column + first) >> shift)) & (row < 48)
    return jnp.where(take, 1.0, 0.0).astype(BF16)


def fold_matrix(width, size):
    row, column = iota((width, LANES), 0), iota((width, LANES), 1)
    shift = size.bit_length() - 1
    return jnp.where((column & 15) == (row >> shift), 1.0, 0.0).astype(BF16)


def head_sums(x, fold):
    hi, mid, lo = parts3(x)
    return mm(hi.astype(BF16), fold) + mm(mid.astype(BF16), fold) + mm(lo.astype(BF16), fold)


def call(body, out_shape, limit=32, after=(), in_specs=None, **kw):
    def run(*args):
        n, m = len(args), len(after)
        specs = [pl.BlockSpec(memory_space=pltpu.VMEM)] * n if in_specs is None else list(in_specs)
        return pl.pallas_call(
            lambda *refs: body(*refs[:n], *refs[n + m :]),
            out_shape=out_shape,
            in_specs=specs + [pl.BlockSpec(memory_space=pl.ANY)] * m,
            compiler_params=pltpu.CompilerParams(vmem_limit_bytes=limit * MIB),
            **kw,
        )(*args, *after)

    return run


def struct(shape, dtype):
    return jax.ShapeDtypeStruct(shape, dtype)


def cost(flops, moved):
    return pl.CostEstimate(flops=int(flops), bytes_accessed=int(moved), transcendentals=0)


SMEM = pl.BlockSpec(memory_space=pltpu.SMEM)


def swap(x, axis, k, keep=None):
    pairs = [(i, i ^ k) for i in range(lax.axis_size(axis))]
    if keep is not None:
        pairs = [pair for pair in pairs if keep(pair[1])]
    return lax.ppermute(x, axis, pairs)


def gather_direct(x, axis):
    return [x] + [swap(x, axis, k) for k in range(1, lax.axis_size(axis))]


def exchange_direct(blocks, axis):
    return [blocks[0]] + [swap(blocks[k], axis, k) for k in range(1, len(blocks))]


def gather_pairs(x, axis):
    even = jnp.stack([x if k == 0 else swap(x, axis, k) for k in range(0, lax.axis_size(axis), 2)])
    return even, swap(even, axis, 1)


def exchange_all(x, axis):
    return lax.all_to_all(x, axis, split_axis=0, concat_axis=0, tiled=True)


def three_rows(x):
    hi, mid, lo = parts3(x)
    row = iota((16, x.shape[1]), 0)
    return jnp.where(row == 0, hi, jnp.where(row == 1, mid, jnp.where(row == 2, lo, 0.0))).astype(BF16)


def head_order(width, size=64):
    heads = width // (3 * size)
    row, column = iota((width, width), 0), iota((width, width), 1)
    take = jnp.zeros((width, width), jnp.bool_)
    for h in range(heads):
        for c in range(3):
            start, target = h * 3 * size + c * size, c * heads * size + h * size
            inside = (column >= target) & (column < target + size)
            take = take | (inside & ((row - start) == (column - target)))
    return jnp.where(take, 1.0, 0.0).astype(BF16)


def early_body(n_space, me_ref, cot_ref, outw_ref, qkvw_ref, dattn_ref, own_ref, wperm_ref, *rest):
    cot_refs, (cols_ref,) = rest[:n_space], rest[n_space:]
    dattn_ref[...] = mm(cot_ref[...], outw_ref[...], NT).astype(BF16)
    block = own_ref.shape[0]
    own_ref[...] = cot_ref[pl.ds(pl.multiple_of(me_ref[0] * block, block), block), :]
    width = cols_ref.shape[2]
    for c in range(n_space):
        cols_ref[c] = cot_ref[:, c * width : (c + 1) * width]
    for k in range(n_space):
        cot_refs[k][...] = cols_ref[me_ref[1] ^ k]
    wperm_ref[...] = mm(qkvw_ref[...], head_order(qkvw_ref.shape[1])).astype(BF16)


def forward_body(
    count, scale, patches_ref, embed_ref, offset_ref, query_ref, wk_ref, wv_ref,
    tokens_ref, value_ref, scores_ref, wback_ref, send_ref, wq_ref, held_ref, max_ref, spread_ref, acc_ref,
):
    i = pl.program_id(0)
    width = wv_ref.shape[1]
    size = width // HEADS

    @pl.when(i == 0)
    def _():
        row, column = iota((LANES, width), 0), iota((LANES, width), 1)
        own = (row & 15) == (column >> (size.bit_length() - 1))
        wq = jnp.zeros((width, LANES), F32)
        for part in parts3(query_ref[...]):
            wq = wq + mm(wk_ref[...], jnp.where(own, part, 0.0).astype(BF16), NT)
        hi, mid, lo = parts3(wq * scale)
        wq_ref[:, :LANES] = hi.astype(BF16)
        wq_ref[:, LANES : 2 * LANES] = mid.astype(BF16)
        wq_ref[:, 2 * LANES :] = lo.astype(BF16)
        group = iota((width, LANES), 1) >> 4
        back = jnp.where((group == 0) | (group == 2), hi, jnp.where(group == 1, mid, 0.0))
        wback_ref[...] = back.astype(BF16)
        spread_ref[...] = spread_matrix(width, size)

    @pl.when(i < count)
    def _():
        tokens = (mm(patches_ref[0], embed_ref[0]) + offset_ref[pl.ds(i, 1), :]).astype(BF16)
        tokens_ref[0] = tokens
        held_ref[i] = tokens
        pieces = mm(tokens, wq_ref[...])
        scores_ref[i] = pieces[:, :LANES] + pieces[:, LANES : 2 * LANES] + pieces[:, 2 * LANES :]

    @pl.when(i >= count)
    def _():
        j = i - count
        top = scores_ref[0]
        for v in range(1, count):
            top = jnp.maximum(top, scores_ref[v])
        max_ref[...] = top
        value = mm(held_ref[j], wv_ref[...])
        value_ref[0] = value
        term = mm(pack(jnp.exp(scores_ref[j] - top)), spread_ref[...]) * value

        @pl.when(j == 0)
        def _():
            acc_ref[...] = term

        @pl.when(j > 0)
        def _():
            acc_ref[...] += term

    @pl.when(i == 2 * count - 1)
    def _():
        top = max_ref[...]
        total = sum(jnp.exp(scores_ref[v] - top) for v in range(count))
        low = iota(top.shape, 1) < LANES // 2
        send_ref[:, :width] = acc_ref[...]
        send_ref[:, width:] = jnp.where(low, top, total)


def pool_body(n_var, in_ref, mixed_ref, packet_ref):
    block, width = mixed_ref.shape
    low = iota((block, LANES), 1) < LANES // 2
    maxima, sums = [], []
    for k in range(n_var):
        both = in_ref[k * block : (k + 1) * block, width:]
        turned = pltpu.roll(both, LANES // 2, 1)
        maxima.append(jnp.where(low, both, turned))
        sums.append(jnp.where(low, turned, both))
    top = functools.reduce(jnp.maximum, maxima)
    factors = [jnp.exp(m - top) for m in maxima]
    total = sum(s * f for s, f in zip(sums, factors))
    spread = spread_matrix(width, width // HEADS)
    mixed = jnp.zeros(mixed_ref.shape, F32)
    for k, factor in enumerate(factors):
        mixed = mixed + in_ref[k * block : (k + 1) * block, :width] * mm(pack(factor / total), spread)
    mixed_ref[...] = mixed
    pooled, stats = mixed.astype(BF16), pack(top, total)
    for k in range(n_var):
        packet_ref[k * block : (k + 1) * block, :width] = pooled
        packet_ref[k * block : (k + 1) * block, width:] = stats


def norm_body(me_ref, in_ref, agg_ref, gain_ref, w_ref, qkv_ref, normed_ref, centred_ref, inv_ref, all_ref, allinv_ref):
    width = agg_ref.shape[0]
    block = centred_ref.shape[0]
    joined = mm(in_ref[:, :width], agg_ref[...]).astype(BF16).astype(F32)
    mean = jnp.mean(joined, axis=-1, keepdims=True)
    spread_sq = jnp.mean((joined - mean) ** 2, axis=-1, keepdims=True)
    inv = lax.rsqrt(spread_sq + EPSILON)
    centred = (joined - mean) * inv
    normed = (centred * gain_ref[...]).astype(BF16)
    qkv_ref[...] = mm(normed, w_ref[...]).astype(BF16)
    normed_ref[...] = normed
    all_ref[...] = centred
    allinv_ref[...] = jnp.broadcast_to(inv, allinv_ref.shape)
    start = pl.multiple_of(me_ref[0] * block, block)
    centred_ref[...] = all_ref[pl.ds(start, block), :]
    inv_ref[...] = allinv_ref[pl.ds(start, block), :]


def attention_body(n_space, size, scale, me_ref, *refs):
    qkv_refs, dattn_refs = refs[:n_space], refs[n_space : 2 * n_space]
    w_ref, normed_ref, attn_ref, dqkv_ref, dn_ref = refs[2 * n_space : 2 * n_space + 5]
    normed_refs = refs[2 * n_space + 5 : 3 * n_space + 5]
    k_ref, v_ref, dk_ref, dv_ref, cols_ref = refs[3 * n_space + 5 :]
    rows, group = dattn_refs[0].shape
    heads = group // size
    for b in range(n_space):
        at = slice(b * rows, (b + 1) * rows)
        k_ref[at, :] = qkv_refs[b][:, group : 2 * group]
        v_ref[at, :] = qkv_refs[b][:, 2 * group :]
    lane_head = iota((rows, group), 1) // size if heads > 1 else None
    for b in range(n_space):
        at = slice(b * rows, (b + 1) * rows)
        queries, d_out = qkv_refs[b][:, :group], dattn_refs[b][...]
        attn = dq = None
        for h in range(heads):
            if heads > 1:
                q_h = jnp.where(lane_head == h, queries.astype(F32), 0.0).astype(BF16)
                do_h = jnp.where(lane_head == h, d_out.astype(F32), 0.0).astype(BF16)
            else:
                q_h, do_h = queries, d_out
            logits = mm(q_h, k_ref[...], NT) * scale
            shifted = jnp.exp(logits - jnp.max(logits, axis=-1, keepdims=True))
            probs = shifted * (1.0 / jnp.sum(shifted, axis=-1, keepdims=True))
            probs_b = probs.astype(BF16)
            attn_h = mm(probs_b, v_ref[...])
            dprob = mm(do_h, v_ref[...], NT)
            delta = jnp.sum(probs * dprob, axis=-1, keepdims=True)
            dscore = (probs * (dprob - delta) * scale).astype(BF16)
            dq_h = mm(dscore, k_ref[...])
            dk = mm(dscore, q_h, TN)
            dv = mm(probs_b, do_h, TN)
            if b == 0 and h == 0:
                dk_ref[...] = dk
                dv_ref[...] = dv
            else:
                dk_ref[...] += dk
                dv_ref[...] += dv
            attn = attn_h if attn is None else jnp.where(lane_head == h, attn_h, attn)
            dq = dq_h if dq is None else jnp.where(lane_head == h, dq_h, dq)
        attn_ref[at, :] = attn.astype(BF16)
        dqkv_ref[at, :group] = dq.astype(BF16)
    dqkv_ref[:, group : 2 * group] = dk_ref[...].astype(BF16)
    dqkv_ref[:, 2 * group :] = dv_ref[...].astype(BF16)
    dn_ref[...] = mm(dqkv_ref[:rows, :], w_ref[...], NT).astype(BF16)
    cols = cols_ref.shape[2]
    for c in range(n_space):
        cols_ref[c] = normed_ref[:, c * cols : (c + 1) * cols]
    for k in range(n_space):
        normed_refs[k][...] = cols_ref[me_ref[1] ^ k]


def head_grads_body(n_space, *refs):
    normed_refs, cot_refs = refs[:n_space], refs[n_space : 2 * n_space]
    dqkv_ref, attn_ref, gqkv_ref, gout_ref = refs[2 * n_space :]
    rows = normed_refs[0].shape[0]
    order = head_order(dqkv_ref.shape[1])
    natural = mm(dqkv_ref[...], order, NT).astype(BF16)
    gqkv, gout = 0.0, 0.0
    for b in range(n_space):
        at = slice(b * rows, (b + 1) * rows)
        gqkv = gqkv + mm(normed_refs[b][...], natural[at, :], TN)
        gout = gout + mm(attn_ref[at, :], cot_refs[b][...], TN)
    gqkv_ref[...] = gqkv
    gout_ref[...] = gout


def joined_body(n_var, in_ref, centred_ref, inv_ref, gain_ref, cot_ref, mixed_ref, agg_ref, packet_ref, dgain_ref):
    block, width = centred_ref.shape
    d_normed = in_ref[:block, :].astype(F32)
    for k in range(1, n_var):
        d_normed = d_normed + in_ref[k * block : (k + 1) * block, :].astype(F32)
    centred = centred_ref[...]
    dgain_ref[...] = jnp.broadcast_to(jnp.sum(d_normed * centred, axis=0, keepdims=True), dgain_ref.shape)
    gained = d_normed * gain_ref[...]
    inner = (
        gained
        - jnp.mean(gained, axis=-1, keepdims=True)
        - centred * jnp.mean(gained * centred, axis=-1, keepdims=True)
    )
    d_joined = (cot_ref[...].astype(F32) + inner * inv_ref[:, :1]).astype(BF16)
    d_pooled = mm(d_joined, agg_ref[...], NT)
    center = pack(head_sums(d_pooled * mixed_ref[...], fold_matrix(width, width // HEADS)))
    for k in range(n_var):
        packet_ref[k * block : (k + 1) * block, :width] = d_joined
        packet_ref[k * block : (k + 1) * block, width:] = center


def out_grad_body(n_space, me_ref, pooled_ref, djoined_ref, dgain_ref, agg_ref, dpool_ref, stat_ref, *refs):
    out_refs, (all_ref, cols_ref) = refs[:n_space], refs[n_space:]
    width = agg_ref.shape[0]
    all_ref[...] = mm(pooled_ref[:, :width], djoined_ref[:, :width], TN)
    cols = cols_ref.shape[2]
    block = out_refs[0].shape[0] - 16
    start = pl.multiple_of(me_ref[0] * block, block)
    own = all_ref[pl.ds(start, block), :].astype(BF16)
    extra = three_rows(dgain_ref[:1, :])
    for c in range(n_space):
        cols_ref[c, :block, :] = own[:, c * cols : (c + 1) * cols]
        cols_ref[c, block:, :] = extra[:, c * cols : (c + 1) * cols]
    for k in range(n_space):
        out_refs[k][...] = cols_ref[me_ref[1] ^ k]
    dpool_ref[...] = mm(djoined_ref[:, :width], agg_ref[...], NT)
    stat_ref[0] = unpack(djoined_ref[:, width:])
    stat_ref[1] = unpack(pooled_ref[:, width:])
    stat_ref[2] = 1.0 / unpack(pooled_ref[:, width:], 3)


def backward_body(
    n_space, me_ref, dpool_ref, stat_ref, tokens_ref, value_ref, scores_ref, patches_ref, wv_ref, wback_ref,
    dvalue_ref, dlogit_ref, keep_ref, send_ref, spread_ref, fold_ref, cols_ref,
):
    width = wv_ref.shape[0]
    size = width // HEADS

    @pl.when(pl.program_id(0) == 0)
    def _():
        spread_ref[...] = spread_matrix(width, size)
        fold_ref[...] = fold_matrix(width, size)

    weight = jnp.exp(scores_ref[0] - stat_ref[1]) * stat_ref[2]
    d_value = (mm(pack(weight), spread_ref[...]) * dpool_ref[...]).astype(BF16)
    dvalue_ref[0] = d_value
    dweight = head_sums(dpool_ref[...] * value_ref[0], fold_ref[...])
    dlogit = weight * (dweight - stat_ref[0])
    hi = dlogit.astype(BF16).astype(F32)
    lo = (dlogit - hi).astype(BF16)
    dlogit_ref[0, :, :LANES] = hi.astype(BF16)
    dlogit_ref[0, :, LANES:] = lo
    group = iota(dlogit.shape, 1) >> 4
    mixed = jnp.where(group < 2, hi, jnp.where(group == 2, lo.astype(F32), 0.0)).astype(BF16)
    d_tokens = (mm(d_value, wv_ref[...], NT) + mm(mixed, wback_ref[...], NT)).astype(BF16)
    grad = mm(patches_ref[0], d_tokens, TN).astype(BF16)
    extra = three_rows(jnp.sum(d_tokens.astype(F32), axis=0, keepdims=True))
    cols = cols_ref.shape[2]
    pixels = patches_ref.shape[2]
    for c in range(n_space):
        cols_ref[c, :pixels, :] = grad[:, c * cols : (c + 1) * cols]
        cols_ref[c, pixels:, :] = extra[:, c * cols : (c + 1) * cols]
    for k in range(0, n_space, 2):
        keep_ref[k // 2, 0] = cols_ref[me_ref[1] ^ k]
        send_ref[k // 2, 0] = cols_ref[me_ref[1] ^ (k + 1)]


def embed_final_body(parts, *refs):
    ins, (grad_ref, offset_ref) = refs[:-2], refs[-2:]
    pixels = grad_ref.shape[1]
    base = 0
    for half in range(2):
        mine = ins[half * parts : (half + 1) * parts]
        for v in range(mine[0].shape[1]):
            total = 0.0
            for ref in mine:
                total = total + (ref[0, v] if len(ref.shape) == 4 else ref[v]).astype(F32)
            grad_ref[base + v] = total[:pixels, :]
            offset_ref[base + v : base + v + 1, :] = jnp.sum(total[pixels:, :], axis=0, keepdims=True)
        base += mine[0].shape[1]


def value_grad_body(n_var, me_ref, tokens_ref, dv0_ref, dv1_ref, dl0_ref, dl1_ref, keep_ref, send_ref, all_ref):
    width = dv0_ref.shape[2]
    flat = lambda ref: ref[...].reshape(ref.shape[0] * ref.shape[1], ref.shape[2])
    tokens = flat(tokens_ref)
    middle = dv0_ref.shape[0] * dv0_ref.shape[1]
    first, second = tokens[:middle, :], tokens[middle:, :]
    all_ref[:, :width] = (mm(first, flat(dv0_ref), TN) + mm(second, flat(dv1_ref), TN)).astype(BF16)
    both = mm(first, flat(dl0_ref), TN) + mm(second, flat(dl1_ref), TN)
    all_ref[:, width:] = pack(both[:, :LANES] + both[:, LANES:])
    block = keep_ref.shape[1]
    count = all_ref.shape[0] // block
    for r in range(count):
        target = pl.program_id(0) * count + r
        same = (target & 1) == (me_ref[0] & 1)
        slot = target >> 1

        @pl.when(same)
        def _():
            keep_ref[slot] = all_ref[r * block : (r + 1) * block, :]

        @pl.when(jnp.logical_not(same))
        def _():
            send_ref[slot] = all_ref[r * block : (r + 1) * block, :]


def pair_sum_body(n_chip, me_ref, keep_ref, got_ref, *out_refs):
    width = keep_ref.shape[2] - LANES
    for k in range(n_chip):
        slot = (me_ref[0] >> 1) ^ k
        mine, other = keep_ref[slot], got_ref[slot]
        out_refs[k][:, :width] = (mine[:, :width].astype(F32) + other[:, :width].astype(F32)).astype(BF16)
        out_refs[k][:, width:] = pack(unpack(mine[:, width:]) + unpack(other[:, width:]))


def out_sum_body(n, *refs):
    total = refs[0][...].astype(F32)
    for ref in refs[1:n]:
        total = total + ref[...].astype(F32)
    out_ref = refs[n]
    block = out_ref.shape[0] - 16
    out_ref[:block, :] = total[:block, :].astype(BF16)
    out_ref[block:, :] = three_rows(jnp.sum(total[block:, :], axis=0, keepdims=True))


def out_final_body(n, me_ref, even_ref, odd_ref, grad_ref, gain_ref):
    block = even_ref.shape[1] - 16
    gain = 0.0
    for k in range(n):
        part = (odd_ref if k % 2 else even_ref)[k // 2].astype(F32)
        start = pl.multiple_of((me_ref[0] ^ k) * block, block)
        grad_ref[pl.ds(start, block), :] = part[:block, :]
        gain = gain + jnp.sum(part[block:, :], axis=0, keepdims=True)
    gain_ref[...] = gain


def packet_split_body(n_in, n_space, me_ref, *refs):
    ins, small_ref = refs[:n_in], refs[n_in]
    out_refs, (cols_ref,) = refs[n_in + 1 : n_in + 1 + n_space], refs[n_in + 1 + n_space :]
    width = ins[0].shape[1] - LANES
    total = sum(ref[:, :width].astype(F32) for ref in ins).astype(BF16)
    small_ref[...] = pack(sum(unpack(ref[:, width:]) for ref in ins))
    half = n_space // 2
    cols = cols_ref.shape[2]
    for c in range(half):
        cols_ref[c] = total[:, c * cols : (c + 1) * cols]
    for k in range(n_space):
        out_refs[k][...] = cols_ref[jnp.maximum((me_ref[1] ^ k) - half, 0)]


def space_sum_body(n, *refs):
    small, large, out_ref = refs[:n], refs[n : 2 * n], refs[2 * n]
    width = large[0].shape[1]
    out_ref[:, :width] = sum(ref[...].astype(F32) for ref in large).astype(BF16)
    out_ref[:, width:] = pack(sum(unpack(ref[...]) for ref in small))


def final_body(n_var, n_space, scale, me_ref, even_ref, odd_ref, query_ref, wk_ref, kv_ref, gq_ref):
    me_v, me_s = me_ref[0], me_ref[1]
    half = n_space // 2
    width = wk_ref.shape[1]
    size = width // HEADS
    cols, qcols = kv_ref.shape[1], gq_ref.shape[1]
    place = pl.multiple_of(jnp.minimum(me_s, half - 1) * cols, LANES)
    spread_kv = spread_matrix(cols, size, place)
    qplace = pl.multiple_of(me_s * qcols, LANES)
    spread_q = spread_matrix(qcols, size, qplace)
    query = query_ref[:, pl.ds(place, cols)] * scale
    block = even_ref.shape[1]
    total = 0.0
    for k in range(n_var):
        part = (odd_ref if k % 2 else even_ref)[k // 2]
        start = pl.multiple_of((me_v ^ k) * block, block)
        packed = part[:, cols:]
        key_grad = mm(packed, spread_kv) * query
        kv_ref[pl.ds(start, block), :] = jnp.where(me_s < half, key_grad, part[:, :cols].astype(F32))
        keys = wk_ref[pl.ds(start, block), pl.ds(qplace, qcols)].astype(F32)
        total = total + jnp.sum(mm(packed, spread_q) * keys, axis=0, keepdims=True)
    gq_ref[...] = total * scale


def shards(
    patches, embed_weight, var_embed, agg_query, agg_kv, agg_out, norm_gain, qkv_weight, out_weight, cotangent
):
    n_var, n_space = lax.axis_size("var"), lax.axis_size("space")
    count, rows, pixels = patches.shape
    width = agg_out.shape[0]
    size = width // HEADS
    scale = 1.0 / math.sqrt(size)
    block = rows // n_var
    cols = width // n_space
    group = out_weight.shape[0]
    drows = width // n_var
    positions = rows * n_space
    kv_cols = 2 * width // n_space
    me = jnp.stack([lax.axis_index("var"), lax.axis_index("space")]).astype(jnp.int32)
    gain = norm_gain.reshape(1, width)
    query = agg_query.reshape(1, width)
    vmem = pl.BlockSpec(memory_space=pltpu.VMEM)
    packet = width + LANES

    dattn, cot_own, w_heads, *cot_cols = call(
        functools.partial(early_body, n_space),
        [struct((rows, group), BF16), struct((block, width), BF16), struct(qkv_weight.shape, BF16)]
        + [struct((rows, cols), BF16)] * n_space,
        in_specs=[SMEM] + [vmem] * 3,
        scratch_shapes=[pltpu.VMEM((n_space, rows, cols), BF16)],
        cost_estimate=cost(2e8, 4e6),
        name="early",
    )(me, cotangent, out_weight, qkv_weight)
    dattn_all = gather_direct(dattn, "space")
    cot_all = exchange_direct(cot_cols, "space")

    whole = lambda shape: pl.BlockSpec(shape, lambda v: (0,) * len(shape))
    last = count - 1
    first_pass = lambda shape: pl.BlockSpec((1,) + shape, lambda i: (jnp.minimum(i, last),) + (0,) * len(shape))
    second_pass = lambda shape: pl.BlockSpec((1,) + shape, lambda i: (jnp.maximum(i - count, 0),) + (0,) * len(shape))
    tokens, value, scores, w_back, send = call(
        functools.partial(forward_body, count, scale),
        [
            struct((count, rows, width), BF16),
            struct((count, rows, width), F32),
            struct((count, rows, LANES), F32),
            struct((width, LANES), BF16),
            struct((rows, packet), F32),
        ],
        limit=48,
        grid=(2 * count,),
        in_specs=[
            first_pass((rows, pixels)),
            first_pass((pixels, width)),
            whole((count, width)),
            whole((1, width)),
            pl.BlockSpec((width, width), lambda v: (0, 0)),
            pl.BlockSpec((width, width), lambda v: (0, 1)),
        ],
        after=[dattn],
        out_specs=[
            first_pass((rows, width)),
            second_pass((rows, width)),
            whole((count, rows, LANES)),
            whole((width, LANES)),
            whole((rows, packet)),
        ],
        scratch_shapes=[
            pltpu.VMEM((width, 3 * LANES), BF16),
            pltpu.VMEM((count, rows, width), BF16),
            pltpu.VMEM((rows, LANES), F32),
            pltpu.VMEM((LANES, width), BF16),
            pltpu.VMEM((rows, width), F32),
        ],
        cost_estimate=cost(6e9, 2e7),
        name="forward",
    )(patches, embed_weight, var_embed, query, agg_kv, agg_kv)

    received = exchange_all(send, "var")
    mixed, pooled_copies = call(
        functools.partial(pool_body, n_var),
        [struct((block, width), F32), struct((rows, packet), BF16)],
        after=dattn_all[1:] + cot_all[1:],
        cost_estimate=cost(1e8, 3e6),
        name="pool",
    )(received)
    pooled_packets = exchange_all(pooled_copies, "var")

    qkv, normed, centred, inv = call(
        norm_body,
        [
            struct((rows, 3 * group), BF16),
            struct((rows, width), BF16),
            struct((block, width), F32),
            struct((block, LANES), F32),
        ],
        in_specs=[SMEM] + [vmem] * 4,
        scratch_shapes=[pltpu.VMEM((rows, width), F32), pltpu.VMEM((rows, LANES), F32)],
        cost_estimate=cost(8e8, 5e6),
        name="norm",
    )(me, pooled_packets, agg_out, gain, w_heads)

    qkv_all = gather_direct(qkv, "space")
    attn, dqkv, d_normed, *normed_cols = call(
        functools.partial(attention_body, n_space, size, scale),
        [struct((positions, group), BF16), struct((positions, 3 * group), BF16), struct((rows, width), BF16)]
        + [struct((rows, cols), BF16)] * n_space,
        limit=48,
        in_specs=[SMEM] + [vmem] * (2 * n_space + 2),
        scratch_shapes=[pltpu.VMEM((positions, group), BF16)] * 2
        + [pltpu.VMEM((positions, group), F32)] * 2
        + [pltpu.VMEM((n_space, rows, cols), BF16)],
        cost_estimate=cost(6e9, 4e6),
        name="attention",
    )(me, *qkv_all, *dattn_all, w_heads, normed)

    dn_received = exchange_all(d_normed, "var")
    normed_all = exchange_direct(normed_cols, "space")
    joined_copies, dgain = call(
        functools.partial(joined_body, n_var),
        [struct((rows, packet), BF16), struct((8, width), F32)],
        after=normed_all[1:],
        cost_estimate=cost(2e8, 3e6),
        name="joined",
    )(dn_received, centred, inv, gain, cot_own, mixed, agg_out)
    joined_packets = exchange_all(joined_copies, "var")

    d_pooled, stat, *out_blocks = call(
        functools.partial(out_grad_body, n_space),
        [struct((rows, width), F32), struct((3, rows, LANES), F32)] + [struct((drows + 16, cols), BF16)] * n_space,
        in_specs=[SMEM] + [vmem] * 4,
        scratch_shapes=[pltpu.VMEM((width, width), F32), pltpu.VMEM((n_space, drows + 16, cols), BF16)],
        cost_estimate=cost(1e9, 5e6),
        name="out_grad",
    )(me, pooled_packets, joined_packets, dgain, agg_out)
    out_all = exchange_direct(out_blocks, "space")

    def backward(start, size_here, after):
        each = lambda shape: pl.BlockSpec((1,) + shape, lambda v: (v + start,) + (0,) * len(shape))
        here = lambda shape: pl.BlockSpec((1,) + shape, lambda v: (v,) + (0,) * len(shape))
        blocks = pl.BlockSpec((n_space // 2, 1, pixels + 16, cols), lambda v: (0, v, 0, 0))
        return call(
            functools.partial(backward_body, n_space),
            [struct((size_here, rows, width), BF16), struct((size_here, rows, 2 * LANES), BF16)]
            + [struct((n_space // 2, size_here, pixels + 16, cols), BF16)] * 2,
            limit=40,
            grid=(size_here,),
            in_specs=[
                SMEM,
                whole((rows, width)),
                whole((3, rows, LANES)),
                each((rows, width)),
                each((rows, width)),
                each((rows, LANES)),
                each((rows, pixels)),
                pl.BlockSpec((width, width), lambda v: (0, 1)),
                whole((width, LANES)),
            ],
            after=after,
            out_specs=[here((rows, width)), here((rows, 2 * LANES)), blocks, blocks],
            scratch_shapes=[
                pltpu.VMEM((LANES, width), BF16),
                pltpu.VMEM((width, LANES), BF16),
                pltpu.VMEM((n_space, pixels + 16, cols), BF16),
            ],
            cost_estimate=cost(4e9, 1.5e7),
            name="backward",
        )(me, d_pooled, stat, tokens, value, scores, patches, agg_kv, w_back)

    def scatter_embed(keep, send):
        arrived = swap(send, "space", 1)
        blocks = {
            2 * j: (keep[j].astype(F32) + arrived[j].astype(F32)).astype(BF16) for j in range(1, n_space // 2)
        }
        sums = list(blocks.values())
        mine, bit = [keep, arrived], 2
        while bit < n_space:
            got = {k ^ bit: swap(blocks[k], "space", bit) for k in blocks if k & bit and k % bit == 0}
            mine.append(got[0])
            for k in got:
                if k:
                    blocks[k] = (blocks[k].astype(F32) + got[k].astype(F32)).astype(BF16)
            bit *= 2
        return mine, sums

    middle = count // 2
    dv0, dl0, keep0, send0 = backward(0, middle, [])
    out_part = call(
        functools.partial(out_sum_body, n_space),
        struct((drows + 16, cols), BF16),
        cost_estimate=cost(1e6, 3e5),
        name="out_sum",
    )(*out_all)
    dv1, dl1, keep1, send1 = backward(middle, count - middle, [out_part, dv0])
    mine0, sums0 = scatter_embed(keep0, send0)
    mine1, sums1 = scatter_embed(keep1, send1)
    out_even, out_odd = gather_pairs(out_part, "var")

    n_chip = n_var // 2
    step = max(drows, 256)
    half_whole = lambda arr: whole(arr.shape)
    kv_keep, kv_send = call(
        functools.partial(value_grad_body, n_var),
        [struct((n_chip, drows, packet), BF16)] * 2,
        limit=48,
        grid=(width // step,),
        in_specs=[SMEM, pl.BlockSpec((count, rows, step), lambda i: (0, 0, i))]
        + [half_whole(x) for x in (dv0, dv1, dl0, dl1)],
        out_specs=[whole((n_chip, drows, packet))] * 2,
        scratch_shapes=[pltpu.VMEM((step, packet), BF16)],
        cost_estimate=cost(4e9, 1e7),
        name="value_grad",
    )(me, tokens, dv0, dv1, dl0, dl1)
    kv_got = swap(kv_send, "var", 1)
    kv_blocks = call(
        functools.partial(pair_sum_body, n_chip),
        [struct((drows, packet), BF16)] * n_chip,
        after=[out_even],
        in_specs=[SMEM] + [vmem] * 2,
        cost_estimate=cost(1e6, 1e6),
        name="pair_sum",
    )(me, kv_keep, kv_got)
    kv_parts = [kv_blocks[0]] + [swap(kv_blocks[k], "var", 2 * k) for k in range(1, n_chip)]
    small, *large = call(
        functools.partial(packet_split_body, n_chip, n_space),
        [struct((drows, LANES), BF16)] + [struct((drows, kv_cols), BF16)] * n_space,
        after=sums0,
        in_specs=[SMEM] + [vmem] * n_chip,
        scratch_shapes=[pltpu.VMEM((n_space // 2, drows, kv_cols), BF16)],
        cost_estimate=cost(1e6, 1e6),
        name="packet_split",
    )(me, *kv_parts)
    small_all = gather_direct(small, "space")
    large_all = [large[0]] + [
        swap(large[k], "space", k, lambda target: target >= n_space // 2) for k in range(1, n_space)
    ]
    kv_sum = call(
        functools.partial(space_sum_body, n_space),
        struct((drows, kv_cols + LANES), BF16),
        after=sums1,
        cost_estimate=cost(1e6, 1e6),
        name="space_sum",
    )(*small_all, *large_all)

    grad_agg_out, grad_gain = call(
        functools.partial(out_final_body, n_var),
        [struct((width, cols), F32), struct((1, cols), F32)],
        in_specs=[SMEM] + [vmem] * 2,
        cost_estimate=cost(1e6, 1e6),
        name="out_final",
    )(me, out_even, out_odd)

    grad_qkv, grad_out = call(
        functools.partial(head_grads_body, n_space),
        [struct((cols, 3 * group), F32), struct((group, cols), F32)],
        cost_estimate=cost(1e9, 3e6),
        name="head_grads",
    )(*normed_all, *cot_all, dqkv, attn)

    kv_even, kv_odd = gather_pairs(kv_sum, "var")
    grad_agg_kv, grad_query = call(
        functools.partial(final_body, n_var, n_space, scale),
        [struct((width, kv_cols), F32), struct((1, cols), F32)],
        grid=(1,),
        in_specs=[SMEM] + [vmem] * 3 + [pl.BlockSpec((width, width), lambda i: (0, 0))],
        cost_estimate=cost(2e8, 5e6),
        name="final",
    )(me, kv_even, kv_odd, query, agg_kv)

    def first_block(x):
        if x.ndim == 4:
            return pl.BlockSpec((1,) + x.shape[1:], lambda i: (0, 0, 0, 0))
        return pl.BlockSpec(x.shape, lambda i: (0, 0, 0))

    grad_embed, grad_var_embed = call(
        functools.partial(embed_final_body, len(mine0)),
        [struct((count, pixels, cols), F32), struct((count, cols), F32)],
        grid=(1,),
        in_specs=[first_block(x) for x in mine0 + mine1],
        cost_estimate=cost(1e6, 1e6),
        name="embed_final",
    )(*mine0, *mine1)

    return (
        grad_embed,
        grad_var_embed,
        grad_query.reshape(cols),
        grad_agg_kv,
        grad_agg_out,
        grad_gain.reshape(cols),
        grad_qkv,
        grad_out,
    )


def solution(mesh):
    return jax.shard_map(
        shards,
        mesh=mesh,
        in_specs=(
            P("var", "space", None),
            P("var", None, None),
            P("var", None),
            P(),
            P(),
            P(),
            P(),
            P(None, "var"),
            P("var", None),
            P("space", None),
        ),
        out_specs=(
            P("var", None, "space"),
            P("var", "space"),
            P("space"),
            P(None, "space"),
            P(None, "space"),
            P("space"),
            P("space", "var"),
            P("var", "space"),
        ),
        check_vma=False,
    )
```

```python
import functools
import math

import jax
import jax.numpy as jnp
from jax import lax
from jax.experimental import pallas as pl
from jax.experimental.pallas import tpu as pltpu
from jax.sharding import PartitionSpec as P

HEADS = 16
LANES = 128
EPSILON = 1e-05
MIB = 1 << 20

LIMITS = {
    "early": 16, "tokens": 20, "forward": 24, "columns": 8, "pool_pair": 16, "pool": 16, "norm": 16, "attention": 24, "dn_pair": 16, "joined": 16,
    "out_grad": 16, "backward": 32, "out_sum": 16, "value_grad": 32, "pair_sum": 16, "packet_split": 16,
    "space_sum": 16, "out_final": 16, "head_grads": 16, "final": 16, "embed_final": 24,
}

F32 = jnp.float32
BF16 = jnp.bfloat16

NN = (((1,), (0,)), ((), ()))
NT = (((1,), (1,)), ((), ()))
TN = (((0,), (0,)), ((), ()))


def mm(a, b, dims=NN):
    return lax.dot_general(a, b, dims, preferred_element_type=F32)


def iota(shape, axis):
    return lax.broadcasted_iota(jnp.int32, shape, axis)


def parts3(x):
    hi = x.astype(BF16).astype(F32)
    rest = x - hi
    mid = rest.astype(BF16).astype(F32)
    return hi, mid, rest - mid


def pack(x, y=None):
    group = iota(x.shape, 1) >> 4
    hi, mid, lo = parts3(x)
    out = jnp.where(group == 0, hi, jnp.where(group == 1, mid, jnp.where(group == 2, lo, 0.0)))
    if y is not None:
        hi, mid, lo = parts3(y)
        out = jnp.where(group == 3, hi, jnp.where(group == 4, mid, jnp.where(group == 5, lo, out)))
    return out.astype(BF16)


def unpack(packed, first_group=0):
    row, column = iota((LANES, LANES), 0), iota((LANES, LANES), 1)
    group = row >> 4
    take = ((row & 15) == (column & 15)) & (group >= first_group) & (group < first_group + 3)
    return mm(packed, jnp.where(take, 1.0, 0.0).astype(BF16))


def spread_matrix(width, size, first=0):
    row, column = iota((LANES, width), 0), iota((LANES, width), 1)
    shift = size.bit_length() - 1
    take = ((row & 15) == ((column + first) >> shift)) & (row < 48)
    return jnp.where(take, 1.0, 0.0).astype(BF16)


def fold_matrix(width, size):
    row, column = iota((width, LANES), 0), iota((width, LANES), 1)
    shift = size.bit_length() - 1
    return jnp.where((column & 15) == (row >> shift), 1.0, 0.0).astype(BF16)


def head_sums(x, fold):
    hi, mid, lo = parts3(x)
    return mm(hi.astype(BF16), fold) + mm(mid.astype(BF16), fold) + mm(lo.astype(BF16), fold)


def call(body, out_shape, limit=16, **kw):
    return pl.pallas_call(
        body,
        out_shape=out_shape,
        compiler_params=pltpu.CompilerParams(vmem_limit_bytes=limit * MIB),
        **kw,
    )


def hold(me, *arrays):
    zero = sum(x[(0,) * x.ndim].astype(F32) * 0 for x in arrays)
    return me + zero.astype(jnp.int32)


def struct(shape, dtype):
    return jax.ShapeDtypeStruct(shape, dtype)


def cost(flops, moved):
    return pl.CostEstimate(flops=int(flops), bytes_accessed=int(moved), transcendentals=0)


SMEM = pl.BlockSpec(memory_space=pltpu.SMEM)


def swap(x, axis, k, keep=None):
    pairs = [(i, i ^ k) for i in range(lax.axis_size(axis))]
    if keep is not None:
        pairs = [pair for pair in pairs if keep(pair[1])]
    return lax.ppermute(x, axis, pairs)


def gather_direct(x, axis):
    return [x] + [swap(x, axis, k) for k in range(1, lax.axis_size(axis))]


def exchange_direct(blocks, axis):
    return [blocks[0]] + [swap(blocks[k], axis, k) for k in range(1, len(blocks))]


def gather_pairs(x, axis, after=()):
    even = [x] + [swap(x, axis, k) for k in range(2, lax.axis_size(axis), 2)]
    even = jnp.stack([late(even[0], *after)] + even[1:])
    return even, swap(even, axis, 1)


def late(x, *arrays):
    for other in arrays:
        x = x + other[(0,) * other.ndim].astype(x.dtype) * 0
    return x


def exchange_pairs(keep, send, combine, after=()):
    parts = combine(keep, swap(late(send, *after), "var", 1))
    return [parts[0]] + [swap(parts[k], "var", 2 * k) for k in range(1, len(parts))]


def pair_rows(me_v, k, odd, block):
    device = (((me_v >> 1) ^ k) << 1) + ((me_v & 1) ^ odd)
    return pl.ds(pl.multiple_of(device * block, block), block)


def three_rows(x):
    hi, mid, lo = parts3(x)
    row = iota((16, x.shape[1]), 0)
    return jnp.where(row == 0, hi, jnp.where(row == 1, mid, jnp.where(row == 2, lo, 0.0))).astype(BF16)


def head_order(width, size=64):
    heads = width // (3 * size)
    row, column = iota((width, width), 0), iota((width, width), 1)
    take = jnp.zeros((width, width), jnp.bool_)
    for h in range(heads):
        for c in range(3):
            start, target = h * 3 * size + c * size, c * heads * size + h * size
            inside = (column >= target) & (column < target + size)
            take = take | (inside & ((row - start) == (column - target)))
    return jnp.where(take, 1.0, 0.0).astype(BF16)


def early_body(n_space, me_ref, cot_ref, outw_ref, qkvw_ref, dattn_ref, own_ref, wperm_ref, *rest):
    cot_refs, (cols_ref,) = rest[:n_space], rest[n_space:]
    dattn_ref[...] = mm(cot_ref[...], outw_ref[...], NT).astype(BF16)
    block = own_ref.shape[0]
    own_ref[...] = cot_ref[pl.ds(pl.multiple_of(me_ref[0] * block, block), block), :]
    width = cols_ref.shape[2]
    for c in range(n_space):
        cols_ref[c] = cot_ref[:, c * width : (c + 1) * width]
    for k in range(n_space):
        cot_refs[k][...] = cols_ref[me_ref[1] ^ k]
    wperm_ref[...] = mm(qkvw_ref[...], head_order(qkvw_ref.shape[1])).astype(BF16)


def tokens_body(
    scale, me_ref, patches_ref, embed_ref, offset_ref, query_ref, wk_ref, tokens_ref, scores_ref, wback_ref, wq_ref
):
    i = pl.program_id(0)
    width = wk_ref.shape[1]
    size = width // HEADS

    @pl.when(i == 0)
    def _():
        row, column = iota((LANES, width), 0), iota((LANES, width), 1)
        own = (row & 15) == (column >> (size.bit_length() - 1))
        wq = jnp.zeros((width, LANES), F32)
        for part in parts3(query_ref[...]):
            wq = wq + mm(wk_ref[...], jnp.where(own, part, 0.0).astype(BF16), NT)
        hi, mid, lo = parts3(wq * scale)
        wq_ref[:, :LANES] = hi.astype(BF16)
        wq_ref[:, LANES : 2 * LANES] = mid.astype(BF16)
        wq_ref[:, 2 * LANES :] = lo.astype(BF16)
        group = iota((width, LANES), 1) >> 4
        back = jnp.where((group == 0) | (group == 2), hi, jnp.where(group == 1, mid, 0.0))
        wback_ref[...] = back.astype(BF16)

    tokens = (mm(patches_ref[0], embed_ref[0]) + offset_ref[pl.ds(i, 1), :]).astype(BF16)
    tokens_ref[0] = tokens
    pieces = mm(tokens, wq_ref[...])
    scores_ref[0] = pieces[:, :LANES] + pieces[:, LANES : 2 * LANES] + pieces[:, 2 * LANES :]


def forward_body(count, me_ref, tokens_ref, scores_ref, wv_ref, value_ref, keep_ref, send_ref, max_ref, spread_ref, acc_ref):
    j = pl.program_id(0)
    width = wv_ref.shape[1]

    @pl.when(j == 0)
    def _():
        spread_ref[...] = spread_matrix(width, width // HEADS)
        top = scores_ref[0]
        for v in range(1, count):
            top = jnp.maximum(top, scores_ref[v])
        max_ref[...] = top

    value = mm(tokens_ref[0], wv_ref[...])
    value_ref[0] = value
    term = mm(pack(jnp.exp(scores_ref[j] - max_ref[...])), spread_ref[...]) * value

    @pl.when(j == 0)
    def _():
        acc_ref[...] = term

    @pl.when(j > 0)
    def _():
        acc_ref[...] += term

    @pl.when(j == count - 1)
    def _():
        top = max_ref[...]
        total = sum(jnp.exp(scores_ref[v] - top) for v in range(count))
        low = iota(top.shape, 1) < LANES // 2
        max_ref[...] = jnp.where(low, top, total)
        block = keep_ref.shape[1]
        core = me_ref[0] & 1
        for c in range(keep_ref.shape[0]):
            for ref, device in ((keep_ref, 2 * c + core), (send_ref, 2 * c + 1 - core)):
                at = pl.ds(pl.multiple_of(device * block, block), block)
                ref[c, :, :width] = acc_ref[at, :]
                ref[c, :, width:] = max_ref[at, :]


def halves_of(both):
    low = iota(both.shape, 1) < LANES // 2
    turned = pltpu.roll(both, LANES // 2, 1)
    return jnp.where(low, both, turned), jnp.where(low, turned, both)


def pool_pair_body(me_ref, keep_ref, got_ref, *out_refs):
    width = keep_ref.shape[2] - LANES
    spread = spread_matrix(width, width // HEADS)
    low = iota((keep_ref.shape[1], LANES), 1) < LANES // 2
    for k, out_ref in enumerate(out_refs):
        slot = (me_ref[0] >> 1) ^ k
        mine, other = keep_ref[slot], got_ref[slot]
        max_a, sum_a = halves_of(mine[:, width:])
        max_b, sum_b = halves_of(other[:, width:])
        top = jnp.maximum(max_a, max_b)
        factor_a, factor_b = jnp.exp(max_a - top), jnp.exp(max_b - top)
        out_ref[:, :width] = mine[:, :width] * mm(pack(factor_a), spread) + other[:, :width] * mm(pack(factor_b), spread)
        out_ref[:, width:] = jnp.where(low, top, sum_a * factor_a + sum_b * factor_b)


def pool_body(n, *refs):
    ins, (mixed_ref, packet_ref) = refs[:n], refs[n:]
    width = mixed_ref.shape[1]
    stats = [halves_of(ref[:, width:]) for ref in ins]
    top = functools.reduce(jnp.maximum, [m for m, _ in stats])
    factors = [jnp.exp(m - top) for m, _ in stats]
    total = sum(s * f for (_, s), f in zip(stats, factors))
    spread = spread_matrix(width, width // HEADS)
    mixed = jnp.zeros(mixed_ref.shape, F32)
    for ref, factor in zip(ins, factors):
        mixed = mixed + ref[:, :width] * mm(pack(factor / total), spread)
    mixed_ref[...] = mixed
    packet_ref[:, :width] = mixed.astype(BF16)
    packet_ref[:, width:] = pack(top, total)


def norm_body(
    me_ref, even_ref, odd_ref, agg_ref, gain_ref, w_ref, qkv_ref, normed_ref, packets_ref, centred_ref, inv_ref,
    all_ref, allinv_ref,
):
    width = agg_ref.shape[0]
    block = centred_ref.shape[0]
    for k in range(even_ref.shape[0]):
        for odd, ref in ((0, even_ref), (1, odd_ref)):
            packets_ref[pair_rows(me_ref[0], k, odd, block), :] = ref[k]
    joined = mm(packets_ref[:, :width], agg_ref[...]).astype(BF16).astype(F32)
    mean = jnp.mean(joined, axis=-1, keepdims=True)
    spread_sq = jnp.mean((joined - mean) ** 2, axis=-1, keepdims=True)
    inv = lax.rsqrt(spread_sq + EPSILON)
    centred = (joined - mean) * inv
    normed = (centred * gain_ref[...]).astype(BF16)
    qkv_ref[...] = mm(normed, w_ref[...]).astype(BF16)
    normed_ref[...] = normed
    all_ref[...] = centred
    allinv_ref[...] = jnp.broadcast_to(inv, allinv_ref.shape)
    start = pl.multiple_of(me_ref[0] * block, block)
    centred_ref[...] = all_ref[pl.ds(start, block), :]
    inv_ref[...] = allinv_ref[pl.ds(start, block), :]


def attention_body(n_space, size, scale, me_ref, *refs):
    qkv_refs, dattn_refs = refs[:n_space], refs[n_space : 2 * n_space]
    w_ref, attn_ref, dqkv_ref, keep_ref, send_ref, k_ref, v_ref, dk_ref, dv_ref, dn_ref = refs[2 * n_space :]
    rows, group = dattn_refs[0].shape
    heads = group // size
    for b in range(n_space):
        at = slice(b * rows, (b + 1) * rows)
        k_ref[at, :] = qkv_refs[b][:, group : 2 * group]
        v_ref[at, :] = qkv_refs[b][:, 2 * group :]
    lane_head = iota((rows, group), 1) // size if heads > 1 else None
    for b in range(n_space):
        at = slice(b * rows, (b + 1) * rows)
        queries, d_out = qkv_refs[b][:, :group], dattn_refs[b][...]
        attn = dq = None
        for h in range(heads):
            if heads > 1:
                q_h = jnp.where(lane_head == h, queries.astype(F32), 0.0).astype(BF16)
                do_h = jnp.where(lane_head == h, d_out.astype(F32), 0.0).astype(BF16)
            else:
                q_h, do_h = queries, d_out
            logits = mm(q_h, k_ref[...], NT) * scale
            shifted = jnp.exp(logits - jnp.max(logits, axis=-1, keepdims=True))
            probs = shifted * (1.0 / jnp.sum(shifted, axis=-1, keepdims=True))
            probs_b = probs.astype(BF16)
            attn_h = mm(probs_b, v_ref[...])
            dprob = mm(do_h, v_ref[...], NT)
            delta = jnp.sum(probs * dprob, axis=-1, keepdims=True)
            dscore = (probs * (dprob - delta) * scale).astype(BF16)
            dq_h = mm(dscore, k_ref[...])
            dk = mm(dscore, q_h, TN)
            dv = mm(probs_b, do_h, TN)
            if b == 0 and h == 0:
                dk_ref[...] = dk
                dv_ref[...] = dv
            else:
                dk_ref[...] += dk
                dv_ref[...] += dv
            attn = attn_h if attn is None else jnp.where(lane_head == h, attn_h, attn)
            dq = dq_h if dq is None else jnp.where(lane_head == h, dq_h, dq)
        attn_ref[at, :] = attn.astype(BF16)
        dqkv_ref[at, :group] = dq.astype(BF16)
    dqkv_ref[:, group : 2 * group] = dk_ref[...].astype(BF16)
    dqkv_ref[:, 2 * group :] = dv_ref[...].astype(BF16)
    dn_ref[...] = mm(dqkv_ref[:rows, :], w_ref[...], NT).astype(BF16)
    block = keep_ref.shape[1]
    core = me_ref[0] & 1
    for c in range(keep_ref.shape[0]):
        for ref, device in ((keep_ref, 2 * c + core), (send_ref, 2 * c + 1 - core)):
            ref[c] = dn_ref[pl.ds(pl.multiple_of(device * block, block), block), :]


def columns_body(n_space, me_ref, in_ref, *refs):
    out_refs, (cols_ref,) = refs[:n_space], refs[n_space:]
    cols = cols_ref.shape[2]
    for c in range(n_space):
        cols_ref[c] = in_ref[:, c * cols : (c + 1) * cols]
    for k in range(n_space):
        out_refs[k][...] = cols_ref[me_ref[1] ^ k]


def head_grads_body(n_space, *refs):
    normed_refs, cot_refs = refs[:n_space], refs[n_space : 2 * n_space]
    dqkv_ref, attn_ref, gqkv_ref, gout_ref = refs[2 * n_space :]
    rows = normed_refs[0].shape[0]
    order = head_order(dqkv_ref.shape[1])
    natural = mm(dqkv_ref[...], order, NT).astype(BF16)
    gqkv, gout = 0.0, 0.0
    for b in range(n_space):
        at = slice(b * rows, (b + 1) * rows)
        gqkv = gqkv + mm(normed_refs[b][...], natural[at, :], TN)
        gout = gout + mm(attn_ref[at, :], cot_refs[b][...], TN)
    gqkv_ref[...] = gqkv
    gout_ref[...] = gout


def dn_pair_body(me_ref, keep_ref, got_ref, *out_refs):
    for k, out_ref in enumerate(out_refs):
        slot = (me_ref[0] >> 1) ^ k
        out_ref[...] = (keep_ref[slot].astype(F32) + got_ref[slot].astype(F32)).astype(BF16)


def joined_body(n, *refs):
    ins = refs[:n]
    centred_ref, inv_ref, gain_ref, cot_ref, mixed_ref, agg_ref, packet_ref, dgain_ref = refs[n:]
    width = centred_ref.shape[1]
    d_normed = sum(ref[...].astype(F32) for ref in ins)
    centred = centred_ref[...]
    dgain_ref[...] = jnp.broadcast_to(jnp.sum(d_normed * centred, axis=0, keepdims=True), dgain_ref.shape)
    gained = d_normed * gain_ref[...]
    inner = (
        gained
        - jnp.mean(gained, axis=-1, keepdims=True)
        - centred * jnp.mean(gained * centred, axis=-1, keepdims=True)
    )
    d_joined = (cot_ref[...].astype(F32) + inner * inv_ref[:, :1]).astype(BF16)
    d_pooled = mm(d_joined, agg_ref[...], NT)
    center = pack(head_sums(d_pooled * mixed_ref[...], fold_matrix(width, width // HEADS)))
    packet_ref[:, :width] = d_joined
    packet_ref[:, width:] = center


def out_grad_body(n_space, me_ref, pooled_ref, even_ref, odd_ref, dgain_ref, agg_ref, dpool_ref, stat_ref, *refs):
    out_refs, (all_ref, cols_ref, djoined_ref) = refs[:n_space], refs[n_space:]
    width = agg_ref.shape[0]
    for k in range(even_ref.shape[0]):
        for odd, ref in ((0, even_ref), (1, odd_ref)):
            djoined_ref[pair_rows(me_ref[0], k, odd, even_ref.shape[1]), :] = ref[k]
    all_ref[...] = mm(pooled_ref[:, :width], djoined_ref[:, :width], TN)
    cols = cols_ref.shape[2]
    block = out_refs[0].shape[0] - 16
    start = pl.multiple_of(me_ref[0] * block, block)
    own = all_ref[pl.ds(start, block), :].astype(BF16)
    extra = three_rows(dgain_ref[:1, :])
    for c in range(n_space):
        cols_ref[c, :block, :] = own[:, c * cols : (c + 1) * cols]
        cols_ref[c, block:, :] = extra[:, c * cols : (c + 1) * cols]
    for k in range(n_space):
        out_refs[k][...] = cols_ref[me_ref[1] ^ k]
    dpool_ref[...] = mm(djoined_ref[:, :width], agg_ref[...], NT)
    stat_ref[0] = unpack(djoined_ref[:, width:])
    stat_ref[1] = unpack(pooled_ref[:, width:])
    stat_ref[2] = 1.0 / unpack(pooled_ref[:, width:], 3)


def backward_body(
    n_space, me_ref, dpool_ref, stat_ref, tokens_ref, value_ref, scores_ref, patches_ref, wv_ref, wback_ref,
    dvalue_ref, dlogit_ref, keep_ref, send_ref, spread_ref, fold_ref, cols_ref,
):
    width = wv_ref.shape[0]
    size = width // HEADS

    @pl.when(pl.program_id(0) == 0)
    def _():
        spread_ref[...] = spread_matrix(width, size)
        fold_ref[...] = fold_matrix(width, size)

    weight = jnp.exp(scores_ref[0] - stat_ref[1]) * stat_ref[2]
    d_value = (mm(pack(weight), spread_ref[...]) * dpool_ref[...]).astype(BF16)
    dvalue_ref[0] = d_value
    dweight = head_sums(dpool_ref[...] * value_ref[0], fold_ref[...])
    dlogit = weight * (dweight - stat_ref[0])
    hi = dlogit.astype(BF16).astype(F32)
    lo = (dlogit - hi).astype(BF16)
    dlogit_ref[0, :, :LANES] = hi.astype(BF16)
    dlogit_ref[0, :, LANES:] = lo
    group = iota(dlogit.shape, 1) >> 4
    mixed = jnp.where(group < 2, hi, jnp.where(group == 2, lo.astype(F32), 0.0)).astype(BF16)
    d_tokens = (mm(d_value, wv_ref[...], NT) + mm(mixed, wback_ref[...], NT)).astype(BF16)
    grad = mm(patches_ref[0], d_tokens, TN).astype(BF16)
    extra = three_rows(jnp.sum(d_tokens.astype(F32), axis=0, keepdims=True))
    cols = cols_ref.shape[2]
    pixels = patches_ref.shape[2]
    for c in range(n_space):
        cols_ref[c, :pixels, :] = grad[:, c * cols : (c + 1) * cols]
        cols_ref[c, pixels:, :] = extra[:, c * cols : (c + 1) * cols]
    for k in range(0, n_space, 2):
        keep_ref[k // 2, 0] = cols_ref[me_ref[1] ^ k]
        send_ref[k // 2, 0] = cols_ref[me_ref[1] ^ (k + 1)]


def embed_final_body(parts, *refs):
    ins, (grad_ref, offset_ref) = refs[:-2], refs[-2:]
    pixels = grad_ref.shape[1]
    base = 0
    for chunk in range(len(ins) // parts):
        mine = ins[chunk * parts : (chunk + 1) * parts]
        for v in range(mine[0].shape[1]):
            total = 0.0
            for ref in mine:
                total = total + (ref[0, v] if len(ref.shape) == 4 else ref[v]).astype(F32)
            grad_ref[base + v] = total[:pixels, :]
            offset_ref[base + v : base + v + 1, :] = jnp.sum(total[pixels:, :], axis=0, keepdims=True)
        base += mine[0].shape[1]


def value_grad_body(chunks, me_ref, tokens_ref, *refs):
    dv_refs, dl_refs, (keep_ref, send_ref, all_ref) = refs[:chunks], refs[chunks : 2 * chunks], refs[2 * chunks :]
    width = dv_refs[0].shape[2]
    total, both, base = 0.0, 0.0, 0
    for dv_ref, dl_ref in zip(dv_refs, dl_refs):
        for v in range(dv_ref.shape[0]):
            tokens = tokens_ref[base + v]
            total = total + mm(tokens, dv_ref[v], TN)
            both = both + mm(tokens, dl_ref[v], TN)
        base += dv_ref.shape[0]
    all_ref[:, :width] = total.astype(BF16)
    all_ref[:, width:] = pack(both[:, :LANES] + both[:, LANES:])
    block = keep_ref.shape[1]
    count = all_ref.shape[0] // block
    for r in range(count):
        target = pl.program_id(0) * count + r
        same = (target & 1) == (me_ref[0] & 1)
        slot = target >> 1

        @pl.when(same)
        def _():
            keep_ref[slot] = all_ref[r * block : (r + 1) * block, :]

        @pl.when(jnp.logical_not(same))
        def _():
            send_ref[slot] = all_ref[r * block : (r + 1) * block, :]


def pair_sum_body(n_chip, me_ref, keep_ref, got_ref, *out_refs):
    width = keep_ref.shape[2] - LANES
    for k in range(n_chip):
        slot = (me_ref[0] >> 1) ^ k
        mine, other = keep_ref[slot], got_ref[slot]
        out_refs[k][:, :width] = (mine[:, :width].astype(F32) + other[:, :width].astype(F32)).astype(BF16)
        out_refs[k][:, width:] = pack(unpack(mine[:, width:]) + unpack(other[:, width:]))


def packet_split_body(n_in, n_space, me_ref, *refs):
    ins, small_ref = refs[:n_in], refs[n_in]
    out_refs, (cols_ref,) = refs[n_in + 1 : n_in + 1 + n_space], refs[n_in + 1 + n_space :]
    width = ins[0].shape[1] - LANES
    total = sum(ref[:, :width].astype(F32) for ref in ins).astype(BF16)
    small_ref[...] = pack(sum(unpack(ref[:, width:]) for ref in ins))
    half = n_space // 2
    cols = cols_ref.shape[2]
    for c in range(half):
        cols_ref[c] = total[:, c * cols : (c + 1) * cols]
    for k in range(n_space):
        out_refs[k][...] = cols_ref[jnp.maximum((me_ref[1] ^ k) - half, 0)]


def space_sum_body(n, me_ref, *refs):
    small, large, outs, out_ref = refs[:n], refs[n : 2 * n], refs[2 * n : 3 * n], refs[3 * n]
    block, width = large[0].shape
    out_ref[:block, :width] = sum(ref[...].astype(F32) for ref in large).astype(BF16)
    out_ref[:block, width : width + LANES] = pack(sum(unpack(ref[...]) for ref in small))
    out_ref[block:, : width + LANES] = jnp.zeros((out_ref.shape[0] - block, width + LANES), BF16)
    total = sum(ref[...].astype(F32) for ref in outs)
    out_ref[:block, width + LANES :] = total[:block, :].astype(BF16)
    out_ref[block:, width + LANES :] = three_rows(jnp.sum(total[block:, :], axis=0, keepdims=True))


def final_body(n_var, n_space, scale, me_ref, even_ref, odd_ref, query_ref, wk_ref, kv_ref, gq_ref, out_ref, gain_ref):
    me_v, me_s = me_ref[0], me_ref[1]
    half = n_space // 2
    width = wk_ref.shape[1]
    size = width // HEADS
    cols, qcols = kv_ref.shape[1], gq_ref.shape[1]
    place = pl.multiple_of(jnp.minimum(me_s, half - 1) * cols, LANES)
    spread_kv = spread_matrix(cols, size, place)
    qplace = pl.multiple_of(me_s * qcols, LANES)
    spread_q = spread_matrix(qcols, size, qplace)
    query = query_ref[:, pl.ds(place, cols)] * scale
    block = even_ref.shape[1] - 16
    total, gain = 0.0, 0.0
    for k in range(n_var):
        part_ref, slot = (odd_ref if k % 2 else even_ref), k // 2
        at = pl.ds(pl.multiple_of((me_v ^ k) * block, block), block)
        packed = part_ref[slot, :block, cols : cols + LANES]
        key_grad = mm(packed, spread_kv) * query
        kv_ref[at, :] = jnp.where(me_s < half, key_grad, part_ref[slot, :block, :cols].astype(F32))
        keys = wk_ref[at, pl.ds(qplace, qcols)].astype(F32)
        total = total + jnp.sum(mm(packed, spread_q) * keys, axis=0, keepdims=True)
        out_ref[at, :] = part_ref[slot, :block, cols + LANES :].astype(F32)
        gain = gain + jnp.sum(part_ref[slot, block:, cols + LANES :].astype(F32), axis=0, keepdims=True)
    gq_ref[...] = total * scale
    gain_ref[...] = gain


def shards(
    patches, embed_weight, var_embed, agg_query, agg_kv, agg_out, norm_gain, qkv_weight, out_weight, cotangent
):
    n_var, n_space = lax.axis_size("var"), lax.axis_size("space")
    count, rows, pixels = patches.shape
    width = agg_out.shape[0]
    size = width // HEADS
    scale = 1.0 / math.sqrt(size)
    block = rows // n_var
    cols = width // n_space
    group = out_weight.shape[0]
    drows = width // n_var
    positions = rows * n_space
    kv_cols = 2 * width // n_space
    me = jnp.stack([lax.axis_index("var"), lax.axis_index("space")]).astype(jnp.int32)
    gain = norm_gain.reshape(1, width)
    query = agg_query.reshape(1, width)
    vmem = pl.BlockSpec(memory_space=pltpu.VMEM)
    packet = width + LANES

    dattn, cot_own, w_heads, *cot_cols = call(
        functools.partial(early_body, n_space),
        [struct((rows, group), BF16), struct((block, width), BF16), struct(qkv_weight.shape, BF16)]
        + [struct((rows, cols), BF16)] * n_space,
        in_specs=[SMEM] + [vmem] * 3,
        scratch_shapes=[pltpu.VMEM((n_space, rows, cols), BF16)],
        limit=LIMITS["early"],
        cost_estimate=cost(2e8, 4e6),
        name="early",
    )(me, cotangent, out_weight, qkv_weight)
    dattn_all = gather_direct(dattn, "space")
    cot_all = exchange_direct(cot_cols, "space")

    whole = lambda shape: pl.BlockSpec(shape, lambda v: (0,) * len(shape))
    every = lambda shape: pl.BlockSpec((1,) + shape, lambda v: (v,) + (0,) * len(shape))
    n_chip = n_var // 2
    tokens, scores, w_back = call(
        functools.partial(tokens_body, scale),
        [struct((count, rows, width), BF16), struct((count, rows, LANES), F32), struct((width, LANES), BF16)],
        limit=LIMITS["tokens"],
        grid=(count,),
        in_specs=[
            SMEM,
            every((rows, pixels)),
            every((pixels, width)),
            whole((count, width)),
            whole((1, width)),
            pl.BlockSpec((width, width), lambda v: (0, 0)),
        ],
        out_specs=[every((rows, width)), every((rows, LANES)), whole((width, LANES))],
        scratch_shapes=[pltpu.VMEM((width, 3 * LANES), BF16)],
        cost_estimate=cost(6e9, 2e7),
        name="tokens",
    )(hold(me, dattn), patches, embed_weight, var_embed, query, agg_kv)
    value, keep, send = call(
        functools.partial(forward_body, count),
        [struct((count, rows, width), F32)] + [struct((n_chip, block, packet), F32)] * 2,
        limit=LIMITS["forward"],
        grid=(count,),
        in_specs=[
            SMEM,
            every((rows, width)),
            whole((count, rows, LANES)),
            pl.BlockSpec((width, width), lambda v: (0, 1)),
        ],
        out_specs=[every((rows, width))] + [whole((n_chip, block, packet))] * 2,
        scratch_shapes=[
            pltpu.VMEM((rows, LANES), F32),
            pltpu.VMEM((LANES, width), BF16),
            pltpu.VMEM((rows, width), F32),
        ],
        cost_estimate=cost(4e9, 1e7),
        name="forward",
    )(hold(me, scores, *dattn_all[1:], *cot_all[1:]), tokens, scores, agg_kv)

    def pool_pairs(mine, got):
        return call(
            pool_pair_body,
            [struct((block, packet), F32)] * n_chip,
            limit=LIMITS["pool_pair"],
            in_specs=[SMEM, vmem, vmem],
            cost_estimate=cost(1e8, 3e6),
            name="pool_pair",
        )(me, mine, got)

    received = exchange_pairs(keep, send, pool_pairs)
    mixed, pooled_packet = call(
        functools.partial(pool_body, n_chip),
        [struct((block, width), F32), struct((block, packet), BF16)],
        limit=LIMITS["pool"],
        cost_estimate=cost(1e8, 2e6),
        name="pool",
    )(*received)
    pooled_even, pooled_odd = gather_pairs(pooled_packet, "var")

    qkv, normed, pooled_packets, centred, inv = call(
        norm_body,
        [
            struct((rows, 3 * group), BF16),
            struct((rows, width), BF16),
            struct((rows, packet), BF16),
            struct((block, width), F32),
            struct((block, LANES), F32),
        ],
        limit=LIMITS["norm"],
        in_specs=[SMEM] + [vmem] * 5,
        scratch_shapes=[pltpu.VMEM((rows, width), F32), pltpu.VMEM((rows, LANES), F32)],
        cost_estimate=cost(8e8, 5e6),
        name="norm",
    )(me, pooled_even, pooled_odd, agg_out, gain, w_heads)

    qkv_all = gather_direct(qkv, "space")
    normed_cols = call(
        functools.partial(columns_body, n_space),
        [struct((rows, cols), BF16)] * n_space,
        limit=LIMITS["columns"],
        in_specs=[SMEM, vmem],
        scratch_shapes=[pltpu.VMEM((n_space, rows, cols), BF16)],
        cost_estimate=cost(1e6, 1e6),
        name="columns",
    )(hold(me, *qkv_all[1:]), normed)
    normed_all = exchange_direct(normed_cols, "space")
    attn, dqkv, dn_keep, dn_send = call(
        functools.partial(attention_body, n_space, size, scale),
        [struct((positions, group), BF16), struct((positions, 3 * group), BF16)]
        + [struct((n_chip, block, width), BF16)] * 2,
        limit=LIMITS["attention"],
        in_specs=[SMEM] + [vmem] * (2 * n_space + 1),
        scratch_shapes=[pltpu.VMEM((positions, group), BF16)] * 2
        + [pltpu.VMEM((positions, group), F32)] * 2
        + [pltpu.VMEM((rows, width), BF16)],
        cost_estimate=cost(6e9, 4e6),
        name="attention",
    )(hold(me, normed_cols[0]), *qkv_all, *dattn_all, w_heads)

    def dn_pairs(mine, got):
        return call(
            dn_pair_body,
            [struct((block, width), BF16)] * n_chip,
            limit=LIMITS["dn_pair"],
            in_specs=[SMEM, vmem, vmem],
            cost_estimate=cost(1e6, 1e6),
            name="dn_pair",
        )(me, mine, got)

    dn_received = exchange_pairs(dn_keep, dn_send, dn_pairs, normed_all[1:])
    joined_packet, dgain = call(
        functools.partial(joined_body, n_chip),
        [struct((block, packet), BF16), struct((8, width), F32)],
        limit=LIMITS["joined"],
        cost_estimate=cost(2e8, 3e6),
        name="joined",
    )(*dn_received, centred, inv, gain, cot_own, mixed, agg_out)
    joined_even, joined_odd = gather_pairs(joined_packet, "var")

    d_pooled, stat, *out_blocks = call(
        functools.partial(out_grad_body, n_space),
        [struct((rows, width), F32), struct((3, rows, LANES), F32)] + [struct((drows + 16, cols), BF16)] * n_space,
        limit=LIMITS["out_grad"],
        in_specs=[SMEM] + [vmem] * 5,
        scratch_shapes=[
            pltpu.VMEM((width, width), F32),
            pltpu.VMEM((n_space, drows + 16, cols), BF16),
            pltpu.VMEM((rows, packet), BF16),
        ],
        cost_estimate=cost(1e9, 5e6),
        name="out_grad",
    )(me, pooled_packets, joined_even, joined_odd, dgain, agg_out)
    out_all = exchange_direct(out_blocks, "space")

    def backward(me, start, size_here, work):
        each = lambda shape: pl.BlockSpec((1,) + shape, lambda v: (v + start,) + (0,) * len(shape))
        here = lambda shape: pl.BlockSpec((1,) + shape, lambda v: (v,) + (0,) * len(shape))
        blocks = pl.BlockSpec((n_space // 2, 1, pixels + 16, cols), lambda v: (0, v, 0, 0))
        return call(
            functools.partial(backward_body, n_space),
            [struct((size_here, rows, width), BF16), struct((size_here, rows, 2 * LANES), BF16)]
            + [struct((n_space // 2, size_here, pixels + 16, cols), BF16)] * 2,
            limit=LIMITS["backward"],
            grid=(size_here,),
            in_specs=[
                SMEM,
                whole((rows, width)),
                whole((3, rows, LANES)),
                each((rows, width)),
                each((rows, width)),
                each((rows, LANES)),
                each((rows, pixels)),
                pl.BlockSpec((width, width), lambda v: (0, 1)),
                whole((width, LANES)),
            ],
            out_specs=[here((rows, width)), here((rows, 2 * LANES)), blocks, blocks],
            scratch_shapes=[
                pltpu.VMEM((LANES, width), BF16),
                pltpu.VMEM((width, LANES), BF16),
                pltpu.VMEM((n_space, pixels + 16, cols), BF16),
            ],
            cost_estimate=work,
            name="backward",
        )(me, d_pooled, stat, tokens, value, scores, patches, agg_kv, w_back)

    def scatter_embed(keep, arrived, after=()):
        blocks = {
            2 * j: (keep[j].astype(F32) + late(arrived[j].astype(F32), *after)).astype(BF16)
            for j in range(1, n_space // 2)
        }
        sums = list(blocks.values())
        mine, bit = [keep, arrived], 2
        while bit < n_space:
            got = {k ^ bit: swap(blocks[k], "space", bit) for k in blocks if k & bit and k % bit == 0}
            mine.append(got[0])
            for k in got:
                if k:
                    blocks[k] = (blocks[k].astype(F32) + got[k].astype(F32)).astype(BF16)
            bit *= 2
        return mine, sums

    first = count // 3
    dv0, dl0, keep0, send0 = backward(me, 0, first, cost(4e9, 1e7))
    dv1, dl1, keep1, send1 = backward(hold(me, dv0), first, count - first, cost(1e6, 1e6))
    mine0, sums0 = scatter_embed(keep0, swap(send0, "space", 1))
    arrived1 = swap(send1, "space", 1)

    step = max(drows, 256)
    d_values, d_logits = (dv0, dv1), (dl0, dl1)
    kv_keep, kv_send = call(
        functools.partial(value_grad_body, len(d_values)),
        [struct((n_chip, drows, packet), BF16)] * 2,
        limit=LIMITS["value_grad"],
        grid=(width // step,),
        in_specs=[SMEM, pl.BlockSpec((count, rows, step), lambda i: (0, 0, i))]
        + [whole(x.shape) for x in d_values + d_logits],
        out_specs=[whole((n_chip, drows, packet))] * 2,
        scratch_shapes=[pltpu.VMEM((step, packet), BF16)],
        cost_estimate=cost(1e6, 1e6),
        name="value_grad",
    )(hold(me, dv1, *sums0), tokens, *d_values, *d_logits)
    kv_got = swap(kv_send, "var", 1)
    kv_blocks = call(
        functools.partial(pair_sum_body, n_chip),
        [struct((drows, packet), BF16)] * n_chip,
        limit=LIMITS["pair_sum"],
        in_specs=[SMEM] + [vmem] * 2,
        cost_estimate=cost(1e6, 1e6),
        name="pair_sum",
    )(me, kv_keep, kv_got)
    kv_parts = [kv_blocks[0]] + [swap(kv_blocks[k], "var", 2 * k) for k in range(1, n_chip)]
    small, *large = call(
        functools.partial(packet_split_body, n_chip, n_space),
        [struct((drows, LANES), BF16)] + [struct((drows, kv_cols), BF16)] * n_space,
        limit=LIMITS["packet_split"],
        in_specs=[SMEM] + [vmem] * n_chip,
        scratch_shapes=[pltpu.VMEM((n_space // 2, drows, kv_cols), BF16)],
        cost_estimate=cost(1e6, 1e6),
        name="packet_split",
    )(hold(me, kv_parts[-1], *mine0[2:]), *kv_parts)
    grad_qkv, grad_out = call(
        functools.partial(head_grads_body, n_space),
        [struct((cols, 3 * group), F32), struct((group, cols), F32)],
        limit=LIMITS["head_grads"],
        cost_estimate=cost(1e9, 3e6),
        name="head_grads",
    )(*normed_all, *cot_all, dqkv, attn)

    mine1, sums1 = scatter_embed(keep1, arrived1, [small])
    small_all = gather_direct(small, "space")
    large_all = [large[0]] + [
        swap(large[k], "space", k, lambda target: target >= n_space // 2) for k in range(1, n_space)
    ]
    kv_sum = call(
        functools.partial(space_sum_body, n_space),
        struct((drows + 16, kv_cols + LANES + cols), BF16),
        limit=LIMITS["space_sum"],
        in_specs=[SMEM] + [vmem] * (3 * n_space),
        cost_estimate=cost(1e6, 1e6),
        name="space_sum",
    )(hold(me, large_all[-1], grad_out, *sums1, *mine0[2:]), *small_all, *large_all, *out_all)

    kv_even, kv_odd = gather_pairs(kv_sum, "var", mine1[2:])
    grad_agg_kv, grad_query, grad_agg_out, grad_gain = call(
        functools.partial(final_body, n_var, n_space, scale),
        [struct((width, kv_cols), F32), struct((1, cols), F32)] + [struct((width, cols), F32), struct((1, cols), F32)],
        grid=(1,),
        in_specs=[SMEM] + [vmem] * 3 + [pl.BlockSpec((width, width), lambda i: (0, 0))],
        limit=LIMITS["final"],
        cost_estimate=cost(2e8, 5e6),
        name="final",
    )(me, kv_even, kv_odd, query, agg_kv)

    def first_block(x):
        if x.ndim == 4:
            return pl.BlockSpec((1,) + x.shape[1:], lambda i: (0, 0, 0, 0))
        return pl.BlockSpec(x.shape, lambda i: (0, 0, 0))

    grad_embed, grad_var_embed = call(
        functools.partial(embed_final_body, len(mine0)),
        [struct((count, pixels, cols), F32), struct((count, cols), F32)],
        grid=(1,),
        in_specs=[first_block(x) for x in mine0 + mine1],
        limit=LIMITS["embed_final"],
        cost_estimate=cost(1e6, 1e6),
        name="embed_final",
    )(*mine0, *mine1)

    return (
        grad_embed,
        grad_var_embed,
        grad_query.reshape(cols),
        grad_agg_kv,
        grad_agg_out,
        grad_gain.reshape(cols),
        grad_qkv,
        grad_out,
    )


def solution(mesh):
    return jax.shard_map(
        shards,
        mesh=mesh,
        in_specs=(
            P("var", "space", None),
            P("var", None, None),
            P("var", None),
            P(),
            P(),
            P(),
            P(),
            P(None, "var"),
            P("var", None),
            P("space", None),
        ),
        out_specs=(
            P("var", None, "space"),
            P("var", "space"),
            P("space"),
            P(None, "space"),
            P(None, "space"),
            P("space"),
            P("space", "var"),
            P("var", "space"),
        ),
        check_vma=False,
    )
```

```python
import functools
import math

import jax
import jax.numpy as jnp
from jax import lax
from jax.experimental import pallas as pl
from jax.experimental.pallas import tpu as pltpu
from jax.sharding import PartitionSpec as P

HEADS = 16
LANES = 128
EPSILON = 1e-05
MIB = 1 << 20

LIMITS = {
    "early": 16, "tokens": 56, "forward": 56, "columns": 8, "pool_pair": 16, "pool": 16, "norm": 16, "attention": 24,
    "dn": 12, "dn_pair": 16, "joined": 16, "prepare": 16, "out_grad": 16, "dvalue": 24, "embed": 24, "value_grad": 32,
    "add": 12, "pair_sum": 16, "packet_split": 16, "space_sum": 16, "head_grads": 16, "final": 16, "embed_final": 24,
}

F32 = jnp.float32
BF16 = jnp.bfloat16

NN = (((1,), (0,)), ((), ()))
NT = (((1,), (1,)), ((), ()))
TN = (((0,), (0,)), ((), ()))


def mm(a, b, dims=NN):
    return lax.dot_general(a, b, dims, preferred_element_type=F32)


def iota(shape, axis):
    return lax.broadcasted_iota(jnp.int32, shape, axis)


def parts3(x):
    hi = x.astype(BF16).astype(F32)
    rest = x - hi
    mid = rest.astype(BF16).astype(F32)
    return hi, mid, rest - mid


def pack(x, y=None):
    group = iota(x.shape, 1) >> 4
    hi, mid, lo = parts3(x)
    out = jnp.where(group == 0, hi, jnp.where(group == 1, mid, jnp.where(group == 2, lo, 0.0)))
    if y is not None:
        hi, mid, lo = parts3(y)
        out = jnp.where(group == 3, hi, jnp.where(group == 4, mid, jnp.where(group == 5, lo, out)))
    return out.astype(BF16)


def unpack(packed, first_group=0):
    row, column = iota((LANES, LANES), 0), iota((LANES, LANES), 1)
    group = row >> 4
    take = ((row & 15) == (column & 15)) & (group >= first_group) & (group < first_group + 3)
    return mm(packed, jnp.where(take, 1.0, 0.0).astype(BF16))


def spread_matrix(width, size, first=0):
    row, column = iota((LANES, width), 0), iota((LANES, width), 1)
    shift = size.bit_length() - 1
    take = ((row & 15) == ((column + first) >> shift)) & (row < 48)
    return jnp.where(take, 1.0, 0.0).astype(BF16)


def fold_matrix(width, size):
    row, column = iota((width, LANES), 0), iota((width, LANES), 1)
    shift = size.bit_length() - 1
    return jnp.where((column & 15) == (row >> shift), 1.0, 0.0).astype(BF16)


def head_sums(x, fold):
    hi, mid, lo = parts3(x)
    return mm(hi.astype(BF16), fold) + mm(mid.astype(BF16), fold) + mm(lo.astype(BF16), fold)


def call(body, out_shape, limit=16, after=(), in_specs=None, **kw):
    def run(*args):
        n, m = len(args), len(after)
        vmem = pl.BlockSpec(memory_space=pltpu.VMEM)
        return pl.pallas_call(
            lambda *refs: body(*refs[:n], *refs[n + m :]),
            out_shape=out_shape,
            in_specs=([vmem] * n if in_specs is None else list(in_specs)) + [vmem] * m,
            compiler_params=pltpu.CompilerParams(vmem_limit_bytes=limit * MIB),
            **kw,
        )(*args, *after)

    return run


def struct(shape, dtype):
    return jax.ShapeDtypeStruct(shape, dtype)


def cost(flops, moved):
    return pl.CostEstimate(flops=int(flops), bytes_accessed=int(moved), transcendentals=0)


SMEM = pl.BlockSpec(memory_space=pltpu.SMEM)


def swap(x, axis, k, keep=None):
    pairs = [(i, i ^ k) for i in range(lax.axis_size(axis))]
    if keep is not None:
        pairs = [pair for pair in pairs if keep(pair[1])]
    return lax.ppermute(x, axis, pairs)


def gather_direct(x, axis):
    return [x] + [swap(x, axis, k) for k in range(1, lax.axis_size(axis))]


def exchange_direct(blocks, axis):
    return [blocks[0]] + [swap(blocks[k], axis, k) for k in range(1, len(blocks))]


def gather_pairs(x, axis, stack=jnp.stack):
    even = [x] + [swap(x, axis, k) for k in range(2, lax.axis_size(axis), 2)]
    even = stack(even)
    return even, swap(even, axis, 1)


def exchange_pairs(keep, send, combine):
    parts = combine(keep, swap(send, "var", 1))
    return [parts[0]] + [swap(parts[k], "var", 2 * k) for k in range(1, len(parts))]


def pair_rows(me_v, k, odd, block):
    device = (((me_v >> 1) ^ k) << 1) + ((me_v & 1) ^ odd)
    return pl.ds(pl.multiple_of(device * block, block), block)


def three_rows(x):
    hi, mid, lo = parts3(x)
    row = iota((16, x.shape[1]), 0)
    return jnp.where(row == 0, hi, jnp.where(row == 1, mid, jnp.where(row == 2, lo, 0.0))).astype(BF16)


def head_order(width, size=64):
    heads = width // (3 * size)
    row, column = iota((width, width), 0), iota((width, width), 1)
    take = jnp.zeros((width, width), jnp.bool_)
    for h in range(heads):
        for c in range(3):
            start, target = h * 3 * size + c * size, c * heads * size + h * size
            inside = (column >= target) & (column < target + size)
            take = take | (inside & ((row - start) == (column - target)))
    return jnp.where(take, 1.0, 0.0).astype(BF16)


def early_body(me_ref, cot_ref, outw_ref, qkvw_ref, dattn_ref, own_ref, wperm_ref):
    dattn_ref[...] = mm(cot_ref[...], outw_ref[...], NT).astype(BF16)
    block = own_ref.shape[0]
    own_ref[...] = cot_ref[pl.ds(pl.multiple_of(me_ref[0] * block, block), block), :]
    wperm_ref[...] = mm(qkvw_ref[...], head_order(qkvw_ref.shape[1])).astype(BF16)


def tokens_body(
    scale, patches_ref, embed_ref, offset_ref, query_ref, wk_ref, tokens_ref, scores_ref, wback_ref, wq_ref
):
    i = pl.program_id(0)
    width = wk_ref.shape[1]
    size = width // HEADS

    @pl.when(i == 0)
    def _():
        row, column = iota((LANES, width), 0), iota((LANES, width), 1)
        own = (row & 15) == (column >> (size.bit_length() - 1))
        wq = jnp.zeros((width, LANES), F32)
        for part in parts3(query_ref[...]):
            wq = wq + mm(wk_ref[...], jnp.where(own, part, 0.0).astype(BF16), NT)
        hi, mid, lo = parts3(wq * scale)
        wq_ref[:, :LANES] = hi.astype(BF16)
        wq_ref[:, LANES : 2 * LANES] = mid.astype(BF16)
        wq_ref[:, 2 * LANES :] = lo.astype(BF16)
        group = iota((width, LANES), 1) >> 4
        back = jnp.where((group == 0) | (group == 2), hi, jnp.where(group == 1, mid, 0.0))
        wback_ref[...] = back.astype(BF16)

    tokens = (mm(patches_ref[0], embed_ref[0]) + offset_ref[pl.ds(i, 1), :]).astype(BF16)
    tokens_ref[0] = tokens
    pieces = mm(tokens, wq_ref[...])
    scores_ref[0] = pieces[:, :LANES] + pieces[:, LANES : 2 * LANES] + pieces[:, 2 * LANES :]


def forward_body(count, me_ref, tokens_ref, scores_ref, wv_ref, value_ref, keep_ref, send_ref, max_ref, spread_ref, acc_ref):
    j = pl.program_id(0)
    width = wv_ref.shape[1]

    @pl.when(j == 0)
    def _():
        spread_ref[...] = spread_matrix(width, width // HEADS)
        top = scores_ref[0]
        for v in range(1, count):
            top = jnp.maximum(top, scores_ref[v])
        max_ref[...] = top

    value = mm(tokens_ref[0], wv_ref[...])
    value_ref[0] = value
    term = mm(pack(jnp.exp(scores_ref[j] - max_ref[...])), spread_ref[...]) * value

    @pl.when(j == 0)
    def _():
        acc_ref[...] = term

    @pl.when(j > 0)
    def _():
        acc_ref[...] += term

    @pl.when(j == count - 1)
    def _():
        top = max_ref[...]
        total = sum(jnp.exp(scores_ref[v] - top) for v in range(count))
        low = iota(top.shape, 1) < LANES // 2
        max_ref[...] = jnp.where(low, top, total)
        block = keep_ref.shape[1]
        core = me_ref[0] & 1
        for c in range(keep_ref.shape[0]):
            for ref, device in ((keep_ref, 2 * c + core), (send_ref, 2 * c + 1 - core)):
                at = pl.ds(pl.multiple_of(device * block, block), block)
                ref[c, :, :width] = acc_ref[at, :]
                ref[c, :, width:] = max_ref[at, :]


def halves_of(both):
    low = iota(both.shape, 1) < LANES // 2
    turned = pltpu.roll(both, LANES // 2, 1)
    return jnp.where(low, both, turned), jnp.where(low, turned, both)


def pool_pair_body(me_ref, keep_ref, got_ref, *out_refs):
    width = keep_ref.shape[2] - LANES
    spread = spread_matrix(width, width // HEADS)
    low = iota((keep_ref.shape[1], LANES), 1) < LANES // 2
    for k, out_ref in enumerate(out_refs):
        slot = (me_ref[0] >> 1) ^ k
        mine, other = keep_ref[slot], got_ref[slot]
        max_a, sum_a = halves_of(mine[:, width:])
        max_b, sum_b = halves_of(other[:, width:])
        top = jnp.maximum(max_a, max_b)
        factor_a, factor_b = jnp.exp(max_a - top), jnp.exp(max_b - top)
        out_ref[:, :width] = mine[:, :width] * mm(pack(factor_a), spread) + other[:, :width] * mm(pack(factor_b), spread)
        out_ref[:, width:] = jnp.where(low, top, sum_a * factor_a + sum_b * factor_b)


def pool_body(n, *refs):
    ins, (mixed_ref, packet_ref) = refs[:n], refs[n:]
    width = mixed_ref.shape[1]
    stats = [halves_of(ref[:, width:]) for ref in ins]
    top = functools.reduce(jnp.maximum, [m for m, _ in stats])
    factors = [jnp.exp(m - top) for m, _ in stats]
    total = sum(s * f for (_, s), f in zip(stats, factors))
    spread = spread_matrix(width, width // HEADS)
    mixed = jnp.zeros(mixed_ref.shape, F32)
    for ref, factor in zip(ins, factors):
        mixed = mixed + ref[:, :width] * mm(pack(factor / total), spread)
    mixed_ref[...] = mixed
    packet_ref[:, :width] = mixed.astype(BF16)
    packet_ref[:, width:] = pack(top, total)


def norm_body(
    me_ref, even_ref, odd_ref, agg_ref, gain_ref, w_ref, qkv_ref, normed_ref, packets_ref, centred_ref, inv_ref,
    all_ref, allinv_ref,
):
    width = agg_ref.shape[0]
    block = centred_ref.shape[0]
    for k in range(even_ref.shape[0]):
        for odd, ref in ((0, even_ref), (1, odd_ref)):
            packets_ref[pair_rows(me_ref[0], k, odd, block), :] = ref[k]
    joined = mm(packets_ref[:, :width], agg_ref[...]).astype(BF16).astype(F32)
    mean = jnp.mean(joined, axis=-1, keepdims=True)
    spread_sq = jnp.mean((joined - mean) ** 2, axis=-1, keepdims=True)
    inv = lax.rsqrt(spread_sq + EPSILON)
    centred = (joined - mean) * inv
    normed = (centred * gain_ref[...]).astype(BF16)
    qkv_ref[...] = mm(normed, w_ref[...]).astype(BF16)
    normed_ref[...] = normed
    all_ref[...] = centred
    allinv_ref[...] = jnp.broadcast_to(inv, allinv_ref.shape)
    start = pl.multiple_of(me_ref[0] * block, block)
    centred_ref[...] = all_ref[pl.ds(start, block), :]
    inv_ref[...] = allinv_ref[pl.ds(start, block), :]


def attention_body(n_space, size, scale, *refs):
    qkv_refs, dattn_refs = refs[:n_space], refs[n_space : 2 * n_space]
    attn_ref, dqkv_ref, k_ref, v_ref, dk_ref, dv_ref = refs[2 * n_space :]
    rows, group = dattn_refs[0].shape
    heads = group // size
    for b in range(n_space):
        at = slice(b * rows, (b + 1) * rows)
        k_ref[at, :] = qkv_refs[b][:, group : 2 * group]
        v_ref[at, :] = qkv_refs[b][:, 2 * group :]
    lane_head = iota((rows, group), 1) // size if heads > 1 else None
    for b in range(n_space):
        at = slice(b * rows, (b + 1) * rows)
        queries, d_out = qkv_refs[b][:, :group], dattn_refs[b][...]
        attn = dq = None
        for h in range(heads):
            if heads > 1:
                q_h = jnp.where(lane_head == h, queries.astype(F32), 0.0).astype(BF16)
                do_h = jnp.where(lane_head == h, d_out.astype(F32), 0.0).astype(BF16)
            else:
                q_h, do_h = queries, d_out
            logits = mm(q_h, k_ref[...], NT) * scale
            shifted = jnp.exp(logits - jnp.max(logits, axis=-1, keepdims=True))
            probs = shifted * (1.0 / jnp.sum(shifted, axis=-1, keepdims=True))
            probs_b = probs.astype(BF16)
            attn_h = mm(probs_b, v_ref[...])
            dprob = mm(do_h, v_ref[...], NT)
            delta = jnp.sum(probs * dprob, axis=-1, keepdims=True)
            dscore = (probs * (dprob - delta) * scale).astype(BF16)
            dq_h = mm(dscore, k_ref[...])
            dk = mm(dscore, q_h, TN)
            dv = mm(probs_b, do_h, TN)
            if b == 0 and h == 0:
                dk_ref[...] = dk
                dv_ref[...] = dv
            else:
                dk_ref[...] += dk
                dv_ref[...] += dv
            attn = attn_h if attn is None else jnp.where(lane_head == h, attn_h, attn)
            dq = dq_h if dq is None else jnp.where(lane_head == h, dq_h, dq)
        attn_ref[at, :] = attn.astype(BF16)
        dqkv_ref[at, :group] = dq.astype(BF16)
    dqkv_ref[:, group : 2 * group] = dk_ref[...].astype(BF16)
    dqkv_ref[:, 2 * group :] = dv_ref[...].astype(BF16)


def dn_body(me_ref, dqkv_ref, w_ref, keep_ref, send_ref, dn_ref):
    dn_ref[...] = mm(dqkv_ref[...], w_ref[...], NT).astype(BF16)
    block = keep_ref.shape[1]
    core = me_ref[0] & 1
    for c in range(keep_ref.shape[0]):
        for ref, device in ((keep_ref, 2 * c + core), (send_ref, 2 * c + 1 - core)):
            ref[c] = dn_ref[pl.ds(pl.multiple_of(device * block, block), block), :]


def columns_body(n_space, me_ref, in_ref, *refs):
    out_refs, (cols_ref,) = refs[:n_space], refs[n_space:]
    cols = cols_ref.shape[2]
    for c in range(n_space):
        cols_ref[c] = in_ref[:, c * cols : (c + 1) * cols]
    for k in range(n_space):
        out_refs[k][...] = cols_ref[me_ref[1] ^ k]


def head_grads_body(n_space, *refs):
    normed_refs, (dqkv_ref, gqkv_ref, flag_ref) = refs[:n_space], refs[n_space:]
    flag_ref[...] = jnp.zeros(flag_ref.shape, F32)
    rows = normed_refs[0].shape[0]
    natural = mm(dqkv_ref[...], head_order(dqkv_ref.shape[1]), NT).astype(BF16)
    gqkv_ref[...] = sum(
        mm(ref[...], natural[b * rows : (b + 1) * rows, :], TN) for b, ref in enumerate(normed_refs)
    )


def dn_pair_body(me_ref, keep_ref, got_ref, *out_refs):
    for k, out_ref in enumerate(out_refs):
        slot = (me_ref[0] >> 1) ^ k
        out_ref[...] = (keep_ref[slot].astype(F32) + got_ref[slot].astype(F32)).astype(BF16)


def joined_body(n, *refs):
    ins = refs[:n]
    centred_ref, inv_ref, gain_ref, cot_ref, mixed_ref, agg_ref, packet_ref, dgain_ref = refs[n:]
    width = centred_ref.shape[1]
    d_normed = sum(ref[...].astype(F32) for ref in ins)
    centred = centred_ref[...]
    dgain_ref[...] = jnp.broadcast_to(jnp.sum(d_normed * centred, axis=0, keepdims=True), dgain_ref.shape)
    gained = d_normed * gain_ref[...]
    inner = (
        gained
        - jnp.mean(gained, axis=-1, keepdims=True)
        - centred * jnp.mean(gained * centred, axis=-1, keepdims=True)
    )
    d_joined = (cot_ref[...].astype(F32) + inner * inv_ref[:, :1]).astype(BF16)
    d_pooled = mm(d_joined, agg_ref[...], NT)
    center = pack(head_sums(d_pooled * mixed_ref[...], fold_matrix(width, width // HEADS)))
    packet_ref[:, :width] = d_joined
    packet_ref[:, width:] = center


def prepare_body(me_ref, pooled_ref, even_ref, odd_ref, agg_ref, djoined_ref, dpool_ref, stat_ref):
    width = agg_ref.shape[0]
    for k in range(even_ref.shape[0]):
        for odd, ref in ((0, even_ref), (1, odd_ref)):
            djoined_ref[pair_rows(me_ref[0], k, odd, even_ref.shape[1]), :] = ref[k]
    dpool_ref[...] = mm(djoined_ref[:, :width], agg_ref[...], NT)
    stat_ref[0] = unpack(djoined_ref[:, width:])
    stat_ref[1] = unpack(pooled_ref[:, width:])
    stat_ref[2] = 1.0 / unpack(pooled_ref[:, width:], 3)


def out_grad_body(me_ref, pooled_ref, djoined_ref, dgain_ref, attn_ref, cot_ref, out_ref, all_ref):
    width = dgain_ref.shape[1]
    all_ref[...] = mm(pooled_ref[:, :width], djoined_ref[:, :width], TN)
    weight_grad = mm(attn_ref[...], cot_ref[...], TN).astype(BF16)
    n_space, height, cols = out_ref.shape
    block = height - 16 - weight_grad.shape[0]
    start = pl.multiple_of(me_ref[0] * block, block)
    own = all_ref[pl.ds(start, block), :].astype(BF16)
    extra = three_rows(dgain_ref[:1, :])
    for c in range(n_space):
        out_ref[c, :block, :] = own[:, c * cols : (c + 1) * cols]
        out_ref[c, block : block + 16, :] = extra[:, c * cols : (c + 1) * cols]
        out_ref[c, block + 16 :, :] = weight_grad[:, c * cols : (c + 1) * cols]


def dvalue_body(dpool_ref, stat_ref, value_ref, scores_ref, dvalue_ref, dlogit_ref, spread_ref, fold_ref):
    width = dpool_ref.shape[1]
    size = width // HEADS

    @pl.when(pl.program_id(0) == 0)
    def _():
        spread_ref[...] = spread_matrix(width, size)
        fold_ref[...] = fold_matrix(width, size)

    weight = jnp.exp(scores_ref[0] - stat_ref[1]) * stat_ref[2]
    dvalue_ref[0] = (mm(pack(weight), spread_ref[...]) * dpool_ref[...]).astype(BF16)
    dweight = head_sums(dpool_ref[...] * value_ref[0], fold_ref[...])
    dlogit = weight * (dweight - stat_ref[0])
    hi = dlogit.astype(BF16)
    dlogit_ref[0, :, :LANES] = hi
    dlogit_ref[0, :, LANES:] = (dlogit - hi.astype(F32)).astype(BF16)


def embed_body(
    n_space, me_ref, dvalue_ref, dlogit_ref, patches_ref, wv_ref, wback_ref, keep_ref, send_ref, cols_ref, extra_ref
):
    v = pl.program_id(0)
    hi, lo = dlogit_ref[0, :, :LANES].astype(F32), dlogit_ref[0, :, LANES:].astype(F32)
    group = iota(hi.shape, 1) >> 4
    mixed = jnp.where(group < 2, hi, jnp.where(group == 2, lo, 0.0)).astype(BF16)
    d_tokens = (mm(dvalue_ref[0], wv_ref[...], NT) + mm(mixed, wback_ref[...], NT)).astype(BF16)
    grad = mm(patches_ref[0], d_tokens, TN).astype(BF16)
    hi, lo, _ = parts3(jnp.sum(d_tokens.astype(F32), axis=0, keepdims=True))
    row = iota(extra_ref.shape, 0)
    extra = jnp.where(row == 2 * v, hi, jnp.where(row == 2 * v + 1, lo, 0.0))

    @pl.when(v == 0)
    def _():
        extra_ref[...] = extra

    @pl.when(v > 0)
    def _():
        extra_ref[...] += extra

    cols = cols_ref.shape[2]
    pixels = patches_ref.shape[2]
    for c in range(n_space):
        cols_ref[c] = grad[:, c * cols : (c + 1) * cols]
    at = pl.ds(pl.multiple_of(v * pixels, pixels), pixels)
    for k in range(0, n_space, 2):
        keep_ref[k // 2, at, :] = cols_ref[me_ref[1] ^ k]
        send_ref[k // 2, at, :] = cols_ref[me_ref[1] ^ (k + 1)]

    @pl.when(v == pl.num_programs(0) - 1)
    def _():
        tail = slice(keep_ref.shape[1] - 16, keep_ref.shape[1])
        for c in range(n_space):
            cols_ref[c, :16, :] = extra_ref[:, c * cols : (c + 1) * cols].astype(BF16)
        for k in range(0, n_space, 2):
            keep_ref[k // 2, tail, :] = cols_ref[me_ref[1] ^ k, :16, :]
            send_ref[k // 2, tail, :] = cols_ref[me_ref[1] ^ (k + 1), :16, :]


def embed_final_body(parts, *refs):
    ins, (grad_ref, offset_ref) = refs[:-2], refs[-2:]
    pixels = grad_ref.shape[1]
    base = 0
    for chunk in range(len(ins) // parts):
        total = 0.0
        for ref in ins[chunk * parts : (chunk + 1) * parts]:
            total = total + (ref[0] if len(ref.shape) == 3 else ref[...]).astype(F32)
        count = (total.shape[0] - 16) // pixels
        for v in range(count):
            grad_ref[base + v] = total[v * pixels : (v + 1) * pixels, :]
            row = count * pixels + 2 * v
            offset_ref[base + v : base + v + 1, :] = total[row : row + 1, :] + total[row + 1 : row + 2, :]
        base += count


def stack_body(*refs):
    for k, ref in enumerate(refs[:-1]):
        refs[-1][k] = ref[...]


def value_grad_body(me_ref, tokens_ref, dv_ref, dl_ref, keep_ref, send_ref, all_ref):
    width = dv_ref.shape[2]
    total, both = 0.0, 0.0
    for v in range(dv_ref.shape[0]):
        total = total + mm(tokens_ref[v], dv_ref[v], TN)
        both = both + mm(tokens_ref[v], dl_ref[v], TN)
    all_ref[:, :width] = total.astype(BF16)
    all_ref[:, width:] = pack(both[:, :LANES] + both[:, LANES:])
    block = keep_ref.shape[1]
    count = all_ref.shape[0] // block
    for r in range(count):
        target = pl.program_id(0) * count + r
        same = (target & 1) == (me_ref[0] & 1)
        slot = target >> 1

        @pl.when(same)
        def _():
            keep_ref[slot] = all_ref[r * block : (r + 1) * block, :]

        @pl.when(jnp.logical_not(same))
        def _():
            send_ref[slot] = all_ref[r * block : (r + 1) * block, :]


def pair_sum_body(n_chip, me_ref, keep_ref, got_ref, *out_refs):
    width = keep_ref.shape[2] - LANES
    for k in range(n_chip):
        slot = (me_ref[0] >> 1) ^ k
        mine, other = keep_ref[slot], got_ref[slot]
        out_refs[k][:, :width] = (mine[:, :width].astype(F32) + other[:, :width].astype(F32)).astype(BF16)
        out_refs[k][:, width:] = pack(unpack(mine[:, width:]) + unpack(other[:, width:]))


def packet_split_body(n_in, n_space, me_ref, *refs):
    ins, gathered_ref = refs[:n_in], refs[n_in]
    small_refs, out_refs = refs[n_in + 1 : n_in + 1 + n_space], refs[n_in + 1 + n_space : n_in + 1 + 2 * n_space]
    cols_ref = refs[-1]
    block, width = ins[0].shape[0], ins[0].shape[1] - LANES
    total = sum(ref[:, :width].astype(F32) for ref in ins).astype(BF16)
    factor = pack(sum(unpack(ref[:, width:]) for ref in ins))
    half = n_space // 2
    cols = cols_ref.shape[2]
    for c in range(half):
        cols_ref[c] = total[:, c * cols : (c + 1) * cols]
    height = gathered_ref.shape[1]
    part = small_refs[0].shape[0] - height
    for k in range(n_space):
        out_refs[k][...] = cols_ref[jnp.maximum((me_ref[1] ^ k) - half, 0)]
        small_refs[k][:height, :] = gathered_ref[me_ref[1] ^ k]
        for piece in range(block // part):
            lanes = slice(piece * LANES, (piece + 1) * LANES)
            small_refs[k][height:, lanes] = factor[piece * part : (piece + 1) * part, :]


def space_sum_body(n, *refs):
    small, large, (out_ref, weight_ref) = refs[:n], refs[n : 2 * n], refs[2 * n :]
    block, width = large[0].shape
    out_ref[:block, :width] = sum(ref[...].astype(F32) for ref in large).astype(BF16)
    height = block + 16 + weight_ref.shape[0]
    part = small[0].shape[0] - height
    for piece in range(block // part):
        lanes = slice(piece * LANES, (piece + 1) * LANES)
        factor = pack(sum(unpack(ref[height:, lanes]) for ref in small))
        out_ref[piece * part : (piece + 1) * part, width : width + LANES] = factor
    out_ref[block:, : width + LANES] = jnp.zeros((out_ref.shape[0] - block, width + LANES), BF16)
    total = sum(ref[:height, :].astype(F32) for ref in small)
    out_ref[:block, width + LANES :] = total[:block, :].astype(BF16)
    out_ref[block:, width + LANES :] = three_rows(jnp.sum(total[block : block + 16, :], axis=0, keepdims=True))
    weight_ref[...] = total[block + 16 :, :]


def add_body(n, keep_ref, got_ref, *refs):
    for j, out_ref in enumerate(refs):
        out_ref[...] = (keep_ref[j + 1].astype(F32) + got_ref[j + 1].astype(F32)).astype(BF16)


def final_body(n_var, n_space, scale, me_ref, even_ref, odd_ref, query_ref, wk_ref, kv_ref, gq_ref, out_ref, gain_ref):
    me_v, me_s = me_ref[0], me_ref[1]
    half = n_space // 2
    width = wk_ref.shape[1]
    size = width // HEADS
    cols, qcols = kv_ref.shape[1], gq_ref.shape[1]
    place = pl.multiple_of(jnp.minimum(me_s, half - 1) * cols, LANES)
    spread_kv = spread_matrix(cols, size, place)
    qplace = pl.multiple_of(me_s * qcols, LANES)
    spread_q = spread_matrix(qcols, size, qplace)
    query = query_ref[:, pl.ds(place, cols)] * scale
    block = even_ref.shape[1] - 16
    total, gain = 0.0, 0.0
    for k in range(n_var):
        part_ref, slot = (odd_ref if k % 2 else even_ref), k // 2
        at = pl.ds(pl.multiple_of((me_v ^ k) * block, block), block)
        packed = part_ref[slot, :block, cols : cols + LANES]
        key_grad = mm(packed, spread_kv) * query
        kv_ref[at, :] = jnp.where(me_s < half, key_grad, part_ref[slot, :block, :cols].astype(F32))
        keys = wk_ref[at, pl.ds(qplace, qcols)].astype(F32)
        total = total + jnp.sum(mm(packed, spread_q) * keys, axis=0, keepdims=True)
        out_ref[at, :] = part_ref[slot, :block, cols + LANES :].astype(F32)
        gain = gain + jnp.sum(part_ref[slot, block:, cols + LANES :].astype(F32), axis=0, keepdims=True)
    gq_ref[...] = total * scale
    gain_ref[...] = gain


def shards(
    patches, embed_weight, var_embed, agg_query, agg_kv, agg_out, norm_gain, qkv_weight, out_weight, cotangent
):
    n_var, n_space = lax.axis_size("var"), lax.axis_size("space")
    count, rows, pixels = patches.shape
    width = agg_out.shape[0]
    size = width // HEADS
    scale = 1.0 / math.sqrt(size)
    block = rows // n_var
    cols = width // n_space
    group = out_weight.shape[0]
    drows = width // n_var
    positions = rows * n_space
    kv_cols = 2 * width // n_space
    me = jnp.stack([lax.axis_index("var"), lax.axis_index("space")]).astype(jnp.int32)
    gain = norm_gain.reshape(1, width)
    query = agg_query.reshape(1, width)
    vmem = pl.BlockSpec(memory_space=pltpu.VMEM)
    packet = width + LANES

    whole = lambda shape: pl.BlockSpec(shape, lambda v: (0,) * len(shape))
    every = lambda shape: pl.BlockSpec((1,) + shape, lambda v: (v,) + (0,) * len(shape))
    n_chip = n_var // 2
    tokens, scores, w_back = call(
        functools.partial(tokens_body, scale),
        [struct((count, rows, width), BF16), struct((count, rows, LANES), F32), struct((width, LANES), BF16)],
        limit=LIMITS["tokens"],
        grid=(count,),
        in_specs=[
            every((rows, pixels)),
            every((pixels, width)),
            whole((count, width)),
            whole((1, width)),
            pl.BlockSpec((width, width), lambda v: (0, 0)),
        ],
        out_specs=[every((rows, width)), every((rows, LANES)), whole((width, LANES))],
        scratch_shapes=[pltpu.VMEM((width, 3 * LANES), BF16)],
        cost_estimate=cost(6e9, 2e7),
        name="tokens",
    )(patches, embed_weight, var_embed, query, agg_kv)
    value, keep, send = call(
        functools.partial(forward_body, count),
        [struct((count, rows, width), F32)] + [struct((n_chip, block, packet), F32)] * 2,
        limit=LIMITS["forward"],
        grid=(count,),
        in_specs=[
            SMEM,
            every((rows, width)),
            whole((count, rows, LANES)),
            pl.BlockSpec((width, width), lambda v: (0, 1)),
        ],
        out_specs=[every((rows, width))] + [whole((n_chip, block, packet))] * 2,
        scratch_shapes=[
            pltpu.VMEM((rows, LANES), F32),
            pltpu.VMEM((LANES, width), BF16),
            pltpu.VMEM((rows, width), F32),
        ],
        cost_estimate=cost(4e9, 1e7),
        name="forward",
    )(me, tokens, scores, agg_kv)

    def pool_pairs(mine, got):
        return call(
            pool_pair_body,
            [struct((block, packet), F32)] * n_chip,
            limit=LIMITS["pool_pair"],
            in_specs=[SMEM, vmem, vmem],
            cost_estimate=cost(1e8, 3e6),
            name="pool_pair",
        )(me, mine, got)

    received = exchange_pairs(keep, send, pool_pairs)
    dattn, cot_own, w_heads = call(
        early_body,
        [struct((rows, group), BF16), struct((block, width), BF16), struct(qkv_weight.shape, BF16)],
        limit=LIMITS["early"],
        after=[received[0]],
        in_specs=[SMEM] + [vmem] * 3,
        cost_estimate=cost(2e8, 4e6),
        name="early",
    )(me, cotangent, out_weight, qkv_weight)
    dattn_all = gather_direct(dattn, "space")

    mixed, pooled_packet = call(
        functools.partial(pool_body, n_chip),
        [struct((block, width), F32), struct((block, packet), BF16)],
        limit=LIMITS["pool"],
        after=dattn_all[1:],
        cost_estimate=cost(1e8, 2e6),
        name="pool",
    )(*received)
    pooled_even, pooled_odd = gather_pairs(pooled_packet, "var")

    qkv, normed, pooled_packets, centred, inv = call(
        norm_body,
        [
            struct((rows, 3 * group), BF16),
            struct((rows, width), BF16),
            struct((rows, packet), BF16),
            struct((block, width), F32),
            struct((block, LANES), F32),
        ],
        limit=LIMITS["norm"],
        in_specs=[SMEM] + [vmem] * 5,
        scratch_shapes=[pltpu.VMEM((rows, width), F32), pltpu.VMEM((rows, LANES), F32)],
        cost_estimate=cost(8e8, 5e6),
        name="norm",
    )(me, pooled_even, pooled_odd, agg_out, gain, w_heads)

    qkv_all = gather_direct(qkv, "space")
    normed_cols = call(
        functools.partial(columns_body, n_space),
        [struct((rows, cols), BF16)] * n_space,
        limit=LIMITS["columns"],
        after=qkv_all[1:],
        in_specs=[SMEM, vmem],
        scratch_shapes=[pltpu.VMEM((n_space, rows, cols), BF16)],
        cost_estimate=cost(1e6, 1e6),
        name="columns",
    )(me, normed)
    normed_all = exchange_direct(normed_cols, "space")
    attn, dqkv = call(
        functools.partial(attention_body, n_space, size, scale),
        [struct((positions, group), BF16), struct((positions, 3 * group), BF16)],
        limit=LIMITS["attention"],
        after=[normed_cols[0]],
        scratch_shapes=[pltpu.VMEM((positions, group), BF16)] * 2 + [pltpu.VMEM((positions, group), F32)] * 2,
        cost_estimate=cost(6e9, 4e6),
        name="attention",
    )(*qkv_all, *dattn_all)
    dn_keep, dn_send = call(
        dn_body,
        [struct((n_chip, block, width), BF16)] * 2,
        limit=LIMITS["dn"],
        after=normed_all[1:],
        grid=(1,),
        in_specs=[SMEM, pl.BlockSpec((rows, 3 * group), lambda i: (0, 0)), vmem],
        scratch_shapes=[pltpu.VMEM((rows, width), BF16)],
        cost_estimate=cost(2e8, 1e6),
        name="dn",
    )(me, dqkv, w_heads)

    def dn_pairs(mine, got):
        return call(
            dn_pair_body,
            [struct((block, width), BF16)] * n_chip,
            limit=LIMITS["dn_pair"],
            in_specs=[SMEM, vmem, vmem],
            cost_estimate=cost(1e6, 1e6),
            name="dn_pair",
        )(me, mine, got)

    dn_received = exchange_pairs(dn_keep, dn_send, dn_pairs)
    joined_packet, dgain = call(
        functools.partial(joined_body, n_chip),
        [struct((block, packet), BF16), struct((8, width), F32)],
        limit=LIMITS["joined"],
        cost_estimate=cost(2e8, 3e6),
        name="joined",
    )(*dn_received, centred, inv, gain, cot_own, mixed, agg_out)
    joined_even, joined_odd = gather_pairs(joined_packet, "var")

    d_joined, d_pooled, stat = call(
        prepare_body,
        [struct((rows, packet), BF16), struct((rows, width), F32), struct((3, rows, LANES), F32)],
        limit=LIMITS["prepare"],
        in_specs=[SMEM] + [vmem] * 4,
        cost_estimate=cost(6e8, 4e6),
        name="prepare",
    )(me, pooled_packets, joined_even, joined_odd, agg_out)
    d_value, d_logit = call(
        dvalue_body,
        [struct((count, rows, width), BF16), struct((count, rows, 2 * LANES), BF16)],
        limit=LIMITS["dvalue"],
        grid=(count,),
        in_specs=[whole((rows, width)), whole((3, rows, LANES)), every((rows, width)), every((rows, LANES))],
        out_specs=[every((rows, width)), every((rows, 2 * LANES))],
        scratch_shapes=[pltpu.VMEM((LANES, width), BF16), pltpu.VMEM((width, LANES), BF16)],
        cost_estimate=cost(4e9, 1e7),
        name="dvalue",
    )(d_pooled, stat, value, scores)

    step = max(drows, 256)
    kv_keep, kv_send = call(
        value_grad_body,
        [struct((n_chip, drows, packet), BF16)] * 2,
        limit=LIMITS["value_grad"],
        grid=(width // step,),
        in_specs=[
            SMEM,
            pl.BlockSpec((count, rows, step), lambda i: (0, 0, i)),
            whole((count, rows, width)),
            whole((count, rows, 2 * LANES)),
        ],
        out_specs=[whole((n_chip, drows, packet))] * 2,
        scratch_shapes=[pltpu.VMEM((step, packet), BF16)],
        cost_estimate=cost(4e9, 1e7),
        name="value_grad",
    )(me, tokens, d_value, d_logit)
    kv_got = swap(kv_send, "var", 1)

    out_block = call(
        out_grad_body,
        struct((n_space, drows + 16 + group, cols), BF16),
        limit=LIMITS["out_grad"],
        after=[kv_keep],
        grid=(1,),
        in_specs=[SMEM] + [whole(x.shape) for x in (pooled_packets, d_joined, dgain)] + [whole((rows, group)), whole((rows, width))],
        out_specs=whole((n_space, drows + 16 + group, cols)),
        scratch_shapes=[pltpu.VMEM((width, width), F32)],
        cost_estimate=cost(6e8, 3e6),
        name="out_grad",
    )(me, pooled_packets, d_joined, dgain, attn, cotangent)

    def embed(start, here, after):
        at = lambda shape: pl.BlockSpec((1,) + shape, lambda v: (v + start,) + (0,) * len(shape))
        half = (n_space // 2, here * pixels + 16, cols)
        return call(
            functools.partial(embed_body, n_space),
            [struct(half, BF16)] * 2,
            limit=LIMITS["embed"],
            after=after,
            grid=(here,),
            in_specs=[
                SMEM,
                at((rows, width)),
                at((rows, 2 * LANES)),
                at((rows, pixels)),
                pl.BlockSpec((width, width), lambda v: (0, 1)),
                whole((width, LANES)),
            ],
            out_specs=[whole(half)] * 2,
            scratch_shapes=[pltpu.VMEM((n_space, pixels, cols), BF16), pltpu.VMEM((16, width), F32)],
            cost_estimate=cost(1.5e9, 4e6),
            name="embed",
        )(me, d_value, d_logit, patches, agg_kv, w_back)

    def scatter_embed(keep, arrived, after):
        n = n_space // 2 - 1
        sums = call(
            functools.partial(add_body, n),
            [struct(keep.shape[1:], BF16)] * n,
            limit=LIMITS["add"],
            after=after,
            cost_estimate=cost(1e6, 1e6),
            name="add",
        )(keep, arrived)
        blocks = {2 * (j + 1): sums[j] for j in range(n)}
        mine, bit = [keep, arrived], 2
        while bit < n_space:
            got = {k ^ bit: swap(blocks[k], "space", bit) for k in blocks if k & bit and k % bit == 0}
            mine.append(got[0])
            for k in got:
                if k:
                    blocks[k] = (blocks[k].astype(F32) + got[k].astype(F32)).astype(BF16)
            bit *= 2
        return mine, list(sums)

    half = count // 2
    keep0, send0 = embed(0, half, [kv_keep])
    arrived0 = swap(send0, "space", 1)
    keep1, send1 = embed(half, count - half, [])
    arrived1 = swap(send1, "space", 1)

    kv_blocks = call(
        functools.partial(pair_sum_body, n_chip),
        [struct((drows, packet), BF16)] * n_chip,
        limit=LIMITS["pair_sum"],
        in_specs=[SMEM] + [vmem] * 2,
        cost_estimate=cost(1e6, 1e6),
        name="pair_sum",
    )(me, kv_keep, kv_got)
    kv_parts = [kv_blocks[0]] + [swap(kv_blocks[k], "var", 2 * k) for k in range(1, n_chip)]
    mine0, sums0 = scatter_embed(keep0, arrived0, [kv_parts[-1]])
    height = drows + 16 + group
    part = drows * LANES // cols
    pieces = call(
        functools.partial(packet_split_body, n_chip, n_space),
        [struct((height + part, cols), BF16)] * n_space + [struct((drows, kv_cols), BF16)] * n_space,
        limit=LIMITS["packet_split"],
        after=sums0,
        in_specs=[SMEM] + [vmem] * (n_chip + 1),
        scratch_shapes=[pltpu.VMEM((n_space // 2, drows, kv_cols), BF16)],
        cost_estimate=cost(1e6, 1e6),
        name="packet_split",
    )(me, *kv_parts, out_block)
    small, large = pieces[:n_space], pieces[n_space:]
    mine1, sums1 = scatter_embed(keep1, arrived1, [small[0]])
    grad_qkv, head_flag = call(
        functools.partial(head_grads_body, n_space),
        [struct((cols, 3 * group), F32), struct((8, LANES), F32)],
        limit=LIMITS["head_grads"],
        cost_estimate=cost(1e9, 3e6),
        name="head_grads",
    )(*normed_all, dqkv)
    small_all = exchange_direct(small, "space")
    large_all = [large[0]] + [
        swap(large[k], "space", k, lambda target: target >= n_space // 2) for k in range(1, n_space)
    ]
    kv_sum, grad_out = call(
        functools.partial(space_sum_body, n_space),
        [struct((drows + 16, kv_cols + LANES + cols), BF16), struct((group, cols), F32)],
        limit=LIMITS["space_sum"],
        after=mine0[2:] + sums1 + [head_flag],
        cost_estimate=cost(1e6, 1e6),
        name="space_sum",
    )(*small_all, *large_all)

    def stack(parts):
        return call(
            stack_body,
            struct((len(parts),) + parts[0].shape, BF16),
            after=mine1[2:],
            cost_estimate=cost(1e6, 1e6),
            name="stack",
        )(*parts)

    kv_even, kv_odd = gather_pairs(kv_sum, "var", stack)
    grad_agg_kv, grad_query, grad_agg_out, grad_gain = call(
        functools.partial(final_body, n_var, n_space, scale),
        [struct((width, kv_cols), F32), struct((1, cols), F32)] + [struct((width, cols), F32), struct((1, cols), F32)],
        grid=(1,),
        in_specs=[SMEM] + [vmem] * 3 + [pl.BlockSpec((width, width), lambda i: (0, 0))],
        limit=LIMITS["final"],
        cost_estimate=cost(2e8, 5e6),
        name="final",
    )(me, kv_even, kv_odd, query, agg_kv)

    def first_block(x):
        if x.ndim == 3:
            return pl.BlockSpec((1,) + x.shape[1:], lambda i: (0, 0, 0))
        return pl.BlockSpec(x.shape, lambda i: (0, 0))

    grad_embed, grad_var_embed = call(
        functools.partial(embed_final_body, len(mine0)),
        [struct((count, pixels, cols), F32), struct((count, cols), F32)],
        grid=(1,),
        in_specs=[first_block(x) for x in mine0 + mine1],
        limit=LIMITS["embed_final"],
        cost_estimate=cost(1e6, 1e6),
        name="embed_final",
    )(*mine0, *mine1)

    return (
        grad_embed,
        grad_var_embed,
        grad_query.reshape(cols),
        grad_agg_kv,
        grad_agg_out,
        grad_gain.reshape(cols),
        grad_qkv,
        grad_out,
    )


def solution(mesh):
    return jax.shard_map(
        shards,
        mesh=mesh,
        in_specs=(
            P("var", "space", None),
            P("var", None, None),
            P("var", None),
            P(),
            P(),
            P(),
            P(),
            P(None, "var"),
            P("var", None),
            P("space", None),
        ),
        out_specs=(
            P("var", None, "space"),
            P("var", "space"),
            P("space"),
            P(None, "space"),
            P(None, "space"),
            P("space"),
            P("space", "var"),
            P("var", "space"),
        ),
        check_vma=False,
    )
```

```python
import functools
import math

import jax
import jax.numpy as jnp
from jax import lax
from jax.experimental import pallas as pl
from jax.experimental.pallas import tpu as pltpu
from jax.sharding import PartitionSpec as P

HEADS = 16
LANES = 128
EPSILON = 1e-05
MIB = 1 << 20

LIMITS = {
    "early": 60, "forward": 56, "columns": 8, "pool_pair": 16, "pool": 16, "norm": 16, "attention": 24,
    "dn": 12, "dn_pair": 16, "joined": 16, "prepare": 16, "out_grad": 16, "dvalue": 24, "embed": 24, "value_grad": 32,
    "add": 12, "pair_sum": 16, "packet_split": 16, "space_sum": 16, "head_grads": 16, "final": 16, "embed_final": 24,
}

F32 = jnp.float32
BF16 = jnp.bfloat16

NN = (((1,), (0,)), ((), ()))
NT = (((1,), (1,)), ((), ()))
TN = (((0,), (0,)), ((), ()))


def mm(a, b, dims=NN):
    return lax.dot_general(a, b, dims, preferred_element_type=F32)


def iota(shape, axis):
    return lax.broadcasted_iota(jnp.int32, shape, axis)


def parts3(x):
    hi = x.astype(BF16).astype(F32)
    rest = x - hi
    mid = rest.astype(BF16).astype(F32)
    return hi, mid, rest - mid


def pack(x, y=None):
    group = iota(x.shape, 1) >> 4
    hi, mid, lo = parts3(x)
    out = jnp.where(group == 0, hi, jnp.where(group == 1, mid, jnp.where(group == 2, lo, 0.0)))
    if y is not None:
        hi, mid, lo = parts3(y)
        out = jnp.where(group == 3, hi, jnp.where(group == 4, mid, jnp.where(group == 5, lo, out)))
    return out.astype(BF16)


def unpack(packed, first_group=0):
    row, column = iota((LANES, LANES), 0), iota((LANES, LANES), 1)
    group = row >> 4
    take = ((row & 15) == (column & 15)) & (group >= first_group) & (group < first_group + 3)
    return mm(packed, jnp.where(take, 1.0, 0.0).astype(BF16))


def spread_matrix(width, size, first=0):
    row, column = iota((LANES, width), 0), iota((LANES, width), 1)
    shift = size.bit_length() - 1
    take = ((row & 15) == ((column + first) >> shift)) & (row < 48)
    return jnp.where(take, 1.0, 0.0).astype(BF16)


def fold_matrix(width, size):
    row, column = iota((width, LANES), 0), iota((width, LANES), 1)
    shift = size.bit_length() - 1
    return jnp.where((column & 15) == (row >> shift), 1.0, 0.0).astype(BF16)


def head_sums(x, fold):
    hi, mid, lo = parts3(x)
    return mm(hi.astype(BF16), fold) + mm(mid.astype(BF16), fold) + mm(lo.astype(BF16), fold)


def call(body, out_shape, limit=16, after=(), in_specs=None, **kw):
    def run(*args):
        n, m = len(args), len(after)
        vmem = pl.BlockSpec(memory_space=pltpu.VMEM)
        return pl.pallas_call(
            lambda *refs: body(*refs[:n], *refs[n + m :]),
            out_shape=out_shape,
            in_specs=([vmem] * n if in_specs is None else list(in_specs)) + [vmem] * m,
            compiler_params=pltpu.CompilerParams(vmem_limit_bytes=limit * MIB),
            **kw,
        )(*args, *after)

    return run


def struct(shape, dtype):
    return jax.ShapeDtypeStruct(shape, dtype)


def cost(flops, moved):
    return pl.CostEstimate(flops=int(flops), bytes_accessed=int(moved), transcendentals=0)


SMEM = pl.BlockSpec(memory_space=pltpu.SMEM)


def swap(x, axis, k, keep=None):
    pairs = [(i, i ^ k) for i in range(lax.axis_size(axis))]
    if keep is not None:
        pairs = [pair for pair in pairs if keep(pair[1])]
    return lax.ppermute(x, axis, pairs)


def gather_direct(x, axis):
    return [x] + [swap(x, axis, k) for k in range(1, lax.axis_size(axis))]


def exchange_direct(blocks, axis):
    return [blocks[0]] + [swap(blocks[k], axis, k) for k in range(1, len(blocks))]


def gather_pairs(x, axis, stack=jnp.stack):
    even = [x] + [swap(x, axis, k) for k in range(2, lax.axis_size(axis), 2)]
    even = stack(even)
    return even, swap(even, axis, 1)


def exchange_pairs(keep, send, combine):
    parts = combine(keep, swap(send, "var", 1))
    return [parts[0]] + [swap(parts[k], "var", 2 * k) for k in range(1, len(parts))]


def pair_rows(me_v, k, odd, block):
    device = (((me_v >> 1) ^ k) << 1) + ((me_v & 1) ^ odd)
    return pl.ds(pl.multiple_of(device * block, block), block)


def three_rows(x):
    hi, mid, lo = parts3(x)
    row = iota((16, x.shape[1]), 0)
    return jnp.where(row == 0, hi, jnp.where(row == 1, mid, jnp.where(row == 2, lo, 0.0))).astype(BF16)


def head_order(width, size=64):
    heads = width // (3 * size)
    row, column = iota((width, width), 0), iota((width, width), 1)
    take = jnp.zeros((width, width), jnp.bool_)
    for h in range(heads):
        for c in range(3):
            start, target = h * 3 * size + c * size, c * heads * size + h * size
            inside = (column >= target) & (column < target + size)
            take = take | (inside & ((row - start) == (column - target)))
    return jnp.where(take, 1.0, 0.0).astype(BF16)


def early_body(me_ref, cot_ref, outw_ref, qkvw_ref, dattn_ref, own_ref, wperm_ref):
    dattn_ref[...] = mm(cot_ref[...], outw_ref[...], NT).astype(BF16)
    block = own_ref.shape[0]
    own_ref[...] = cot_ref[pl.ds(pl.multiple_of(me_ref[0] * block, block), block), :]
    wperm_ref[...] = mm(qkvw_ref[...], head_order(qkvw_ref.shape[1])).astype(BF16)


def forward_step(fresh, patches_ref, embed_ref, offset, wq_ref, wv_ref, spread_ref, outs, state):
    tokens_ref, value_ref, scores_ref = outs
    acc_ref, max_ref, sum_ref = state
    tokens = (mm(patches_ref[0], embed_ref[0]) + offset).astype(BF16)
    tokens_ref[0] = tokens
    pieces = mm(tokens, wq_ref[...])
    scores = pieces[:, :LANES] + pieces[:, LANES : 2 * LANES] + pieces[:, 2 * LANES :]
    scores_ref[0] = scores
    value = mm(tokens, wv_ref[...])
    value_ref[0] = value

    @pl.when(fresh)
    def _():
        max_ref[...] = scores
        sum_ref[...] = jnp.ones_like(scores)
        acc_ref[...] = value

    @pl.when(jnp.logical_not(fresh))
    def _():
        top = jnp.maximum(max_ref[...], scores)
        old, new = jnp.exp(max_ref[...] - top), jnp.exp(scores - top)
        max_ref[...] = top
        sum_ref[...] = sum_ref[...] * old + new
        acc_ref[...] = acc_ref[...] * mm(pack(old), spread_ref[...]) + value * mm(pack(new), spread_ref[...])


def first_body(
    scale, patches_ref, embed_ref, offset_ref, query_ref, wk_ref, wv_ref,
    tokens_ref, value_ref, scores_ref, wq_ref, wback_ref, acc_ref, max_ref, sum_ref, spread_ref,
):
    v = pl.program_id(0)
    width = wk_ref.shape[1]
    size = width // HEADS

    @pl.when(v == 0)
    def _():
        row, column = iota((LANES, width), 0), iota((LANES, width), 1)
        own = (row & 15) == (column >> (size.bit_length() - 1))
        wq = jnp.zeros((width, LANES), F32)
        for part in parts3(query_ref[...]):
            wq = wq + mm(wk_ref[...], jnp.where(own, part, 0.0).astype(BF16), NT)
        hi, mid, lo = parts3(wq * scale)
        wq_ref[:, :LANES] = hi.astype(BF16)
        wq_ref[:, LANES : 2 * LANES] = mid.astype(BF16)
        wq_ref[:, 2 * LANES :] = lo.astype(BF16)
        group = iota((width, LANES), 1) >> 4
        back = jnp.where((group == 0) | (group == 2), hi, jnp.where(group == 1, mid, 0.0))
        wback_ref[...] = back.astype(BF16)
        spread_ref[...] = spread_matrix(width, size)

    forward_step(
        v == 0, patches_ref, embed_ref, offset_ref[pl.ds(v, 1), :], wq_ref, wv_ref, spread_ref,
        (tokens_ref, value_ref, scores_ref), (acc_ref, max_ref, sum_ref),
    )


def second_body(
    start, me_ref, patches_ref, embed_ref, offset_ref, wq_ref, wv_ref, acc0_ref, max0_ref, sum0_ref,
    tokens_ref, value_ref, scores_ref, keep_ref, send_ref, spread_ref, acc_ref, max_ref, sum_ref,
):
    v = pl.program_id(0)
    width = wv_ref.shape[1]

    @pl.when(v == 0)
    def _():
        spread_ref[...] = spread_matrix(width, width // HEADS)
        acc_ref[...] = acc0_ref[...]
        max_ref[...] = max0_ref[...]
        sum_ref[...] = sum0_ref[...]

    forward_step(
        v < 0, patches_ref, embed_ref, offset_ref[pl.ds(start + v, 1), :], wq_ref, wv_ref, spread_ref,
        (tokens_ref, value_ref, scores_ref), (acc_ref, max_ref, sum_ref),
    )

    @pl.when(v == pl.num_programs(0) - 1)
    def _():
        low = iota(max_ref.shape, 1) < LANES // 2
        max_ref[...] = jnp.where(low, max_ref[...], sum_ref[...])
        block = keep_ref.shape[1]
        core = me_ref[0] & 1
        for c in range(keep_ref.shape[0]):
            for ref, device in ((keep_ref, 2 * c + core), (send_ref, 2 * c + 1 - core)):
                at = pl.ds(pl.multiple_of(device * block, block), block)
                ref[c, :, :width] = acc_ref[at, :]
                ref[c, :, width:] = max_ref[at, :]


def halves_of(both):
    low = iota(both.shape, 1) < LANES // 2
    turned = pltpu.roll(both, LANES // 2, 1)
    return jnp.where(low, both, turned), jnp.where(low, turned, both)


def pool_pair_body(me_ref, keep_ref, got_ref, *out_refs):
    width = keep_ref.shape[2] - LANES
    spread = spread_matrix(width, width // HEADS)
    low = iota((keep_ref.shape[1], LANES), 1) < LANES // 2
    for k, out_ref in enumerate(out_refs):
        slot = (me_ref[0] >> 1) ^ k
        mine, other = keep_ref[slot], got_ref[slot]
        max_a, sum_a = halves_of(mine[:, width:])
        max_b, sum_b = halves_of(other[:, width:])
        top = jnp.maximum(max_a, max_b)
        factor_a, factor_b = jnp.exp(max_a - top), jnp.exp(max_b - top)
        out_ref[:, :width] = mine[:, :width] * mm(pack(factor_a), spread) + other[:, :width] * mm(pack(factor_b), spread)
        out_ref[:, width:] = jnp.where(low, top, sum_a * factor_a + sum_b * factor_b)


def pool_body(n, *refs):
    ins, (mixed_ref, packet_ref) = refs[:n], refs[n:]
    width = mixed_ref.shape[1]
    stats = [halves_of(ref[:, width:]) for ref in ins]
    top = functools.reduce(jnp.maximum, [m for m, _ in stats])
    factors = [jnp.exp(m - top) for m, _ in stats]
    total = sum(s * f for (_, s), f in zip(stats, factors))
    spread = spread_matrix(width, width // HEADS)
    mixed = jnp.zeros(mixed_ref.shape, F32)
    for ref, factor in zip(ins, factors):
        mixed = mixed + ref[:, :width] * mm(pack(factor / total), spread)
    mixed_ref[...] = mixed
    packet_ref[:, :width] = mixed.astype(BF16)
    packet_ref[:, width:] = pack(top, total)


def norm_body(
    me_ref, even_ref, odd_ref, agg_ref, gain_ref, w_ref, qkv_ref, normed_ref, packets_ref, centred_ref, inv_ref,
    all_ref, allinv_ref,
):
    width = agg_ref.shape[0]
    block = centred_ref.shape[0]
    for k in range(even_ref.shape[0]):
        for odd, ref in ((0, even_ref), (1, odd_ref)):
            packets_ref[pair_rows(me_ref[0], k, odd, block), :] = ref[k]
    joined = mm(packets_ref[:, :width], agg_ref[...]).astype(BF16).astype(F32)
    mean = jnp.mean(joined, axis=-1, keepdims=True)
    spread_sq = jnp.mean((joined - mean) ** 2, axis=-1, keepdims=True)
    inv = lax.rsqrt(spread_sq + EPSILON)
    centred = (joined - mean) * inv
    normed = (centred * gain_ref[...]).astype(BF16)
    qkv_ref[...] = mm(normed, w_ref[...]).astype(BF16)
    normed_ref[...] = normed
    all_ref[...] = centred
    allinv_ref[...] = jnp.broadcast_to(inv, allinv_ref.shape)
    start = pl.multiple_of(me_ref[0] * block, block)
    centred_ref[...] = all_ref[pl.ds(start, block), :]
    inv_ref[...] = allinv_ref[pl.ds(start, block), :]


def attention_body(n_space, size, scale, *refs):
    qkv_refs, dattn_refs = refs[:n_space], refs[n_space : 2 * n_space]
    attn_ref, dqkv_ref, k_ref, v_ref, dk_ref, dv_ref = refs[2 * n_space :]
    rows, group = dattn_refs[0].shape
    heads = group // size
    for b in range(n_space):
        at = slice(b * rows, (b + 1) * rows)
        k_ref[at, :] = qkv_refs[b][:, group : 2 * group]
        v_ref[at, :] = qkv_refs[b][:, 2 * group :]
    lane_head = iota((rows, group), 1) // size if heads > 1 else None
    for b in range(n_space):
        at = slice(b * rows, (b + 1) * rows)
        queries, d_out = qkv_refs[b][:, :group], dattn_refs[b][...]
        attn = dq = None
        for h in range(heads):
            if heads > 1:
                q_h = jnp.where(lane_head == h, queries.astype(F32), 0.0).astype(BF16)
                do_h = jnp.where(lane_head == h, d_out.astype(F32), 0.0).astype(BF16)
            else:
                q_h, do_h = queries, d_out
            logits = mm(q_h, k_ref[...], NT) * scale
            shifted = jnp.exp(logits - jnp.max(logits, axis=-1, keepdims=True))
            probs = shifted * (1.0 / jnp.sum(shifted, axis=-1, keepdims=True))
            probs_b = probs.astype(BF16)
            attn_h = mm(probs_b, v_ref[...])
            dprob = mm(do_h, v_ref[...], NT)
            delta = jnp.sum(probs * dprob, axis=-1, keepdims=True)
            dscore = (probs * (dprob - delta) * scale).astype(BF16)
            dq_h = mm(dscore, k_ref[...])
            dk = mm(dscore, q_h, TN)
            dv = mm(probs_b, do_h, TN)
            if b == 0 and h == 0:
                dk_ref[...] = dk
                dv_ref[...] = dv
            else:
                dk_ref[...] += dk
                dv_ref[...] += dv
            attn = attn_h if attn is None else jnp.where(lane_head == h, attn_h, attn)
            dq = dq_h if dq is None else jnp.where(lane_head == h, dq_h, dq)
        attn_ref[at, :] = attn.astype(BF16)
        dqkv_ref[at, :group] = dq.astype(BF16)
    dqkv_ref[:, group : 2 * group] = dk_ref[...].astype(BF16)
    dqkv_ref[:, 2 * group :] = dv_ref[...].astype(BF16)


def dn_body(me_ref, dqkv_ref, w_ref, keep_ref, send_ref, dn_ref):
    dn_ref[...] = mm(dqkv_ref[...], w_ref[...], NT).astype(BF16)
    block = keep_ref.shape[1]
    core = me_ref[0] & 1
    for c in range(keep_ref.shape[0]):
        for ref, device in ((keep_ref, 2 * c + core), (send_ref, 2 * c + 1 - core)):
            ref[c] = dn_ref[pl.ds(pl.multiple_of(device * block, block), block), :]


def columns_body(n_space, me_ref, in_ref, *refs):
    out_refs, (cols_ref,) = refs[:n_space], refs[n_space:]
    cols = cols_ref.shape[2]
    for c in range(n_space):
        cols_ref[c] = in_ref[:, c * cols : (c + 1) * cols]
    for k in range(n_space):
        out_refs[k][...] = cols_ref[me_ref[1] ^ k]


def head_grads_body(n_space, *refs):
    normed_refs, (dqkv_ref, gqkv_ref, flag_ref) = refs[:n_space], refs[n_space:]
    flag_ref[...] = jnp.zeros(flag_ref.shape, F32)
    rows = normed_refs[0].shape[0]
    natural = mm(dqkv_ref[...], head_order(dqkv_ref.shape[1]), NT).astype(BF16)
    gqkv_ref[...] = sum(
        mm(ref[...], natural[b * rows : (b + 1) * rows, :], TN) for b, ref in enumerate(normed_refs)
    )


def dn_pair_body(me_ref, keep_ref, got_ref, *out_refs):
    for k, out_ref in enumerate(out_refs):
        slot = (me_ref[0] >> 1) ^ k
        out_ref[...] = (keep_ref[slot].astype(F32) + got_ref[slot].astype(F32)).astype(BF16)


def joined_body(n, *refs):
    ins = refs[:n]
    centred_ref, inv_ref, gain_ref, cot_ref, mixed_ref, agg_ref, packet_ref, dgain_ref = refs[n:]
    width = centred_ref.shape[1]
    d_normed = sum(ref[...].astype(F32) for ref in ins)
    centred = centred_ref[...]
    dgain_ref[...] = jnp.broadcast_to(jnp.sum(d_normed * centred, axis=0, keepdims=True), dgain_ref.shape)
    gained = d_normed * gain_ref[...]
    inner = (
        gained
        - jnp.mean(gained, axis=-1, keepdims=True)
        - centred * jnp.mean(gained * centred, axis=-1, keepdims=True)
    )
    d_joined = (cot_ref[...].astype(F32) + inner * inv_ref[:, :1]).astype(BF16)
    d_pooled = mm(d_joined, agg_ref[...], NT)
    center = pack(head_sums(d_pooled * mixed_ref[...], fold_matrix(width, width // HEADS)))
    packet_ref[:, :width] = d_joined
    packet_ref[:, width:] = center


def prepare_body(me_ref, pooled_ref, even_ref, odd_ref, agg_ref, djoined_ref, dpool_ref, stat_ref):
    width = agg_ref.shape[0]
    for k in range(even_ref.shape[0]):
        for odd, ref in ((0, even_ref), (1, odd_ref)):
            djoined_ref[pair_rows(me_ref[0], k, odd, even_ref.shape[1]), :] = ref[k]
    dpool_ref[...] = mm(djoined_ref[:, :width], agg_ref[...], NT)
    stat_ref[0] = unpack(djoined_ref[:, width:])
    stat_ref[1] = unpack(pooled_ref[:, width:])
    stat_ref[2] = 1.0 / unpack(pooled_ref[:, width:], 3)


def out_grad_body(me_ref, pooled_ref, djoined_ref, dgain_ref, attn_ref, cot_ref, out_ref, all_ref):
    width = dgain_ref.shape[1]
    all_ref[...] = mm(pooled_ref[:, :width], djoined_ref[:, :width], TN)
    weight_grad = mm(attn_ref[...], cot_ref[...], TN).astype(BF16)
    n_space, height, cols = out_ref.shape
    block = height - 16 - weight_grad.shape[0]
    start = pl.multiple_of(me_ref[0] * block, block)
    own = all_ref[pl.ds(start, block), :].astype(BF16)
    extra = three_rows(dgain_ref[:1, :])
    for c in range(n_space):
        out_ref[c, :block, :] = own[:, c * cols : (c + 1) * cols]
        out_ref[c, block : block + 16, :] = extra[:, c * cols : (c + 1) * cols]
        out_ref[c, block + 16 :, :] = weight_grad[:, c * cols : (c + 1) * cols]


def dvalue_body(dpool_ref, stat_ref, value_ref, scores_ref, dvalue_ref, dlogit_ref, spread_ref, fold_ref):
    width = dpool_ref.shape[1]
    size = width // HEADS

    @pl.when(pl.program_id(0) == 0)
    def _():
        spread_ref[...] = spread_matrix(width, size)
        fold_ref[...] = fold_matrix(width, size)

    weight = jnp.exp(scores_ref[0] - stat_ref[1]) * stat_ref[2]
    dvalue_ref[0] = (mm(pack(weight), spread_ref[...]) * dpool_ref[...]).astype(BF16)
    dweight = head_sums(dpool_ref[...] * value_ref[0], fold_ref[...])
    dlogit = weight * (dweight - stat_ref[0])
    hi = dlogit.astype(BF16)
    dlogit_ref[0, :, :LANES] = hi
    dlogit_ref[0, :, LANES:] = (dlogit - hi.astype(F32)).astype(BF16)


def embed_body(
    n_space, me_ref, dvalue_ref, dlogit_ref, patches_ref, wv_ref, wback_ref, keep_ref, send_ref, cols_ref, extra_ref
):
    v = pl.program_id(0)
    hi, lo = dlogit_ref[0, :, :LANES].astype(F32), dlogit_ref[0, :, LANES:].astype(F32)
    group = iota(hi.shape, 1) >> 4
    mixed = jnp.where(group < 2, hi, jnp.where(group == 2, lo, 0.0)).astype(BF16)
    d_tokens = (mm(dvalue_ref[0], wv_ref[...], NT) + mm(mixed, wback_ref[...], NT)).astype(BF16)
    grad = mm(patches_ref[0], d_tokens, TN).astype(BF16)
    hi, lo, _ = parts3(jnp.sum(d_tokens.astype(F32), axis=0, keepdims=True))
    row = iota(extra_ref.shape, 0)
    extra = jnp.where(row == 2 * v, hi, jnp.where(row == 2 * v + 1, lo, 0.0))

    @pl.when(v == 0)
    def _():
        extra_ref[...] = extra

    @pl.when(v > 0)
    def _():
        extra_ref[...] += extra

    cols = cols_ref.shape[2]
    pixels = patches_ref.shape[2]
    for c in range(n_space):
        cols_ref[c] = grad[:, c * cols : (c + 1) * cols]
    at = pl.ds(pl.multiple_of(v * pixels, pixels), pixels)
    for k in range(0, n_space, 2):
        keep_ref[k // 2, at, :] = cols_ref[me_ref[1] ^ k]
        send_ref[k // 2, at, :] = cols_ref[me_ref[1] ^ (k + 1)]

    @pl.when(v == pl.num_programs(0) - 1)
    def _():
        tail = slice(keep_ref.shape[1] - 16, keep_ref.shape[1])
        for c in range(n_space):
            cols_ref[c, :16, :] = extra_ref[:, c * cols : (c + 1) * cols].astype(BF16)
        for k in range(0, n_space, 2):
            keep_ref[k // 2, tail, :] = cols_ref[me_ref[1] ^ k, :16, :]
            send_ref[k // 2, tail, :] = cols_ref[me_ref[1] ^ (k + 1), :16, :]


def embed_final_body(parts, *refs):
    ins, (grad_ref, offset_ref) = refs[:-2], refs[-2:]
    pixels = grad_ref.shape[1]
    base = 0
    for chunk in range(len(ins) // parts):
        total = 0.0
        for ref in ins[chunk * parts : (chunk + 1) * parts]:
            total = total + (ref[0] if len(ref.shape) == 3 else ref[...]).astype(F32)
        count = (total.shape[0] - 16) // pixels
        for v in range(count):
            grad_ref[base + v] = total[v * pixels : (v + 1) * pixels, :]
            row = count * pixels + 2 * v
            offset_ref[base + v : base + v + 1, :] = total[row : row + 1, :] + total[row + 1 : row + 2, :]
        base += count


def stack_body(*refs):
    for k, ref in enumerate(refs[:-1]):
        refs[-1][k] = ref[...]


def value_grad_body(me_ref, *refs):
    tokens_refs, dv_refs, dl_refs, (keep_ref, send_ref, all_ref) = refs[:2], refs[2:4], refs[4:6], refs[6:]
    width = dv_refs[0].shape[2]
    total, both = 0.0, 0.0
    for tokens_ref, dv_ref, dl_ref in zip(tokens_refs, dv_refs, dl_refs):
        for v in range(dv_ref.shape[0]):
            total = total + mm(tokens_ref[v], dv_ref[v], TN)
            both = both + mm(tokens_ref[v], dl_ref[v], TN)
    all_ref[:, :width] = total.astype(BF16)
    all_ref[:, width:] = pack(both[:, :LANES] + both[:, LANES:])
    block = keep_ref.shape[1]
    count = all_ref.shape[0] // block
    for r in range(count):
        target = pl.program_id(0) * count + r
        same = (target & 1) == (me_ref[0] & 1)
        slot = target >> 1

        @pl.when(same)
        def _():
            keep_ref[slot] = all_ref[r * block : (r + 1) * block, :]

        @pl.when(jnp.logical_not(same))
        def _():
            send_ref[slot] = all_ref[r * block : (r + 1) * block, :]


def pair_sum_body(n_chip, me_ref, keep_ref, got_ref, *out_refs):
    width = keep_ref.shape[2] - LANES
    for k in range(n_chip):
        slot = (me_ref[0] >> 1) ^ k
        mine, other = keep_ref[slot], got_ref[slot]
        out_refs[k][:, :width] = (mine[:, :width].astype(F32) + other[:, :width].astype(F32)).astype(BF16)
        out_refs[k][:, width:] = pack(unpack(mine[:, width:]) + unpack(other[:, width:]))


def packet_split_body(n_in, n_space, me_ref, *refs):
    ins, gathered_ref, out_refs, (cols_ref,) = refs[:n_in], refs[n_in], refs[n_in + 1 : -1], refs[-1:]
    block, width = ins[0].shape[0], ins[0].shape[1] - LANES
    total = sum(ref[:, :width].astype(F32) for ref in ins).astype(BF16)
    factor = pack(sum(unpack(ref[:, width:]) for ref in ins))
    half = n_space // 2
    cols = cols_ref.shape[2] // 2
    for c in range(half):
        cols_ref[c] = total[:, 2 * c * cols : 2 * (c + 1) * cols]
    height = gathered_ref.shape[1]
    part = out_refs[0].shape[0] - height - 2 * block
    for k in range(n_space):
        out_refs[k][:height, :] = gathered_ref[me_ref[1] ^ k]
        for piece in range(block // part):
            lanes = slice(piece * LANES, (piece + 1) * LANES)
            out_refs[k][height : height + part, lanes] = factor[piece * part : (piece + 1) * part, :]
        large = cols_ref[jnp.maximum((me_ref[1] ^ k) - half, 0)]
        out_refs[k][height + part : height + part + block, :] = large[:, :cols]
        out_refs[k][height + part + block :, :] = large[:, cols:]


def space_sum_body(n, *refs):
    ins, (out_ref, weight_ref) = refs[:n], refs[n:]
    cols = ins[0].shape[1]
    width = out_ref.shape[1] - LANES - cols
    block = out_ref.shape[0] - 16
    height = block + 16 + weight_ref.shape[0]
    part = ins[0].shape[0] - height - 2 * block
    total = sum(ref[...].astype(F32) for ref in ins)
    for piece in range(2):
        at = slice(height + part + piece * block, height + part + (piece + 1) * block)
        out_ref[:block, piece * cols : (piece + 1) * cols] = total[at, :].astype(BF16)
    for piece in range(block // part):
        lanes = slice(piece * LANES, (piece + 1) * LANES)
        factor = pack(sum(unpack(ref[height : height + part, lanes]) for ref in ins))
        out_ref[piece * part : (piece + 1) * part, width : width + LANES] = factor
    out_ref[block:, : width + LANES] = jnp.zeros((16, width + LANES), BF16)
    out_ref[:block, width + LANES :] = total[:block, :].astype(BF16)
    out_ref[block:, width + LANES :] = three_rows(jnp.sum(total[block : block + 16, :], axis=0, keepdims=True))
    weight_ref[...] = total[block + 16 : height, :]


def add_body(n, keep_ref, got_ref, *refs):
    for j, out_ref in enumerate(refs):
        out_ref[...] = (keep_ref[j + 1].astype(F32) + got_ref[j + 1].astype(F32)).astype(BF16)


def final_body(n_var, n_space, scale, me_ref, even_ref, odd_ref, query_ref, wk_ref, kv_ref, gq_ref, out_ref, gain_ref):
    me_v, me_s = me_ref[0], me_ref[1]
    half = n_space // 2
    width = wk_ref.shape[1]
    size = width // HEADS
    cols, qcols = kv_ref.shape[1], gq_ref.shape[1]
    place = pl.multiple_of(jnp.minimum(me_s, half - 1) * cols, LANES)
    spread_kv = spread_matrix(cols, size, place)
    qplace = pl.multiple_of(me_s * qcols, LANES)
    spread_q = spread_matrix(qcols, size, qplace)
    query = query_ref[:, pl.ds(place, cols)] * scale
    block = even_ref.shape[1] - 16
    total, gain = 0.0, 0.0
    for k in range(n_var):
        part_ref, slot = (odd_ref if k % 2 else even_ref), k // 2
        at = pl.ds(pl.multiple_of((me_v ^ k) * block, block), block)
        packed = part_ref[slot, :block, cols : cols + LANES]
        key_grad = mm(packed, spread_kv) * query
        kv_ref[at, :] = jnp.where(me_s < half, key_grad, part_ref[slot, :block, :cols].astype(F32))
        keys = wk_ref[at, pl.ds(qplace, qcols)].astype(F32)
        total = total + jnp.sum(mm(packed, spread_q) * keys, axis=0, keepdims=True)
        out_ref[at, :] = part_ref[slot, :block, cols + LANES :].astype(F32)
        gain = gain + jnp.sum(part_ref[slot, block:, cols + LANES :].astype(F32), axis=0, keepdims=True)
    gq_ref[...] = total * scale
    gain_ref[...] = gain


def shards(
    patches, embed_weight, var_embed, agg_query, agg_kv, agg_out, norm_gain, qkv_weight, out_weight, cotangent
):
    n_var, n_space = lax.axis_size("var"), lax.axis_size("space")
    count, rows, pixels = patches.shape
    width = agg_out.shape[0]
    size = width // HEADS
    scale = 1.0 / math.sqrt(size)
    block = rows // n_var
    cols = width // n_space
    group = out_weight.shape[0]
    drows = width // n_var
    positions = rows * n_space
    kv_cols = 2 * width // n_space
    me = jnp.stack([lax.axis_index("var"), lax.axis_index("space")]).astype(jnp.int32)
    gain = norm_gain.reshape(1, width)
    query = agg_query.reshape(1, width)
    vmem = pl.BlockSpec(memory_space=pltpu.VMEM)
    packet = width + LANES

    whole = lambda shape: pl.BlockSpec(shape, lambda v: (0,) * len(shape))
    every = lambda shape: pl.BlockSpec((1,) + shape, lambda v: (v,) + (0,) * len(shape))
    n_chip = n_var // 2
    half = count // 2

    dattn, cot_own, w_heads = call(
        early_body,
        [struct((rows, group), BF16), struct((block, width), BF16), struct(qkv_weight.shape, BF16)],
        limit=LIMITS["early"],
        grid=(1,),
        in_specs=[SMEM] + [whole(x.shape) for x in (cotangent, out_weight, qkv_weight)],
        out_specs=[whole((rows, group)), whole((block, width)), whole(qkv_weight.shape)],
        cost_estimate=cost(2e8, 4e6),
        name="early",
    )(me, cotangent, out_weight, qkv_weight)
    dattn_all = gather_direct(dattn, "space")

    def forward_outs(here):
        shapes = [((here, rows, width), BF16), ((here, rows, width), F32), ((here, rows, LANES), F32)]
        return [struct(*x) for x in shapes], [every(x[1:]) for x, _ in shapes]

    def inputs(start):
        at = lambda shape: pl.BlockSpec((1,) + shape, lambda v: (v + start,) + (0,) * len(shape))
        return [at((rows, pixels)), at((pixels, width)), whole((count, width))]

    state = [((rows, width), F32), ((rows, LANES), F32), ((rows, LANES), F32)]
    out_shapes, out_specs = forward_outs(half)
    tokens0, value0, scores0, w_query, w_back, *state0 = call(
        functools.partial(first_body, scale),
        out_shapes
        + [struct((width, 3 * LANES), BF16), struct((width, LANES), BF16)]
        + [struct(*x) for x in state],
        limit=LIMITS["forward"],
        after=[dattn],
        grid=(half,),
        in_specs=inputs(0)
        + [
            whole((1, width)),
            pl.BlockSpec((width, width), lambda v: (0, 0)),
            pl.BlockSpec((width, width), lambda v: (0, 1)),
        ],
        out_specs=out_specs + [whole((width, 3 * LANES)), whole((width, LANES))] + [whole(x) for x, _ in state],
        scratch_shapes=[pltpu.VMEM((LANES, width), BF16)],
        cost_estimate=cost(6e9, 2e7),
        name="forward_first",
    )(patches, embed_weight, var_embed, query, agg_kv, agg_kv)
    out_shapes, out_specs = forward_outs(count - half)
    tokens1, value1, scores1, keep, send = call(
        functools.partial(second_body, half),
        out_shapes + [struct((n_chip, block, packet), F32)] * 2,
        limit=LIMITS["forward"],
        after=dattn_all[1:],
        grid=(count - half,),
        in_specs=[SMEM]
        + inputs(half)
        + [whole((width, 3 * LANES)), pl.BlockSpec((width, width), lambda v: (0, 1))]
        + [whole(x) for x, _ in state],
        out_specs=out_specs + [whole((n_chip, block, packet))] * 2,
        scratch_shapes=[pltpu.VMEM((LANES, width), BF16)] + [pltpu.VMEM(*x) for x in state],
        cost_estimate=cost(4e9, 1e7),
        name="forward_second",
    )(me, patches, embed_weight, var_embed, w_query, agg_kv, *state0)

    def pool_pairs(mine, got):
        return call(
            pool_pair_body,
            [struct((block, packet), F32)] * n_chip,
            limit=LIMITS["pool_pair"],
            in_specs=[SMEM, vmem, vmem],
            cost_estimate=cost(1e8, 3e6),
            name="pool_pair",
        )(me, mine, got)

    received = exchange_pairs(keep, send, pool_pairs)
    mixed, pooled_packet = call(
        functools.partial(pool_body, n_chip),
        [struct((block, width), F32), struct((block, packet), BF16)],
        limit=LIMITS["pool"],
        cost_estimate=cost(1e8, 2e6),
        name="pool",
    )(*received)
    pooled_even, pooled_odd = gather_pairs(pooled_packet, "var")

    qkv, normed, pooled_packets, centred, inv = call(
        norm_body,
        [
            struct((rows, 3 * group), BF16),
            struct((rows, width), BF16),
            struct((rows, packet), BF16),
            struct((block, width), F32),
            struct((block, LANES), F32),
        ],
        limit=LIMITS["norm"],
        in_specs=[SMEM] + [vmem] * 5,
        scratch_shapes=[pltpu.VMEM((rows, width), F32), pltpu.VMEM((rows, LANES), F32)],
        cost_estimate=cost(8e8, 5e6),
        name="norm",
    )(me, pooled_even, pooled_odd, agg_out, gain, w_heads)

    qkv_all = gather_direct(qkv, "space")
    normed_cols = call(
        functools.partial(columns_body, n_space),
        [struct((rows, cols), BF16)] * n_space,
        limit=LIMITS["columns"],
        after=qkv_all[1:],
        in_specs=[SMEM, vmem],
        scratch_shapes=[pltpu.VMEM((n_space, rows, cols), BF16)],
        cost_estimate=cost(1e6, 1e6),
        name="columns",
    )(me, normed)
    normed_all = exchange_direct(normed_cols, "space")
    attn, dqkv = call(
        functools.partial(attention_body, n_space, size, scale),
        [struct((positions, group), BF16), struct((positions, 3 * group), BF16)],
        limit=LIMITS["attention"],
        after=[normed_cols[0]],
        scratch_shapes=[pltpu.VMEM((positions, group), BF16)] * 2 + [pltpu.VMEM((positions, group), F32)] * 2,
        cost_estimate=cost(6e9, 4e6),
        name="attention",
    )(*qkv_all, *dattn_all)
    dn_keep, dn_send = call(
        dn_body,
        [struct((n_chip, block, width), BF16)] * 2,
        limit=LIMITS["dn"],
        after=normed_all[1:],
        grid=(1,),
        in_specs=[SMEM, pl.BlockSpec((rows, 3 * group), lambda i: (0, 0)), vmem],
        scratch_shapes=[pltpu.VMEM((rows, width), BF16)],
        cost_estimate=cost(2e8, 1e6),
        name="dn",
    )(me, dqkv, w_heads)

    def dn_pairs(mine, got):
        return call(
            dn_pair_body,
            [struct((block, width), BF16)] * n_chip,
            limit=LIMITS["dn_pair"],
            in_specs=[SMEM, vmem, vmem],
            cost_estimate=cost(1e6, 1e6),
            name="dn_pair",
        )(me, mine, got)

    dn_received = exchange_pairs(dn_keep, dn_send, dn_pairs)
    joined_packet, dgain = call(
        functools.partial(joined_body, n_chip),
        [struct((block, packet), BF16), struct((8, width), F32)],
        limit=LIMITS["joined"],
        cost_estimate=cost(2e8, 3e6),
        name="joined",
    )(*dn_received, centred, inv, gain, cot_own, mixed, agg_out)
    joined_even, joined_odd = gather_pairs(joined_packet, "var")

    d_joined, d_pooled, stat = call(
        prepare_body,
        [struct((rows, packet), BF16), struct((rows, width), F32), struct((3, rows, LANES), F32)],
        limit=LIMITS["prepare"],
        in_specs=[SMEM] + [vmem] * 4,
        cost_estimate=cost(6e8, 4e6),
        name="prepare",
    )(me, pooled_packets, joined_even, joined_odd, agg_out)
    def d_values(value, scores):
        here = value.shape[0]
        return call(
            dvalue_body,
            [struct((here, rows, width), BF16), struct((here, rows, 2 * LANES), BF16)],
            limit=LIMITS["dvalue"],
            grid=(here,),
            in_specs=[whole((rows, width)), whole((3, rows, LANES)), every((rows, width)), every((rows, LANES))],
            out_specs=[every((rows, width)), every((rows, 2 * LANES))],
            scratch_shapes=[pltpu.VMEM((LANES, width), BF16), pltpu.VMEM((width, LANES), BF16)],
            cost_estimate=cost(2e9, 5e6),
            name="dvalue",
        )(d_pooled, stat, value, scores)

    def embed(start, d_value, d_logit, after):
        here = d_value.shape[0]
        at = lambda shape: pl.BlockSpec((1,) + shape, lambda v: (v + start,) + (0,) * len(shape))
        blocks = (n_space // 2, here * pixels + 16, cols)
        return call(
            functools.partial(embed_body, n_space),
            [struct(blocks, BF16)] * 2,
            limit=LIMITS["embed"],
            after=after,
            grid=(here,),
            in_specs=[
                SMEM,
                every((rows, width)),
                every((rows, 2 * LANES)),
                at((rows, pixels)),
                pl.BlockSpec((width, width), lambda v: (0, 1)),
                whole((width, LANES)),
            ],
            out_specs=[whole(blocks)] * 2,
            scratch_shapes=[pltpu.VMEM((n_space, pixels, cols), BF16), pltpu.VMEM((16, width), F32)],
            cost_estimate=cost(1.5e9, 4e6),
            name="embed",
        )(me, d_value, d_logit, patches, agg_kv, w_back)

    dv0, dl0 = d_values(value0, scores0)
    dv1, dl1 = d_values(value1, scores1)

    step = max(drows, 256)
    kv_keep, kv_send = call(
        value_grad_body,
        [struct((n_chip, drows, packet), BF16)] * 2,
        limit=LIMITS["value_grad"],
        grid=(width // step,),
        in_specs=[SMEM]
        + [pl.BlockSpec(x.shape[:2] + (step,), lambda i: (0, 0, i)) for x in (tokens0, tokens1)]
        + [whole(x.shape) for x in (dv0, dv1, dl0, dl1)],
        out_specs=[whole((n_chip, drows, packet))] * 2,
        scratch_shapes=[pltpu.VMEM((step, packet), BF16)],
        cost_estimate=cost(4e9, 1e7),
        name="value_grad",
    )(me, tokens0, tokens1, dv0, dv1, dl0, dl1)
    kv_got = swap(kv_send, "var", 1)

    out_block = call(
        out_grad_body,
        struct((n_space, drows + 16 + group, cols), BF16),
        limit=LIMITS["out_grad"],
        after=[kv_keep],
        grid=(1,),
        in_specs=[SMEM] + [whole(x.shape) for x in (pooled_packets, d_joined, dgain)] + [whole((rows, group)), whole((rows, width))],
        out_specs=whole((n_space, drows + 16 + group, cols)),
        scratch_shapes=[pltpu.VMEM((width, width), F32)],
        cost_estimate=cost(6e8, 3e6),
        name="out_grad",
    )(me, pooled_packets, d_joined, dgain, attn, cotangent)

    def scatter_embed(keep, arrived, after):
        n = n_space // 2 - 1
        sums = call(
            functools.partial(add_body, n),
            [struct(keep.shape[1:], BF16)] * n,
            limit=LIMITS["add"],
            after=after,
            cost_estimate=cost(1e6, 1e6),
            name="add",
        )(keep, arrived)
        blocks = {2 * (j + 1): sums[j] for j in range(n)}
        mine, bit = [keep, arrived], 2
        while bit < n_space:
            got = {k ^ bit: swap(blocks[k], "space", bit) for k in blocks if k & bit and k % bit == 0}
            mine.append(got[0])
            for k in got:
                if k:
                    blocks[k] = (blocks[k].astype(F32) + got[k].astype(F32)).astype(BF16)
            bit *= 2
        return mine, list(sums)

    keep0, send0 = embed(0, dv0, dl0, [kv_keep])
    arrived0 = swap(send0, "space", 1)
    kv_blocks = call(
        functools.partial(pair_sum_body, n_chip),
        [struct((drows, packet), BF16)] * n_chip,
        limit=LIMITS["pair_sum"],
        after=[keep0],
        in_specs=[SMEM] + [vmem] * 2,
        cost_estimate=cost(1e6, 1e6),
        name="pair_sum",
    )(me, kv_keep, kv_got)
    kv_parts = [kv_blocks[0]] + [swap(kv_blocks[k], "var", 2 * k) for k in range(1, n_chip)]
    keep1, send1 = embed(half, dv1, dl1, [kv_blocks[0]])
    arrived1 = swap(send1, "space", 1)
    height = drows + 16 + group
    part = drows * LANES // cols
    pieces = call(
        functools.partial(packet_split_body, n_chip, n_space),
        [struct((height + part + 2 * drows, cols), BF16)] * n_space,
        limit=LIMITS["packet_split"],
        in_specs=[SMEM] + [vmem] * (n_chip + 1),
        scratch_shapes=[pltpu.VMEM((n_space // 2, drows, kv_cols), BF16)],
        cost_estimate=cost(1e6, 1e6),
        name="packet_split",
    )(me, *kv_parts, out_block)
    pieces_all = exchange_direct(pieces, "space")
    mine0, sums0 = scatter_embed(keep0, arrived0, [pieces[0]])
    mine1, sums1 = scatter_embed(keep1, arrived1, sums0)
    grad_qkv, head_flag = call(
        functools.partial(head_grads_body, n_space),
        [struct((cols, 3 * group), F32), struct((8, LANES), F32)],
        limit=LIMITS["head_grads"],
        cost_estimate=cost(1e9, 3e6),
        name="head_grads",
    )(*normed_all, dqkv)
    kv_sum, grad_out = call(
        functools.partial(space_sum_body, n_space),
        [struct((drows + 16, kv_cols + LANES + cols), BF16), struct((group, cols), F32)],
        limit=LIMITS["space_sum"],
        after=sums1 + [head_flag],
        cost_estimate=cost(1e6, 1e6),
        name="space_sum",
    )(*pieces_all)

    def stack(parts):
        return call(
            stack_body,
            struct((len(parts),) + parts[0].shape, BF16),
            after=mine0[2:] + mine1[2:],
            cost_estimate=cost(1e6, 1e6),
            name="stack",
        )(*parts)

    kv_even, kv_odd = gather_pairs(kv_sum, "var", stack)
    grad_agg_kv, grad_query, grad_agg_out, grad_gain = call(
        functools.partial(final_body, n_var, n_space, scale),
        [struct((width, kv_cols), F32), struct((1, cols), F32)] + [struct((width, cols), F32), struct((1, cols), F32)],
        grid=(1,),
        in_specs=[SMEM] + [vmem] * 3 + [pl.BlockSpec((width, width), lambda i: (0, 0))],
        limit=LIMITS["final"],
        cost_estimate=cost(2e8, 5e6),
        name="final",
    )(me, kv_even, kv_odd, query, agg_kv)

    def first_block(x):
        if x.ndim == 3:
            return pl.BlockSpec((1,) + x.shape[1:], lambda i: (0, 0, 0))
        return pl.BlockSpec(x.shape, lambda i: (0, 0))

    grad_embed, grad_var_embed = call(
        functools.partial(embed_final_body, len(mine0)),
        [struct((count, pixels, cols), F32), struct((count, cols), F32)],
        grid=(1,),
        in_specs=[first_block(x) for x in mine0 + mine1],
        limit=LIMITS["embed_final"],
        cost_estimate=cost(1e6, 1e6),
        name="embed_final",
    )(*mine0, *mine1)

    return (
        grad_embed,
        grad_var_embed,
        grad_query.reshape(cols),
        grad_agg_kv,
        grad_agg_out,
        grad_gain.reshape(cols),
        grad_qkv,
        grad_out,
    )


def solution(mesh):
    return jax.shard_map(
        shards,
        mesh=mesh,
        in_specs=(
            P("var", "space", None),
            P("var", None, None),
            P("var", None),
            P(),
            P(),
            P(),
            P(),
            P(None, "var"),
            P("var", None),
            P("space", None),
        ),
        out_specs=(
            P("var", None, "space"),
            P("var", "space"),
            P("space"),
            P(None, "space"),
            P(None, "space"),
            P("space"),
            P("space", "var"),
            P("var", "space"),
        ),
        check_vma=False,
    )
```

```python
import functools
import math

import jax
import jax.numpy as jnp
from jax import lax
from jax.experimental import pallas as pl
from jax.experimental.pallas import tpu as pltpu
from jax.sharding import PartitionSpec as P

HEADS = 16
LANES = 128
EPSILON = 1e-05
MIB = 1 << 20

LIMITS = {
    "early": 60, "first": 56, "forward": 24, "columns": 8, "pool_pair": 16, "pool": 16, "norm": 16, "attention": 24,
    "dn": 12, "dn_pair": 16, "joined": 16, "prepare": 16, "out_grad": 16, "dvalue": 24, "embed": 24, "value_grad": 32,
    "add": 12, "pair_sum": 16, "packet_split": 16, "space_sum": 16, "head_grads": 16, "final": 16, "embed_final": 24,
}

F32 = jnp.float32
BF16 = jnp.bfloat16

NN = (((1,), (0,)), ((), ()))
NT = (((1,), (1,)), ((), ()))
TN = (((0,), (0,)), ((), ()))


def mm(a, b, dims=NN):
    return lax.dot_general(a, b, dims, preferred_element_type=F32)


def iota(shape, axis):
    return lax.broadcasted_iota(jnp.int32, shape, axis)


def parts3(x):
    hi = x.astype(BF16).astype(F32)
    rest = x - hi
    mid = rest.astype(BF16).astype(F32)
    return hi, mid, rest - mid


def pack(x, y=None):
    group = iota(x.shape, 1) >> 4
    hi, mid, lo = parts3(x)
    out = jnp.where(group == 0, hi, jnp.where(group == 1, mid, jnp.where(group == 2, lo, 0.0)))
    if y is not None:
        hi, mid, lo = parts3(y)
        out = jnp.where(group == 3, hi, jnp.where(group == 4, mid, jnp.where(group == 5, lo, out)))
    return out.astype(BF16)


def unpack(packed, first_group=0):
    row, column = iota((LANES, LANES), 0), iota((LANES, LANES), 1)
    group = row >> 4
    take = ((row & 15) == (column & 15)) & (group >= first_group) & (group < first_group + 3)
    return mm(packed, jnp.where(take, 1.0, 0.0).astype(BF16))


def spread_matrix(width, size, first=0):
    row, column = iota((LANES, width), 0), iota((LANES, width), 1)
    shift = size.bit_length() - 1
    take = ((row & 15) == ((column + first) >> shift)) & (row < 48)
    return jnp.where(take, 1.0, 0.0).astype(BF16)


def fold_matrix(width, size):
    row, column = iota((width, LANES), 0), iota((width, LANES), 1)
    shift = size.bit_length() - 1
    return jnp.where((column & 15) == (row >> shift), 1.0, 0.0).astype(BF16)


def head_sums(x, fold):
    hi, mid, lo = parts3(x)
    return mm(hi.astype(BF16), fold) + mm(mid.astype(BF16), fold) + mm(lo.astype(BF16), fold)


def call(body, out_shape, limit=16, after=(), in_specs=None, **kw):
    def run(*args):
        n, m = len(args), len(after)
        vmem = pl.BlockSpec(memory_space=pltpu.VMEM)
        return pl.pallas_call(
            lambda *refs: body(*refs[:n], *refs[n + m :]),
            out_shape=out_shape,
            in_specs=([vmem] * n if in_specs is None else list(in_specs)) + [vmem] * m,
            compiler_params=pltpu.CompilerParams(vmem_limit_bytes=limit * MIB),
            **kw,
        )(*args, *after)

    return run


def struct(shape, dtype):
    return jax.ShapeDtypeStruct(shape, dtype)


def cost(flops, moved):
    return pl.CostEstimate(flops=int(flops), bytes_accessed=int(moved), transcendentals=0)


SMEM = pl.BlockSpec(memory_space=pltpu.SMEM)


def swap(x, axis, k, keep=None):
    pairs = [(i, i ^ k) for i in range(lax.axis_size(axis))]
    if keep is not None:
        pairs = [pair for pair in pairs if keep(pair[1])]
    return lax.ppermute(x, axis, pairs)


def gather_direct(x, axis):
    return [x] + [swap(x, axis, k) for k in range(1, lax.axis_size(axis))]


def exchange_direct(blocks, axis):
    return [blocks[0]] + [swap(blocks[k], axis, k) for k in range(1, len(blocks))]


def gather_pairs(x, axis, stack=jnp.stack):
    even = [x] + [swap(x, axis, k) for k in range(2, lax.axis_size(axis), 2)]
    even = stack(even)
    return even, swap(even, axis, 1)


def exchange_pairs(keep, send, combine):
    parts = combine(keep, swap(send, "var", 1))
    return [parts[0]] + [swap(parts[k], "var", 2 * k) for k in range(1, len(parts))]


def pair_rows(me_v, k, odd, block):
    device = (((me_v >> 1) ^ k) << 1) + ((me_v & 1) ^ odd)
    return pl.ds(pl.multiple_of(device * block, block), block)


def three_rows(x):
    hi, mid, lo = parts3(x)
    row = iota((16, x.shape[1]), 0)
    return jnp.where(row == 0, hi, jnp.where(row == 1, mid, jnp.where(row == 2, lo, 0.0))).astype(BF16)


def head_order(width, size=64):
    heads = width // (3 * size)
    row, column = iota((width, width), 0), iota((width, width), 1)
    take = jnp.zeros((width, width), jnp.bool_)
    for h in range(heads):
        for c in range(3):
            start, target = h * 3 * size + c * size, c * heads * size + h * size
            inside = (column >= target) & (column < target + size)
            take = take | (inside & ((row - start) == (column - target)))
    return jnp.where(take, 1.0, 0.0).astype(BF16)


def early_body(me_ref, cot_ref, outw_ref, qkvw_ref, dattn_ref, own_ref, wperm_ref):
    dattn_ref[...] = mm(cot_ref[...], outw_ref[...], NT).astype(BF16)
    block = own_ref.shape[0]
    own_ref[...] = cot_ref[pl.ds(pl.multiple_of(me_ref[0] * block, block), block), :]
    wperm_ref[...] = mm(qkvw_ref[...], head_order(qkvw_ref.shape[1])).astype(BF16)


def forward_part(start, patches_ref, embed_ref, offset_ref, wq, wv_ref, spread, outs, state):
    tokens_ref, value_ref, scores_ref = outs
    here = tokens_ref.shape[0]
    width = tokens_ref.shape[2]
    for v in range(here):
        u = start + v
        tokens = (mm(patches_ref[u], embed_ref[u]) + offset_ref[u : u + 1, :]).astype(BF16)
        tokens_ref[v] = tokens
        pieces = mm(tokens, wq)
        scores_ref[v] = pieces[:, :LANES] + pieces[:, LANES : 2 * LANES] + pieces[:, 2 * LANES :]
        value_ref[v] = mm(tokens, wv_ref[:, width:])
    top = functools.reduce(jnp.maximum, [scores_ref[v] for v in range(here)])
    total, acc = 0.0, 0.0
    if state is not None:
        top = jnp.maximum(top, state[0])
        old = jnp.exp(state[0] - top)
        total, acc = state[1] * old, state[2] * mm(pack(old), spread)
    for v in range(here):
        new = jnp.exp(scores_ref[v] - top)
        total = total + new
        acc = acc + value_ref[v] * mm(pack(new), spread)
    return top, total, acc


def first_body(
    scale, patches_hbm, embed_hbm, offset_ref, query_ref, kv_hbm,
    tokens_ref, value_ref, scores_ref, wq_ref, wback_ref, acc_ref, max_ref, sum_ref,
    patches_ref, embed_ref, kv_ref, semaphores,
):
    here, _, width = tokens_ref.shape
    size = width // HEADS
    copies = [
        pltpu.make_async_copy(source, target, semaphores.at[i])
        for i, (source, target) in enumerate(
            (
                (kv_hbm.at[:, pl.ds(0, width)], kv_ref.at[:, pl.ds(0, width)]),
                (patches_hbm.at[pl.ds(0, here)], patches_ref),
                (embed_hbm.at[pl.ds(0, here)], embed_ref),
                (kv_hbm.at[:, pl.ds(width, width)], kv_ref.at[:, pl.ds(width, width)]),
            )
        )
    ]
    for copy in copies:
        copy.start()
    copies[0].wait()
    row, column = iota((LANES, width), 0), iota((LANES, width), 1)
    own = (row & 15) == (column >> (size.bit_length() - 1))
    wq = jnp.zeros((width, LANES), F32)
    for part in parts3(query_ref[...]):
        wq = wq + mm(kv_ref[:, :width], jnp.where(own, part, 0.0).astype(BF16), NT)
    hi, mid, lo = parts3(wq * scale)
    wq_ref[:, :LANES] = hi.astype(BF16)
    wq_ref[:, LANES : 2 * LANES] = mid.astype(BF16)
    wq_ref[:, 2 * LANES :] = lo.astype(BF16)
    group = iota((width, LANES), 1) >> 4
    back = jnp.where((group == 0) | (group == 2), hi, jnp.where(group == 1, mid, 0.0))
    wback_ref[...] = back.astype(BF16)
    for copy in copies[1:]:
        copy.wait()
    max_ref[...], sum_ref[...], acc_ref[...] = forward_part(
        0, patches_ref, embed_ref, offset_ref, wq_ref[...], kv_ref, spread_matrix(width, size),
        (tokens_ref, value_ref, scores_ref), None,
    )


def second_body(
    start, me_ref, patches_ref, embed_ref, offset_ref, wq_ref, kv_ref, acc0_ref, max0_ref, sum0_ref,
    tokens_ref, value_ref, scores_ref, keep_ref, send_ref, acc_ref, max_ref,
):
    width = tokens_ref.shape[2]
    top, total, acc = forward_part(
        start, patches_ref, embed_ref, offset_ref, wq_ref[...], kv_ref, spread_matrix(width, width // HEADS),
        (tokens_ref, value_ref, scores_ref), (max0_ref[...], sum0_ref[...], acc0_ref[...]),
    )
    acc_ref[...] = acc
    max_ref[...] = jnp.where(iota(top.shape, 1) < LANES // 2, top, total)
    block = keep_ref.shape[1]
    core = me_ref[0] & 1
    for c in range(keep_ref.shape[0]):
        for ref, device in ((keep_ref, 2 * c + core), (send_ref, 2 * c + 1 - core)):
            at = pl.ds(pl.multiple_of(device * block, block), block)
            ref[c, :, :width] = acc_ref[at, :]
            ref[c, :, width:] = max_ref[at, :]


def halves_of(both):
    low = iota(both.shape, 1) < LANES // 2
    turned = pltpu.roll(both, LANES // 2, 1)
    return jnp.where(low, both, turned), jnp.where(low, turned, both)


def pool_pair_body(me_ref, keep_ref, got_ref, *out_refs):
    width = keep_ref.shape[2] - LANES
    spread = spread_matrix(width, width // HEADS)
    low = iota((keep_ref.shape[1], LANES), 1) < LANES // 2
    for k, out_ref in enumerate(out_refs):
        slot = (me_ref[0] >> 1) ^ k
        mine, other = keep_ref[slot], got_ref[slot]
        max_a, sum_a = halves_of(mine[:, width:])
        max_b, sum_b = halves_of(other[:, width:])
        top = jnp.maximum(max_a, max_b)
        factor_a, factor_b = jnp.exp(max_a - top), jnp.exp(max_b - top)
        out_ref[:, :width] = mine[:, :width] * mm(pack(factor_a), spread) + other[:, :width] * mm(pack(factor_b), spread)
        out_ref[:, width:] = jnp.where(low, top, sum_a * factor_a + sum_b * factor_b)


def pool_body(n, *refs):
    ins, (mixed_ref, packet_ref) = refs[:n], refs[n:]
    width = mixed_ref.shape[1]
    stats = [halves_of(ref[:, width:]) for ref in ins]
    top = functools.reduce(jnp.maximum, [m for m, _ in stats])
    factors = [jnp.exp(m - top) for m, _ in stats]
    total = sum(s * f for (_, s), f in zip(stats, factors))
    spread = spread_matrix(width, width // HEADS)
    mixed = jnp.zeros(mixed_ref.shape, F32)
    for ref, factor in zip(ins, factors):
        mixed = mixed + ref[:, :width] * mm(pack(factor / total), spread)
    mixed_ref[...] = mixed
    packet_ref[:, :width] = mixed.astype(BF16)
    packet_ref[:, width:] = pack(top, total)


def norm_body(
    me_ref, even_ref, odd_ref, agg_ref, gain_ref, w_ref, qkv_ref, normed_ref, packets_ref, centred_ref, inv_ref,
    all_ref, allinv_ref,
):
    width = agg_ref.shape[0]
    block = centred_ref.shape[0]
    for k in range(even_ref.shape[0]):
        for odd, ref in ((0, even_ref), (1, odd_ref)):
            packets_ref[pair_rows(me_ref[0], k, odd, block), :] = ref[k]
    joined = mm(packets_ref[:, :width], agg_ref[...]).astype(BF16).astype(F32)
    mean = jnp.mean(joined, axis=-1, keepdims=True)
    spread_sq = jnp.mean((joined - mean) ** 2, axis=-1, keepdims=True)
    inv = lax.rsqrt(spread_sq + EPSILON)
    centred = (joined - mean) * inv
    normed = (centred * gain_ref[...]).astype(BF16)
    qkv_ref[...] = mm(normed, w_ref[...]).astype(BF16)
    normed_ref[...] = normed
    all_ref[...] = centred
    allinv_ref[...] = jnp.broadcast_to(inv, allinv_ref.shape)
    start = pl.multiple_of(me_ref[0] * block, block)
    centred_ref[...] = all_ref[pl.ds(start, block), :]
    inv_ref[...] = allinv_ref[pl.ds(start, block), :]


def attention_body(n_space, size, scale, *refs):
    qkv_refs, dattn_refs = refs[:n_space], refs[n_space : 2 * n_space]
    attn_ref, dqkv_ref, k_ref, v_ref, dk_ref, dv_ref = refs[2 * n_space :]
    rows, group = dattn_refs[0].shape
    heads = group // size
    for b in range(n_space):
        at = slice(b * rows, (b + 1) * rows)
        k_ref[at, :] = qkv_refs[b][:, group : 2 * group]
        v_ref[at, :] = qkv_refs[b][:, 2 * group :]
    lane_head = iota((rows, group), 1) // size if heads > 1 else None
    for b in range(n_space):
        at = slice(b * rows, (b + 1) * rows)
        queries, d_out = qkv_refs[b][:, :group], dattn_refs[b][...]
        attn = dq = None
        for h in range(heads):
            if heads > 1:
                q_h = jnp.where(lane_head == h, queries.astype(F32), 0.0).astype(BF16)
                do_h = jnp.where(lane_head == h, d_out.astype(F32), 0.0).astype(BF16)
            else:
                q_h, do_h = queries, d_out
            logits = mm(q_h, k_ref[...], NT) * scale
            shifted = jnp.exp(logits - jnp.max(logits, axis=-1, keepdims=True))
            probs = shifted * (1.0 / jnp.sum(shifted, axis=-1, keepdims=True))
            probs_b = probs.astype(BF16)
            attn_h = mm(probs_b, v_ref[...])
            dprob = mm(do_h, v_ref[...], NT)
            delta = jnp.sum(probs * dprob, axis=-1, keepdims=True)
            dscore = (probs * (dprob - delta) * scale).astype(BF16)
            dq_h = mm(dscore, k_ref[...])
            dk = mm(dscore, q_h, TN)
            dv = mm(probs_b, do_h, TN)
            if b == 0 and h == 0:
                dk_ref[...] = dk
                dv_ref[...] = dv
            else:
                dk_ref[...] += dk
                dv_ref[...] += dv
            attn = attn_h if attn is None else jnp.where(lane_head == h, attn_h, attn)
            dq = dq_h if dq is None else jnp.where(lane_head == h, dq_h, dq)
        attn_ref[at, :] = attn.astype(BF16)
        dqkv_ref[at, :group] = dq.astype(BF16)
    dqkv_ref[:, group : 2 * group] = dk_ref[...].astype(BF16)
    dqkv_ref[:, 2 * group :] = dv_ref[...].astype(BF16)


def dn_body(me_ref, dqkv_ref, w_ref, keep_ref, send_ref, dn_ref):
    dn_ref[...] = mm(dqkv_ref[...], w_ref[...], NT).astype(BF16)
    block = keep_ref.shape[1]
    core = me_ref[0] & 1
    for c in range(keep_ref.shape[0]):
        for ref, device in ((keep_ref, 2 * c + core), (send_ref, 2 * c + 1 - core)):
            ref[c] = dn_ref[pl.ds(pl.multiple_of(device * block, block), block), :]


def columns_body(n_space, me_ref, in_ref, *refs):
    out_refs, (cols_ref,) = refs[:n_space], refs[n_space:]
    cols = cols_ref.shape[2]
    for c in range(n_space):
        cols_ref[c] = in_ref[:, c * cols : (c + 1) * cols]
    for k in range(n_space):
        out_refs[k][...] = cols_ref[me_ref[1] ^ k]


def head_grads_body(n_space, *refs):
    normed_refs, (dqkv_ref, gqkv_ref, flag_ref) = refs[:n_space], refs[n_space:]
    flag_ref[...] = jnp.zeros(flag_ref.shape, F32)
    rows = normed_refs[0].shape[0]
    natural = mm(dqkv_ref[...], head_order(dqkv_ref.shape[1]), NT).astype(BF16)
    gqkv_ref[...] = sum(
        mm(ref[...], natural[b * rows : (b + 1) * rows, :], TN) for b, ref in enumerate(normed_refs)
    )


def dn_pair_body(me_ref, keep_ref, got_ref, *out_refs):
    for k, out_ref in enumerate(out_refs):
        slot = (me_ref[0] >> 1) ^ k
        out_ref[...] = (keep_ref[slot].astype(F32) + got_ref[slot].astype(F32)).astype(BF16)


def joined_body(n, *refs):
    ins = refs[:n]
    centred_ref, inv_ref, gain_ref, cot_ref, mixed_ref, agg_ref, packet_ref, dgain_ref = refs[n:]
    width = centred_ref.shape[1]
    d_normed = sum(ref[...].astype(F32) for ref in ins)
    centred = centred_ref[...]
    dgain_ref[...] = jnp.broadcast_to(jnp.sum(d_normed * centred, axis=0, keepdims=True), dgain_ref.shape)
    gained = d_normed * gain_ref[...]
    inner = (
        gained
        - jnp.mean(gained, axis=-1, keepdims=True)
        - centred * jnp.mean(gained * centred, axis=-1, keepdims=True)
    )
    d_joined = (cot_ref[...].astype(F32) + inner * inv_ref[:, :1]).astype(BF16)
    d_pooled = mm(d_joined, agg_ref[...], NT)
    center = pack(head_sums(d_pooled * mixed_ref[...], fold_matrix(width, width // HEADS)))
    packet_ref[:, :width] = d_joined
    packet_ref[:, width:] = center


def prepare_body(me_ref, pooled_ref, even_ref, odd_ref, agg_ref, djoined_ref, dpool_ref, stat_ref):
    width = agg_ref.shape[0]
    for k in range(even_ref.shape[0]):
        for odd, ref in ((0, even_ref), (1, odd_ref)):
            djoined_ref[pair_rows(me_ref[0], k, odd, even_ref.shape[1]), :] = ref[k]
    dpool_ref[...] = mm(djoined_ref[:, :width], agg_ref[...], NT)
    stat_ref[0] = unpack(djoined_ref[:, width:])
    stat_ref[1] = unpack(pooled_ref[:, width:])
    stat_ref[2] = 1.0 / unpack(pooled_ref[:, width:], 3)


def out_grad_body(me_ref, pooled_ref, djoined_ref, dgain_ref, attn_ref, cot_ref, out_ref, all_ref):
    width = dgain_ref.shape[1]
    all_ref[...] = mm(pooled_ref[:, :width], djoined_ref[:, :width], TN)
    weight_grad = mm(attn_ref[...], cot_ref[...], TN).astype(BF16)
    n_space, height, cols = out_ref.shape
    block = height - 16 - weight_grad.shape[0]
    start = pl.multiple_of(me_ref[0] * block, block)
    own = all_ref[pl.ds(start, block), :].astype(BF16)
    extra = three_rows(dgain_ref[:1, :])
    for c in range(n_space):
        out_ref[c, :block, :] = own[:, c * cols : (c + 1) * cols]
        out_ref[c, block : block + 16, :] = extra[:, c * cols : (c + 1) * cols]
        out_ref[c, block + 16 :, :] = weight_grad[:, c * cols : (c + 1) * cols]


def dvalue_body(dpool_ref, stat_ref, value_ref, scores_ref, dvalue_ref, dlogit_ref, spread_ref, fold_ref):
    width = dpool_ref.shape[1]
    size = width // HEADS

    @pl.when(pl.program_id(0) == 0)
    def _():
        spread_ref[...] = spread_matrix(width, size)
        fold_ref[...] = fold_matrix(width, size)

    weight = jnp.exp(scores_ref[0] - stat_ref[1]) * stat_ref[2]
    dvalue_ref[0] = (mm(pack(weight), spread_ref[...]) * dpool_ref[...]).astype(BF16)
    dweight = head_sums(dpool_ref[...] * value_ref[0], fold_ref[...])
    dlogit = weight * (dweight - stat_ref[0])
    hi = dlogit.astype(BF16)
    dlogit_ref[0, :, :LANES] = hi
    dlogit_ref[0, :, LANES:] = (dlogit - hi.astype(F32)).astype(BF16)


def embed_body(
    n_space, me_ref, dvalue_ref, dlogit_ref, patches_ref, wv_ref, wback_ref, keep_ref, send_ref, cols_ref, extra_ref
):
    v = pl.program_id(0)
    hi, lo = dlogit_ref[0, :, :LANES].astype(F32), dlogit_ref[0, :, LANES:].astype(F32)
    group = iota(hi.shape, 1) >> 4
    mixed = jnp.where(group < 2, hi, jnp.where(group == 2, lo, 0.0)).astype(BF16)
    d_tokens = (mm(dvalue_ref[0], wv_ref[...], NT) + mm(mixed, wback_ref[...], NT)).astype(BF16)
    grad = mm(patches_ref[0], d_tokens, TN).astype(BF16)
    hi, lo, _ = parts3(jnp.sum(d_tokens.astype(F32), axis=0, keepdims=True))
    row = iota(extra_ref.shape, 0)
    extra = jnp.where(row == 2 * v, hi, jnp.where(row == 2 * v + 1, lo, 0.0))

    @pl.when(v == 0)
    def _():
        extra_ref[...] = extra

    @pl.when(v > 0)
    def _():
        extra_ref[...] += extra

    cols = cols_ref.shape[2]
    pixels = patches_ref.shape[2]
    for c in range(n_space):
        cols_ref[c] = grad[:, c * cols : (c + 1) * cols]
    at = pl.ds(pl.multiple_of(v * pixels, pixels), pixels)
    for k in range(0, n_space, 2):
        keep_ref[k // 2, at, :] = cols_ref[me_ref[1] ^ k]
        send_ref[k // 2, at, :] = cols_ref[me_ref[1] ^ (k + 1)]

    @pl.when(v == pl.num_programs(0) - 1)
    def _():
        tail = slice(keep_ref.shape[1] - 16, keep_ref.shape[1])
        for c in range(n_space):
            cols_ref[c, :16, :] = extra_ref[:, c * cols : (c + 1) * cols].astype(BF16)
        for k in range(0, n_space, 2):
            keep_ref[k // 2, tail, :] = cols_ref[me_ref[1] ^ k, :16, :]
            send_ref[k // 2, tail, :] = cols_ref[me_ref[1] ^ (k + 1), :16, :]


def embed_final_body(parts, *refs):
    ins, (grad_ref, offset_ref) = refs[:-2], refs[-2:]
    pixels = grad_ref.shape[1]
    base = 0
    for chunk in range(len(ins) // parts):
        total = 0.0
        for ref in ins[chunk * parts : (chunk + 1) * parts]:
            total = total + (ref[0] if len(ref.shape) == 3 else ref[...]).astype(F32)
        count = (total.shape[0] - 16) // pixels
        for v in range(count):
            grad_ref[base + v] = total[v * pixels : (v + 1) * pixels, :]
            row = count * pixels + 2 * v
            offset_ref[base + v : base + v + 1, :] = total[row : row + 1, :] + total[row + 1 : row + 2, :]
        base += count


def stack_body(*refs):
    for k, ref in enumerate(refs[:-1]):
        refs[-1][k] = ref[...]


def value_grad_body(me_ref, *refs):
    tokens_refs, dv_refs, dl_refs, (keep_ref, send_ref, all_ref) = refs[:2], refs[2:4], refs[4:6], refs[6:]
    width = dv_refs[0].shape[2]
    total, both = 0.0, 0.0
    for tokens_ref, dv_ref, dl_ref in zip(tokens_refs, dv_refs, dl_refs):
        for v in range(dv_ref.shape[0]):
            total = total + mm(tokens_ref[v], dv_ref[v], TN)
            both = both + mm(tokens_ref[v], dl_ref[v], TN)
    all_ref[:, :width] = total.astype(BF16)
    all_ref[:, width:] = pack(both[:, :LANES] + both[:, LANES:])
    block = keep_ref.shape[1]
    count = all_ref.shape[0] // block
    for r in range(count):
        target = pl.program_id(0) * count + r
        same = (target & 1) == (me_ref[0] & 1)
        slot = target >> 1

        @pl.when(same)
        def _():
            keep_ref[slot] = all_ref[r * block : (r + 1) * block, :]

        @pl.when(jnp.logical_not(same))
        def _():
            send_ref[slot] = all_ref[r * block : (r + 1) * block, :]


def pair_sum_body(n_chip, me_ref, keep_ref, got_ref, *out_refs):
    width = keep_ref.shape[2] - LANES
    for k in range(n_chip):
        slot = (me_ref[0] >> 1) ^ k
        mine, other = keep_ref[slot], got_ref[slot]
        out_refs[k][:, :width] = (mine[:, :width].astype(F32) + other[:, :width].astype(F32)).astype(BF16)
        out_refs[k][:, width:] = pack(unpack(mine[:, width:]) + unpack(other[:, width:]))


def packet_split_body(n_in, me_ref, *refs):
    ins, (gathered_ref, keep_ref, send_ref, cols_ref) = refs[:n_in], refs[n_in:]
    block, width = ins[0].shape[0], ins[0].shape[1] - LANES
    total = sum(ref[:, :width].astype(F32) for ref in ins).astype(BF16)
    factor = pack(sum(unpack(ref[:, width:]) for ref in ins))
    n_space, height, cols = gathered_ref.shape
    half = n_space // 2
    for c in range(half):
        cols_ref[c] = total[:, 2 * c * cols : 2 * (c + 1) * cols]
    part = keep_ref.shape[1] - height - 2 * block
    for k in range(n_space):
        ref = (send_ref if k % 2 else keep_ref).at[k // 2]
        ref[:height, :] = gathered_ref[me_ref[1] ^ k]
        for piece in range(block // part):
            lanes = slice(piece * LANES, (piece + 1) * LANES)
            ref[height : height + part, lanes] = factor[piece * part : (piece + 1) * part, :]
        large = cols_ref[jnp.maximum((me_ref[1] ^ k) - half, 0)]
        ref[height + part : height + part + block, :] = large[:, :cols]
        ref[height + part + block :, :] = large[:, cols:]


def message_add_body(block, height, part, mine_ref, got_ref, *refs):
    for j, out_ref in enumerate(refs):
        mine, got = mine_ref.at[j + 1], got_ref.at[j + 1]
        total = mine[...].astype(F32) + got[...].astype(F32)
        out_ref[...] = total.astype(BF16)
        out_ref[block : block + 16, :] = three_rows(jnp.sum(total[block : block + 16, :], axis=0, keepdims=True))
        for piece in range(out_ref.shape[1] // LANES):
            at = slice(height, height + part), slice(piece * LANES, (piece + 1) * LANES)
            out_ref[at] = pack(unpack(mine[at]) + unpack(got[at]))


def space_sum_body(keep_ref, got_ref, *refs):
    ins, (out_ref, weight_ref) = [keep_ref.at[0], got_ref.at[0]] + list(refs[:-2]), refs[-2:]
    cols = weight_ref.shape[1]
    width = out_ref.shape[1] - LANES - cols
    block = out_ref.shape[0] - 16
    height = block + 16 + weight_ref.shape[0]
    part = keep_ref.shape[1] - height - 2 * block
    total = sum(ref[...].astype(F32) for ref in ins)
    for piece in range(2):
        at = slice(height + part + piece * block, height + part + (piece + 1) * block)
        out_ref[:block, piece * cols : (piece + 1) * cols] = total[at, :].astype(BF16)
    for piece in range(block // part):
        lanes = slice(piece * LANES, (piece + 1) * LANES)
        factor = pack(sum(unpack(ref[height : height + part, lanes]) for ref in ins))
        out_ref[piece * part : (piece + 1) * part, width : width + LANES] = factor
    out_ref[block:, : width + LANES] = jnp.zeros((16, width + LANES), BF16)
    out_ref[:block, width + LANES :] = total[:block, :].astype(BF16)
    out_ref[block:, width + LANES :] = three_rows(jnp.sum(total[block : block + 16, :], axis=0, keepdims=True))
    weight_ref[...] = total[block + 16 : height, :]


def add_body(n, keep_ref, got_ref, *refs):
    for j, out_ref in enumerate(refs):
        out_ref[...] = (keep_ref[j + 1].astype(F32) + got_ref[j + 1].astype(F32)).astype(BF16)


def final_body(n_var, n_space, scale, me_ref, even_ref, odd_ref, query_ref, wk_ref, kv_ref, gq_ref, out_ref, gain_ref):
    me_v, me_s = me_ref[0], me_ref[1]
    half = n_space // 2
    width = wk_ref.shape[1]
    size = width // HEADS
    cols, qcols = kv_ref.shape[1], gq_ref.shape[1]
    place = pl.multiple_of(jnp.minimum(me_s, half - 1) * cols, LANES)
    spread_kv = spread_matrix(cols, size, place)
    qplace = pl.multiple_of(me_s * qcols, LANES)
    spread_q = spread_matrix(qcols, size, qplace)
    query = query_ref[:, pl.ds(place, cols)] * scale
    block = even_ref.shape[1] - 16
    total, gain = 0.0, 0.0
    for k in range(n_var):
        part_ref, slot = (odd_ref if k % 2 else even_ref), k // 2
        at = pl.ds(pl.multiple_of((me_v ^ k) * block, block), block)
        packed = part_ref[slot, :block, cols : cols + LANES]
        key_grad = mm(packed, spread_kv) * query
        kv_ref[at, :] = jnp.where(me_s < half, key_grad, part_ref[slot, :block, :cols].astype(F32))
        keys = wk_ref[at, pl.ds(qplace, qcols)].astype(F32)
        total = total + jnp.sum(mm(packed, spread_q) * keys, axis=0, keepdims=True)
        out_ref[at, :] = part_ref[slot, :block, cols + LANES :].astype(F32)
        gain = gain + jnp.sum(part_ref[slot, block:, cols + LANES :].astype(F32), axis=0, keepdims=True)
    gq_ref[...] = total * scale
    gain_ref[...] = gain


def shards(
    patches, embed_weight, var_embed, agg_query, agg_kv, agg_out, norm_gain, qkv_weight, out_weight, cotangent
):
    n_var, n_space = lax.axis_size("var"), lax.axis_size("space")
    count, rows, pixels = patches.shape
    width = agg_out.shape[0]
    size = width // HEADS
    scale = 1.0 / math.sqrt(size)
    block = rows // n_var
    cols = width // n_space
    group = out_weight.shape[0]
    drows = width // n_var
    positions = rows * n_space
    kv_cols = 2 * width // n_space
    me = jnp.stack([lax.axis_index("var"), lax.axis_index("space")]).astype(jnp.int32)
    gain = norm_gain.reshape(1, width)
    query = agg_query.reshape(1, width)
    vmem = pl.BlockSpec(memory_space=pltpu.VMEM)
    hbm = pl.BlockSpec(memory_space=pltpu.HBM)
    packet = width + LANES

    whole = lambda shape: pl.BlockSpec(shape, lambda v: (0,) * len(shape))
    every = lambda shape: pl.BlockSpec((1,) + shape, lambda v: (v,) + (0,) * len(shape))
    n_chip = n_var // 2
    half = count // 2

    dattn, cot_own, w_heads = call(
        early_body,
        [struct((rows, group), BF16), struct((block, width), BF16), struct(qkv_weight.shape, BF16)],
        limit=LIMITS["early"],
        grid=(1,),
        in_specs=[SMEM] + [whole(x.shape) for x in (cotangent, out_weight, qkv_weight)],
        out_specs=[whole((rows, group)), whole((block, width)), whole(qkv_weight.shape)],
        cost_estimate=cost(2e8, 4e6),
        name="early",
    )(me, cotangent, out_weight, qkv_weight)
    dattn_all = gather_direct(dattn, "space")

    def forward_outs(here):
        return [struct((here, rows, width), BF16), struct((here, rows, width), F32), struct((here, rows, LANES), F32)]

    tokens0, value0, scores0, w_query, w_back, *state0 = call(
        functools.partial(first_body, scale),
        forward_outs(half)
        + [struct((width, 3 * LANES), BF16), struct((width, LANES), BF16)]
        + [struct((rows, width), F32), struct((rows, LANES), F32), struct((rows, LANES), F32)],
        limit=LIMITS["first"],
        after=[dattn],
        in_specs=[hbm, hbm, vmem, vmem, hbm],
        scratch_shapes=[
            pltpu.VMEM((half, rows, pixels), BF16),
            pltpu.VMEM((half, pixels, width), BF16),
            pltpu.VMEM(agg_kv.shape, BF16),
            pltpu.SemaphoreType.DMA((4,)),
        ],
        cost_estimate=cost(6e9, 2e7),
        name="forward_first",
    )(patches, embed_weight, var_embed, query, agg_kv)
    tokens1, value1, scores1, keep, send = call(
        functools.partial(second_body, half),
        forward_outs(count - half) + [struct((n_chip, block, packet), F32)] * 2,
        limit=LIMITS["forward"],
        after=dattn_all[1:],
        in_specs=[SMEM] + [vmem] * 8,
        scratch_shapes=[pltpu.VMEM((rows, width), F32), pltpu.VMEM((rows, LANES), F32)],
        cost_estimate=cost(4e9, 1e7),
        name="forward_second",
    )(me, patches, embed_weight, var_embed, w_query, agg_kv, *state0)

    def pool_pairs(mine, got):
        return call(
            pool_pair_body,
            [struct((block, packet), F32)] * n_chip,
            limit=LIMITS["pool_pair"],
            in_specs=[SMEM, vmem, vmem],
            cost_estimate=cost(1e8, 3e6),
            name="pool_pair",
        )(me, mine, got)

    received = exchange_pairs(keep, send, pool_pairs)
    mixed, pooled_packet = call(
        functools.partial(pool_body, n_chip),
        [struct((block, width), F32), struct((block, packet), BF16)],
        limit=LIMITS["pool"],
        cost_estimate=cost(1e8, 2e6),
        name="pool",
    )(*received)
    pooled_even, pooled_odd = gather_pairs(pooled_packet, "var")

    qkv, normed, pooled_packets, centred, inv = call(
        norm_body,
        [
            struct((rows, 3 * group), BF16),
            struct((rows, width), BF16),
            struct((rows, packet), BF16),
            struct((block, width), F32),
            struct((block, LANES), F32),
        ],
        limit=LIMITS["norm"],
        in_specs=[SMEM] + [vmem] * 5,
        scratch_shapes=[pltpu.VMEM((rows, width), F32), pltpu.VMEM((rows, LANES), F32)],
        cost_estimate=cost(8e8, 5e6),
        name="norm",
    )(me, pooled_even, pooled_odd, agg_out, gain, w_heads)

    qkv_all = gather_direct(qkv, "space")
    normed_cols = call(
        functools.partial(columns_body, n_space),
        [struct((rows, cols), BF16)] * n_space,
        limit=LIMITS["columns"],
        after=qkv_all[1:],
        in_specs=[SMEM, vmem],
        scratch_shapes=[pltpu.VMEM((n_space, rows, cols), BF16)],
        cost_estimate=cost(1e6, 1e6),
        name="columns",
    )(me, normed)
    normed_all = exchange_direct(normed_cols, "space")
    attn, dqkv = call(
        functools.partial(attention_body, n_space, size, scale),
        [struct((positions, group), BF16), struct((positions, 3 * group), BF16)],
        limit=LIMITS["attention"],
        after=[normed_cols[0]],
        scratch_shapes=[pltpu.VMEM((positions, group), BF16)] * 2 + [pltpu.VMEM((positions, group), F32)] * 2,
        cost_estimate=cost(6e9, 4e6),
        name="attention",
    )(*qkv_all, *dattn_all)
    dn_keep, dn_send = call(
        dn_body,
        [struct((n_chip, block, width), BF16)] * 2,
        limit=LIMITS["dn"],
        after=normed_all[1:],
        grid=(1,),
        in_specs=[SMEM, pl.BlockSpec((rows, 3 * group), lambda i: (0, 0)), vmem],
        scratch_shapes=[pltpu.VMEM((rows, width), BF16)],
        cost_estimate=cost(2e8, 1e6),
        name="dn",
    )(me, dqkv, w_heads)

    def dn_pairs(mine, got):
        return call(
            dn_pair_body,
            [struct((block, width), BF16)] * n_chip,
            limit=LIMITS["dn_pair"],
            in_specs=[SMEM, vmem, vmem],
            cost_estimate=cost(1e6, 1e6),
            name="dn_pair",
        )(me, mine, got)

    dn_received = exchange_pairs(dn_keep, dn_send, dn_pairs)
    joined_packet, dgain = call(
        functools.partial(joined_body, n_chip),
        [struct((block, packet), BF16), struct((8, width), F32)],
        limit=LIMITS["joined"],
        cost_estimate=cost(2e8, 3e6),
        name="joined",
    )(*dn_received, centred, inv, gain, cot_own, mixed, agg_out)
    joined_even, joined_odd = gather_pairs(joined_packet, "var")

    d_joined, d_pooled, stat = call(
        prepare_body,
        [struct((rows, packet), BF16), struct((rows, width), F32), struct((3, rows, LANES), F32)],
        limit=LIMITS["prepare"],
        in_specs=[SMEM] + [vmem] * 4,
        cost_estimate=cost(6e8, 4e6),
        name="prepare",
    )(me, pooled_packets, joined_even, joined_odd, agg_out)
    def d_values(value, scores):
        here = value.shape[0]
        return call(
            dvalue_body,
            [struct((here, rows, width), BF16), struct((here, rows, 2 * LANES), BF16)],
            limit=LIMITS["dvalue"],
            grid=(here,),
            in_specs=[whole((rows, width)), whole((3, rows, LANES)), every((rows, width)), every((rows, LANES))],
            out_specs=[every((rows, width)), every((rows, 2 * LANES))],
            scratch_shapes=[pltpu.VMEM((LANES, width), BF16), pltpu.VMEM((width, LANES), BF16)],
            cost_estimate=cost(2e9, 5e6),
            name="dvalue",
        )(d_pooled, stat, value, scores)

    def embed(start, d_value, d_logit, after):
        here = d_value.shape[0]
        at = lambda shape: pl.BlockSpec((1,) + shape, lambda v: (v + start,) + (0,) * len(shape))
        blocks = (n_space // 2, here * pixels + 16, cols)
        return call(
            functools.partial(embed_body, n_space),
            [struct(blocks, BF16)] * 2,
            limit=LIMITS["embed"],
            after=after,
            grid=(here,),
            in_specs=[
                SMEM,
                every((rows, width)),
                every((rows, 2 * LANES)),
                at((rows, pixels)),
                pl.BlockSpec((width, width), lambda v: (0, 1)),
                whole((width, LANES)),
            ],
            out_specs=[whole(blocks)] * 2,
            scratch_shapes=[pltpu.VMEM((n_space, pixels, cols), BF16), pltpu.VMEM((16, width), F32)],
            cost_estimate=cost(1.5e9, 4e6),
            name="embed",
        )(me, d_value, d_logit, patches, agg_kv, w_back)

    dv0, dl0 = d_values(value0, scores0)
    dv1, dl1 = d_values(value1, scores1)

    step = max(drows, 256)
    kv_keep, kv_send = call(
        value_grad_body,
        [struct((n_chip, drows, packet), BF16)] * 2,
        limit=LIMITS["value_grad"],
        grid=(width // step,),
        in_specs=[SMEM]
        + [pl.BlockSpec(x.shape[:2] + (step,), lambda i: (0, 0, i)) for x in (tokens0, tokens1)]
        + [whole(x.shape) for x in (dv0, dv1, dl0, dl1)],
        out_specs=[whole((n_chip, drows, packet))] * 2,
        scratch_shapes=[pltpu.VMEM((step, packet), BF16)],
        cost_estimate=cost(4e9, 1e7),
        name="value_grad",
    )(me, tokens0, tokens1, dv0, dv1, dl0, dl1)
    kv_got = swap(kv_send, "var", 1)

    out_block = call(
        out_grad_body,
        struct((n_space, drows + 16 + group, cols), BF16),
        limit=LIMITS["out_grad"],
        after=[kv_keep],
        grid=(1,),
        in_specs=[SMEM] + [whole(x.shape) for x in (pooled_packets, d_joined, dgain)] + [whole((rows, group)), whole((rows, width))],
        out_specs=whole((n_space, drows + 16 + group, cols)),
        scratch_shapes=[pltpu.VMEM((width, width), F32)],
        cost_estimate=cost(6e8, 3e6),
        name="out_grad",
    )(me, pooled_packets, d_joined, dgain, attn, cotangent)

    def scatter_embed(keep, arrived, after):
        n = n_space // 2 - 1
        sums = call(
            functools.partial(add_body, n),
            [struct(keep.shape[1:], BF16)] * n,
            limit=LIMITS["add"],
            after=after,
            cost_estimate=cost(1e6, 1e6),
            name="add",
        )(keep, arrived)
        blocks = {2 * (j + 1): sums[j] for j in range(n)}
        mine, bit = [keep, arrived], 2
        while bit < n_space:
            got = {k ^ bit: swap(blocks[k], "space", bit) for k in blocks if k & bit and k % bit == 0}
            mine.append(got[0])
            for k in got:
                if k:
                    blocks[k] = (blocks[k].astype(F32) + got[k].astype(F32)).astype(BF16)
            bit *= 2
        return mine, list(sums)

    keep0, send0 = embed(0, dv0, dl0, [kv_keep])
    arrived0 = swap(send0, "space", 1)
    kv_blocks = call(
        functools.partial(pair_sum_body, n_chip),
        [struct((drows, packet), BF16)] * n_chip,
        limit=LIMITS["pair_sum"],
        after=[keep0],
        in_specs=[SMEM] + [vmem] * 2,
        cost_estimate=cost(1e6, 1e6),
        name="pair_sum",
    )(me, kv_keep, kv_got)
    kv_parts = [kv_blocks[0]] + [swap(kv_blocks[k], "var", 2 * k) for k in range(1, n_chip)]
    mine0, sums0 = scatter_embed(keep0, arrived0, [kv_blocks[0]])
    height = drows + 16 + group
    part = drows * LANES // cols
    message = (height + part + 2 * drows, cols)
    message_keep, message_send = call(
        functools.partial(packet_split_body, n_chip),
        [struct((n_space // 2,) + message, BF16)] * 2,
        limit=LIMITS["packet_split"],
        after=sums0,
        in_specs=[SMEM] + [vmem] * (n_chip + 1),
        scratch_shapes=[pltpu.VMEM((n_space // 2, drows, kv_cols), BF16)],
        cost_estimate=cost(1e6, 1e6),
        name="packet_split",
    )(me, *kv_parts, out_block)
    message_got = swap(message_send, "space", 1)
    keep1, send1 = embed(half, dv1, dl1, mine0[2:] or sums0)
    arrived1 = swap(send1, "space", 1)

    def message_add(mine, got):
        return call(
            functools.partial(message_add_body, drows, height, part),
            [struct(message, BF16)] * (mine.shape[0] - 1),
            after=[keep1],
            cost_estimate=cost(1e6, 1e6),
            name="message_add",
        )(mine, got)

    later, bit = message_add(message_keep, message_got), 2
    message_parts = []
    while bit < n_space:
        got = {j: swap(later[j], "space", bit) for j in range(0, len(later), 2)}
        message_parts.append(got[0])
        rest = [j for j in range(1, len(later), 2)]
        if rest:
            pad = [later[0]] + [later[j] for j in rest]
            pad_got = [later[0]] + [got[j + 1] for j in rest]
            later = message_add(jnp.stack(pad), jnp.stack(pad_got))
        bit *= 2
    mine1, sums1 = scatter_embed(keep1, arrived1, [])
    grad_qkv, head_flag = call(
        functools.partial(head_grads_body, n_space),
        [struct((cols, 3 * group), F32), struct((8, LANES), F32)],
        limit=LIMITS["head_grads"],
        cost_estimate=cost(1e9, 3e6),
        name="head_grads",
    )(*normed_all, dqkv)
    one = pl.BlockSpec((1,) + message, lambda i: (0, 0, 0))
    kv_sum, grad_out = call(
        space_sum_body,
        [struct((drows + 16, kv_cols + LANES + cols), BF16), struct((group, cols), F32)],
        limit=LIMITS["space_sum"],
        after=[head_flag],
        grid=(1,),
        in_specs=[one, one] + [whole(message)] * len(message_parts),
        cost_estimate=cost(1e6, 1e6),
        name="space_sum",
    )(message_keep, message_got, *message_parts)

    def stack(parts):
        return call(
            stack_body,
            struct((len(parts),) + parts[0].shape, BF16),
            after=sums1,
            cost_estimate=cost(1e6, 1e6),
            name="stack",
        )(*parts)

    kv_even, kv_odd = gather_pairs(kv_sum, "var", stack)
    grad_agg_kv, grad_query, grad_agg_out, grad_gain = call(
        functools.partial(final_body, n_var, n_space, scale),
        [struct((width, kv_cols), F32), struct((1, cols), F32)] + [struct((width, cols), F32), struct((1, cols), F32)],
        grid=(1,),
        in_specs=[SMEM] + [vmem] * 3 + [pl.BlockSpec((width, width), lambda i: (0, 0))],
        limit=LIMITS["final"],
        cost_estimate=cost(2e8, 5e6),
        name="final",
    )(me, kv_even, kv_odd, query, agg_kv)

    def first_block(x):
        if x.ndim == 3:
            return pl.BlockSpec((1,) + x.shape[1:], lambda i: (0, 0, 0))
        return pl.BlockSpec(x.shape, lambda i: (0, 0))

    grad_embed, grad_var_embed = call(
        functools.partial(embed_final_body, len(mine0)),
        [struct((count, pixels, cols), F32), struct((count, cols), F32)],
        grid=(1,),
        in_specs=[first_block(x) for x in mine0 + mine1],
        limit=LIMITS["embed_final"],
        cost_estimate=cost(1e6, 1e6),
        name="embed_final",
    )(*mine0, *mine1)

    return (
        grad_embed,
        grad_var_embed,
        grad_query.reshape(cols),
        grad_agg_kv,
        grad_agg_out,
        grad_gain.reshape(cols),
        grad_qkv,
        grad_out,
    )


def solution(mesh):
    return jax.shard_map(
        shards,
        mesh=mesh,
        in_specs=(
            P("var", "space", None),
            P("var", None, None),
            P("var", None),
            P(),
            P(),
            P(),
            P(),
            P(None, "var"),
            P("var", None),
            P("space", None),
        ),
        out_specs=(
            P("var", None, "space"),
            P("var", "space"),
            P("space"),
            P(None, "space"),
            P(None, "space"),
            P("space"),
            P("space", "var"),
            P("var", "space"),
        ),
        check_vma=False,
    )
```

```python
import functools
import math

import jax
import jax.numpy as jnp
from jax import lax
from jax.experimental import pallas as pl
from jax.experimental.pallas import tpu as pltpu
from jax.sharding import PartitionSpec as P

HEADS = 16
LANES = 128
EPSILON = 1e-05
MIB = 1 << 20

LIMITS = {
    "early": 60, "forward": 24, "columns": 8, "pool_pair": 16, "pool": 16, "norm": 16, "attention": 24,
    "dn": 12, "dn_pair": 16, "joined": 16, "prepare": 16, "out_grad": 16, "dvalue": 24, "embed": 24, "value_grad": 32,
    "add": 12, "pair_sum": 16, "packet_split": 16, "space_sum": 16, "head_grads": 16, "final": 16, "embed_final": 24,
}

F32 = jnp.float32
BF16 = jnp.bfloat16

NN = (((1,), (0,)), ((), ()))
NT = (((1,), (1,)), ((), ()))
TN = (((0,), (0,)), ((), ()))


def mm(a, b, dims=NN):
    return lax.dot_general(a, b, dims, preferred_element_type=F32)


def iota(shape, axis):
    return lax.broadcasted_iota(jnp.int32, shape, axis)


def parts3(x):
    hi = x.astype(BF16).astype(F32)
    rest = x - hi
    mid = rest.astype(BF16).astype(F32)
    return hi, mid, rest - mid


def pack(x, y=None):
    group = iota(x.shape, 1) >> 4
    hi, mid, lo = parts3(x)
    out = jnp.where(group == 0, hi, jnp.where(group == 1, mid, jnp.where(group == 2, lo, 0.0)))
    if y is not None:
        hi, mid, lo = parts3(y)
        out = jnp.where(group == 3, hi, jnp.where(group == 4, mid, jnp.where(group == 5, lo, out)))
    return out.astype(BF16)


def unpack(packed, first_group=0):
    row, column = iota((LANES, LANES), 0), iota((LANES, LANES), 1)
    group = row >> 4
    take = ((row & 15) == (column & 15)) & (group >= first_group) & (group < first_group + 3)
    return mm(packed, jnp.where(take, 1.0, 0.0).astype(BF16))


def spread_matrix(width, size, first=0):
    row, column = iota((LANES, width), 0), iota((LANES, width), 1)
    shift = size.bit_length() - 1
    take = ((row & 15) == ((column + first) >> shift)) & (row < 48)
    return jnp.where(take, 1.0, 0.0).astype(BF16)


def fold_matrix(width, size):
    row, column = iota((width, LANES), 0), iota((width, LANES), 1)
    shift = size.bit_length() - 1
    return jnp.where((column & 15) == (row >> shift), 1.0, 0.0).astype(BF16)


def head_sums(x, fold):
    hi, mid, lo = parts3(x)
    return mm(hi.astype(BF16), fold) + mm(mid.astype(BF16), fold) + mm(lo.astype(BF16), fold)


def call(body, out_shape, limit=16, after=(), in_specs=None, **kw):
    def run(*args):
        n, m = len(args), len(after)
        vmem = pl.BlockSpec(memory_space=pltpu.VMEM)
        return pl.pallas_call(
            lambda *refs: body(*refs[:n], *refs[n + m :]),
            out_shape=out_shape,
            in_specs=([vmem] * n if in_specs is None else list(in_specs)) + [vmem] * m,
            compiler_params=pltpu.CompilerParams(vmem_limit_bytes=limit * MIB),
            **kw,
        )(*args, *after)

    return run


def struct(shape, dtype):
    return jax.ShapeDtypeStruct(shape, dtype)


def cost(flops, moved):
    return pl.CostEstimate(flops=int(flops), bytes_accessed=int(moved), transcendentals=0)


SMEM = pl.BlockSpec(memory_space=pltpu.SMEM)


def swap(x, axis, k, keep=None):
    pairs = [(i, i ^ k) for i in range(lax.axis_size(axis))]
    if keep is not None:
        pairs = [pair for pair in pairs if keep(pair[1])]
    return lax.ppermute(x, axis, pairs)


def gather_direct(x, axis):
    return [x] + [swap(x, axis, k) for k in range(1, lax.axis_size(axis))]


def exchange_direct(blocks, axis):
    return [blocks[0]] + [swap(blocks[k], axis, k) for k in range(1, len(blocks))]


def gather_pairs(x, axis, stack=jnp.stack):
    even = [x] + [swap(x, axis, k) for k in range(2, lax.axis_size(axis), 2)]
    even = stack(even)
    return even, swap(even, axis, 1)


def exchange_pairs(keep, send, combine):
    parts = combine(keep, swap(send, "var", 1))
    return [parts[0]] + [swap(parts[k], "var", 2 * k) for k in range(1, len(parts))]


def pair_rows(me_v, k, odd, block):
    device = (((me_v >> 1) ^ k) << 1) + ((me_v & 1) ^ odd)
    return pl.ds(pl.multiple_of(device * block, block), block)


def three_rows(x):
    hi, mid, lo = parts3(x)
    row = iota((16, x.shape[1]), 0)
    return jnp.where(row == 0, hi, jnp.where(row == 1, mid, jnp.where(row == 2, lo, 0.0))).astype(BF16)


def head_order(width, size=64):
    heads = width // (3 * size)
    row, column = iota((width, width), 0), iota((width, width), 1)
    take = jnp.zeros((width, width), jnp.bool_)
    for h in range(heads):
        for c in range(3):
            start, target = h * 3 * size + c * size, c * heads * size + h * size
            inside = (column >= target) & (column < target + size)
            take = take | (inside & ((row - start) == (column - target)))
    return jnp.where(take, 1.0, 0.0).astype(BF16)


def early_body(me_ref, cot_ref, outw_ref, qkvw_ref, dattn_ref, own_ref, wperm_ref):
    dattn_ref[...] = mm(cot_ref[...], outw_ref[...], NT).astype(BF16)
    block = own_ref.shape[0]
    own_ref[...] = cot_ref[pl.ds(pl.multiple_of(me_ref[0] * block, block), block), :]
    wperm_ref[...] = mm(qkvw_ref[...], head_order(qkvw_ref.shape[1])).astype(BF16)


def forward_part(start, patches_ref, embed_ref, offset_ref, wq, wv_ref, spread, outs, state):
    tokens_ref, value_ref, scores_ref = outs
    here = tokens_ref.shape[0]
    width = tokens_ref.shape[2]
    for v in range(here):
        u = start + v
        tokens = (mm(patches_ref[u], embed_ref[u]) + offset_ref[u : u + 1, :]).astype(BF16)
        tokens_ref[v] = tokens
        pieces = mm(tokens, wq)
        scores_ref[v] = pieces[:, :LANES] + pieces[:, LANES : 2 * LANES] + pieces[:, 2 * LANES :]
        value_ref[v] = mm(tokens, wv_ref[:, width:])
    top = functools.reduce(jnp.maximum, [scores_ref[v] for v in range(here)])
    total, acc = 0.0, 0.0
    if state is not None:
        top = jnp.maximum(top, state[0])
        old = jnp.exp(state[0] - top)
        total, acc = state[1] * old, state[2] * mm(pack(old), spread)
    for v in range(here):
        new = jnp.exp(scores_ref[v] - top)
        total = total + new
        acc = acc + value_ref[v] * mm(pack(new), spread)
    return top, total, acc


def first_body(
    scale, patches_ref, embed_ref, offset_ref, query_ref, kv_ref,
    tokens_ref, value_ref, scores_ref, wq_ref, wback_ref, acc_ref, max_ref, sum_ref,
):
    width = tokens_ref.shape[2]
    size = width // HEADS
    row, column = iota((LANES, width), 0), iota((LANES, width), 1)
    own = (row & 15) == (column >> (size.bit_length() - 1))
    wq = jnp.zeros((width, LANES), F32)
    for part in parts3(query_ref[...]):
        wq = wq + mm(kv_ref[:, :width], jnp.where(own, part, 0.0).astype(BF16), NT)
    hi, mid, lo = parts3(wq * scale)
    wq_ref[:, :LANES] = hi.astype(BF16)
    wq_ref[:, LANES : 2 * LANES] = mid.astype(BF16)
    wq_ref[:, 2 * LANES :] = lo.astype(BF16)
    group = iota((width, LANES), 1) >> 4
    back = jnp.where((group == 0) | (group == 2), hi, jnp.where(group == 1, mid, 0.0))
    wback_ref[...] = back.astype(BF16)
    max_ref[...], sum_ref[...], acc_ref[...] = forward_part(
        0, patches_ref, embed_ref, offset_ref, wq_ref[...], kv_ref, spread_matrix(width, size),
        (tokens_ref, value_ref, scores_ref), None,
    )


def second_body(
    start, me_ref, patches_ref, embed_ref, offset_ref, wq_ref, kv_ref, acc0_ref, max0_ref, sum0_ref,
    tokens_ref, value_ref, scores_ref, keep_ref, send_ref, acc_ref, max_ref,
):
    width = tokens_ref.shape[2]
    top, total, acc = forward_part(
        start, patches_ref, embed_ref, offset_ref, wq_ref[...], kv_ref, spread_matrix(width, width // HEADS),
        (tokens_ref, value_ref, scores_ref), (max0_ref[...], sum0_ref[...], acc0_ref[...]),
    )
    acc_ref[...] = acc
    max_ref[...] = jnp.where(iota(top.shape, 1) < LANES // 2, top, total)
    block = keep_ref.shape[1]
    core = me_ref[0] & 1
    for c in range(keep_ref.shape[0]):
        for ref, device in ((keep_ref, 2 * c + core), (send_ref, 2 * c + 1 - core)):
            at = pl.ds(pl.multiple_of(device * block, block), block)
            ref[c, :, :width] = acc_ref[at, :]
            ref[c, :, width:] = max_ref[at, :]


def halves_of(both):
    low = iota(both.shape, 1) < LANES // 2
    turned = pltpu.roll(both, LANES // 2, 1)
    return jnp.where(low, both, turned), jnp.where(low, turned, both)


def pool_pair_body(me_ref, keep_ref, got_ref, *out_refs):
    width = keep_ref.shape[2] - LANES
    spread = spread_matrix(width, width // HEADS)
    low = iota((keep_ref.shape[1], LANES), 1) < LANES // 2
    for k, out_ref in enumerate(out_refs):
        slot = (me_ref[0] >> 1) ^ k
        mine, other = keep_ref[slot], got_ref[slot]
        max_a, sum_a = halves_of(mine[:, width:])
        max_b, sum_b = halves_of(other[:, width:])
        top = jnp.maximum(max_a, max_b)
        factor_a, factor_b = jnp.exp(max_a - top), jnp.exp(max_b - top)
        out_ref[:, :width] = mine[:, :width] * mm(pack(factor_a), spread) + other[:, :width] * mm(pack(factor_b), spread)
        out_ref[:, width:] = jnp.where(low, top, sum_a * factor_a + sum_b * factor_b)


def pool_body(n, *refs):
    ins, (mixed_ref, packet_ref) = refs[:n], refs[n:]
    width = mixed_ref.shape[1]
    stats = [halves_of(ref[:, width:]) for ref in ins]
    top = functools.reduce(jnp.maximum, [m for m, _ in stats])
    factors = [jnp.exp(m - top) for m, _ in stats]
    total = sum(s * f for (_, s), f in zip(stats, factors))
    spread = spread_matrix(width, width // HEADS)
    mixed = jnp.zeros(mixed_ref.shape, F32)
    for ref, factor in zip(ins, factors):
        mixed = mixed + ref[:, :width] * mm(pack(factor / total), spread)
    mixed_ref[...] = mixed
    packet_ref[:, :width] = mixed.astype(BF16)
    packet_ref[:, width:] = pack(top, total)


def norm_body(
    me_ref, even_ref, odd_ref, agg_ref, gain_ref, w_ref, qkv_ref, normed_ref, packets_ref, centred_ref, inv_ref,
    all_ref, allinv_ref,
):
    width = agg_ref.shape[0]
    block = centred_ref.shape[0]
    for k in range(even_ref.shape[0]):
        for odd, ref in ((0, even_ref), (1, odd_ref)):
            packets_ref[pair_rows(me_ref[0], k, odd, block), :] = ref[k]
    joined = mm(packets_ref[:, :width], agg_ref[...]).astype(BF16).astype(F32)
    mean = jnp.mean(joined, axis=-1, keepdims=True)
    spread_sq = jnp.mean((joined - mean) ** 2, axis=-1, keepdims=True)
    inv = lax.rsqrt(spread_sq + EPSILON)
    centred = (joined - mean) * inv
    normed = (centred * gain_ref[...]).astype(BF16)
    qkv_ref[...] = mm(normed, w_ref[...]).astype(BF16)
    normed_ref[...] = normed
    all_ref[...] = centred
    allinv_ref[...] = jnp.broadcast_to(inv, allinv_ref.shape)
    start = pl.multiple_of(me_ref[0] * block, block)
    centred_ref[...] = all_ref[pl.ds(start, block), :]
    inv_ref[...] = allinv_ref[pl.ds(start, block), :]


def attention_body(n_space, size, scale, *refs):
    qkv_refs, dattn_refs = refs[:n_space], refs[n_space : 2 * n_space]
    attn_ref, dqkv_ref, k_ref, v_ref, dk_ref, dv_ref = refs[2 * n_space :]
    rows, group = dattn_refs[0].shape
    heads = group // size
    for b in range(n_space):
        at = slice(b * rows, (b + 1) * rows)
        k_ref[at, :] = qkv_refs[b][:, group : 2 * group]
        v_ref[at, :] = qkv_refs[b][:, 2 * group :]
    lane_head = iota((rows, group), 1) // size if heads > 1 else None
    for b in range(n_space):
        at = slice(b * rows, (b + 1) * rows)
        queries, d_out = qkv_refs[b][:, :group], dattn_refs[b][...]
        attn = dq = None
        for h in range(heads):
            if heads > 1:
                q_h = jnp.where(lane_head == h, queries.astype(F32), 0.0).astype(BF16)
                do_h = jnp.where(lane_head == h, d_out.astype(F32), 0.0).astype(BF16)
            else:
                q_h, do_h = queries, d_out
            logits = mm(q_h, k_ref[...], NT) * scale
            shifted = jnp.exp(logits - jnp.max(logits, axis=-1, keepdims=True))
            probs = shifted * (1.0 / jnp.sum(shifted, axis=-1, keepdims=True))
            probs_b = probs.astype(BF16)
            attn_h = mm(probs_b, v_ref[...])
            dprob = mm(do_h, v_ref[...], NT)
            delta = jnp.sum(probs * dprob, axis=-1, keepdims=True)
            dscore = (probs * (dprob - delta) * scale).astype(BF16)
            dq_h = mm(dscore, k_ref[...])
            dk = mm(dscore, q_h, TN)
            dv = mm(probs_b, do_h, TN)
            if b == 0 and h == 0:
                dk_ref[...] = dk
                dv_ref[...] = dv
            else:
                dk_ref[...] += dk
                dv_ref[...] += dv
            attn = attn_h if attn is None else jnp.where(lane_head == h, attn_h, attn)
            dq = dq_h if dq is None else jnp.where(lane_head == h, dq_h, dq)
        attn_ref[at, :] = attn.astype(BF16)
        dqkv_ref[at, :group] = dq.astype(BF16)
    dqkv_ref[:, group : 2 * group] = dk_ref[...].astype(BF16)
    dqkv_ref[:, 2 * group :] = dv_ref[...].astype(BF16)


def dn_body(me_ref, dqkv_ref, w_ref, keep_ref, send_ref, dn_ref):
    dn_ref[...] = mm(dqkv_ref[...], w_ref[...], NT).astype(BF16)
    block = keep_ref.shape[1]
    core = me_ref[0] & 1
    for c in range(keep_ref.shape[0]):
        for ref, device in ((keep_ref, 2 * c + core), (send_ref, 2 * c + 1 - core)):
            ref[c] = dn_ref[pl.ds(pl.multiple_of(device * block, block), block), :]


def columns_body(n_space, me_ref, in_ref, *refs):
    out_refs, (cols_ref,) = refs[:n_space], refs[n_space:]
    cols = cols_ref.shape[2]
    for c in range(n_space):
        cols_ref[c] = in_ref[:, c * cols : (c + 1) * cols]
    for k in range(n_space):
        out_refs[k][...] = cols_ref[me_ref[1] ^ k]


def head_grads_body(n_space, *refs):
    normed_refs, (dqkv_ref, gqkv_ref, flag_ref) = refs[:n_space], refs[n_space:]
    flag_ref[...] = jnp.zeros(flag_ref.shape, F32)
    rows = normed_refs[0].shape[0]
    natural = mm(dqkv_ref[...], head_order(dqkv_ref.shape[1]), NT).astype(BF16)
    gqkv_ref[...] = sum(
        mm(ref[...], natural[b * rows : (b + 1) * rows, :], TN) for b, ref in enumerate(normed_refs)
    )


def dn_pair_body(me_ref, keep_ref, got_ref, *out_refs):
    for k, out_ref in enumerate(out_refs):
        slot = (me_ref[0] >> 1) ^ k
        out_ref[...] = (keep_ref[slot].astype(F32) + got_ref[slot].astype(F32)).astype(BF16)


def joined_body(n, *refs):
    ins = refs[:n]
    centred_ref, inv_ref, gain_ref, cot_ref, mixed_ref, agg_ref, packet_ref, dgain_ref = refs[n:]
    width = centred_ref.shape[1]
    d_normed = sum(ref[...].astype(F32) for ref in ins)
    centred = centred_ref[...]
    dgain_ref[...] = jnp.broadcast_to(jnp.sum(d_normed * centred, axis=0, keepdims=True), dgain_ref.shape)
    gained = d_normed * gain_ref[...]
    inner = (
        gained
        - jnp.mean(gained, axis=-1, keepdims=True)
        - centred * jnp.mean(gained * centred, axis=-1, keepdims=True)
    )
    d_joined = (cot_ref[...].astype(F32) + inner * inv_ref[:, :1]).astype(BF16)
    d_pooled = mm(d_joined, agg_ref[...], NT)
    center = pack(head_sums(d_pooled * mixed_ref[...], fold_matrix(width, width // HEADS)))
    packet_ref[:, :width] = d_joined
    packet_ref[:, width:] = center


def prepare_body(me_ref, pooled_ref, even_ref, odd_ref, agg_ref, djoined_ref, dpool_ref, stat_ref):
    width = agg_ref.shape[0]
    for k in range(even_ref.shape[0]):
        for odd, ref in ((0, even_ref), (1, odd_ref)):
            djoined_ref[pair_rows(me_ref[0], k, odd, even_ref.shape[1]), :] = ref[k]
    dpool_ref[...] = mm(djoined_ref[:, :width], agg_ref[...], NT)
    stat_ref[0] = unpack(djoined_ref[:, width:])
    stat_ref[1] = unpack(pooled_ref[:, width:])
    stat_ref[2] = 1.0 / unpack(pooled_ref[:, width:], 3)


def out_grad_body(me_ref, pooled_ref, djoined_ref, dgain_ref, attn_ref, cot_ref, keep_ref, send_ref, all_ref, cols_ref):
    width = dgain_ref.shape[1]
    all_ref[...] = mm(pooled_ref[:, :width], djoined_ref[:, :width], TN)
    weight_grad = mm(attn_ref[...], cot_ref[...], TN).astype(BF16)
    n_space, height, cols = cols_ref.shape
    block = height - 16 - weight_grad.shape[0]
    start = pl.multiple_of(me_ref[0] * block, block)
    own = all_ref[pl.ds(start, block), :].astype(BF16)
    extra = three_rows(dgain_ref[:1, :])
    for c in range(n_space):
        cols_ref[c, :block, :] = own[:, c * cols : (c + 1) * cols]
        cols_ref[c, block : block + 16, :] = extra[:, c * cols : (c + 1) * cols]
        cols_ref[c, block + 16 :, :] = weight_grad[:, c * cols : (c + 1) * cols]
    for k in range(n_space):
        (send_ref if k % 2 else keep_ref)[k // 2] = cols_ref[me_ref[1] ^ k]


def out_add_body(block, mine_ref, got_ref, *refs):
    for j, out_ref in enumerate(refs):
        total = mine_ref[j + 1].astype(F32) + got_ref[j + 1].astype(F32)
        out_ref[...] = total.astype(BF16)
        out_ref[block : block + 16, :] = three_rows(jnp.sum(total[block : block + 16, :], axis=0, keepdims=True))


def dvalue_body(dpool_ref, stat_ref, value_ref, scores_ref, dvalue_ref, dlogit_ref, spread_ref, fold_ref):
    width = dpool_ref.shape[1]
    size = width // HEADS

    @pl.when(pl.program_id(0) == 0)
    def _():
        spread_ref[...] = spread_matrix(width, size)
        fold_ref[...] = fold_matrix(width, size)

    weight = jnp.exp(scores_ref[0] - stat_ref[1]) * stat_ref[2]
    dvalue_ref[0] = (mm(pack(weight), spread_ref[...]) * dpool_ref[...]).astype(BF16)
    dweight = head_sums(dpool_ref[...] * value_ref[0], fold_ref[...])
    dlogit = weight * (dweight - stat_ref[0])
    hi = dlogit.astype(BF16)
    dlogit_ref[0, :, :LANES] = hi
    dlogit_ref[0, :, LANES:] = (dlogit - hi.astype(F32)).astype(BF16)


def embed_body(
    n_space, me_ref, dvalue_ref, dlogit_ref, patches_ref, wv_ref, wback_ref, keep_ref, send_ref, cols_ref, extra_ref
):
    v = pl.program_id(0)
    hi, lo = dlogit_ref[0, :, :LANES].astype(F32), dlogit_ref[0, :, LANES:].astype(F32)
    group = iota(hi.shape, 1) >> 4
    mixed = jnp.where(group < 2, hi, jnp.where(group == 2, lo, 0.0)).astype(BF16)
    d_tokens = (mm(dvalue_ref[0], wv_ref[...], NT) + mm(mixed, wback_ref[...], NT)).astype(BF16)
    grad = mm(patches_ref[0], d_tokens, TN).astype(BF16)
    hi, lo, _ = parts3(jnp.sum(d_tokens.astype(F32), axis=0, keepdims=True))
    row = iota(extra_ref.shape, 0)
    extra = jnp.where(row == 2 * v, hi, jnp.where(row == 2 * v + 1, lo, 0.0))

    @pl.when(v == 0)
    def _():
        extra_ref[...] = extra

    @pl.when(v > 0)
    def _():
        extra_ref[...] += extra

    cols = cols_ref.shape[2]
    pixels = patches_ref.shape[2]
    for c in range(n_space):
        cols_ref[c] = grad[:, c * cols : (c + 1) * cols]
    at = pl.ds(pl.multiple_of(v * pixels, pixels), pixels)
    for k in range(0, n_space, 2):
        keep_ref[k // 2, at, :] = cols_ref[me_ref[1] ^ k]
        send_ref[k // 2, at, :] = cols_ref[me_ref[1] ^ (k + 1)]

    @pl.when(v == pl.num_programs(0) - 1)
    def _():
        tail = slice(keep_ref.shape[1] - 16, keep_ref.shape[1])
        for c in range(n_space):
            cols_ref[c, :16, :] = extra_ref[:, c * cols : (c + 1) * cols].astype(BF16)
        for k in range(0, n_space, 2):
            keep_ref[k // 2, tail, :] = cols_ref[me_ref[1] ^ k, :16, :]
            send_ref[k // 2, tail, :] = cols_ref[me_ref[1] ^ (k + 1), :16, :]


def embed_final_body(parts, *refs):
    ins, (grad_ref, offset_ref) = refs[:-2], refs[-2:]
    pixels = grad_ref.shape[1]
    base = 0
    for chunk in range(len(ins) // parts):
        total = 0.0
        for ref in ins[chunk * parts : (chunk + 1) * parts]:
            total = total + (ref[0] if len(ref.shape) == 3 else ref[...]).astype(F32)
        count = (total.shape[0] - 16) // pixels
        for v in range(count):
            grad_ref[base + v] = total[v * pixels : (v + 1) * pixels, :]
            row = count * pixels + 2 * v
            offset_ref[base + v : base + v + 1, :] = total[row : row + 1, :] + total[row + 1 : row + 2, :]
        base += count


def stack_body(*refs):
    for k, ref in enumerate(refs[:-1]):
        refs[-1][k] = ref[...]


def value_grad_body(me_ref, *refs):
    tokens_refs, dv_refs, dl_refs, (keep_ref, send_ref, all_ref) = refs[:2], refs[2:4], refs[4:6], refs[6:]
    width = dv_refs[0].shape[2]
    total, both = 0.0, 0.0
    for tokens_ref, dv_ref, dl_ref in zip(tokens_refs, dv_refs, dl_refs):
        for v in range(dv_ref.shape[0]):
            total = total + mm(tokens_ref[v], dv_ref[v], TN)
            both = both + mm(tokens_ref[v], dl_ref[v], TN)
    all_ref[:, :width] = total.astype(BF16)
    all_ref[:, width:] = pack(both[:, :LANES] + both[:, LANES:])
    block = keep_ref.shape[1]
    count = all_ref.shape[0] // block
    for r in range(count):
        target = pl.program_id(0) * count + r
        same = (target & 1) == (me_ref[0] & 1)
        slot = target >> 1

        @pl.when(same)
        def _():
            keep_ref[slot] = all_ref[r * block : (r + 1) * block, :]

        @pl.when(jnp.logical_not(same))
        def _():
            send_ref[slot] = all_ref[r * block : (r + 1) * block, :]


def pair_sum_body(n_chip, me_ref, keep_ref, got_ref, *out_refs):
    width = keep_ref.shape[2] - LANES
    for k in range(n_chip):
        slot = (me_ref[0] >> 1) ^ k
        mine, other = keep_ref[slot], got_ref[slot]
        out_refs[k][:, :width] = (mine[:, :width].astype(F32) + other[:, :width].astype(F32)).astype(BF16)
        out_refs[k][:, width:] = pack(unpack(mine[:, width:]) + unpack(other[:, width:]))


def packet_split_body(n_in, n_space, me_ref, *refs):
    ins, out_refs, (cols_ref,) = refs[:n_in], refs[n_in:-1], refs[-1:]
    block, width = ins[0].shape[0], ins[0].shape[1] - LANES
    total = sum(ref[:, :width].astype(F32) for ref in ins).astype(BF16)
    factor = pack(sum(unpack(ref[:, width:]) for ref in ins))
    half = n_space // 2
    cols = cols_ref.shape[2] // 2
    for c in range(half):
        cols_ref[c] = total[:, 2 * c * cols : 2 * (c + 1) * cols]
    part = out_refs[0].shape[0] - 2 * block
    for k in range(n_space):
        for piece in range(block // part):
            lanes = slice(piece * LANES, (piece + 1) * LANES)
            out_refs[k][:part, lanes] = factor[piece * part : (piece + 1) * part, :]
        large = cols_ref[jnp.maximum((me_ref[1] ^ k) - half, 0)]
        out_refs[k][part : part + block, :] = large[:, :cols]
        out_refs[k][part + block :, :] = large[:, cols:]


def space_sum_body(n, *refs):
    ins, outs, (out_ref, weight_ref) = refs[:n], list(refs[n:-2]), refs[-2:]
    outs = [ref.at[0] if len(ref.shape) == 3 else ref for ref in outs]
    cols = ins[0].shape[1]
    width = out_ref.shape[1] - LANES - cols
    block = out_ref.shape[0] - 16
    part = ins[0].shape[0] - 2 * block
    for piece in range(2):
        at = slice(part + piece * block, part + (piece + 1) * block)
        out_ref[:block, piece * cols : (piece + 1) * cols] = sum(ref[at, :].astype(F32) for ref in ins).astype(BF16)
    for piece in range(block // part):
        lanes = slice(piece * LANES, (piece + 1) * LANES)
        factor = pack(sum(unpack(ref[:part, lanes]) for ref in ins))
        out_ref[piece * part : (piece + 1) * part, width : width + LANES] = factor
    out_ref[block:, : width + LANES] = jnp.zeros((16, width + LANES), BF16)
    total = sum(ref[...].astype(F32) for ref in outs)
    out_ref[:block, width + LANES :] = total[:block, :].astype(BF16)
    out_ref[block:, width + LANES :] = three_rows(jnp.sum(total[block : block + 16, :], axis=0, keepdims=True))
    weight_ref[...] = total[block + 16 :, :]


def add_body(n, keep_ref, got_ref, *refs):
    for j, out_ref in enumerate(refs):
        out_ref[...] = (keep_ref[j + 1].astype(F32) + got_ref[j + 1].astype(F32)).astype(BF16)


def final_body(n_var, n_space, scale, me_ref, even_ref, odd_ref, query_ref, wk_ref, kv_ref, gq_ref, out_ref, gain_ref):
    me_v, me_s = me_ref[0], me_ref[1]
    half = n_space // 2
    width = wk_ref.shape[1]
    size = width // HEADS
    cols, qcols = kv_ref.shape[1], gq_ref.shape[1]
    place = pl.multiple_of(jnp.minimum(me_s, half - 1) * cols, LANES)
    spread_kv = spread_matrix(cols, size, place)
    qplace = pl.multiple_of(me_s * qcols, LANES)
    spread_q = spread_matrix(qcols, size, qplace)
    query = query_ref[:, pl.ds(place, cols)] * scale
    block = even_ref.shape[1] - 16
    total, gain = 0.0, 0.0
    for k in range(n_var):
        part_ref, slot = (odd_ref if k % 2 else even_ref), k // 2
        at = pl.ds(pl.multiple_of((me_v ^ k) * block, block), block)
        packed = part_ref[slot, :block, cols : cols + LANES]
        key_grad = mm(packed, spread_kv) * query
        kv_ref[at, :] = jnp.where(me_s < half, key_grad, part_ref[slot, :block, :cols].astype(F32))
        keys = wk_ref[at, pl.ds(qplace, qcols)].astype(F32)
        total = total + jnp.sum(mm(packed, spread_q) * keys, axis=0, keepdims=True)
        out_ref[at, :] = part_ref[slot, :block, cols + LANES :].astype(F32)
        gain = gain + jnp.sum(part_ref[slot, block:, cols + LANES :].astype(F32), axis=0, keepdims=True)
    gq_ref[...] = total * scale
    gain_ref[...] = gain


def shards(
    patches, embed_weight, var_embed, agg_query, agg_kv, agg_out, norm_gain, qkv_weight, out_weight, cotangent
):
    n_var, n_space = lax.axis_size("var"), lax.axis_size("space")
    count, rows, pixels = patches.shape
    width = agg_out.shape[0]
    size = width // HEADS
    scale = 1.0 / math.sqrt(size)
    block = rows // n_var
    cols = width // n_space
    group = out_weight.shape[0]
    drows = width // n_var
    positions = rows * n_space
    kv_cols = 2 * width // n_space
    me = jnp.stack([lax.axis_index("var"), lax.axis_index("space")]).astype(jnp.int32)
    gain = norm_gain.reshape(1, width)
    query = agg_query.reshape(1, width)
    vmem = pl.BlockSpec(memory_space=pltpu.VMEM)
    packet = width + LANES

    whole = lambda shape: pl.BlockSpec(shape, lambda v: (0,) * len(shape))
    every = lambda shape: pl.BlockSpec((1,) + shape, lambda v: (v,) + (0,) * len(shape))
    n_chip = n_var // 2
    half = count // 2

    dattn, cot_own, w_heads = call(
        early_body,
        [struct((rows, group), BF16), struct((block, width), BF16), struct(qkv_weight.shape, BF16)],
        limit=LIMITS["early"],
        grid=(1,),
        in_specs=[SMEM] + [whole(x.shape) for x in (cotangent, out_weight, qkv_weight)],
        out_specs=[whole((rows, group)), whole((block, width)), whole(qkv_weight.shape)],
        cost_estimate=cost(2e8, 4e6),
        name="early",
    )(me, cotangent, out_weight, qkv_weight)
    dattn_all = gather_direct(dattn, "space")

    def forward_outs(here):
        return [struct((here, rows, width), BF16), struct((here, rows, width), F32), struct((here, rows, LANES), F32)]

    tokens0, value0, scores0, w_query, w_back, *state0 = call(
        functools.partial(first_body, scale),
        forward_outs(half)
        + [struct((width, 3 * LANES), BF16), struct((width, LANES), BF16)]
        + [struct((rows, width), F32), struct((rows, LANES), F32), struct((rows, LANES), F32)],
        limit=LIMITS["forward"],
        after=[dattn],
        cost_estimate=cost(6e9, 2e7),
        name="forward_first",
    )(patches, embed_weight, var_embed, query, agg_kv)
    tokens1, value1, scores1, keep, send = call(
        functools.partial(second_body, half),
        forward_outs(count - half) + [struct((n_chip, block, packet), F32)] * 2,
        limit=LIMITS["forward"],
        after=dattn_all[1:],
        in_specs=[SMEM] + [vmem] * 8,
        scratch_shapes=[pltpu.VMEM((rows, width), F32), pltpu.VMEM((rows, LANES), F32)],
        cost_estimate=cost(4e9, 1e7),
        name="forward_second",
    )(me, patches, embed_weight, var_embed, w_query, agg_kv, *state0)

    def pool_pairs(mine, got):
        return call(
            pool_pair_body,
            [struct((block, packet), F32)] * n_chip,
            limit=LIMITS["pool_pair"],
            in_specs=[SMEM, vmem, vmem],
            cost_estimate=cost(1e8, 3e6),
            name="pool_pair",
        )(me, mine, got)

    received = exchange_pairs(keep, send, pool_pairs)
    mixed, pooled_packet = call(
        functools.partial(pool_body, n_chip),
        [struct((block, width), F32), struct((block, packet), BF16)],
        limit=LIMITS["pool"],
        cost_estimate=cost(1e8, 2e6),
        name="pool",
    )(*received)
    pooled_even, pooled_odd = gather_pairs(pooled_packet, "var")

    qkv, normed, pooled_packets, centred, inv = call(
        norm_body,
        [
            struct((rows, 3 * group), BF16),
            struct((rows, width), BF16),
            struct((rows, packet), BF16),
            struct((block, width), F32),
            struct((block, LANES), F32),
        ],
        limit=LIMITS["norm"],
        in_specs=[SMEM] + [vmem] * 5,
        scratch_shapes=[pltpu.VMEM((rows, width), F32), pltpu.VMEM((rows, LANES), F32)],
        cost_estimate=cost(8e8, 5e6),
        name="norm",
    )(me, pooled_even, pooled_odd, agg_out, gain, w_heads)

    qkv_all = gather_direct(qkv, "space")
    normed_cols = call(
        functools.partial(columns_body, n_space),
        [struct((rows, cols), BF16)] * n_space,
        limit=LIMITS["columns"],
        after=qkv_all[1:],
        in_specs=[SMEM, vmem],
        scratch_shapes=[pltpu.VMEM((n_space, rows, cols), BF16)],
        cost_estimate=cost(1e6, 1e6),
        name="columns",
    )(me, normed)
    normed_all = exchange_direct(normed_cols, "space")
    attn, dqkv = call(
        functools.partial(attention_body, n_space, size, scale),
        [struct((positions, group), BF16), struct((positions, 3 * group), BF16)],
        limit=LIMITS["attention"],
        after=[normed_cols[0]],
        scratch_shapes=[pltpu.VMEM((positions, group), BF16)] * 2 + [pltpu.VMEM((positions, group), F32)] * 2,
        cost_estimate=cost(6e9, 4e6),
        name="attention",
    )(*qkv_all, *dattn_all)
    dn_keep, dn_send = call(
        dn_body,
        [struct((n_chip, block, width), BF16)] * 2,
        limit=LIMITS["dn"],
        after=normed_all[1:],
        grid=(1,),
        in_specs=[SMEM, pl.BlockSpec((rows, 3 * group), lambda i: (0, 0)), vmem],
        scratch_shapes=[pltpu.VMEM((rows, width), BF16)],
        cost_estimate=cost(2e8, 1e6),
        name="dn",
    )(me, dqkv, w_heads)

    def dn_pairs(mine, got):
        return call(
            dn_pair_body,
            [struct((block, width), BF16)] * n_chip,
            limit=LIMITS["dn_pair"],
            in_specs=[SMEM, vmem, vmem],
            cost_estimate=cost(1e6, 1e6),
            name="dn_pair",
        )(me, mine, got)

    dn_received = exchange_pairs(dn_keep, dn_send, dn_pairs)
    joined_packet, dgain = call(
        functools.partial(joined_body, n_chip),
        [struct((block, packet), BF16), struct((8, width), F32)],
        limit=LIMITS["joined"],
        cost_estimate=cost(2e8, 3e6),
        name="joined",
    )(*dn_received, centred, inv, gain, cot_own, mixed, agg_out)
    joined_even, joined_odd = gather_pairs(joined_packet, "var")

    d_joined, d_pooled, stat = call(
        prepare_body,
        [struct((rows, packet), BF16), struct((rows, width), F32), struct((3, rows, LANES), F32)],
        limit=LIMITS["prepare"],
        in_specs=[SMEM] + [vmem] * 4,
        cost_estimate=cost(6e8, 4e6),
        name="prepare",
    )(me, pooled_packets, joined_even, joined_odd, agg_out)
    height = drows + 16 + group
    out_keep, out_send = call(
        out_grad_body,
        [struct((n_space // 2, height, cols), BF16)] * 2,
        limit=LIMITS["out_grad"],
        grid=(1,),
        in_specs=[SMEM] + [whole(x.shape) for x in (pooled_packets, d_joined, dgain)] + [whole((rows, group)), whole((rows, width))],
        out_specs=[whole((n_space // 2, height, cols))] * 2,
        scratch_shapes=[pltpu.VMEM((width, width), F32), pltpu.VMEM((n_space, height, cols), BF16)],
        cost_estimate=cost(6e8, 3e6),
        name="out_grad",
    )(me, pooled_packets, d_joined, dgain, attn, cotangent)
    out_got = swap(out_send, "space", 1)

    def out_add(mine, got):
        return call(
            functools.partial(out_add_body, drows),
            [struct((height, cols), BF16)] * (mine.shape[0] - 1),
            cost_estimate=cost(1e6, 1e6),
            name="out_add",
        )(mine, got)

    later, bit = out_add(out_keep, out_got), 2
    out_later, out_parts = later, [out_keep, out_got]
    while bit < n_space:
        got = {j: swap(later[j], "space", bit) for j in range(0, len(later), 2)}
        out_parts.append(got[0])
        rest = list(range(1, len(later), 2))
        if rest:
            mine = jnp.stack([later[0]] + [later[j] for j in rest])
            later = out_add(mine, jnp.stack([later[0]] + [got[j + 1] for j in rest]))
        bit *= 2

    def d_values(value, scores, after):
        here = value.shape[0]
        return call(
            dvalue_body,
            [struct((here, rows, width), BF16), struct((here, rows, 2 * LANES), BF16)],
            limit=LIMITS["dvalue"],
            after=after,
            grid=(here,),
            in_specs=[whole((rows, width)), whole((3, rows, LANES)), every((rows, width)), every((rows, LANES))],
            out_specs=[every((rows, width)), every((rows, 2 * LANES))],
            scratch_shapes=[pltpu.VMEM((LANES, width), BF16), pltpu.VMEM((width, LANES), BF16)],
            cost_estimate=cost(2e9, 5e6),
            name="dvalue",
        )(d_pooled, stat, value, scores)

    def embed(start, d_value, d_logit, after):
        here = d_value.shape[0]
        at = lambda shape: pl.BlockSpec((1,) + shape, lambda v: (v + start,) + (0,) * len(shape))
        blocks = (n_space // 2, here * pixels + 16, cols)
        return call(
            functools.partial(embed_body, n_space),
            [struct(blocks, BF16)] * 2,
            limit=LIMITS["embed"],
            after=after,
            grid=(here,),
            in_specs=[
                SMEM,
                every((rows, width)),
                every((rows, 2 * LANES)),
                at((rows, pixels)),
                pl.BlockSpec((width, width), lambda v: (0, 1)),
                whole((width, LANES)),
            ],
            out_specs=[whole(blocks)] * 2,
            scratch_shapes=[pltpu.VMEM((n_space, pixels, cols), BF16), pltpu.VMEM((16, width), F32)],
            cost_estimate=cost(1.5e9, 4e6),
            name="embed",
        )(me, d_value, d_logit, patches, agg_kv, w_back)

    dv0, dl0 = d_values(value0, scores0, [out_keep])
    dv1, dl1 = d_values(value1, scores1, [])

    step = max(drows, 256)
    kv_keep, kv_send = call(
        value_grad_body,
        [struct((n_chip, drows, packet), BF16)] * 2,
        limit=LIMITS["value_grad"],
        after=out_later,
        grid=(width // step,),
        in_specs=[SMEM]
        + [pl.BlockSpec(x.shape[:2] + (step,), lambda i: (0, 0, i)) for x in (tokens0, tokens1)]
        + [whole(x.shape) for x in (dv0, dv1, dl0, dl1)],
        out_specs=[whole((n_chip, drows, packet))] * 2,
        scratch_shapes=[pltpu.VMEM((step, packet), BF16)],
        cost_estimate=cost(4e9, 1e7),
        name="value_grad",
    )(me, tokens0, tokens1, dv0, dv1, dl0, dl1)
    kv_got = swap(kv_send, "var", 1)

    def scatter_embed(keep, arrived, after):
        n = n_space // 2 - 1
        sums = call(
            functools.partial(add_body, n),
            [struct(keep.shape[1:], BF16)] * n,
            limit=LIMITS["add"],
            after=after,
            cost_estimate=cost(1e6, 1e6),
            name="add",
        )(keep, arrived)
        blocks = {2 * (j + 1): sums[j] for j in range(n)}
        mine, bit = [keep, arrived], 2
        while bit < n_space:
            got = {k ^ bit: swap(blocks[k], "space", bit) for k in blocks if k & bit and k % bit == 0}
            mine.append(got[0])
            for k in got:
                if k:
                    blocks[k] = (blocks[k].astype(F32) + got[k].astype(F32)).astype(BF16)
            bit *= 2
        return mine, list(sums)

    keep0, send0 = embed(0, dv0, dl0, [kv_keep])
    arrived0 = swap(send0, "space", 1)
    kv_blocks = call(
        functools.partial(pair_sum_body, n_chip),
        [struct((drows, packet), BF16)] * n_chip,
        limit=LIMITS["pair_sum"],
        after=[keep0],
        in_specs=[SMEM] + [vmem] * 2,
        cost_estimate=cost(1e6, 1e6),
        name="pair_sum",
    )(me, kv_keep, kv_got)
    kv_parts = [kv_blocks[0]] + [swap(kv_blocks[k], "var", 2 * k) for k in range(1, n_chip)]
    keep1, send1 = embed(half, dv1, dl1, [kv_blocks[0]] + out_parts[2:])
    arrived1 = swap(send1, "space", 1)
    part = drows * LANES // cols
    pieces = call(
        functools.partial(packet_split_body, n_chip, n_space),
        [struct((part + 2 * drows, cols), BF16)] * n_space,
        limit=LIMITS["packet_split"],
        in_specs=[SMEM] + [vmem] * n_chip,
        scratch_shapes=[pltpu.VMEM((n_space // 2, drows, kv_cols), BF16)],
        cost_estimate=cost(1e6, 1e6),
        name="packet_split",
    )(me, *kv_parts)
    pieces_all = exchange_direct(pieces, "space")
    mine0, sums0 = scatter_embed(keep0, arrived0, [pieces[0]])
    mine1, sums1 = scatter_embed(keep1, arrived1, sums0)
    grad_qkv, head_flag = call(
        functools.partial(head_grads_body, n_space),
        [struct((cols, 3 * group), F32), struct((8, LANES), F32)],
        limit=LIMITS["head_grads"],
        cost_estimate=cost(1e9, 3e6),
        name="head_grads",
    )(*normed_all, dqkv)
    first_slot = lambda x: pl.BlockSpec((1,) + x.shape[1:], lambda i: (0, 0, 0)) if x.ndim == 3 else whole(x.shape)
    kv_sum, grad_out = call(
        functools.partial(space_sum_body, n_space),
        [struct((drows + 16, kv_cols + LANES + cols), BF16), struct((group, cols), F32)],
        limit=LIMITS["space_sum"],
        after=sums1 + [head_flag],
        grid=(1,),
        in_specs=[first_slot(x) for x in list(pieces_all) + out_parts],
        cost_estimate=cost(1e6, 1e6),
        name="space_sum",
    )(*pieces_all, *out_parts)

    def stack(parts):
        return call(
            stack_body,
            struct((len(parts),) + parts[0].shape, BF16),
            after=mine0[2:] + mine1[2:],
            cost_estimate=cost(1e6, 1e6),
            name="stack",
        )(*parts)

    kv_even, kv_odd = gather_pairs(kv_sum, "var", stack)
    grad_agg_kv, grad_query, grad_agg_out, grad_gain = call(
        functools.partial(final_body, n_var, n_space, scale),
        [struct((width, kv_cols), F32), struct((1, cols), F32)] + [struct((width, cols), F32), struct((1, cols), F32)],
        grid=(1,),
        in_specs=[SMEM] + [vmem] * 3 + [pl.BlockSpec((width, width), lambda i: (0, 0))],
        limit=LIMITS["final"],
        cost_estimate=cost(2e8, 5e6),
        name="final",
    )(me, kv_even, kv_odd, query, agg_kv)

    def first_block(x):
        if x.ndim == 3:
            return pl.BlockSpec((1,) + x.shape[1:], lambda i: (0, 0, 0))
        return pl.BlockSpec(x.shape, lambda i: (0, 0))

    grad_embed, grad_var_embed = call(
        functools.partial(embed_final_body, len(mine0)),
        [struct((count, pixels, cols), F32), struct((count, cols), F32)],
        grid=(1,),
        in_specs=[first_block(x) for x in mine0 + mine1],
        limit=LIMITS["embed_final"],
        cost_estimate=cost(1e6, 1e6),
        name="embed_final",
    )(*mine0, *mine1)

    return (
        grad_embed,
        grad_var_embed,
        grad_query.reshape(cols),
        grad_agg_kv,
        grad_agg_out,
        grad_gain.reshape(cols),
        grad_qkv,
        grad_out,
    )


def solution(mesh):
    return jax.shard_map(
        shards,
        mesh=mesh,
        in_specs=(
            P("var", "space", None),
            P("var", None, None),
            P("var", None),
            P(),
            P(),
            P(),
            P(),
            P(None, "var"),
            P("var", None),
            P("space", None),
        ),
        out_specs=(
            P("var", None, "space"),
            P("var", "space"),
            P("space"),
            P(None, "space"),
            P(None, "space"),
            P("space"),
            P("space", "var"),
            P("var", "space"),
        ),
        check_vma=False,
    )
```

```python
import functools
import math

import jax
import jax.numpy as jnp
from jax import lax
from jax.experimental import pallas as pl
from jax.experimental.pallas import tpu as pltpu
from jax.sharding import PartitionSpec as P

HEADS = 16
LANES = 128
EPSILON = 1e-05
MIB = 1 << 20

LIMITS = {
    "early": 60, "forward": 24, "columns": 8, "pool_pair": 16, "pool": 16, "norm": 16, "attention": 24,
    "dn": 12, "dn_pair": 16, "joined": 16, "prepare": 16, "out_grad": 16, "dvalue": 24, "embed": 24, "value_grad": 32,
    "add": 12, "pair_sum": 16, "packet_split": 16, "space_sum": 16, "head_grads": 16, "final": 16, "embed_final": 24,
}

F32 = jnp.float32
BF16 = jnp.bfloat16

NN = (((1,), (0,)), ((), ()))
NT = (((1,), (1,)), ((), ()))
TN = (((0,), (0,)), ((), ()))


def mm(a, b, dims=NN):
    return lax.dot_general(a, b, dims, preferred_element_type=F32)


def iota(shape, axis):
    return lax.broadcasted_iota(jnp.int32, shape, axis)


def parts3(x):
    hi = x.astype(BF16).astype(F32)
    rest = x - hi
    mid = rest.astype(BF16).astype(F32)
    return hi, mid, rest - mid


def pack(x, y=None):
    group = iota(x.shape, 1) >> 4
    hi, mid, lo = parts3(x)
    out = jnp.where(group == 0, hi, jnp.where(group == 1, mid, jnp.where(group == 2, lo, 0.0)))
    if y is not None:
        hi, mid, lo = parts3(y)
        out = jnp.where(group == 3, hi, jnp.where(group == 4, mid, jnp.where(group == 5, lo, out)))
    return out.astype(BF16)


def unpack(packed, first_group=0):
    row, column = iota((LANES, LANES), 0), iota((LANES, LANES), 1)
    group = row >> 4
    take = ((row & 15) == (column & 15)) & (group >= first_group) & (group < first_group + 3)
    return mm(packed, jnp.where(take, 1.0, 0.0).astype(BF16))


def spread_matrix(width, size, first=0):
    row, column = iota((LANES, width), 0), iota((LANES, width), 1)
    shift = size.bit_length() - 1
    take = ((row & 15) == ((column + first) >> shift)) & (row < 48)
    return jnp.where(take, 1.0, 0.0).astype(BF16)


def fold_matrix(width, size):
    row, column = iota((width, LANES), 0), iota((width, LANES), 1)
    shift = size.bit_length() - 1
    return jnp.where((column & 15) == (row >> shift), 1.0, 0.0).astype(BF16)


def head_sums(x, fold):
    hi, mid, lo = parts3(x)
    return mm(hi.astype(BF16), fold) + mm(mid.astype(BF16), fold) + mm(lo.astype(BF16), fold)


def call(body, out_shape, limit=16, after=(), in_specs=None, **kw):
    def run(*args):
        n, m = len(args), len(after)
        vmem = pl.BlockSpec(memory_space=pltpu.VMEM)
        return pl.pallas_call(
            lambda *refs: body(*refs[:n], *refs[n + m :]),
            out_shape=out_shape,
            in_specs=([vmem] * n if in_specs is None else list(in_specs)) + [vmem] * m,
            compiler_params=pltpu.CompilerParams(vmem_limit_bytes=limit * MIB),
            **kw,
        )(*args, *after)

    return run


def struct(shape, dtype):
    return jax.ShapeDtypeStruct(shape, dtype)


def cost(flops, moved):
    return pl.CostEstimate(flops=int(flops), bytes_accessed=int(moved), transcendentals=0)


SMEM = pl.BlockSpec(memory_space=pltpu.SMEM)


def swap(x, axis, k, keep=None):
    pairs = [(i, i ^ k) for i in range(lax.axis_size(axis))]
    if keep is not None:
        pairs = [pair for pair in pairs if keep(pair[1])]
    return lax.ppermute(x, axis, pairs)


def gather_direct(x, axis):
    return [x] + [swap(x, axis, k) for k in range(1, lax.axis_size(axis))]


def exchange_direct(blocks, axis):
    return [blocks[0]] + [swap(blocks[k], axis, k) for k in range(1, len(blocks))]


def gather_pairs(x, axis, stack=jnp.stack):
    even = [x] + [swap(x, axis, k) for k in range(2, lax.axis_size(axis), 2)]
    even = stack(even)
    return even, swap(even, axis, 1)


def exchange_pairs(keep, send, combine):
    parts = combine(keep, swap(send, "var", 1))
    return [parts[0]] + [swap(parts[k], "var", 2 * k) for k in range(1, len(parts))]


def pair_rows(me_v, k, odd, block):
    device = (((me_v >> 1) ^ k) << 1) + ((me_v & 1) ^ odd)
    return pl.ds(pl.multiple_of(device * block, block), block)


def three_rows(x):
    hi, mid, lo = parts3(x)
    row = iota((16, x.shape[1]), 0)
    return jnp.where(row == 0, hi, jnp.where(row == 1, mid, jnp.where(row == 2, lo, 0.0))).astype(BF16)


def head_order(width, size=64):
    heads = width // (3 * size)
    row, column = iota((width, width), 0), iota((width, width), 1)
    take = jnp.zeros((width, width), jnp.bool_)
    for h in range(heads):
        for c in range(3):
            start, target = h * 3 * size + c * size, c * heads * size + h * size
            inside = (column >= target) & (column < target + size)
            take = take | (inside & ((row - start) == (column - target)))
    return jnp.where(take, 1.0, 0.0).astype(BF16)


def early_body(me_ref, cot_ref, outw_ref, qkvw_ref, dattn_ref, own_ref, wperm_ref):
    dattn_ref[...] = mm(cot_ref[...], outw_ref[...], NT).astype(BF16)
    block = own_ref.shape[0]
    own_ref[...] = cot_ref[pl.ds(pl.multiple_of(me_ref[0] * block, block), block), :]
    wperm_ref[...] = mm(qkvw_ref[...], head_order(qkvw_ref.shape[1])).astype(BF16)


def forward_part(start, patches_ref, embed_ref, offset_ref, wq, wv_ref, spread, outs, state):
    tokens_ref, value_ref, scores_ref = outs
    here = tokens_ref.shape[0]
    width = tokens_ref.shape[2]
    for v in range(here):
        u = start + v
        tokens = (mm(patches_ref[u], embed_ref[u]) + offset_ref[u : u + 1, :]).astype(BF16)
        tokens_ref[v] = tokens
        pieces = mm(tokens, wq)
        scores_ref[v] = pieces[:, :LANES] + pieces[:, LANES : 2 * LANES] + pieces[:, 2 * LANES :]
        value_ref[v] = mm(tokens, wv_ref[:, width:])
    top = functools.reduce(jnp.maximum, [scores_ref[v] for v in range(here)])
    total, acc = 0.0, 0.0
    if state is not None:
        top = jnp.maximum(top, state[0])
        old = jnp.exp(state[0] - top)
        total, acc = state[1] * old, state[2] * mm(pack(old), spread)
    for v in range(here):
        new = jnp.exp(scores_ref[v] - top)
        total = total + new
        acc = acc + value_ref[v] * mm(pack(new), spread)
    return top, total, acc


def first_body(
    scale, patches_ref, embed_ref, offset_ref, query_ref, kv_ref,
    tokens_ref, value_ref, scores_ref, wq_ref, wback_ref, acc_ref, max_ref, sum_ref,
):
    width = tokens_ref.shape[2]
    size = width // HEADS
    row, column = iota((LANES, width), 0), iota((LANES, width), 1)
    own = (row & 15) == (column >> (size.bit_length() - 1))
    wq = jnp.zeros((width, LANES), F32)
    for part in parts3(query_ref[...]):
        wq = wq + mm(kv_ref[:, :width], jnp.where(own, part, 0.0).astype(BF16), NT)
    hi, mid, lo = parts3(wq * scale)
    wq_ref[:, :LANES] = hi.astype(BF16)
    wq_ref[:, LANES : 2 * LANES] = mid.astype(BF16)
    wq_ref[:, 2 * LANES :] = lo.astype(BF16)
    group = iota((width, LANES), 1) >> 4
    back = jnp.where((group == 0) | (group == 2), hi, jnp.where(group == 1, mid, 0.0))
    wback_ref[...] = back.astype(BF16)
    max_ref[...], sum_ref[...], acc_ref[...] = forward_part(
        0, patches_ref, embed_ref, offset_ref, wq_ref[...], kv_ref, spread_matrix(width, size),
        (tokens_ref, value_ref, scores_ref), None,
    )


def second_body(
    start, me_ref, patches_ref, embed_ref, offset_ref, wq_ref, kv_ref, acc0_ref, max0_ref, sum0_ref,
    tokens_ref, value_ref, scores_ref, keep_ref, send_ref, acc_ref, max_ref,
):
    width = tokens_ref.shape[2]
    top, total, acc = forward_part(
        start, patches_ref, embed_ref, offset_ref, wq_ref[...], kv_ref, spread_matrix(width, width // HEADS),
        (tokens_ref, value_ref, scores_ref), (max0_ref[...], sum0_ref[...], acc0_ref[...]),
    )
    acc_ref[...] = acc
    max_ref[...] = jnp.where(iota(top.shape, 1) < LANES // 2, top, total)
    block = keep_ref.shape[1]
    core = me_ref[0] & 1
    for c in range(keep_ref.shape[0]):
        for ref, device in ((keep_ref, 2 * c + core), (send_ref, 2 * c + 1 - core)):
            at = pl.ds(pl.multiple_of(device * block, block), block)
            ref[c, :, :width] = acc_ref[at, :]
            ref[c, :, width:] = max_ref[at, :]


def halves_of(both):
    low = iota(both.shape, 1) < LANES // 2
    turned = pltpu.roll(both, LANES // 2, 1)
    return jnp.where(low, both, turned), jnp.where(low, turned, both)


def pool_pair_body(me_ref, keep_ref, got_ref, *out_refs):
    width = keep_ref.shape[2] - LANES
    spread = spread_matrix(width, width // HEADS)
    low = iota((keep_ref.shape[1], LANES), 1) < LANES // 2
    for k, out_ref in enumerate(out_refs):
        slot = (me_ref[0] >> 1) ^ k
        mine, other = keep_ref[slot], got_ref[slot]
        max_a, sum_a = halves_of(mine[:, width:])
        max_b, sum_b = halves_of(other[:, width:])
        top = jnp.maximum(max_a, max_b)
        factor_a, factor_b = jnp.exp(max_a - top), jnp.exp(max_b - top)
        out_ref[:, :width] = mine[:, :width] * mm(pack(factor_a), spread) + other[:, :width] * mm(pack(factor_b), spread)
        out_ref[:, width:] = jnp.where(low, top, sum_a * factor_a + sum_b * factor_b)


def pool_body(n, *refs):
    ins, (mixed_ref, packet_ref) = refs[:n], refs[n:]
    width = mixed_ref.shape[1]
    stats = [halves_of(ref[:, width:]) for ref in ins]
    top = functools.reduce(jnp.maximum, [m for m, _ in stats])
    factors = [jnp.exp(m - top) for m, _ in stats]
    total = sum(s * f for (_, s), f in zip(stats, factors))
    spread = spread_matrix(width, width // HEADS)
    mixed = jnp.zeros(mixed_ref.shape, F32)
    for ref, factor in zip(ins, factors):
        mixed = mixed + ref[:, :width] * mm(pack(factor / total), spread)
    mixed_ref[...] = mixed
    packet_ref[:, :width] = mixed.astype(BF16)
    packet_ref[:, width:] = pack(top, total)


def norm_body(
    me_ref, even_ref, odd_ref, agg_ref, gain_ref, w_ref, qkv_ref, normed_ref, packets_ref, centred_ref, inv_ref,
    all_ref, allinv_ref,
):
    width = agg_ref.shape[0]
    block = centred_ref.shape[0]
    for k in range(even_ref.shape[0]):
        for odd, ref in ((0, even_ref), (1, odd_ref)):
            packets_ref[pair_rows(me_ref[0], k, odd, block), :] = ref[k]
    joined = mm(packets_ref[:, :width], agg_ref[...]).astype(BF16).astype(F32)
    mean = jnp.mean(joined, axis=-1, keepdims=True)
    spread_sq = jnp.mean((joined - mean) ** 2, axis=-1, keepdims=True)
    inv = lax.rsqrt(spread_sq + EPSILON)
    centred = (joined - mean) * inv
    normed = (centred * gain_ref[...]).astype(BF16)
    qkv_ref[...] = mm(normed, w_ref[...]).astype(BF16)
    normed_ref[...] = normed
    all_ref[...] = centred
    allinv_ref[...] = jnp.broadcast_to(inv, allinv_ref.shape)
    start = pl.multiple_of(me_ref[0] * block, block)
    centred_ref[...] = all_ref[pl.ds(start, block), :]
    inv_ref[...] = allinv_ref[pl.ds(start, block), :]


def attention_body(n_space, size, scale, *refs):
    qkv_refs, dattn_refs = refs[:n_space], refs[n_space : 2 * n_space]
    attn_ref, dqkv_ref, k_ref, v_ref, dk_ref, dv_ref = refs[2 * n_space :]
    rows, group = dattn_refs[0].shape
    heads = group // size
    for b in range(n_space):
        at = slice(b * rows, (b + 1) * rows)
        k_ref[at, :] = qkv_refs[b][:, group : 2 * group]
        v_ref[at, :] = qkv_refs[b][:, 2 * group :]
    lane_head = iota((rows, group), 1) // size if heads > 1 else None
    for b in range(n_space):
        at = slice(b * rows, (b + 1) * rows)
        queries, d_out = qkv_refs[b][:, :group], dattn_refs[b][...]
        attn = dq = None
        for h in range(heads):
            if heads > 1:
                q_h = jnp.where(lane_head == h, queries.astype(F32), 0.0).astype(BF16)
                do_h = jnp.where(lane_head == h, d_out.astype(F32), 0.0).astype(BF16)
            else:
                q_h, do_h = queries, d_out
            logits = mm((q_h.astype(F32) * scale).astype(BF16), k_ref[...], NT)
            shifted = jnp.exp(logits - jnp.max(logits, axis=-1, keepdims=True))
            probs = shifted * (1.0 / jnp.sum(shifted, axis=-1, keepdims=True))
            probs_b = probs.astype(BF16)
            attn_h = mm(probs_b, v_ref[...])
            dprob = mm((do_h.astype(F32) * scale).astype(BF16), v_ref[...], NT)
            delta = jnp.sum(probs * dprob, axis=-1, keepdims=True)
            dscore = (probs * (dprob - delta)).astype(BF16)
            dq_h = mm(dscore, k_ref[...])
            dk = mm(dscore, q_h, TN)
            dv = mm(probs_b, do_h, TN)
            if b == 0 and h == 0:
                dk_ref[...] = dk
                dv_ref[...] = dv
            else:
                dk_ref[...] += dk
                dv_ref[...] += dv
            attn = attn_h if attn is None else jnp.where(lane_head == h, attn_h, attn)
            dq = dq_h if dq is None else jnp.where(lane_head == h, dq_h, dq)
        attn_ref[at, :] = attn.astype(BF16)
        dqkv_ref[at, :group] = dq.astype(BF16)
    dqkv_ref[:, group : 2 * group] = dk_ref[...].astype(BF16)
    dqkv_ref[:, 2 * group :] = dv_ref[...].astype(BF16)


def dn_body(me_ref, dqkv_ref, w_ref, keep_ref, send_ref, dn_ref):
    dn_ref[...] = mm(dqkv_ref[...], w_ref[...], NT).astype(BF16)
    block = keep_ref.shape[1]
    core = me_ref[0] & 1
    for c in range(keep_ref.shape[0]):
        for ref, device in ((keep_ref, 2 * c + core), (send_ref, 2 * c + 1 - core)):
            ref[c] = dn_ref[pl.ds(pl.multiple_of(device * block, block), block), :]


def columns_body(n_space, me_ref, in_ref, *refs):
    out_refs, (cols_ref,) = refs[:n_space], refs[n_space:]
    cols = cols_ref.shape[2]
    for c in range(n_space):
        cols_ref[c] = in_ref[:, c * cols : (c + 1) * cols]
    for k in range(n_space):
        out_refs[k][...] = cols_ref[me_ref[1] ^ k]


def head_grads_body(n_space, *refs):
    normed_refs, (dqkv_ref, gqkv_ref, flag_ref) = refs[:n_space], refs[n_space:]
    flag_ref[...] = jnp.zeros(flag_ref.shape, F32)
    rows = normed_refs[0].shape[0]
    natural = mm(dqkv_ref[...], head_order(dqkv_ref.shape[1]), NT).astype(BF16)
    gqkv_ref[...] = sum(
        mm(ref[...], natural[b * rows : (b + 1) * rows, :], TN) for b, ref in enumerate(normed_refs)
    )


def dn_pair_body(me_ref, keep_ref, got_ref, *out_refs):
    for k, out_ref in enumerate(out_refs):
        slot = (me_ref[0] >> 1) ^ k
        out_ref[...] = (keep_ref[slot].astype(F32) + got_ref[slot].astype(F32)).astype(BF16)


def joined_body(n, *refs):
    ins = refs[:n]
    centred_ref, inv_ref, gain_ref, cot_ref, mixed_ref, agg_ref, packet_ref, dgain_ref = refs[n:]
    width = centred_ref.shape[1]
    d_normed = sum(ref[...].astype(F32) for ref in ins)
    centred = centred_ref[...]
    dgain_ref[...] = jnp.broadcast_to(jnp.sum(d_normed * centred, axis=0, keepdims=True), dgain_ref.shape)
    gained = d_normed * gain_ref[...]
    inner = (
        gained
        - jnp.mean(gained, axis=-1, keepdims=True)
        - centred * jnp.mean(gained * centred, axis=-1, keepdims=True)
    )
    d_joined = (cot_ref[...].astype(F32) + inner * inv_ref[:, :1]).astype(BF16)
    d_pooled = mm(d_joined, agg_ref[...], NT)
    center = pack(head_sums(d_pooled * mixed_ref[...], fold_matrix(width, width // HEADS)))
    packet_ref[:, :width] = d_joined
    packet_ref[:, width:] = center


def prepare_body(me_ref, pooled_ref, even_ref, odd_ref, agg_ref, djoined_ref, dpool_ref, stat_ref):
    width = agg_ref.shape[0]
    for k in range(even_ref.shape[0]):
        for odd, ref in ((0, even_ref), (1, odd_ref)):
            djoined_ref[pair_rows(me_ref[0], k, odd, even_ref.shape[1]), :] = ref[k]
    dpool_ref[...] = mm(djoined_ref[:, :width], agg_ref[...], NT)
    stat_ref[0] = unpack(djoined_ref[:, width:])
    stat_ref[1] = unpack(pooled_ref[:, width:])
    stat_ref[2] = 1.0 / unpack(pooled_ref[:, width:], 3)


def out_grad_body(me_ref, pooled_ref, djoined_ref, dgain_ref, attn_ref, cot_ref, keep_ref, send_ref, all_ref, cols_ref):
    width = dgain_ref.shape[1]
    all_ref[...] = mm(pooled_ref[:, :width], djoined_ref[:, :width], TN)
    weight_grad = mm(attn_ref[...], cot_ref[...], TN).astype(BF16)
    n_space, height, cols = cols_ref.shape
    block = height - 16 - weight_grad.shape[0]
    start = pl.multiple_of(me_ref[0] * block, block)
    own = all_ref[pl.ds(start, block), :].astype(BF16)
    extra = three_rows(dgain_ref[:1, :])
    for c in range(n_space):
        cols_ref[c, :block, :] = own[:, c * cols : (c + 1) * cols]
        cols_ref[c, block : block + 16, :] = extra[:, c * cols : (c + 1) * cols]
        cols_ref[c, block + 16 :, :] = weight_grad[:, c * cols : (c + 1) * cols]
    for k in range(n_space):
        (send_ref if k % 2 else keep_ref)[k // 2] = cols_ref[me_ref[1] ^ k]


def out_add_body(block, mine_ref, got_ref, *refs):
    for j, out_ref in enumerate(refs):
        total = mine_ref[j + 1].astype(F32) + got_ref[j + 1].astype(F32)
        out_ref[...] = total.astype(BF16)
        out_ref[block : block + 16, :] = three_rows(jnp.sum(total[block : block + 16, :], axis=0, keepdims=True))


def dvalue_body(dpool_ref, stat_ref, value_ref, scores_ref, dvalue_ref, dlogit_ref, spread_ref, fold_ref):
    width = dpool_ref.shape[1]
    size = width // HEADS

    @pl.when(pl.program_id(0) == 0)
    def _():
        spread_ref[...] = spread_matrix(width, size)
        fold_ref[...] = fold_matrix(width, size)

    weight = jnp.exp(scores_ref[0] - stat_ref[1]) * stat_ref[2]
    dvalue_ref[0] = (mm(pack(weight), spread_ref[...]) * dpool_ref[...]).astype(BF16)
    dweight = head_sums(dpool_ref[...] * value_ref[0], fold_ref[...])
    dlogit = weight * (dweight - stat_ref[0])
    hi = dlogit.astype(BF16)
    dlogit_ref[0, :, :LANES] = hi
    dlogit_ref[0, :, LANES:] = (dlogit - hi.astype(F32)).astype(BF16)


def embed_body(
    n_space, me_ref, dvalue_ref, dlogit_ref, patches_ref, wv_ref, wback_ref, keep_ref, send_ref, cols_ref, extra_ref
):
    v = pl.program_id(0)
    hi, lo = dlogit_ref[0, :, :LANES].astype(F32), dlogit_ref[0, :, LANES:].astype(F32)
    group = iota(hi.shape, 1) >> 4
    mixed = jnp.where(group < 2, hi, jnp.where(group == 2, lo, 0.0)).astype(BF16)
    d_tokens = (mm(dvalue_ref[0], wv_ref[...], NT) + mm(mixed, wback_ref[...], NT)).astype(BF16)
    grad = mm(patches_ref[0], d_tokens, TN).astype(BF16)
    hi, lo, _ = parts3(jnp.sum(d_tokens.astype(F32), axis=0, keepdims=True))
    row = iota(extra_ref.shape, 0)
    extra = jnp.where(row == 2 * v, hi, jnp.where(row == 2 * v + 1, lo, 0.0))

    @pl.when(v == 0)
    def _():
        extra_ref[...] = extra

    @pl.when(v > 0)
    def _():
        extra_ref[...] += extra

    cols = cols_ref.shape[2]
    pixels = patches_ref.shape[2]
    for c in range(n_space):
        cols_ref[c] = grad[:, c * cols : (c + 1) * cols]
    at = pl.ds(pl.multiple_of(v * pixels, pixels), pixels)
    for k in range(0, n_space, 2):
        keep_ref[k // 2, at, :] = cols_ref[me_ref[1] ^ k]
        send_ref[k // 2, at, :] = cols_ref[me_ref[1] ^ (k + 1)]

    @pl.when(v == pl.num_programs(0) - 1)
    def _():
        tail = slice(keep_ref.shape[1] - 16, keep_ref.shape[1])
        for c in range(n_space):
            cols_ref[c, :16, :] = extra_ref[:, c * cols : (c + 1) * cols].astype(BF16)
        for k in range(0, n_space, 2):
            keep_ref[k // 2, tail, :] = cols_ref[me_ref[1] ^ k, :16, :]
            send_ref[k // 2, tail, :] = cols_ref[me_ref[1] ^ (k + 1), :16, :]


def embed_final_body(parts, *refs):
    ins, (grad_ref, offset_ref) = refs[:-2], refs[-2:]
    pixels = grad_ref.shape[1]
    base = 0
    for chunk in range(len(ins) // parts):
        total = 0.0
        for ref in ins[chunk * parts : (chunk + 1) * parts]:
            total = total + (ref[0] if len(ref.shape) == 3 else ref[...]).astype(F32)
        count = (total.shape[0] - 16) // pixels
        for v in range(count):
            grad_ref[base + v] = total[v * pixels : (v + 1) * pixels, :]
            row = count * pixels + 2 * v
            offset_ref[base + v : base + v + 1, :] = total[row : row + 1, :] + total[row + 1 : row + 2, :]
        base += count


def stack_body(*refs):
    for k, ref in enumerate(refs[:-1]):
        refs[-1][k] = ref[...]


def value_grad_body(me_ref, *refs):
    tokens_refs, dv_refs, dl_refs, (keep_ref, send_ref, all_ref) = refs[:2], refs[2:4], refs[4:6], refs[6:]
    width = dv_refs[0].shape[2]
    total, both = 0.0, 0.0
    for tokens_ref, dv_ref, dl_ref in zip(tokens_refs, dv_refs, dl_refs):
        for v in range(dv_ref.shape[0]):
            total = total + mm(tokens_ref[v], dv_ref[v], TN)
            both = both + mm(tokens_ref[v], dl_ref[v], TN)
    all_ref[:, :width] = total.astype(BF16)
    all_ref[:, width:] = pack(both[:, :LANES] + both[:, LANES:])
    block = keep_ref.shape[1]
    count = all_ref.shape[0] // block
    for r in range(count):
        target = pl.program_id(0) * count + r
        same = (target & 1) == (me_ref[0] & 1)
        slot = target >> 1

        @pl.when(same)
        def _():
            keep_ref[slot] = all_ref[r * block : (r + 1) * block, :]

        @pl.when(jnp.logical_not(same))
        def _():
            send_ref[slot] = all_ref[r * block : (r + 1) * block, :]


def pair_sum_body(n_chip, me_ref, keep_ref, got_ref, *out_refs):
    width = keep_ref.shape[2] - LANES
    for k in range(n_chip):
        slot = (me_ref[0] >> 1) ^ k
        mine, other = keep_ref[slot], got_ref[slot]
        out_refs[k][:, :width] = (mine[:, :width].astype(F32) + other[:, :width].astype(F32)).astype(BF16)
        out_refs[k][:, width:] = pack(unpack(mine[:, width:]) + unpack(other[:, width:]))


def packet_split_body(n_in, n_space, me_ref, *refs):
    ins, out_refs, (cols_ref,) = refs[:n_in], refs[n_in:-1], refs[-1:]
    block, width = ins[0].shape[0], ins[0].shape[1] - LANES
    total = sum(ref[:, :width].astype(F32) for ref in ins).astype(BF16)
    factor = pack(sum(unpack(ref[:, width:]) for ref in ins))
    half = n_space // 2
    cols = cols_ref.shape[2] // 2
    for c in range(half):
        cols_ref[c] = total[:, 2 * c * cols : 2 * (c + 1) * cols]
    part = out_refs[0].shape[0] - 2 * block
    for k in range(n_space):
        for piece in range(block // part):
            lanes = slice(piece * LANES, (piece + 1) * LANES)
            out_refs[k][:part, lanes] = factor[piece * part : (piece + 1) * part, :]
        large = cols_ref[jnp.maximum((me_ref[1] ^ k) - half, 0)]
        out_refs[k][part : part + block, :] = large[:, :cols]
        out_refs[k][part + block :, :] = large[:, cols:]


def space_sum_body(n, *refs):
    ins, outs, (out_ref, weight_ref) = refs[:n], list(refs[n:-2]), refs[-2:]
    outs = [ref.at[0] if len(ref.shape) == 3 else ref for ref in outs]
    cols = ins[0].shape[1]
    width = out_ref.shape[1] - LANES - cols
    block = out_ref.shape[0] - 16
    part = ins[0].shape[0] - 2 * block
    for piece in range(2):
        at = slice(part + piece * block, part + (piece + 1) * block)
        out_ref[:block, piece * cols : (piece + 1) * cols] = sum(ref[at, :].astype(F32) for ref in ins).astype(BF16)
    for piece in range(block // part):
        lanes = slice(piece * LANES, (piece + 1) * LANES)
        factor = pack(sum(unpack(ref[:part, lanes]) for ref in ins))
        out_ref[piece * part : (piece + 1) * part, width : width + LANES] = factor
    out_ref[block:, : width + LANES] = jnp.zeros((16, width + LANES), BF16)
    total = sum(ref[...].astype(F32) for ref in outs)
    out_ref[:block, width + LANES :] = total[:block, :].astype(BF16)
    out_ref[block:, width + LANES :] = three_rows(jnp.sum(total[block : block + 16, :], axis=0, keepdims=True))
    weight_ref[...] = total[block + 16 :, :]


def add_body(n, keep_ref, got_ref, *refs):
    for j, out_ref in enumerate(refs):
        out_ref[...] = (keep_ref[j + 1].astype(F32) + got_ref[j + 1].astype(F32)).astype(BF16)


def final_body(n_var, n_space, scale, me_ref, even_ref, odd_ref, query_ref, wk_ref, kv_ref, gq_ref, out_ref, gain_ref):
    me_v, me_s = me_ref[0], me_ref[1]
    half = n_space // 2
    width = wk_ref.shape[1]
    size = width // HEADS
    cols, qcols = kv_ref.shape[1], gq_ref.shape[1]
    place = pl.multiple_of(jnp.minimum(me_s, half - 1) * cols, LANES)
    spread_kv = spread_matrix(cols, size, place)
    qplace = pl.multiple_of(me_s * qcols, LANES)
    spread_q = spread_matrix(qcols, size, qplace)
    query = query_ref[:, pl.ds(place, cols)] * scale
    block = even_ref.shape[1] - 16
    total, gain = 0.0, 0.0
    for k in range(n_var):
        part_ref, slot = (odd_ref if k % 2 else even_ref), k // 2
        at = pl.ds(pl.multiple_of((me_v ^ k) * block, block), block)
        packed = part_ref[slot, :block, cols : cols + LANES]
        key_grad = mm(packed, spread_kv) * query
        kv_ref[at, :] = jnp.where(me_s < half, key_grad, part_ref[slot, :block, :cols].astype(F32))
        keys = wk_ref[at, pl.ds(qplace, qcols)].astype(F32)
        total = total + jnp.sum(mm(packed, spread_q) * keys, axis=0, keepdims=True)
        out_ref[at, :] = part_ref[slot, :block, cols + LANES :].astype(F32)
        gain = gain + jnp.sum(part_ref[slot, block:, cols + LANES :].astype(F32), axis=0, keepdims=True)
    gq_ref[...] = total * scale
    gain_ref[...] = gain


def shards(
    patches, embed_weight, var_embed, agg_query, agg_kv, agg_out, norm_gain, qkv_weight, out_weight, cotangent
):
    n_var, n_space = lax.axis_size("var"), lax.axis_size("space")
    count, rows, pixels = patches.shape
    width = agg_out.shape[0]
    size = width // HEADS
    scale = 1.0 / math.sqrt(size)
    block = rows // n_var
    cols = width // n_space
    group = out_weight.shape[0]
    drows = width // n_var
    positions = rows * n_space
    kv_cols = 2 * width // n_space
    me = jnp.stack([lax.axis_index("var"), lax.axis_index("space")]).astype(jnp.int32)
    gain = norm_gain.reshape(1, width)
    query = agg_query.reshape(1, width)
    vmem = pl.BlockSpec(memory_space=pltpu.VMEM)
    packet = width + LANES

    whole = lambda shape: pl.BlockSpec(shape, lambda v: (0,) * len(shape))
    every = lambda shape: pl.BlockSpec((1,) + shape, lambda v: (v,) + (0,) * len(shape))
    n_chip = n_var // 2
    half = count // 2

    dattn, cot_own, w_heads = call(
        early_body,
        [struct((rows, group), BF16), struct((block, width), BF16), struct(qkv_weight.shape, BF16)],
        limit=LIMITS["early"],
        grid=(1,),
        in_specs=[SMEM] + [whole(x.shape) for x in (cotangent, out_weight, qkv_weight)],
        out_specs=[whole((rows, group)), whole((block, width)), whole(qkv_weight.shape)],
        cost_estimate=cost(2e8, 4e6),
        name="early",
    )(me, cotangent, out_weight, qkv_weight)
    dattn_all = gather_direct(dattn, "space")

    def forward_outs(here):
        return [struct((here, rows, width), BF16), struct((here, rows, width), F32), struct((here, rows, LANES), F32)]

    tokens0, value0, scores0, w_query, w_back, *state0 = call(
        functools.partial(first_body, scale),
        forward_outs(half)
        + [struct((width, 3 * LANES), BF16), struct((width, LANES), BF16)]
        + [struct((rows, width), F32), struct((rows, LANES), F32), struct((rows, LANES), F32)],
        limit=LIMITS["forward"],
        cost_estimate=cost(6e9, 2e7),
        name="forward_first",
    )(patches, embed_weight, var_embed, query, agg_kv)
    tokens1, value1, scores1, keep, send = call(
        functools.partial(second_body, half),
        forward_outs(count - half) + [struct((n_chip, block, packet), F32)] * 2,
        limit=LIMITS["forward"],
        after=dattn_all[1:],
        in_specs=[SMEM] + [vmem] * 8,
        scratch_shapes=[pltpu.VMEM((rows, width), F32), pltpu.VMEM((rows, LANES), F32)],
        cost_estimate=cost(4e9, 1e7),
        name="forward_second",
    )(me, patches, embed_weight, var_embed, w_query, agg_kv, *state0)

    def pool_pairs(mine, got):
        return call(
            pool_pair_body,
            [struct((block, packet), F32)] * n_chip,
            limit=LIMITS["pool_pair"],
            in_specs=[SMEM, vmem, vmem],
            cost_estimate=cost(1e8, 3e6),
            name="pool_pair",
        )(me, mine, got)

    received = exchange_pairs(keep, send, pool_pairs)
    mixed, pooled_packet = call(
        functools.partial(pool_body, n_chip),
        [struct((block, width), F32), struct((block, packet), BF16)],
        limit=LIMITS["pool"],
        cost_estimate=cost(1e8, 2e6),
        name="pool",
    )(*received)
    pooled_even, pooled_odd = gather_pairs(pooled_packet, "var")

    qkv, normed, pooled_packets, centred, inv = call(
        norm_body,
        [
            struct((rows, 3 * group), BF16),
            struct((rows, width), BF16),
            struct((rows, packet), BF16),
            struct((block, width), F32),
            struct((block, LANES), F32),
        ],
        limit=LIMITS["norm"],
        in_specs=[SMEM] + [vmem] * 5,
        scratch_shapes=[pltpu.VMEM((rows, width), F32), pltpu.VMEM((rows, LANES), F32)],
        cost_estimate=cost(8e8, 5e6),
        name="norm",
    )(me, pooled_even, pooled_odd, agg_out, gain, w_heads)

    qkv_all = gather_direct(qkv, "space")
    normed_cols = call(
        functools.partial(columns_body, n_space),
        [struct((rows, cols), BF16)] * n_space,
        limit=LIMITS["columns"],
        after=qkv_all[1:],
        in_specs=[SMEM, vmem],
        scratch_shapes=[pltpu.VMEM((n_space, rows, cols), BF16)],
        cost_estimate=cost(1e6, 1e6),
        name="columns",
    )(me, normed)
    normed_all = exchange_direct(normed_cols, "space")
    attn, dqkv = call(
        functools.partial(attention_body, n_space, size, scale),
        [struct((positions, group), BF16), struct((positions, 3 * group), BF16)],
        limit=LIMITS["attention"],
        after=[normed_cols[0]],
        scratch_shapes=[pltpu.VMEM((positions, group), BF16)] * 2 + [pltpu.VMEM((positions, group), F32)] * 2,
        cost_estimate=cost(6e9, 4e6),
        name="attention",
    )(*qkv_all, *dattn_all)
    dn_keep, dn_send = call(
        dn_body,
        [struct((n_chip, block, width), BF16)] * 2,
        limit=LIMITS["dn"],
        after=normed_all[1:],
        grid=(1,),
        in_specs=[SMEM, pl.BlockSpec((rows, 3 * group), lambda i: (0, 0)), vmem],
        scratch_shapes=[pltpu.VMEM((rows, width), BF16)],
        cost_estimate=cost(2e8, 1e6),
        name="dn",
    )(me, dqkv, w_heads)

    def dn_pairs(mine, got):
        return call(
            dn_pair_body,
            [struct((block, width), BF16)] * n_chip,
            limit=LIMITS["dn_pair"],
            in_specs=[SMEM, vmem, vmem],
            cost_estimate=cost(1e6, 1e6),
            name="dn_pair",
        )(me, mine, got)

    dn_received = exchange_pairs(dn_keep, dn_send, dn_pairs)
    joined_packet, dgain = call(
        functools.partial(joined_body, n_chip),
        [struct((block, packet), BF16), struct((8, width), F32)],
        limit=LIMITS["joined"],
        cost_estimate=cost(2e8, 3e6),
        name="joined",
    )(*dn_received, centred, inv, gain, cot_own, mixed, agg_out)
    joined_even, joined_odd = gather_pairs(joined_packet, "var")

    d_joined, d_pooled, stat = call(
        prepare_body,
        [struct((rows, packet), BF16), struct((rows, width), F32), struct((3, rows, LANES), F32)],
        limit=LIMITS["prepare"],
        in_specs=[SMEM] + [vmem] * 4,
        cost_estimate=cost(6e8, 4e6),
        name="prepare",
    )(me, pooled_packets, joined_even, joined_odd, agg_out)
    height = drows + 16 + group
    out_keep, out_send = call(
        out_grad_body,
        [struct((n_space // 2, height, cols), BF16)] * 2,
        limit=LIMITS["out_grad"],
        grid=(1,),
        in_specs=[SMEM] + [whole(x.shape) for x in (pooled_packets, d_joined, dgain)] + [whole((rows, group)), whole((rows, width))],
        out_specs=[whole((n_space // 2, height, cols))] * 2,
        scratch_shapes=[pltpu.VMEM((width, width), F32), pltpu.VMEM((n_space, height, cols), BF16)],
        cost_estimate=cost(6e8, 3e6),
        name="out_grad",
    )(me, pooled_packets, d_joined, dgain, attn, cotangent)
    out_got = swap(out_send, "space", 1)

    def out_add(mine, got):
        return call(
            functools.partial(out_add_body, drows),
            [struct((height, cols), BF16)] * (mine.shape[0] - 1),
            cost_estimate=cost(1e6, 1e6),
            name="out_add",
        )(mine, got)

    later, bit = out_add(out_keep, out_got), 2
    out_later, out_parts = later, [out_keep, out_got]
    while bit < n_space:
        got = {j: swap(later[j], "space", bit) for j in range(0, len(later), 2)}
        out_parts.append(got[0])
        rest = list(range(1, len(later), 2))
        if rest:
            mine = jnp.stack([later[0]] + [later[j] for j in rest])
            later = out_add(mine, jnp.stack([later[0]] + [got[j + 1] for j in rest]))
        bit *= 2

    def d_values(value, scores, after):
        here = value.shape[0]
        return call(
            dvalue_body,
            [struct((here, rows, width), BF16), struct((here, rows, 2 * LANES), BF16)],
            limit=LIMITS["dvalue"],
            after=after,
            grid=(here,),
            in_specs=[whole((rows, width)), whole((3, rows, LANES)), every((rows, width)), every((rows, LANES))],
            out_specs=[every((rows, width)), every((rows, 2 * LANES))],
            scratch_shapes=[pltpu.VMEM((LANES, width), BF16), pltpu.VMEM((width, LANES), BF16)],
            cost_estimate=cost(2e9, 5e6),
            name="dvalue",
        )(d_pooled, stat, value, scores)

    def embed(start, d_value, d_logit, after):
        here = d_value.shape[0]
        at = lambda shape: pl.BlockSpec((1,) + shape, lambda v: (v + start,) + (0,) * len(shape))
        blocks = (n_space // 2, here * pixels + 16, cols)
        return call(
            functools.partial(embed_body, n_space),
            [struct(blocks, BF16)] * 2,
            limit=LIMITS["embed"],
            after=after,
            grid=(here,),
            in_specs=[
                SMEM,
                every((rows, width)),
                every((rows, 2 * LANES)),
                at((rows, pixels)),
                pl.BlockSpec((width, width), lambda v: (0, 1)),
                whole((width, LANES)),
            ],
            out_specs=[whole(blocks)] * 2,
            scratch_shapes=[pltpu.VMEM((n_space, pixels, cols), BF16), pltpu.VMEM((16, width), F32)],
            cost_estimate=cost(1.5e9, 4e6),
            name="embed",
        )(me, d_value, d_logit, patches, agg_kv, w_back)

    dv0, dl0 = d_values(value0, scores0, [out_keep])
    dv1, dl1 = d_values(value1, scores1, [])

    step = max(drows, 256)
    kv_keep, kv_send = call(
        value_grad_body,
        [struct((n_chip, drows, packet), BF16)] * 2,
        limit=LIMITS["value_grad"],
        after=out_later,
        grid=(width // step,),
        in_specs=[SMEM]
        + [pl.BlockSpec(x.shape[:2] + (step,), lambda i: (0, 0, i)) for x in (tokens0, tokens1)]
        + [whole(x.shape) for x in (dv0, dv1, dl0, dl1)],
        out_specs=[whole((n_chip, drows, packet))] * 2,
        scratch_shapes=[pltpu.VMEM((step, packet), BF16)],
        cost_estimate=cost(4e9, 1e7),
        name="value_grad",
    )(me, tokens0, tokens1, dv0, dv1, dl0, dl1)
    kv_got = swap(kv_send, "var", 1)

    def scatter_embed(keep, arrived, after):
        n = n_space // 2 - 1
        sums = call(
            functools.partial(add_body, n),
            [struct(keep.shape[1:], BF16)] * n,
            limit=LIMITS["add"],
            after=after,
            cost_estimate=cost(1e6, 1e6),
            name="add",
        )(keep, arrived)
        blocks = {2 * (j + 1): sums[j] for j in range(n)}
        mine, bit = [keep, arrived], 2
        while bit < n_space:
            got = {k ^ bit: swap(blocks[k], "space", bit) for k in blocks if k & bit and k % bit == 0}
            mine.append(got[0])
            for k in got:
                if k:
                    blocks[k] = (blocks[k].astype(F32) + got[k].astype(F32)).astype(BF16)
            bit *= 2
        return mine, list(sums)

    keep0, send0 = embed(0, dv0, dl0, [kv_keep])
    arrived0 = swap(send0, "space", 1)
    kv_blocks = call(
        functools.partial(pair_sum_body, n_chip),
        [struct((drows, packet), BF16)] * n_chip,
        limit=LIMITS["pair_sum"],
        after=[keep0],
        in_specs=[SMEM] + [vmem] * 2,
        cost_estimate=cost(1e6, 1e6),
        name="pair_sum",
    )(me, kv_keep, kv_got)
    kv_parts = [kv_blocks[0]] + [swap(kv_blocks[k], "var", 2 * k) for k in range(1, n_chip)]
    keep1, send1 = embed(half, dv1, dl1, [kv_blocks[0]] + out_parts[2:])
    arrived1 = swap(send1, "space", 1)
    part = drows * LANES // cols
    pieces = call(
        functools.partial(packet_split_body, n_chip, n_space),
        [struct((part + 2 * drows, cols), BF16)] * n_space,
        limit=LIMITS["packet_split"],
        in_specs=[SMEM] + [vmem] * n_chip,
        scratch_shapes=[pltpu.VMEM((n_space // 2, drows, kv_cols), BF16)],
        cost_estimate=cost(1e6, 1e6),
        name="packet_split",
    )(me, *kv_parts)
    pieces_all = exchange_direct(pieces, "space")
    mine0, sums0 = scatter_embed(keep0, arrived0, [pieces[0]])
    mine1, sums1 = scatter_embed(keep1, arrived1, sums0)
    grad_qkv, head_flag = call(
        functools.partial(head_grads_body, n_space),
        [struct((cols, 3 * group), F32), struct((8, LANES), F32)],
        limit=LIMITS["head_grads"],
        cost_estimate=cost(1e9, 3e6),
        name="head_grads",
    )(*normed_all, dqkv)
    first_slot = lambda x: pl.BlockSpec((1,) + x.shape[1:], lambda i: (0, 0, 0)) if x.ndim == 3 else whole(x.shape)
    kv_sum, grad_out = call(
        functools.partial(space_sum_body, n_space),
        [struct((drows + 16, kv_cols + LANES + cols), BF16), struct((group, cols), F32)],
        limit=LIMITS["space_sum"],
        after=sums1 + [head_flag],
        grid=(1,),
        in_specs=[first_slot(x) for x in list(pieces_all) + out_parts],
        cost_estimate=cost(1e6, 1e6),
        name="space_sum",
    )(*pieces_all, *out_parts)

    def stack(parts):
        return call(
            stack_body,
            struct((len(parts),) + parts[0].shape, BF16),
            after=mine0[2:] + mine1[2:],
            cost_estimate=cost(1e6, 1e6),
            name="stack",
        )(*parts)

    kv_even, kv_odd = gather_pairs(kv_sum, "var", stack)
    grad_agg_kv, grad_query, grad_agg_out, grad_gain = call(
        functools.partial(final_body, n_var, n_space, scale),
        [struct((width, kv_cols), F32), struct((1, cols), F32)] + [struct((width, cols), F32), struct((1, cols), F32)],
        grid=(1,),
        in_specs=[SMEM] + [vmem] * 3 + [pl.BlockSpec((width, width), lambda i: (0, 0))],
        limit=LIMITS["final"],
        cost_estimate=cost(2e8, 5e6),
        name="final",
    )(me, kv_even, kv_odd, query, agg_kv)

    def first_block(x):
        if x.ndim == 3:
            return pl.BlockSpec((1,) + x.shape[1:], lambda i: (0, 0, 0))
        return pl.BlockSpec(x.shape, lambda i: (0, 0))

    grad_embed, grad_var_embed = call(
        functools.partial(embed_final_body, len(mine0)),
        [struct((count, pixels, cols), F32), struct((count, cols), F32)],
        grid=(1,),
        in_specs=[first_block(x) for x in mine0 + mine1],
        limit=LIMITS["embed_final"],
        cost_estimate=cost(1e6, 1e6),
        name="embed_final",
    )(*mine0, *mine1)

    return (
        grad_embed,
        grad_var_embed,
        grad_query.reshape(cols),
        grad_agg_kv,
        grad_agg_out,
        grad_gain.reshape(cols),
        grad_qkv,
        grad_out,
    )


def solution(mesh):
    return jax.shard_map(
        shards,
        mesh=mesh,
        in_specs=(
            P("var", "space", None),
            P("var", None, None),
            P("var", None),
            P(),
            P(),
            P(),
            P(),
            P(None, "var"),
            P("var", None),
            P("space", None),
        ),
        out_specs=(
            P("var", None, "space"),
            P("var", "space"),
            P("space"),
            P(None, "space"),
            P(None, "space"),
            P("space"),
            P("space", "var"),
            P("var", "space"),
        ),
        check_vma=False,
    )
```

```python
import functools
import math

import jax
import jax.numpy as jnp
from jax import lax
from jax.experimental import pallas as pl
from jax.experimental.pallas import tpu as pltpu
from jax.sharding import PartitionSpec as P

HEADS = 16
LANES = 128
EPSILON = 1e-05
MIB = 1 << 20

LIMITS = {
    "early": 60, "forward": 24, "columns": 8, "pool_pair": 16, "pool": 16, "norm": 16, "attention": 24,
    "dn": 12, "dn_pair": 16, "joined": 16, "prepare": 16, "out_grad": 16, "dvalue": 24, "embed": 24, "value_grad": 32,
    "add": 12, "pair_sum": 16, "packet_split": 16, "space_sum": 16, "head_grads": 16, "final": 16, "embed_final": 24,
}

F32 = jnp.float32
BF16 = jnp.bfloat16

NN = (((1,), (0,)), ((), ()))
NT = (((1,), (1,)), ((), ()))
TN = (((0,), (0,)), ((), ()))


def mm(a, b, dims=NN):
    return lax.dot_general(a, b, dims, preferred_element_type=F32)


def iota(shape, axis):
    return lax.broadcasted_iota(jnp.int32, shape, axis)


def parts3(x):
    hi = x.astype(BF16).astype(F32)
    rest = x - hi
    mid = rest.astype(BF16).astype(F32)
    return hi, mid, rest - mid


def pack(x, y=None):
    group = iota(x.shape, 1) >> 4
    hi, mid, lo = parts3(x)
    out = jnp.where(group == 0, hi, jnp.where(group == 1, mid, jnp.where(group == 2, lo, 0.0)))
    if y is not None:
        hi, mid, lo = parts3(y)
        out = jnp.where(group == 3, hi, jnp.where(group == 4, mid, jnp.where(group == 5, lo, out)))
    return out.astype(BF16)


def unpack(packed, first_group=0):
    row, column = iota((LANES, LANES), 0), iota((LANES, LANES), 1)
    group = row >> 4
    take = ((row & 15) == (column & 15)) & (group >= first_group) & (group < first_group + 3)
    return mm(packed, jnp.where(take, 1.0, 0.0).astype(BF16))


def spread_matrix(width, size, first=0):
    row, column = iota((LANES, width), 0), iota((LANES, width), 1)
    shift = size.bit_length() - 1
    take = ((row & 15) == ((column + first) >> shift)) & (row < 48)
    return jnp.where(take, 1.0, 0.0).astype(BF16)


def fold_matrix(width, size):
    row, column = iota((width, LANES), 0), iota((width, LANES), 1)
    shift = size.bit_length() - 1
    return jnp.where((column & 15) == (row >> shift), 1.0, 0.0).astype(BF16)


def head_sums(x, fold):
    hi, mid, lo = parts3(x)
    return mm(hi.astype(BF16), fold) + mm(mid.astype(BF16), fold) + mm(lo.astype(BF16), fold)


def call(body, out_shape, limit=16, after=(), in_specs=None, **kw):
    def run(*args):
        n, m = len(args), len(after)
        vmem = pl.BlockSpec(memory_space=pltpu.VMEM)
        return pl.pallas_call(
            lambda *refs: body(*refs[:n], *refs[n + m :]),
            out_shape=out_shape,
            in_specs=([vmem] * n if in_specs is None else list(in_specs)) + [vmem] * m,
            compiler_params=pltpu.CompilerParams(vmem_limit_bytes=limit * MIB),
            **kw,
        )(*args, *after)

    return run


def struct(shape, dtype):
    return jax.ShapeDtypeStruct(shape, dtype)


def cost(flops, moved):
    return pl.CostEstimate(flops=int(flops), bytes_accessed=int(moved), transcendentals=0)


SMEM = pl.BlockSpec(memory_space=pltpu.SMEM)


def swap(x, axis, k, keep=None):
    pairs = [(i, i ^ k) for i in range(lax.axis_size(axis))]
    if keep is not None:
        pairs = [pair for pair in pairs if keep(pair[1])]
    return lax.ppermute(x, axis, pairs)


def gather_direct(x, axis):
    return [x] + [swap(x, axis, k) for k in range(1, lax.axis_size(axis))]


def exchange_direct(blocks, axis):
    return [blocks[0]] + [swap(blocks[k], axis, k) for k in range(1, len(blocks))]


def gather_pairs(x, axis, stack=jnp.stack):
    even = [x] + [swap(x, axis, k) for k in range(2, lax.axis_size(axis), 2)]
    even = stack(even)
    return even, swap(even, axis, 1)


def exchange_pairs(keep, send, combine):
    parts = combine(keep, swap(send, "var", 1))
    return [parts[0]] + [swap(parts[k], "var", 2 * k) for k in range(1, len(parts))]


def pair_rows(me_v, k, odd, block):
    device = (((me_v >> 1) ^ k) << 1) + ((me_v & 1) ^ odd)
    return pl.ds(pl.multiple_of(device * block, block), block)


def three_rows(x):
    hi, mid, lo = parts3(x)
    row = iota((16, x.shape[1]), 0)
    return jnp.where(row == 0, hi, jnp.where(row == 1, mid, jnp.where(row == 2, lo, 0.0))).astype(BF16)


def head_order(width, size=64):
    heads = width // (3 * size)
    row, column = iota((width, width), 0), iota((width, width), 1)
    take = jnp.zeros((width, width), jnp.bool_)
    for h in range(heads):
        for c in range(3):
            start, target = h * 3 * size + c * size, c * heads * size + h * size
            inside = (column >= target) & (column < target + size)
            take = take | (inside & ((row - start) == (column - target)))
    return jnp.where(take, 1.0, 0.0).astype(BF16)


def early_body(me_ref, cot_ref, outw_ref, qkvw_ref, dattn_ref, own_ref, wperm_ref):
    dattn_ref[...] = mm(cot_ref[...], outw_ref[...], NT).astype(BF16)
    block = own_ref.shape[0]
    own_ref[...] = cot_ref[pl.ds(pl.multiple_of(me_ref[0] * block, block), block), :]
    wperm_ref[...] = mm(qkvw_ref[...], head_order(qkvw_ref.shape[1])).astype(BF16)


def forward_part(start, patches_ref, embed_ref, offset_ref, wq, wv_ref, spread, outs, state):
    tokens_ref, value_ref, scores_ref = outs
    here = tokens_ref.shape[0]
    width = tokens_ref.shape[2]
    for v in range(here):
        u = start + v
        tokens = (mm(patches_ref[u], embed_ref[u]) + offset_ref[u : u + 1, :]).astype(BF16)
        tokens_ref[v] = tokens
        pieces = mm(tokens, wq)
        scores_ref[v] = pieces[:, :LANES] + pieces[:, LANES : 2 * LANES] + pieces[:, 2 * LANES :]
        value_ref[v] = mm(tokens, wv_ref[:, width:])
    top = functools.reduce(jnp.maximum, [scores_ref[v] for v in range(here)])
    total, acc = 0.0, 0.0
    if state is not None:
        top = jnp.maximum(top, state[0])
        old = jnp.exp(state[0] - top)
        total, acc = state[1] * old, state[2] * mm(pack(old), spread)
    for v in range(here):
        new = jnp.exp(scores_ref[v] - top)
        total = total + new
        acc = acc + value_ref[v] * mm(pack(new), spread)
    return top, total, acc


def first_body(
    scale, patches_ref, embed_ref, offset_ref, query_ref, kv_ref,
    tokens_ref, value_ref, scores_ref, wq_ref, wback_ref, acc_ref, max_ref, sum_ref,
):
    width = tokens_ref.shape[2]
    size = width // HEADS
    row, column = iota((LANES, width), 0), iota((LANES, width), 1)
    own = (row & 15) == (column >> (size.bit_length() - 1))
    wq = jnp.zeros((width, LANES), F32)
    for part in parts3(query_ref[...]):
        wq = wq + mm(kv_ref[:, :width], jnp.where(own, part, 0.0).astype(BF16), NT)
    hi, mid, lo = parts3(wq * scale)
    wq_ref[:, :LANES] = hi.astype(BF16)
    wq_ref[:, LANES : 2 * LANES] = mid.astype(BF16)
    wq_ref[:, 2 * LANES :] = lo.astype(BF16)
    group = iota((width, LANES), 1) >> 4
    back = jnp.where((group == 0) | (group == 2), hi, jnp.where(group == 1, mid, 0.0))
    wback_ref[...] = back.astype(BF16)
    max_ref[...], sum_ref[...], acc_ref[...] = forward_part(
        0, patches_ref, embed_ref, offset_ref, wq_ref[...], kv_ref, spread_matrix(width, size),
        (tokens_ref, value_ref, scores_ref), None,
    )


def second_body(
    start, me_ref, patches_ref, embed_ref, offset_ref, wq_ref, kv_ref, acc0_ref, max0_ref, sum0_ref,
    tokens_ref, value_ref, scores_ref, keep_ref, send_ref, acc_ref, max_ref,
):
    width = tokens_ref.shape[2]
    top, total, acc = forward_part(
        start, patches_ref, embed_ref, offset_ref, wq_ref[...], kv_ref, spread_matrix(width, width // HEADS),
        (tokens_ref, value_ref, scores_ref), (max0_ref[...], sum0_ref[...], acc0_ref[...]),
    )
    acc_ref[...] = acc
    max_ref[...] = jnp.where(iota(top.shape, 1) < LANES // 2, top, total)
    block = keep_ref.shape[1]
    core = me_ref[0] & 1
    for c in range(keep_ref.shape[0]):
        for ref, device in ((keep_ref, 2 * c + core), (send_ref, 2 * c + 1 - core)):
            at = pl.ds(pl.multiple_of(device * block, block), block)
            ref[c, :, :width] = acc_ref[at, :]
            ref[c, :, width:] = max_ref[at, :]


def halves_of(both):
    low = iota(both.shape, 1) < LANES // 2
    turned = pltpu.roll(both, LANES // 2, 1)
    return jnp.where(low, both, turned), jnp.where(low, turned, both)


def pool_pair_body(me_ref, keep_ref, got_ref, *out_refs):
    width = keep_ref.shape[2] - LANES
    spread = spread_matrix(width, width // HEADS)
    low = iota((keep_ref.shape[1], LANES), 1) < LANES // 2
    for k, out_ref in enumerate(out_refs):
        slot = (me_ref[0] >> 1) ^ k
        mine, other = keep_ref[slot], got_ref[slot]
        max_a, sum_a = halves_of(mine[:, width:])
        max_b, sum_b = halves_of(other[:, width:])
        top = jnp.maximum(max_a, max_b)
        factor_a, factor_b = jnp.exp(max_a - top), jnp.exp(max_b - top)
        out_ref[:, :width] = mine[:, :width] * mm(pack(factor_a), spread) + other[:, :width] * mm(pack(factor_b), spread)
        out_ref[:, width:] = jnp.where(low, top, sum_a * factor_a + sum_b * factor_b)


def pool_body(n, *refs):
    ins, (mixed_ref, packet_ref) = refs[:n], refs[n:]
    width = mixed_ref.shape[1]
    stats = [halves_of(ref[:, width:]) for ref in ins]
    top = functools.reduce(jnp.maximum, [m for m, _ in stats])
    factors = [jnp.exp(m - top) for m, _ in stats]
    total = sum(s * f for (_, s), f in zip(stats, factors))
    spread = spread_matrix(width, width // HEADS)
    mixed = jnp.zeros(mixed_ref.shape, F32)
    for ref, factor in zip(ins, factors):
        mixed = mixed + ref[:, :width] * mm(pack(factor / total), spread)
    mixed_ref[...] = mixed
    packet_ref[:, :width] = mixed.astype(BF16)
    packet_ref[:, width:] = pack(top, total)


def norm_body(
    me_ref, even_ref, odd_ref, agg_ref, gain_ref, w_ref, qkv_ref, normed_ref, packets_ref, centred_ref, inv_ref,
    all_ref, allinv_ref,
):
    width = agg_ref.shape[0]
    block = centred_ref.shape[0]
    for k in range(even_ref.shape[0]):
        for odd, ref in ((0, even_ref), (1, odd_ref)):
            packets_ref[pair_rows(me_ref[0], k, odd, block), :] = ref[k]
    joined = mm(packets_ref[:, :width], agg_ref[...]).astype(BF16).astype(F32)
    mean = jnp.mean(joined, axis=-1, keepdims=True)
    spread_sq = jnp.mean((joined - mean) ** 2, axis=-1, keepdims=True)
    inv = lax.rsqrt(spread_sq + EPSILON)
    centred = (joined - mean) * inv
    normed = (centred * gain_ref[...]).astype(BF16)
    qkv_ref[...] = mm(normed, w_ref[...]).astype(BF16)
    normed_ref[...] = normed
    all_ref[...] = centred
    allinv_ref[...] = jnp.broadcast_to(inv, allinv_ref.shape)
    start = pl.multiple_of(me_ref[0] * block, block)
    centred_ref[...] = all_ref[pl.ds(start, block), :]
    inv_ref[...] = allinv_ref[pl.ds(start, block), :]


def attention_body(n_space, size, scale, *refs):
    qkv_refs, dattn_refs = refs[:n_space], refs[n_space : 2 * n_space]
    attn_ref, dqkv_ref, q_ref, k_ref, v_ref, do_ref, dk_ref, dv_ref = refs[2 * n_space :]
    rows, group = dattn_refs[0].shape
    heads = group // size
    for b in range(n_space):
        at = slice(b * rows, (b + 1) * rows)
        q_ref[at, :] = qkv_refs[b][:, :group]
        k_ref[at, :] = qkv_refs[b][:, group : 2 * group]
        v_ref[at, :] = qkv_refs[b][:, 2 * group :]
        do_ref[at, :] = dattn_refs[b][...]
    dk_ref[...] = jnp.zeros(dk_ref.shape, F32)
    dv_ref[...] = jnp.zeros(dv_ref.shape, F32)

    def step(b, carry):
        at = pl.ds(pl.multiple_of(b * rows, rows), rows)
        queries, d_out = q_ref[at, :], do_ref[at, :]
        lane_head = iota((rows, group), 1) // size if heads > 1 else None
        attn = dq = None
        for h in range(heads):
            if heads > 1:
                q_h = jnp.where(lane_head == h, queries.astype(F32), 0.0).astype(BF16)
                do_h = jnp.where(lane_head == h, d_out.astype(F32), 0.0).astype(BF16)
            else:
                q_h, do_h = queries, d_out
            logits = mm((q_h.astype(F32) * scale).astype(BF16), k_ref[...], NT)
            shifted = jnp.exp(logits - jnp.max(logits, axis=-1, keepdims=True))
            probs = shifted * (1.0 / jnp.sum(shifted, axis=-1, keepdims=True))
            probs_b = probs.astype(BF16)
            attn_h = mm(probs_b, v_ref[...])
            dprob = mm((do_h.astype(F32) * scale).astype(BF16), v_ref[...], NT)
            delta = jnp.sum(probs * dprob, axis=-1, keepdims=True)
            dscore = (probs * (dprob - delta)).astype(BF16)
            dq_h = mm(dscore, k_ref[...])
            dk_ref[...] += mm(dscore, q_h, TN)
            dv_ref[...] += mm(probs_b, do_h, TN)
            attn = attn_h if attn is None else jnp.where(lane_head == h, attn_h, attn)
            dq = dq_h if dq is None else jnp.where(lane_head == h, dq_h, dq)
        attn_ref[at, :] = attn.astype(BF16)
        dqkv_ref[at, :group] = dq.astype(BF16)
        return carry

    lax.fori_loop(0, n_space, step, 0, unroll=2)
    dqkv_ref[:, group : 2 * group] = dk_ref[...].astype(BF16)
    dqkv_ref[:, 2 * group :] = dv_ref[...].astype(BF16)


def dn_body(me_ref, dqkv_ref, w_ref, keep_ref, send_ref, dn_ref):
    dn_ref[...] = mm(dqkv_ref[...], w_ref[...], NT).astype(BF16)
    block = keep_ref.shape[1]
    core = me_ref[0] & 1
    for c in range(keep_ref.shape[0]):
        for ref, device in ((keep_ref, 2 * c + core), (send_ref, 2 * c + 1 - core)):
            ref[c] = dn_ref[pl.ds(pl.multiple_of(device * block, block), block), :]


def columns_body(n_space, me_ref, in_ref, *refs):
    out_refs, (cols_ref,) = refs[:n_space], refs[n_space:]
    cols = cols_ref.shape[2]
    for c in range(n_space):
        cols_ref[c] = in_ref[:, c * cols : (c + 1) * cols]
    for k in range(n_space):
        out_refs[k][...] = cols_ref[me_ref[1] ^ k]


def head_grads_body(n_space, *refs):
    normed_refs, (dqkv_ref, gqkv_ref, flag_ref) = refs[:n_space], refs[n_space:]
    flag_ref[...] = jnp.zeros(flag_ref.shape, F32)
    rows = normed_refs[0].shape[0]
    natural = mm(dqkv_ref[...], head_order(dqkv_ref.shape[1]), NT).astype(BF16)
    gqkv_ref[...] = sum(
        mm(ref[...], natural[b * rows : (b + 1) * rows, :], TN) for b, ref in enumerate(normed_refs)
    )


def dn_pair_body(me_ref, keep_ref, got_ref, *out_refs):
    for k, out_ref in enumerate(out_refs):
        slot = (me_ref[0] >> 1) ^ k
        out_ref[...] = (keep_ref[slot].astype(F32) + got_ref[slot].astype(F32)).astype(BF16)


def joined_body(n, *refs):
    ins = refs[:n]
    centred_ref, inv_ref, gain_ref, cot_ref, mixed_ref, agg_ref, packet_ref, dgain_ref = refs[n:]
    width = centred_ref.shape[1]
    d_normed = sum(ref[...].astype(F32) for ref in ins)
    centred = centred_ref[...]
    dgain_ref[...] = jnp.broadcast_to(jnp.sum(d_normed * centred, axis=0, keepdims=True), dgain_ref.shape)
    gained = d_normed * gain_ref[...]
    inner = (
        gained
        - jnp.mean(gained, axis=-1, keepdims=True)
        - centred * jnp.mean(gained * centred, axis=-1, keepdims=True)
    )
    d_joined = (cot_ref[...].astype(F32) + inner * inv_ref[:, :1]).astype(BF16)
    d_pooled = mm(d_joined, agg_ref[...], NT)
    center = pack(head_sums(d_pooled * mixed_ref[...], fold_matrix(width, width // HEADS)))
    packet_ref[:, :width] = d_joined
    packet_ref[:, width:] = center


def prepare_body(me_ref, pooled_ref, even_ref, odd_ref, agg_ref, djoined_ref, dpool_ref, stat_ref):
    width = agg_ref.shape[0]
    for k in range(even_ref.shape[0]):
        for odd, ref in ((0, even_ref), (1, odd_ref)):
            djoined_ref[pair_rows(me_ref[0], k, odd, even_ref.shape[1]), :] = ref[k]
    dpool_ref[...] = mm(djoined_ref[:, :width], agg_ref[...], NT)
    stat_ref[0] = unpack(djoined_ref[:, width:])
    stat_ref[1] = unpack(pooled_ref[:, width:])
    stat_ref[2] = 1.0 / unpack(pooled_ref[:, width:], 3)


def out_grad_body(me_ref, pooled_ref, djoined_ref, dgain_ref, attn_ref, cot_ref, keep_ref, send_ref, all_ref, cols_ref):
    width = dgain_ref.shape[1]
    all_ref[...] = mm(pooled_ref[:, :width], djoined_ref[:, :width], TN)
    weight_grad = mm(attn_ref[...], cot_ref[...], TN).astype(BF16)
    n_space, height, cols = cols_ref.shape
    block = height - 16 - weight_grad.shape[0]
    start = pl.multiple_of(me_ref[0] * block, block)
    own = all_ref[pl.ds(start, block), :].astype(BF16)
    extra = three_rows(dgain_ref[:1, :])
    for c in range(n_space):
        cols_ref[c, :block, :] = own[:, c * cols : (c + 1) * cols]
        cols_ref[c, block : block + 16, :] = extra[:, c * cols : (c + 1) * cols]
        cols_ref[c, block + 16 :, :] = weight_grad[:, c * cols : (c + 1) * cols]
    for k in range(n_space):
        (send_ref if k % 2 else keep_ref)[k // 2] = cols_ref[me_ref[1] ^ k]


def out_add_body(block, mine_ref, got_ref, *refs):
    for j, out_ref in enumerate(refs):
        total = mine_ref[j + 1].astype(F32) + got_ref[j + 1].astype(F32)
        out_ref[...] = total.astype(BF16)
        out_ref[block : block + 16, :] = three_rows(jnp.sum(total[block : block + 16, :], axis=0, keepdims=True))


def dvalue_body(dpool_ref, stat_ref, value_ref, scores_ref, dvalue_ref, dlogit_ref, spread_ref, fold_ref):
    width = dpool_ref.shape[1]
    size = width // HEADS

    @pl.when(pl.program_id(0) == 0)
    def _():
        spread_ref[...] = spread_matrix(width, size)
        fold_ref[...] = fold_matrix(width, size)

    weight = jnp.exp(scores_ref[0] - stat_ref[1]) * stat_ref[2]
    dvalue_ref[0] = (mm(pack(weight), spread_ref[...]) * dpool_ref[...]).astype(BF16)
    dweight = head_sums(dpool_ref[...] * value_ref[0], fold_ref[...])
    dlogit = weight * (dweight - stat_ref[0])
    hi = dlogit.astype(BF16)
    dlogit_ref[0, :, :LANES] = hi
    dlogit_ref[0, :, LANES:] = (dlogit - hi.astype(F32)).astype(BF16)


def embed_body(
    n_space, me_ref, dvalue_ref, dlogit_ref, patches_ref, wv_ref, wback_ref, keep_ref, send_ref, cols_ref, extra_ref
):
    v = pl.program_id(0)
    hi, lo = dlogit_ref[0, :, :LANES].astype(F32), dlogit_ref[0, :, LANES:].astype(F32)
    group = iota(hi.shape, 1) >> 4
    mixed = jnp.where(group < 2, hi, jnp.where(group == 2, lo, 0.0)).astype(BF16)
    d_tokens = (mm(dvalue_ref[0], wv_ref[...], NT) + mm(mixed, wback_ref[...], NT)).astype(BF16)
    grad = mm(patches_ref[0], d_tokens, TN).astype(BF16)
    hi, lo, _ = parts3(jnp.sum(d_tokens.astype(F32), axis=0, keepdims=True))
    row = iota(extra_ref.shape, 0)
    extra = jnp.where(row == 2 * v, hi, jnp.where(row == 2 * v + 1, lo, 0.0))

    @pl.when(v == 0)
    def _():
        extra_ref[...] = extra

    @pl.when(v > 0)
    def _():
        extra_ref[...] += extra

    cols = cols_ref.shape[2]
    pixels = patches_ref.shape[2]
    for c in range(n_space):
        cols_ref[c] = grad[:, c * cols : (c + 1) * cols]
    at = pl.ds(pl.multiple_of(v * pixels, pixels), pixels)
    for k in range(0, n_space, 2):
        keep_ref[k // 2, at, :] = cols_ref[me_ref[1] ^ k]
        send_ref[k // 2, at, :] = cols_ref[me_ref[1] ^ (k + 1)]

    @pl.when(v == pl.num_programs(0) - 1)
    def _():
        tail = slice(keep_ref.shape[1] - 16, keep_ref.shape[1])
        for c in range(n_space):
            cols_ref[c, :16, :] = extra_ref[:, c * cols : (c + 1) * cols].astype(BF16)
        for k in range(0, n_space, 2):
            keep_ref[k // 2, tail, :] = cols_ref[me_ref[1] ^ k, :16, :]
            send_ref[k // 2, tail, :] = cols_ref[me_ref[1] ^ (k + 1), :16, :]


def embed_final_body(parts, *refs):
    ins, (grad_ref, offset_ref) = refs[:-2], refs[-2:]
    pixels = grad_ref.shape[1]
    base = 0
    for chunk in range(len(ins) // parts):
        total = 0.0
        for ref in ins[chunk * parts : (chunk + 1) * parts]:
            total = total + (ref[0] if len(ref.shape) == 3 else ref[...]).astype(F32)
        count = (total.shape[0] - 16) // pixels
        for v in range(count):
            grad_ref[base + v] = total[v * pixels : (v + 1) * pixels, :]
            row = count * pixels + 2 * v
            offset_ref[base + v : base + v + 1, :] = total[row : row + 1, :] + total[row + 1 : row + 2, :]
        base += count


def stack_body(*refs):
    for k, ref in enumerate(refs[:-1]):
        refs[-1][k] = ref[...]


def value_grad_body(me_ref, *refs):
    tokens_refs, dv_refs, dl_refs, (keep_ref, send_ref, all_ref) = refs[:2], refs[2:4], refs[4:6], refs[6:]
    width = dv_refs[0].shape[2]
    total, both = 0.0, 0.0
    for tokens_ref, dv_ref, dl_ref in zip(tokens_refs, dv_refs, dl_refs):
        for v in range(dv_ref.shape[0]):
            total = total + mm(tokens_ref[v], dv_ref[v], TN)
            both = both + mm(tokens_ref[v], dl_ref[v], TN)
    all_ref[:, :width] = total.astype(BF16)
    all_ref[:, width:] = pack(both[:, :LANES] + both[:, LANES:])
    block = keep_ref.shape[1]
    count = all_ref.shape[0] // block
    for r in range(count):
        target = pl.program_id(0) * count + r
        same = (target & 1) == (me_ref[0] & 1)
        slot = target >> 1

        @pl.when(same)
        def _():
            keep_ref[slot] = all_ref[r * block : (r + 1) * block, :]

        @pl.when(jnp.logical_not(same))
        def _():
            send_ref[slot] = all_ref[r * block : (r + 1) * block, :]


def pair_sum_body(n_chip, me_ref, keep_ref, got_ref, *out_refs):
    width = keep_ref.shape[2] - LANES
    for k in range(n_chip):
        slot = (me_ref[0] >> 1) ^ k
        mine, other = keep_ref[slot], got_ref[slot]
        out_refs[k][:, :width] = (mine[:, :width].astype(F32) + other[:, :width].astype(F32)).astype(BF16)
        out_refs[k][:, width:] = pack(unpack(mine[:, width:]) + unpack(other[:, width:]))


def packet_split_body(n_in, n_space, me_ref, *refs):
    ins, out_refs, (cols_ref,) = refs[:n_in], refs[n_in:-1], refs[-1:]
    block, width = ins[0].shape[0], ins[0].shape[1] - LANES
    total = sum(ref[:, :width].astype(F32) for ref in ins).astype(BF16)
    factor = pack(sum(unpack(ref[:, width:]) for ref in ins))
    half = n_space // 2
    cols = cols_ref.shape[2] // 2
    for c in range(half):
        cols_ref[c] = total[:, 2 * c * cols : 2 * (c + 1) * cols]
    part = out_refs[0].shape[0] - 2 * block
    for k in range(n_space):
        for piece in range(block // part):
            lanes = slice(piece * LANES, (piece + 1) * LANES)
            out_refs[k][:part, lanes] = factor[piece * part : (piece + 1) * part, :]
        large = cols_ref[jnp.maximum((me_ref[1] ^ k) - half, 0)]
        out_refs[k][part : part + block, :] = large[:, :cols]
        out_refs[k][part + block :, :] = large[:, cols:]


def space_sum_body(n, *refs):
    ins, outs, (out_ref, weight_ref) = refs[:n], list(refs[n:-2]), refs[-2:]
    outs = [ref.at[0] if len(ref.shape) == 3 else ref for ref in outs]
    cols = ins[0].shape[1]
    width = out_ref.shape[1] - LANES - cols
    block = out_ref.shape[0] - 16
    part = ins[0].shape[0] - 2 * block
    for piece in range(2):
        at = slice(part + piece * block, part + (piece + 1) * block)
        out_ref[:block, piece * cols : (piece + 1) * cols] = sum(ref[at, :].astype(F32) for ref in ins).astype(BF16)
    for piece in range(block // part):
        lanes = slice(piece * LANES, (piece + 1) * LANES)
        factor = pack(sum(unpack(ref[:part, lanes]) for ref in ins))
        out_ref[piece * part : (piece + 1) * part, width : width + LANES] = factor
    out_ref[block:, : width + LANES] = jnp.zeros((16, width + LANES), BF16)
    total = sum(ref[...].astype(F32) for ref in outs)
    out_ref[:block, width + LANES :] = total[:block, :].astype(BF16)
    out_ref[block:, width + LANES :] = three_rows(jnp.sum(total[block : block + 16, :], axis=0, keepdims=True))
    weight_ref[...] = total[block + 16 :, :]


def add_body(n, keep_ref, got_ref, *refs):
    for j, out_ref in enumerate(refs):
        out_ref[...] = (keep_ref[j + 1].astype(F32) + got_ref[j + 1].astype(F32)).astype(BF16)


def final_body(n_var, n_space, scale, me_ref, even_ref, odd_ref, query_ref, wk_ref, kv_ref, gq_ref, out_ref, gain_ref):
    me_v, me_s = me_ref[0], me_ref[1]
    half = n_space // 2
    width = wk_ref.shape[1]
    size = width // HEADS
    cols, qcols = kv_ref.shape[1], gq_ref.shape[1]
    place = pl.multiple_of(jnp.minimum(me_s, half - 1) * cols, LANES)
    spread_kv = spread_matrix(cols, size, place)
    qplace = pl.multiple_of(me_s * qcols, LANES)
    spread_q = spread_matrix(qcols, size, qplace)
    query = query_ref[:, pl.ds(place, cols)] * scale
    block = even_ref.shape[1] - 16
    total, gain = 0.0, 0.0
    for k in range(n_var):
        part_ref, slot = (odd_ref if k % 2 else even_ref), k // 2
        at = pl.ds(pl.multiple_of((me_v ^ k) * block, block), block)
        packed = part_ref[slot, :block, cols : cols + LANES]
        key_grad = mm(packed, spread_kv) * query
        kv_ref[at, :] = jnp.where(me_s < half, key_grad, part_ref[slot, :block, :cols].astype(F32))
        keys = wk_ref[at, pl.ds(qplace, qcols)].astype(F32)
        total = total + jnp.sum(mm(packed, spread_q) * keys, axis=0, keepdims=True)
        out_ref[at, :] = part_ref[slot, :block, cols + LANES :].astype(F32)
        gain = gain + jnp.sum(part_ref[slot, block:, cols + LANES :].astype(F32), axis=0, keepdims=True)
    gq_ref[...] = total * scale
    gain_ref[...] = gain


def shards(
    patches, embed_weight, var_embed, agg_query, agg_kv, agg_out, norm_gain, qkv_weight, out_weight, cotangent
):
    n_var, n_space = lax.axis_size("var"), lax.axis_size("space")
    count, rows, pixels = patches.shape
    width = agg_out.shape[0]
    size = width // HEADS
    scale = 1.0 / math.sqrt(size)
    block = rows // n_var
    cols = width // n_space
    group = out_weight.shape[0]
    drows = width // n_var
    positions = rows * n_space
    kv_cols = 2 * width // n_space
    me = jnp.stack([lax.axis_index("var"), lax.axis_index("space")]).astype(jnp.int32)
    gain = norm_gain.reshape(1, width)
    query = agg_query.reshape(1, width)
    vmem = pl.BlockSpec(memory_space=pltpu.VMEM)
    packet = width + LANES

    whole = lambda shape: pl.BlockSpec(shape, lambda v: (0,) * len(shape))
    every = lambda shape: pl.BlockSpec((1,) + shape, lambda v: (v,) + (0,) * len(shape))
    n_chip = n_var // 2
    half = count // 2

    dattn, cot_own, w_heads = call(
        early_body,
        [struct((rows, group), BF16), struct((block, width), BF16), struct(qkv_weight.shape, BF16)],
        limit=LIMITS["early"],
        grid=(1,),
        in_specs=[SMEM] + [whole(x.shape) for x in (cotangent, out_weight, qkv_weight)],
        out_specs=[whole((rows, group)), whole((block, width)), whole(qkv_weight.shape)],
        cost_estimate=cost(2e8, 4e6),
        name="early",
    )(me, cotangent, out_weight, qkv_weight)
    dattn_all = gather_direct(dattn, "space")

    def forward_outs(here):
        return [struct((here, rows, width), BF16), struct((here, rows, width), F32), struct((here, rows, LANES), F32)]

    tokens0, value0, scores0, w_query, w_back, *state0 = call(
        functools.partial(first_body, scale),
        forward_outs(half)
        + [struct((width, 3 * LANES), BF16), struct((width, LANES), BF16)]
        + [struct((rows, width), F32), struct((rows, LANES), F32), struct((rows, LANES), F32)],
        limit=LIMITS["forward"],
        cost_estimate=cost(6e9, 2e7),
        name="forward_first",
    )(patches, embed_weight, var_embed, query, agg_kv)
    tokens1, value1, scores1, keep, send = call(
        functools.partial(second_body, half),
        forward_outs(count - half) + [struct((n_chip, block, packet), F32)] * 2,
        limit=LIMITS["forward"],
        after=dattn_all[1:],
        in_specs=[SMEM] + [vmem] * 8,
        scratch_shapes=[pltpu.VMEM((rows, width), F32), pltpu.VMEM((rows, LANES), F32)],
        cost_estimate=cost(4e9, 1e7),
        name="forward_second",
    )(me, patches, embed_weight, var_embed, w_query, agg_kv, *state0)

    def pool_pairs(mine, got):
        return call(
            pool_pair_body,
            [struct((block, packet), F32)] * n_chip,
            limit=LIMITS["pool_pair"],
            in_specs=[SMEM, vmem, vmem],
            cost_estimate=cost(1e8, 3e6),
            name="pool_pair",
        )(me, mine, got)

    received = exchange_pairs(keep, send, pool_pairs)
    mixed, pooled_packet = call(
        functools.partial(pool_body, n_chip),
        [struct((block, width), F32), struct((block, packet), BF16)],
        limit=LIMITS["pool"],
        cost_estimate=cost(1e8, 2e6),
        name="pool",
    )(*received)
    pooled_even, pooled_odd = gather_pairs(pooled_packet, "var")

    qkv, normed, pooled_packets, centred, inv = call(
        norm_body,
        [
            struct((rows, 3 * group), BF16),
            struct((rows, width), BF16),
            struct((rows, packet), BF16),
            struct((block, width), F32),
            struct((block, LANES), F32),
        ],
        limit=LIMITS["norm"],
        in_specs=[SMEM] + [vmem] * 5,
        scratch_shapes=[pltpu.VMEM((rows, width), F32), pltpu.VMEM((rows, LANES), F32)],
        cost_estimate=cost(8e8, 5e6),
        name="norm",
    )(me, pooled_even, pooled_odd, agg_out, gain, w_heads)

    qkv_all = gather_direct(qkv, "space")
    normed_cols = call(
        functools.partial(columns_body, n_space),
        [struct((rows, cols), BF16)] * n_space,
        limit=LIMITS["columns"],
        after=qkv_all[1:],
        in_specs=[SMEM, vmem],
        scratch_shapes=[pltpu.VMEM((n_space, rows, cols), BF16)],
        cost_estimate=cost(1e6, 1e6),
        name="columns",
    )(me, normed)
    normed_all = exchange_direct(normed_cols, "space")
    attn, dqkv = call(
        functools.partial(attention_body, n_space, size, scale),
        [struct((positions, group), BF16), struct((positions, 3 * group), BF16)],
        limit=LIMITS["attention"],
        after=[normed_cols[0]],
        scratch_shapes=[pltpu.VMEM((positions, group), BF16)] * 4 + [pltpu.VMEM((positions, group), F32)] * 2,
        cost_estimate=cost(6e9, 4e6),
        name="attention",
    )(*qkv_all, *dattn_all)
    dn_keep, dn_send = call(
        dn_body,
        [struct((n_chip, block, width), BF16)] * 2,
        limit=LIMITS["dn"],
        after=normed_all[1:],
        grid=(1,),
        in_specs=[SMEM, pl.BlockSpec((rows, 3 * group), lambda i: (0, 0)), vmem],
        scratch_shapes=[pltpu.VMEM((rows, width), BF16)],
        cost_estimate=cost(2e8, 1e6),
        name="dn",
    )(me, dqkv, w_heads)

    def dn_pairs(mine, got):
        return call(
            dn_pair_body,
            [struct((block, width), BF16)] * n_chip,
            limit=LIMITS["dn_pair"],
            in_specs=[SMEM, vmem, vmem],
            cost_estimate=cost(1e6, 1e6),
            name="dn_pair",
        )(me, mine, got)

    dn_received = exchange_pairs(dn_keep, dn_send, dn_pairs)
    joined_packet, dgain = call(
        functools.partial(joined_body, n_chip),
        [struct((block, packet), BF16), struct((8, width), F32)],
        limit=LIMITS["joined"],
        cost_estimate=cost(2e8, 3e6),
        name="joined",
    )(*dn_received, centred, inv, gain, cot_own, mixed, agg_out)
    joined_even, joined_odd = gather_pairs(joined_packet, "var")

    d_joined, d_pooled, stat = call(
        prepare_body,
        [struct((rows, packet), BF16), struct((rows, width), F32), struct((3, rows, LANES), F32)],
        limit=LIMITS["prepare"],
        in_specs=[SMEM] + [vmem] * 4,
        cost_estimate=cost(6e8, 4e6),
        name="prepare",
    )(me, pooled_packets, joined_even, joined_odd, agg_out)
    height = drows + 16 + group
    out_keep, out_send = call(
        out_grad_body,
        [struct((n_space // 2, height, cols), BF16)] * 2,
        limit=LIMITS["out_grad"],
        grid=(1,),
        in_specs=[SMEM] + [whole(x.shape) for x in (pooled_packets, d_joined, dgain)] + [whole((rows, group)), whole((rows, width))],
        out_specs=[whole((n_space // 2, height, cols))] * 2,
        scratch_shapes=[pltpu.VMEM((width, width), F32), pltpu.VMEM((n_space, height, cols), BF16)],
        cost_estimate=cost(6e8, 3e6),
        name="out_grad",
    )(me, pooled_packets, d_joined, dgain, attn, cotangent)
    out_got = swap(out_send, "space", 1)

    def out_add(mine, got):
        return call(
            functools.partial(out_add_body, drows),
            [struct((height, cols), BF16)] * (mine.shape[0] - 1),
            cost_estimate=cost(1e6, 1e6),
            name="out_add",
        )(mine, got)

    later, bit = out_add(out_keep, out_got), 2
    out_later, out_parts = later, [out_keep, out_got]
    while bit < n_space:
        got = {j: swap(later[j], "space", bit) for j in range(0, len(later), 2)}
        out_parts.append(got[0])
        rest = list(range(1, len(later), 2))
        if rest:
            mine = jnp.stack([later[0]] + [later[j] for j in rest])
            later = out_add(mine, jnp.stack([later[0]] + [got[j + 1] for j in rest]))
        bit *= 2

    def d_values(value, scores, after):
        here = value.shape[0]
        return call(
            dvalue_body,
            [struct((here, rows, width), BF16), struct((here, rows, 2 * LANES), BF16)],
            limit=LIMITS["dvalue"],
            after=after,
            grid=(here,),
            in_specs=[whole((rows, width)), whole((3, rows, LANES)), every((rows, width)), every((rows, LANES))],
            out_specs=[every((rows, width)), every((rows, 2 * LANES))],
            scratch_shapes=[pltpu.VMEM((LANES, width), BF16), pltpu.VMEM((width, LANES), BF16)],
            cost_estimate=cost(2e9, 5e6),
            name="dvalue",
        )(d_pooled, stat, value, scores)

    def embed(start, d_value, d_logit, after):
        here = d_value.shape[0]
        at = lambda shape: pl.BlockSpec((1,) + shape, lambda v: (v + start,) + (0,) * len(shape))
        blocks = (n_space // 2, here * pixels + 16, cols)
        return call(
            functools.partial(embed_body, n_space),
            [struct(blocks, BF16)] * 2,
            limit=LIMITS["embed"],
            after=after,
            grid=(here,),
            in_specs=[
                SMEM,
                every((rows, width)),
                every((rows, 2 * LANES)),
                at((rows, pixels)),
                pl.BlockSpec((width, width), lambda v: (0, 1)),
                whole((width, LANES)),
            ],
            out_specs=[whole(blocks)] * 2,
            scratch_shapes=[pltpu.VMEM((n_space, pixels, cols), BF16), pltpu.VMEM((16, width), F32)],
            cost_estimate=cost(1.5e9, 4e6),
            name="embed",
        )(me, d_value, d_logit, patches, agg_kv, w_back)

    dv0, dl0 = d_values(value0, scores0, [out_keep])
    dv1, dl1 = d_values(value1, scores1, [])

    step = max(drows, 256)
    kv_keep, kv_send = call(
        value_grad_body,
        [struct((n_chip, drows, packet), BF16)] * 2,
        limit=LIMITS["value_grad"],
        after=out_later,
        grid=(width // step,),
        in_specs=[SMEM]
        + [pl.BlockSpec(x.shape[:2] + (step,), lambda i: (0, 0, i)) for x in (tokens0, tokens1)]
        + [whole(x.shape) for x in (dv0, dv1, dl0, dl1)],
        out_specs=[whole((n_chip, drows, packet))] * 2,
        scratch_shapes=[pltpu.VMEM((step, packet), BF16)],
        cost_estimate=cost(4e9, 1e7),
        name="value_grad",
    )(me, tokens0, tokens1, dv0, dv1, dl0, dl1)
    kv_got = swap(kv_send, "var", 1)

    def scatter_embed(keep, arrived, after):
        n = n_space // 2 - 1
        sums = call(
            functools.partial(add_body, n),
            [struct(keep.shape[1:], BF16)] * n,
            limit=LIMITS["add"],
            after=after,
            cost_estimate=cost(1e6, 1e6),
            name="add",
        )(keep, arrived)
        blocks = {2 * (j + 1): sums[j] for j in range(n)}
        mine, bit = [keep, arrived], 2
        while bit < n_space:
            got = {k ^ bit: swap(blocks[k], "space", bit) for k in blocks if k & bit and k % bit == 0}
            mine.append(got[0])
            for k in got:
                if k:
                    blocks[k] = (blocks[k].astype(F32) + got[k].astype(F32)).astype(BF16)
            bit *= 2
        return mine, list(sums)

    keep0, send0 = embed(0, dv0, dl0, [kv_keep])
    arrived0 = swap(send0, "space", 1)
    kv_blocks = call(
        functools.partial(pair_sum_body, n_chip),
        [struct((drows, packet), BF16)] * n_chip,
        limit=LIMITS["pair_sum"],
        after=[keep0],
        in_specs=[SMEM] + [vmem] * 2,
        cost_estimate=cost(1e6, 1e6),
        name="pair_sum",
    )(me, kv_keep, kv_got)
    kv_parts = [kv_blocks[0]] + [swap(kv_blocks[k], "var", 2 * k) for k in range(1, n_chip)]
    keep1, send1 = embed(half, dv1, dl1, [kv_blocks[0]] + out_parts[2:])
    arrived1 = swap(send1, "space", 1)
    part = drows * LANES // cols
    pieces = call(
        functools.partial(packet_split_body, n_chip, n_space),
        [struct((part + 2 * drows, cols), BF16)] * n_space,
        limit=LIMITS["packet_split"],
        in_specs=[SMEM] + [vmem] * n_chip,
        scratch_shapes=[pltpu.VMEM((n_space // 2, drows, kv_cols), BF16)],
        cost_estimate=cost(1e6, 1e6),
        name="packet_split",
    )(me, *kv_parts)
    pieces_all = exchange_direct(pieces, "space")
    mine0, sums0 = scatter_embed(keep0, arrived0, [pieces[0]])
    mine1, sums1 = scatter_embed(keep1, arrived1, sums0)
    grad_qkv, head_flag = call(
        functools.partial(head_grads_body, n_space),
        [struct((cols, 3 * group), F32), struct((8, LANES), F32)],
        limit=LIMITS["head_grads"],
        cost_estimate=cost(1e9, 3e6),
        name="head_grads",
    )(*normed_all, dqkv)
    first_slot = lambda x: pl.BlockSpec((1,) + x.shape[1:], lambda i: (0, 0, 0)) if x.ndim == 3 else whole(x.shape)
    kv_sum, grad_out = call(
        functools.partial(space_sum_body, n_space),
        [struct((drows + 16, kv_cols + LANES + cols), BF16), struct((group, cols), F32)],
        limit=LIMITS["space_sum"],
        after=sums1 + [head_flag],
        grid=(1,),
        in_specs=[first_slot(x) for x in list(pieces_all) + out_parts],
        cost_estimate=cost(1e6, 1e6),
        name="space_sum",
    )(*pieces_all, *out_parts)

    def stack(parts):
        return call(
            stack_body,
            struct((len(parts),) + parts[0].shape, BF16),
            after=mine0[2:] + mine1[2:],
            cost_estimate=cost(1e6, 1e6),
            name="stack",
        )(*parts)

    kv_even, kv_odd = gather_pairs(kv_sum, "var", stack)
    grad_agg_kv, grad_query, grad_agg_out, grad_gain = call(
        functools.partial(final_body, n_var, n_space, scale),
        [struct((width, kv_cols), F32), struct((1, cols), F32)] + [struct((width, cols), F32), struct((1, cols), F32)],
        grid=(1,),
        in_specs=[SMEM] + [vmem] * 3 + [pl.BlockSpec((width, width), lambda i: (0, 0))],
        limit=LIMITS["final"],
        cost_estimate=cost(2e8, 5e6),
        name="final",
    )(me, kv_even, kv_odd, query, agg_kv)

    def first_block(x):
        if x.ndim == 3:
            return pl.BlockSpec((1,) + x.shape[1:], lambda i: (0, 0, 0))
        return pl.BlockSpec(x.shape, lambda i: (0, 0))

    grad_embed, grad_var_embed = call(
        functools.partial(embed_final_body, len(mine0)),
        [struct((count, pixels, cols), F32), struct((count, cols), F32)],
        grid=(1,),
        in_specs=[first_block(x) for x in mine0 + mine1],
        limit=LIMITS["embed_final"],
        cost_estimate=cost(1e6, 1e6),
        name="embed_final",
    )(*mine0, *mine1)

    return (
        grad_embed,
        grad_var_embed,
        grad_query.reshape(cols),
        grad_agg_kv,
        grad_agg_out,
        grad_gain.reshape(cols),
        grad_qkv,
        grad_out,
    )


def solution(mesh):
    return jax.shard_map(
        shards,
        mesh=mesh,
        in_specs=(
            P("var", "space", None),
            P("var", None, None),
            P("var", None),
            P(),
            P(),
            P(),
            P(),
            P(None, "var"),
            P("var", None),
            P("space", None),
        ),
        out_specs=(
            P("var", None, "space"),
            P("var", "space"),
            P("space"),
            P(None, "space"),
            P(None, "space"),
            P("space"),
            P("space", "var"),
            P("var", "space"),
        ),
        check_vma=False,
    )
```

```python
import functools
import math

import jax
import jax.numpy as jnp
from jax import lax
from jax.experimental import pallas as pl
from jax.experimental.pallas import tpu as pltpu
from jax.sharding import PartitionSpec as P

HEADS = 16
LANES = 128
EPSILON = 1e-05
MIB = 1 << 20

LIMITS = {
    "early": 60, "forward": 24, "columns": 8, "pool_pair": 16, "pool": 16, "norm": 16, "attention": 24,
    "dn": 12, "dn_pair": 16, "joined": 16, "prepare": 16, "out_grad": 16, "dvalue": 24, "embed": 24, "value_grad": 32,
    "add": 12, "pair_sum": 16, "packet_split": 16, "space_sum": 16, "head_grads": 16, "final": 16, "embed_final": 24,
}

F32 = jnp.float32
BF16 = jnp.bfloat16

NN = (((1,), (0,)), ((), ()))
NT = (((1,), (1,)), ((), ()))
TN = (((0,), (0,)), ((), ()))


def mm(a, b, dims=NN):
    return lax.dot_general(a, b, dims, preferred_element_type=F32)


def iota(shape, axis):
    return lax.broadcasted_iota(jnp.int32, shape, axis)


def parts3(x):
    hi = x.astype(BF16).astype(F32)
    rest = x - hi
    mid = rest.astype(BF16).astype(F32)
    return hi, mid, rest - mid


def pack(x, y=None):
    group = iota(x.shape, 1) >> 4
    hi, mid, lo = parts3(x)
    out = jnp.where(group == 0, hi, jnp.where(group == 1, mid, jnp.where(group == 2, lo, 0.0)))
    if y is not None:
        hi, mid, lo = parts3(y)
        out = jnp.where(group == 3, hi, jnp.where(group == 4, mid, jnp.where(group == 5, lo, out)))
    return out.astype(BF16)


def unpack(packed, first_group=0):
    row, column = iota((LANES, LANES), 0), iota((LANES, LANES), 1)
    group = row >> 4
    take = ((row & 15) == (column & 15)) & (group >= first_group) & (group < first_group + 3)
    return mm(packed, jnp.where(take, 1.0, 0.0).astype(BF16))


def spread_matrix(width, size, first=0):
    row, column = iota((LANES, width), 0), iota((LANES, width), 1)
    shift = size.bit_length() - 1
    take = ((row & 15) == ((column + first) >> shift)) & (row < 48)
    return jnp.where(take, 1.0, 0.0).astype(BF16)


def fold_matrix(width, size):
    row, column = iota((width, LANES), 0), iota((width, LANES), 1)
    shift = size.bit_length() - 1
    return jnp.where((column & 15) == (row >> shift), 1.0, 0.0).astype(BF16)


def head_sums(x, fold):
    hi, mid, lo = parts3(x)
    return mm(hi.astype(BF16), fold) + mm(mid.astype(BF16), fold) + mm(lo.astype(BF16), fold)


def call(body, out_shape, limit=16, after=(), in_specs=None, **kw):
    def run(*args):
        n, m = len(args), len(after)
        vmem = pl.BlockSpec(memory_space=pltpu.VMEM)
        return pl.pallas_call(
            lambda *refs: body(*refs[:n], *refs[n + m :]),
            out_shape=out_shape,
            in_specs=([vmem] * n if in_specs is None else list(in_specs)) + [vmem] * m,
            compiler_params=pltpu.CompilerParams(vmem_limit_bytes=limit * MIB),
            **kw,
        )(*args, *after)

    return run


def struct(shape, dtype):
    return jax.ShapeDtypeStruct(shape, dtype)


def cost(flops, moved):
    return pl.CostEstimate(flops=int(flops), bytes_accessed=int(moved), transcendentals=0)


SMEM = pl.BlockSpec(memory_space=pltpu.SMEM)


def swap(x, axis, k, keep=None):
    pairs = [(i, i ^ k) for i in range(lax.axis_size(axis))]
    if keep is not None:
        pairs = [pair for pair in pairs if keep(pair[1])]
    return lax.ppermute(x, axis, pairs)


def gather_direct(x, axis):
    return [x] + [swap(x, axis, k) for k in range(1, lax.axis_size(axis))]


def exchange_direct(blocks, axis):
    return [blocks[0]] + [swap(blocks[k], axis, k) for k in range(1, len(blocks))]


def gather_pairs(x, axis, stack=jnp.stack):
    even = [x] + [swap(x, axis, k) for k in range(2, lax.axis_size(axis), 2)]
    even = stack(even)
    return even, swap(even, axis, 1)


def exchange_pairs(keep, send, combine):
    parts = combine(keep, swap(send, "var", 1))
    return [parts[0]] + [swap(parts[k], "var", 2 * k) for k in range(1, len(parts))]


def pair_rows(me_v, k, odd, block):
    device = (((me_v >> 1) ^ k) << 1) + ((me_v & 1) ^ odd)
    return pl.ds(pl.multiple_of(device * block, block), block)


def three_rows(x):
    hi, mid, lo = parts3(x)
    row = iota((16, x.shape[1]), 0)
    return jnp.where(row == 0, hi, jnp.where(row == 1, mid, jnp.where(row == 2, lo, 0.0))).astype(BF16)


def head_order(width, size=64):
    heads = width // (3 * size)
    row, column = iota((width, width), 0), iota((width, width), 1)
    take = jnp.zeros((width, width), jnp.bool_)
    for h in range(heads):
        for c in range(3):
            start, target = h * 3 * size + c * size, c * heads * size + h * size
            inside = (column >= target) & (column < target + size)
            take = take | (inside & ((row - start) == (column - target)))
    return jnp.where(take, 1.0, 0.0).astype(BF16)


def early_body(me_ref, cot_ref, outw_ref, qkvw_ref, dattn_ref, own_ref, wperm_ref):
    dattn_ref[...] = mm(cot_ref[...], outw_ref[...], NT).astype(BF16)
    block = own_ref.shape[0]
    own_ref[...] = cot_ref[pl.ds(pl.multiple_of(me_ref[0] * block, block), block), :]
    wperm_ref[...] = mm(qkvw_ref[...], head_order(qkvw_ref.shape[1])).astype(BF16)


def forward_part(start, patches_ref, embed_ref, offset_ref, wq, wv_ref, spread, outs, state):
    tokens_ref, value_ref, scores_ref = outs
    here = tokens_ref.shape[0]
    width = tokens_ref.shape[2]
    for v in range(here):
        u = start + v
        tokens = (mm(patches_ref[u], embed_ref[u]) + offset_ref[u : u + 1, :]).astype(BF16)
        tokens_ref[v] = tokens
        pieces = mm(tokens, wq)
        scores_ref[v] = pieces[:, :LANES] + pieces[:, LANES : 2 * LANES] + pieces[:, 2 * LANES :]
        value_ref[v] = mm(tokens, wv_ref[:, width:])
    top = functools.reduce(jnp.maximum, [scores_ref[v] for v in range(here)])
    total, acc = 0.0, 0.0
    if state is not None:
        top = jnp.maximum(top, state[0])
        old = jnp.exp(state[0] - top)
        total, acc = state[1] * old, state[2] * mm(pack(old), spread)
    for v in range(here):
        new = jnp.exp(scores_ref[v] - top)
        total = total + new
        acc = acc + value_ref[v] * mm(pack(new), spread)
    return top, total, acc


def first_body(
    scale, patches_ref, embed_ref, offset_ref, query_ref, kv_ref,
    tokens_ref, value_ref, scores_ref, wq_ref, wback_ref, acc_ref, max_ref, sum_ref,
):
    width = tokens_ref.shape[2]
    size = width // HEADS
    row, column = iota((LANES, width), 0), iota((LANES, width), 1)
    own = (row & 15) == (column >> (size.bit_length() - 1))
    wq = jnp.zeros((width, LANES), F32)
    for part in parts3(query_ref[...]):
        wq = wq + mm(kv_ref[:, :width], jnp.where(own, part, 0.0).astype(BF16), NT)
    hi, mid, lo = parts3(wq * scale)
    wq_ref[:, :LANES] = hi.astype(BF16)
    wq_ref[:, LANES : 2 * LANES] = mid.astype(BF16)
    wq_ref[:, 2 * LANES :] = lo.astype(BF16)
    group = iota((width, LANES), 1) >> 4
    back = jnp.where((group == 0) | (group == 2), hi, jnp.where(group == 1, mid, 0.0))
    wback_ref[...] = back.astype(BF16)
    max_ref[...], sum_ref[...], acc_ref[...] = forward_part(
        0, patches_ref, embed_ref, offset_ref, wq_ref[...], kv_ref, spread_matrix(width, size),
        (tokens_ref, value_ref, scores_ref), None,
    )


def second_body(
    start, me_ref, patches_ref, embed_ref, offset_ref, wq_ref, kv_ref, acc0_ref, max0_ref, sum0_ref,
    tokens_ref, value_ref, scores_ref, keep_ref, send_ref, acc_ref, max_ref,
):
    width = tokens_ref.shape[2]
    top, total, acc = forward_part(
        start, patches_ref, embed_ref, offset_ref, wq_ref[...], kv_ref, spread_matrix(width, width // HEADS),
        (tokens_ref, value_ref, scores_ref), (max0_ref[...], sum0_ref[...], acc0_ref[...]),
    )
    acc_ref[...] = acc
    max_ref[...] = jnp.where(iota(top.shape, 1) < LANES // 2, top, total)
    block = keep_ref.shape[1]
    core = me_ref[0] & 1
    for c in range(keep_ref.shape[0]):
        for ref, device in ((keep_ref, 2 * c + core), (send_ref, 2 * c + 1 - core)):
            at = pl.ds(pl.multiple_of(device * block, block), block)
            ref[c, :, :width] = acc_ref[at, :]
            ref[c, :, width:] = max_ref[at, :]


def halves_of(both):
    low = iota(both.shape, 1) < LANES // 2
    turned = pltpu.roll(both, LANES // 2, 1)
    return jnp.where(low, both, turned), jnp.where(low, turned, both)


def pool_pair_body(me_ref, keep_ref, got_ref, *out_refs):
    width = keep_ref.shape[2] - LANES
    spread = spread_matrix(width, width // HEADS)
    low = iota((keep_ref.shape[1], LANES), 1) < LANES // 2
    for k, out_ref in enumerate(out_refs):
        slot = (me_ref[0] >> 1) ^ k
        mine, other = keep_ref[slot], got_ref[slot]
        max_a, sum_a = halves_of(mine[:, width:])
        max_b, sum_b = halves_of(other[:, width:])
        top = jnp.maximum(max_a, max_b)
        factor_a, factor_b = jnp.exp(max_a - top), jnp.exp(max_b - top)
        out_ref[:, :width] = mine[:, :width] * mm(pack(factor_a), spread) + other[:, :width] * mm(pack(factor_b), spread)
        out_ref[:, width:] = jnp.where(low, top, sum_a * factor_a + sum_b * factor_b)


def pool_body(n, *refs):
    ins, (mixed_ref, packet_ref) = refs[:n], refs[n:]
    width = mixed_ref.shape[1]
    stats = [halves_of(ref[:, width:]) for ref in ins]
    top = functools.reduce(jnp.maximum, [m for m, _ in stats])
    factors = [jnp.exp(m - top) for m, _ in stats]
    total = sum(s * f for (_, s), f in zip(stats, factors))
    spread = spread_matrix(width, width // HEADS)
    mixed = jnp.zeros(mixed_ref.shape, F32)
    for ref, factor in zip(ins, factors):
        mixed = mixed + ref[:, :width] * mm(pack(factor / total), spread)
    mixed_ref[...] = mixed
    packet_ref[:, :width] = mixed.astype(BF16)
    packet_ref[:, width:] = pack(top, total)


def norm_body(
    me_ref, even_ref, odd_ref, agg_ref, gain_ref, w_ref, qkv_ref, normed_ref, packets_ref, centred_ref, inv_ref,
    all_ref, allinv_ref,
):
    width = agg_ref.shape[0]
    block = centred_ref.shape[0]
    for k in range(even_ref.shape[0]):
        for odd, ref in ((0, even_ref), (1, odd_ref)):
            packets_ref[pair_rows(me_ref[0], k, odd, block), :] = ref[k]
    joined = mm(packets_ref[:, :width], agg_ref[...]).astype(BF16).astype(F32)
    mean = jnp.mean(joined, axis=-1, keepdims=True)
    spread_sq = jnp.mean((joined - mean) ** 2, axis=-1, keepdims=True)
    inv = lax.rsqrt(spread_sq + EPSILON)
    centred = (joined - mean) * inv
    normed = (centred * gain_ref[...]).astype(BF16)
    qkv_ref[...] = mm(normed, w_ref[...]).astype(BF16)
    normed_ref[...] = normed
    all_ref[...] = centred
    allinv_ref[...] = jnp.broadcast_to(inv, allinv_ref.shape)
    start = pl.multiple_of(me_ref[0] * block, block)
    centred_ref[...] = all_ref[pl.ds(start, block), :]
    inv_ref[...] = allinv_ref[pl.ds(start, block), :]


def attention_body(n_space, size, scale, *refs):
    qkv_refs, dattn_refs = refs[:n_space], refs[n_space : 2 * n_space]
    attn_ref, dqkv_ref, q_ref, k_ref, v_ref, do_ref, dk_ref, dv_ref = refs[2 * n_space :]
    rows, group = dattn_refs[0].shape
    heads = group // size
    for b in range(n_space):
        at = slice(b * rows, (b + 1) * rows)
        q_ref[at, :] = qkv_refs[b][:, :group]
        k_ref[at, :] = qkv_refs[b][:, group : 2 * group]
        v_ref[at, :] = qkv_refs[b][:, 2 * group :]
        do_ref[at, :] = dattn_refs[b][...]
    dk_ref[...] = jnp.zeros(dk_ref.shape, F32)
    dv_ref[...] = jnp.zeros(dv_ref.shape, F32)

    def step(b, carry):
        at = pl.ds(pl.multiple_of(b * rows, rows), rows)
        queries, d_out = q_ref[at, :], do_ref[at, :]
        lane_head = iota((rows, group), 1) // size if heads > 1 else None
        attn = dq = None
        for h in range(heads):
            if heads > 1:
                q_h = jnp.where(lane_head == h, queries.astype(F32), 0.0).astype(BF16)
                do_h = jnp.where(lane_head == h, d_out.astype(F32), 0.0).astype(BF16)
            else:
                q_h, do_h = queries, d_out
            logits = mm((q_h.astype(F32) * scale).astype(BF16), k_ref[...], NT)
            shifted = jnp.exp(logits - jnp.max(logits, axis=-1, keepdims=True))
            probs = shifted * (1.0 / jnp.sum(shifted, axis=-1, keepdims=True))
            probs_b = probs.astype(BF16)
            attn_h = mm(probs_b, v_ref[...])
            dprob = mm((do_h.astype(F32) * scale).astype(BF16), v_ref[...], NT)
            delta = jnp.sum(probs * dprob, axis=-1, keepdims=True)
            dscore = (probs * (dprob - delta)).astype(BF16)
            dq_h = mm(dscore, k_ref[...])
            dk_ref[...] += mm(dscore, q_h, TN)
            dv_ref[...] += mm(probs_b, do_h, TN)
            attn = attn_h if attn is None else jnp.where(lane_head == h, attn_h, attn)
            dq = dq_h if dq is None else jnp.where(lane_head == h, dq_h, dq)
        attn_ref[at, :] = attn.astype(BF16)
        dqkv_ref[at, :group] = dq.astype(BF16)
        return carry

    lax.fori_loop(0, n_space, step, 0, unroll=2)
    dqkv_ref[:, group : 2 * group] = dk_ref[...].astype(BF16)
    dqkv_ref[:, 2 * group :] = dv_ref[...].astype(BF16)


def dn_body(me_ref, dqkv_ref, w_ref, keep_ref, send_ref, dn_ref):
    dn_ref[...] = mm(dqkv_ref[...], w_ref[...], NT).astype(BF16)
    block = keep_ref.shape[1]
    core = me_ref[0] & 1
    for c in range(keep_ref.shape[0]):
        for ref, device in ((keep_ref, 2 * c + core), (send_ref, 2 * c + 1 - core)):
            ref[c] = dn_ref[pl.ds(pl.multiple_of(device * block, block), block), :]


def columns_body(n_space, me_ref, in_ref, *refs):
    out_refs, (cols_ref,) = refs[:n_space], refs[n_space:]
    cols = cols_ref.shape[2]
    for c in range(n_space):
        cols_ref[c] = in_ref[:, c * cols : (c + 1) * cols]
    for k in range(n_space):
        out_refs[k][...] = cols_ref[me_ref[1] ^ k]


def head_grads_body(n_space, *refs):
    normed_refs, (dqkv_ref, gqkv_ref, flag_ref) = refs[:n_space], refs[n_space:]
    flag_ref[...] = jnp.zeros(flag_ref.shape, F32)
    rows = normed_refs[0].shape[0]
    natural = mm(dqkv_ref[...], head_order(dqkv_ref.shape[1]), NT).astype(BF16)
    gqkv_ref[...] = sum(
        mm(ref[...], natural[b * rows : (b + 1) * rows, :], TN) for b, ref in enumerate(normed_refs)
    )


def dn_pair_body(me_ref, keep_ref, got_ref, *out_refs):
    for k, out_ref in enumerate(out_refs):
        slot = (me_ref[0] >> 1) ^ k
        out_ref[...] = (keep_ref[slot].astype(F32) + got_ref[slot].astype(F32)).astype(BF16)


def joined_body(n, *refs):
    ins = refs[:n]
    centred_ref, inv_ref, gain_ref, cot_ref, mixed_ref, agg_ref, packet_ref, dgain_ref = refs[n:]
    width = centred_ref.shape[1]
    d_normed = sum(ref[...].astype(F32) for ref in ins)
    centred = centred_ref[...]
    dgain_ref[...] = jnp.broadcast_to(jnp.sum(d_normed * centred, axis=0, keepdims=True), dgain_ref.shape)
    gained = d_normed * gain_ref[...]
    inner = (
        gained
        - jnp.mean(gained, axis=-1, keepdims=True)
        - centred * jnp.mean(gained * centred, axis=-1, keepdims=True)
    )
    d_joined = (cot_ref[...].astype(F32) + inner * inv_ref[:, :1]).astype(BF16)
    d_pooled = mm(d_joined, agg_ref[...], NT)
    center = pack(head_sums(d_pooled * mixed_ref[...], fold_matrix(width, width // HEADS)))
    packet_ref[:, :width] = d_joined
    packet_ref[:, width:] = center


def prepare_body(me_ref, pooled_ref, even_ref, odd_ref, agg_ref, djoined_ref, dpool_ref, stat_ref):
    width = agg_ref.shape[0]
    for k in range(even_ref.shape[0]):
        for odd, ref in ((0, even_ref), (1, odd_ref)):
            djoined_ref[pair_rows(me_ref[0], k, odd, even_ref.shape[1]), :] = ref[k]
    dpool_ref[...] = mm(djoined_ref[:, :width], agg_ref[...], NT)
    stat_ref[0] = unpack(djoined_ref[:, width:])
    stat_ref[1] = unpack(pooled_ref[:, width:])
    stat_ref[2] = 1.0 / unpack(pooled_ref[:, width:], 3)


def out_grad_body(me_ref, pooled_ref, djoined_ref, dgain_ref, attn_ref, cot_ref, keep_ref, send_ref, all_ref, cols_ref):
    width = dgain_ref.shape[1]
    all_ref[...] = mm(pooled_ref[:, :width], djoined_ref[:, :width], TN)
    weight_grad = mm(attn_ref[...], cot_ref[...], TN).astype(BF16)
    n_space, height, cols = cols_ref.shape
    block = height - 16 - weight_grad.shape[0]
    start = pl.multiple_of(me_ref[0] * block, block)
    own = all_ref[pl.ds(start, block), :].astype(BF16)
    extra = three_rows(dgain_ref[:1, :])
    for c in range(n_space):
        cols_ref[c, :block, :] = own[:, c * cols : (c + 1) * cols]
        cols_ref[c, block : block + 16, :] = extra[:, c * cols : (c + 1) * cols]
        cols_ref[c, block + 16 :, :] = weight_grad[:, c * cols : (c + 1) * cols]
    for k in range(n_space):
        (send_ref if k % 2 else keep_ref)[k // 2] = cols_ref[me_ref[1] ^ k]


def out_add_body(block, mine_ref, got_ref, *refs):
    for j, out_ref in enumerate(refs):
        total = mine_ref[j + 1].astype(F32) + got_ref[j + 1].astype(F32)
        out_ref[...] = total.astype(BF16)
        out_ref[block : block + 16, :] = three_rows(jnp.sum(total[block : block + 16, :], axis=0, keepdims=True))


def dvalue_body(dpool_ref, stat_ref, value_ref, scores_ref, dvalue_ref, dlogit_ref, spread_ref, fold_ref):
    width = dpool_ref.shape[1]
    size = width // HEADS

    @pl.when(pl.program_id(0) == 0)
    def _():
        spread_ref[...] = spread_matrix(width, size)
        fold_ref[...] = fold_matrix(width, size)

    weight = jnp.exp(scores_ref[0] - stat_ref[1]) * stat_ref[2]
    dvalue_ref[0] = (mm(pack(weight), spread_ref[...]) * dpool_ref[...]).astype(BF16)
    dweight = head_sums(dpool_ref[...] * value_ref[0], fold_ref[...])
    dlogit = weight * (dweight - stat_ref[0])
    hi = dlogit.astype(BF16)
    dlogit_ref[0, :, :LANES] = hi
    dlogit_ref[0, :, LANES:] = (dlogit - hi.astype(F32)).astype(BF16)


def embed_body(
    n_space, me_ref, dvalue_ref, dlogit_ref, patches_ref, wv_ref, wback_ref, keep_ref, send_ref, cols_ref, extra_ref
):
    v = pl.program_id(0)
    hi, lo = dlogit_ref[0, :, :LANES].astype(F32), dlogit_ref[0, :, LANES:].astype(F32)
    group = iota(hi.shape, 1) >> 4
    mixed = jnp.where(group < 2, hi, jnp.where(group == 2, lo, 0.0)).astype(BF16)
    d_tokens = (mm(dvalue_ref[0], wv_ref[...], NT) + mm(mixed, wback_ref[...], NT)).astype(BF16)
    grad = mm(patches_ref[0], d_tokens, TN).astype(BF16)
    hi, lo, _ = parts3(jnp.sum(d_tokens.astype(F32), axis=0, keepdims=True))
    row = iota(extra_ref.shape, 0)
    extra = jnp.where(row == 2 * v, hi, jnp.where(row == 2 * v + 1, lo, 0.0))

    @pl.when(v == 0)
    def _():
        extra_ref[...] = extra

    @pl.when(v > 0)
    def _():
        extra_ref[...] += extra

    cols = cols_ref.shape[2]
    pixels = patches_ref.shape[2]
    for c in range(n_space):
        cols_ref[c] = grad[:, c * cols : (c + 1) * cols]
    at = pl.ds(pl.multiple_of(v * pixels, pixels), pixels)
    for k in range(0, n_space, 2):
        keep_ref[k // 2, at, :] = cols_ref[me_ref[1] ^ k]
        send_ref[k // 2, at, :] = cols_ref[me_ref[1] ^ (k + 1)]

    @pl.when(v == pl.num_programs(0) - 1)
    def _():
        tail = slice(keep_ref.shape[1] - 16, keep_ref.shape[1])
        for c in range(n_space):
            cols_ref[c, :16, :] = extra_ref[:, c * cols : (c + 1) * cols].astype(BF16)
        for k in range(0, n_space, 2):
            keep_ref[k // 2, tail, :] = cols_ref[me_ref[1] ^ k, :16, :]
            send_ref[k // 2, tail, :] = cols_ref[me_ref[1] ^ (k + 1), :16, :]


def embed_final_body(parts, *refs):
    ins, (grad_ref, offset_ref) = refs[:-2], refs[-2:]
    pixels = grad_ref.shape[1]
    base = 0
    for chunk in range(len(ins) // parts):
        total = 0.0
        for ref in ins[chunk * parts : (chunk + 1) * parts]:
            total = total + (ref[0] if len(ref.shape) == 3 else ref[...]).astype(F32)
        count = (total.shape[0] - 16) // pixels
        for v in range(count):
            grad_ref[base + v] = total[v * pixels : (v + 1) * pixels, :]
            row = count * pixels + 2 * v
            offset_ref[base + v : base + v + 1, :] = total[row : row + 1, :] + total[row + 1 : row + 2, :]
        base += count


def stack_body(*refs):
    for k, ref in enumerate(refs[:-1]):
        refs[-1][k] = ref[...]


def value_grad_body(me_ref, *refs):
    tokens_refs, dv_refs, dl_refs, (keep_ref, send_ref, all_ref) = refs[:2], refs[2:4], refs[4:6], refs[6:]
    width = dv_refs[0].shape[2]
    total, both = 0.0, 0.0
    for tokens_ref, dv_ref, dl_ref in zip(tokens_refs, dv_refs, dl_refs):
        for v in range(dv_ref.shape[0]):
            total = total + mm(tokens_ref[v], dv_ref[v], TN)
            both = both + mm(tokens_ref[v], dl_ref[v], TN)
    all_ref[:, :width] = total.astype(BF16)
    all_ref[:, width:] = pack(both[:, :LANES] + both[:, LANES:])
    block = keep_ref.shape[1]
    count = all_ref.shape[0] // block
    for r in range(count):
        target = pl.program_id(0) * count + r
        same = (target & 1) == (me_ref[0] & 1)
        slot = target >> 1

        @pl.when(same)
        def _():
            keep_ref[slot] = all_ref[r * block : (r + 1) * block, :]

        @pl.when(jnp.logical_not(same))
        def _():
            send_ref[slot] = all_ref[r * block : (r + 1) * block, :]


def pair_sum_body(n_chip, me_ref, keep_ref, got_ref, *out_refs):
    width = keep_ref.shape[2] - LANES
    for k in range(n_chip):
        slot = (me_ref[0] >> 1) ^ k
        mine, other = keep_ref[slot], got_ref[slot]
        out_refs[k][:, :width] = (mine[:, :width].astype(F32) + other[:, :width].astype(F32)).astype(BF16)
        out_refs[k][:, width:] = pack(unpack(mine[:, width:]) + unpack(other[:, width:]))


def packet_split_body(n_in, n_space, me_ref, *refs):
    ins, out_refs, (cols_ref,) = refs[:n_in], refs[n_in:-1], refs[-1:]
    block, width = ins[0].shape[0], ins[0].shape[1] - LANES
    total = sum(ref[:, :width].astype(F32) for ref in ins).astype(BF16)
    factor = pack(sum(unpack(ref[:, width:]) for ref in ins))
    half = n_space // 2
    cols = cols_ref.shape[2] // 2
    for c in range(half):
        cols_ref[c] = total[:, 2 * c * cols : 2 * (c + 1) * cols]
    part = out_refs[0].shape[0] - 2 * block
    for k in range(n_space):
        for piece in range(block // part):
            lanes = slice(piece * LANES, (piece + 1) * LANES)
            out_refs[k][:part, lanes] = factor[piece * part : (piece + 1) * part, :]
        large = cols_ref[jnp.maximum((me_ref[1] ^ k) - half, 0)]
        out_refs[k][part : part + block, :] = large[:, :cols]
        out_refs[k][part + block :, :] = large[:, cols:]


def space_sum_body(n, *refs):
    ins, outs, (out_ref, weight_ref) = refs[:n], list(refs[n:-2]), refs[-2:]
    outs = [ref.at[0] if len(ref.shape) == 3 else ref for ref in outs]
    cols = ins[0].shape[1]
    width = out_ref.shape[1] - LANES - cols
    block = out_ref.shape[0] - 16
    part = ins[0].shape[0] - 2 * block
    for piece in range(2):
        at = slice(part + piece * block, part + (piece + 1) * block)
        out_ref[:block, piece * cols : (piece + 1) * cols] = sum(ref[at, :].astype(F32) for ref in ins).astype(BF16)
    for piece in range(block // part):
        lanes = slice(piece * LANES, (piece + 1) * LANES)
        factor = pack(sum(unpack(ref[:part, lanes]) for ref in ins))
        out_ref[piece * part : (piece + 1) * part, width : width + LANES] = factor
    out_ref[block:, : width + LANES] = jnp.zeros((16, width + LANES), BF16)
    total = sum(ref[...].astype(F32) for ref in outs)
    out_ref[:block, width + LANES :] = total[:block, :].astype(BF16)
    out_ref[block:, width + LANES :] = three_rows(jnp.sum(total[block : block + 16, :], axis=0, keepdims=True))
    weight_ref[...] = total[block + 16 :, :]


def add_body(n, keep_ref, got_ref, *refs):
    for j, out_ref in enumerate(refs):
        out_ref[...] = (keep_ref[j + 1].astype(F32) + got_ref[j + 1].astype(F32)).astype(BF16)


def final_body(n_var, n_space, scale, me_ref, even_ref, odd_ref, query_ref, wk_ref, kv_ref, gq_ref, out_ref, gain_ref):
    me_v, me_s = me_ref[0], me_ref[1]
    half = n_space // 2
    width = wk_ref.shape[1]
    size = width // HEADS
    cols, qcols = kv_ref.shape[1], gq_ref.shape[1]
    place = pl.multiple_of(jnp.minimum(me_s, half - 1) * cols, LANES)
    spread_kv = spread_matrix(cols, size, place)
    qplace = pl.multiple_of(me_s * qcols, LANES)
    spread_q = spread_matrix(qcols, size, qplace)
    query = query_ref[:, pl.ds(place, cols)] * scale
    block = even_ref.shape[1] - 16
    total, gain = 0.0, 0.0
    for k in range(n_var):
        part_ref, slot = (odd_ref if k % 2 else even_ref), k // 2
        at = pl.ds(pl.multiple_of((me_v ^ k) * block, block), block)
        packed = part_ref[slot, :block, cols : cols + LANES]
        key_grad = mm(packed, spread_kv) * query
        kv_ref[at, :] = jnp.where(me_s < half, key_grad, part_ref[slot, :block, :cols].astype(F32))
        keys = wk_ref[at, pl.ds(qplace, qcols)].astype(F32)
        total = total + jnp.sum(mm(packed, spread_q) * keys, axis=0, keepdims=True)
        out_ref[at, :] = part_ref[slot, :block, cols + LANES :].astype(F32)
        gain = gain + jnp.sum(part_ref[slot, block:, cols + LANES :].astype(F32), axis=0, keepdims=True)
    gq_ref[...] = total * scale
    gain_ref[...] = gain


def shards(
    patches, embed_weight, var_embed, agg_query, agg_kv, agg_out, norm_gain, qkv_weight, out_weight, cotangent
):
    n_var, n_space = lax.axis_size("var"), lax.axis_size("space")
    count, rows, pixels = patches.shape
    width = agg_out.shape[0]
    size = width // HEADS
    scale = 1.0 / math.sqrt(size)
    block = rows // n_var
    cols = width // n_space
    group = out_weight.shape[0]
    drows = width // n_var
    positions = rows * n_space
    kv_cols = 2 * width // n_space
    me = jnp.stack([lax.axis_index("var"), lax.axis_index("space")]).astype(jnp.int32)
    gain = norm_gain.reshape(1, width)
    query = agg_query.reshape(1, width)
    vmem = pl.BlockSpec(memory_space=pltpu.VMEM)
    packet = width + LANES

    whole = lambda shape: pl.BlockSpec(shape, lambda v: (0,) * len(shape))
    every = lambda shape: pl.BlockSpec((1,) + shape, lambda v: (v,) + (0,) * len(shape))
    n_chip = n_var // 2
    half = count // 2

    dattn, cot_own, w_heads = call(
        early_body,
        [struct((rows, group), BF16), struct((block, width), BF16), struct(qkv_weight.shape, BF16)],
        limit=LIMITS["early"],
        grid=(1,),
        in_specs=[SMEM] + [whole(x.shape) for x in (cotangent, out_weight, qkv_weight)],
        out_specs=[whole((rows, group)), whole((block, width)), whole(qkv_weight.shape)],
        cost_estimate=cost(2e8, 4e6),
        name="early",
    )(me, cotangent, out_weight, qkv_weight)
    dattn_all = gather_direct(dattn, "space")

    def forward_outs(here):
        return [struct((here, rows, width), BF16), struct((here, rows, width), F32), struct((here, rows, LANES), F32)]

    tokens0, value0, scores0, w_query, w_back, *state0 = call(
        functools.partial(first_body, scale),
        forward_outs(half)
        + [struct((width, 3 * LANES), BF16), struct((width, LANES), BF16)]
        + [struct((rows, width), F32), struct((rows, LANES), F32), struct((rows, LANES), F32)],
        limit=LIMITS["forward"],
        cost_estimate=cost(6e9, 2e7),
        name="forward_first",
    )(patches, embed_weight, var_embed, query, agg_kv)
    tokens1, value1, scores1, keep, send = call(
        functools.partial(second_body, half),
        forward_outs(count - half) + [struct((n_chip, block, packet), F32)] * 2,
        limit=LIMITS["forward"],
        after=dattn_all[1:],
        in_specs=[SMEM] + [vmem] * 8,
        scratch_shapes=[pltpu.VMEM((rows, width), F32), pltpu.VMEM((rows, LANES), F32)],
        cost_estimate=cost(4e9, 1e7),
        name="forward_second",
    )(me, patches, embed_weight, var_embed, w_query, agg_kv, *state0)

    def pool_pairs(mine, got):
        return call(
            pool_pair_body,
            [struct((block, packet), F32)] * n_chip,
            limit=LIMITS["pool_pair"],
            in_specs=[SMEM, vmem, vmem],
            cost_estimate=cost(1e8, 3e6),
            name="pool_pair",
        )(me, mine, got)

    received = exchange_pairs(keep, send, pool_pairs)
    mixed, pooled_packet = call(
        functools.partial(pool_body, n_chip),
        [struct((block, width), F32), struct((block, packet), BF16)],
        limit=LIMITS["pool"],
        cost_estimate=cost(1e8, 2e6),
        name="pool",
    )(*received)
    pooled_even, pooled_odd = gather_pairs(pooled_packet, "var")

    qkv, normed, pooled_packets, centred, inv = call(
        norm_body,
        [
            struct((rows, 3 * group), BF16),
            struct((rows, width), BF16),
            struct((rows, packet), BF16),
            struct((block, width), F32),
            struct((block, LANES), F32),
        ],
        limit=LIMITS["norm"],
        in_specs=[SMEM] + [vmem] * 5,
        scratch_shapes=[pltpu.VMEM((rows, width), F32), pltpu.VMEM((rows, LANES), F32)],
        cost_estimate=cost(8e8, 5e6),
        name="norm",
    )(me, pooled_even, pooled_odd, agg_out, gain, w_heads)

    qkv_all = gather_direct(qkv, "space")
    normed_cols = call(
        functools.partial(columns_body, n_space),
        [struct((rows, cols), BF16)] * n_space,
        limit=LIMITS["columns"],
        after=qkv_all[1:],
        in_specs=[SMEM, vmem],
        scratch_shapes=[pltpu.VMEM((n_space, rows, cols), BF16)],
        cost_estimate=cost(1e6, 1e6),
        name="columns",
    )(me, normed)
    normed_all = exchange_direct(normed_cols, "space")
    attn, dqkv = call(
        functools.partial(attention_body, n_space, size, scale),
        [struct((positions, group), BF16), struct((positions, 3 * group), BF16)],
        limit=LIMITS["attention"],
        after=[normed_cols[0]],
        scratch_shapes=[pltpu.VMEM((positions, group), BF16)] * 4 + [pltpu.VMEM((positions, group), F32)] * 2,
        cost_estimate=cost(6e9, 4e6),
        name="attention",
    )(*qkv_all, *dattn_all)
    dn_keep, dn_send = call(
        dn_body,
        [struct((n_chip, block, width), BF16)] * 2,
        limit=LIMITS["dn"],
        after=normed_all[1:],
        grid=(1,),
        in_specs=[SMEM, pl.BlockSpec((rows, 3 * group), lambda i: (0, 0)), vmem],
        scratch_shapes=[pltpu.VMEM((rows, width), BF16)],
        cost_estimate=cost(2e8, 1e6),
        name="dn",
    )(me, dqkv, w_heads)

    def dn_pairs(mine, got):
        return call(
            dn_pair_body,
            [struct((block, width), BF16)] * n_chip,
            limit=LIMITS["dn_pair"],
            in_specs=[SMEM, vmem, vmem],
            cost_estimate=cost(1e6, 1e6),
            name="dn_pair",
        )(me, mine, got)

    dn_received = exchange_pairs(dn_keep, dn_send, dn_pairs)
    joined_packet, dgain = call(
        functools.partial(joined_body, n_chip),
        [struct((block, packet), BF16), struct((8, width), F32)],
        limit=LIMITS["joined"],
        cost_estimate=cost(2e8, 3e6),
        name="joined",
    )(*dn_received, centred, inv, gain, cot_own, mixed, agg_out)
    joined_even, joined_odd = gather_pairs(joined_packet, "var")

    d_joined, d_pooled, stat = call(
        prepare_body,
        [struct((rows, packet), BF16), struct((rows, width), F32), struct((3, rows, LANES), F32)],
        limit=LIMITS["prepare"],
        in_specs=[SMEM] + [vmem] * 4,
        cost_estimate=cost(6e8, 4e6),
        name="prepare",
    )(me, pooled_packets, joined_even, joined_odd, agg_out)
    height = drows + 16 + group
    out_keep, out_send = call(
        out_grad_body,
        [struct((n_space // 2, height, cols), BF16)] * 2,
        limit=LIMITS["out_grad"],
        grid=(1,),
        in_specs=[SMEM] + [whole(x.shape) for x in (pooled_packets, d_joined, dgain)] + [whole((rows, group)), whole((rows, width))],
        out_specs=[whole((n_space // 2, height, cols))] * 2,
        scratch_shapes=[pltpu.VMEM((width, width), F32), pltpu.VMEM((n_space, height, cols), BF16)],
        cost_estimate=cost(6e8, 3e6),
        name="out_grad",
    )(me, pooled_packets, d_joined, dgain, attn, cotangent)
    out_got = swap(out_send, "space", 1)

    def out_add(mine, got):
        return call(
            functools.partial(out_add_body, drows),
            [struct((height, cols), BF16)] * (mine.shape[0] - 1),
            cost_estimate=cost(1e6, 1e6),
            name="out_add",
        )(mine, got)

    later, bit = out_add(out_keep, out_got), 2
    out_later, out_parts = later, [out_keep, out_got]
    while bit < n_space:
        got = {j: swap(later[j], "space", bit) for j in range(0, len(later), 2)}
        out_parts.append(got[0])
        rest = list(range(1, len(later), 2))
        if rest:
            mine = jnp.stack([later[0]] + [later[j] for j in rest])
            later = out_add(mine, jnp.stack([later[0]] + [got[j + 1] for j in rest]))
        bit *= 2

    def d_values(value, scores, after):
        here = value.shape[0]
        return call(
            dvalue_body,
            [struct((here, rows, width), BF16), struct((here, rows, 2 * LANES), BF16)],
            limit=LIMITS["dvalue"],
            after=after,
            grid=(here,),
            in_specs=[whole((rows, width)), whole((3, rows, LANES)), every((rows, width)), every((rows, LANES))],
            out_specs=[every((rows, width)), every((rows, 2 * LANES))],
            scratch_shapes=[pltpu.VMEM((LANES, width), BF16), pltpu.VMEM((width, LANES), BF16)],
            cost_estimate=cost(2e9, 5e6),
            name="dvalue",
        )(d_pooled, stat, value, scores)

    def embed(start, d_value, d_logit, after):
        here = d_value.shape[0]
        at = lambda shape: pl.BlockSpec((1,) + shape, lambda v: (v + start,) + (0,) * len(shape))
        blocks = (n_space // 2, here * pixels + 16, cols)
        return call(
            functools.partial(embed_body, n_space),
            [struct(blocks, BF16)] * 2,
            limit=LIMITS["embed"],
            after=after,
            grid=(here,),
            in_specs=[
                SMEM,
                every((rows, width)),
                every((rows, 2 * LANES)),
                at((rows, pixels)),
                pl.BlockSpec((width, width), lambda v: (0, 1)),
                whole((width, LANES)),
            ],
            out_specs=[whole(blocks)] * 2,
            scratch_shapes=[pltpu.VMEM((n_space, pixels, cols), BF16), pltpu.VMEM((16, width), F32)],
            cost_estimate=cost(1.5e9, 4e6),
            name="embed",
        )(me, d_value, d_logit, patches, agg_kv, w_back)

    dv0, dl0 = d_values(value0, scores0, [out_keep])
    dv1, dl1 = d_values(value1, scores1, [])

    step = max(drows, 256)
    kv_keep, kv_send = call(
        value_grad_body,
        [struct((n_chip, drows, packet), BF16)] * 2,
        limit=LIMITS["value_grad"],
        after=out_later,
        grid=(width // step,),
        in_specs=[SMEM]
        + [pl.BlockSpec(x.shape[:2] + (step,), lambda i: (0, 0, i)) for x in (tokens0, tokens1)]
        + [whole(x.shape) for x in (dv0, dv1, dl0, dl1)],
        out_specs=[whole((n_chip, drows, packet))] * 2,
        scratch_shapes=[pltpu.VMEM((step, packet), BF16)],
        cost_estimate=cost(4e9, 1e7),
        name="value_grad",
    )(me, tokens0, tokens1, dv0, dv1, dl0, dl1)
    kv_got = swap(kv_send, "var", 1)

    def scatter_embed(keep, arrived, after):
        n = n_space // 2 - 1
        sums = call(
            functools.partial(add_body, n),
            [struct(keep.shape[1:], BF16)] * n,
            limit=LIMITS["add"],
            after=after,
            cost_estimate=cost(1e6, 1e6),
            name="add",
        )(keep, arrived)
        blocks = {2 * (j + 1): sums[j] for j in range(n)}
        mine, bit = [keep, arrived], 2
        while bit < n_space:
            got = {k ^ bit: swap(blocks[k], "space", bit) for k in blocks if k & bit and k % bit == 0}
            mine.append(got[0])
            for k in got:
                if k:
                    blocks[k] = (blocks[k].astype(F32) + got[k].astype(F32)).astype(BF16)
            bit *= 2
        return mine, list(sums)

    keep0, send0 = embed(0, dv0, dl0, [kv_keep])
    arrived0 = swap(send0, "space", 1)
    kv_blocks = call(
        functools.partial(pair_sum_body, n_chip),
        [struct((drows, packet), BF16)] * n_chip,
        limit=LIMITS["pair_sum"],
        after=[keep0],
        in_specs=[SMEM] + [vmem] * 2,
        cost_estimate=cost(1e6, 1e6),
        name="pair_sum",
    )(me, kv_keep, kv_got)
    kv_parts = [kv_blocks[0]] + [swap(kv_blocks[k], "var", 2 * k) for k in range(1, n_chip)]
    keep1, send1 = embed(half, dv1, dl1, [kv_blocks[0]] + out_parts[2:])
    arrived1 = swap(send1, "space", 1)
    mine0, sums0 = scatter_embed(keep0, arrived0, [kv_parts[1]])
    part = drows * LANES // cols
    pieces = call(
        functools.partial(packet_split_body, n_chip, n_space),
        [struct((part + 2 * drows, cols), BF16)] * n_space,
        limit=LIMITS["packet_split"],
        after=sums0,
        in_specs=[SMEM] + [vmem] * n_chip,
        scratch_shapes=[pltpu.VMEM((n_space // 2, drows, kv_cols), BF16)],
        cost_estimate=cost(1e6, 1e6),
        name="packet_split",
    )(me, *kv_parts)
    pieces_all = exchange_direct(pieces, "space")
    mine1, sums1 = scatter_embed(keep1, arrived1, sums0)
    grad_qkv, head_flag = call(
        functools.partial(head_grads_body, n_space),
        [struct((cols, 3 * group), F32), struct((8, LANES), F32)],
        limit=LIMITS["head_grads"],
        cost_estimate=cost(1e9, 3e6),
        name="head_grads",
    )(*normed_all, dqkv)
    first_slot = lambda x: pl.BlockSpec((1,) + x.shape[1:], lambda i: (0, 0, 0)) if x.ndim == 3 else whole(x.shape)
    kv_sum, grad_out = call(
        functools.partial(space_sum_body, n_space),
        [struct((drows + 16, kv_cols + LANES + cols), BF16), struct((group, cols), F32)],
        limit=LIMITS["space_sum"],
        after=sums1 + mine0[2:] + [head_flag],
        grid=(1,),
        in_specs=[first_slot(x) for x in list(pieces_all) + out_parts],
        cost_estimate=cost(1e6, 1e6),
        name="space_sum",
    )(*pieces_all, *out_parts)

    def stack(parts):
        return call(
            stack_body,
            struct((len(parts),) + parts[0].shape, BF16),
            after=mine1[2:],
            cost_estimate=cost(1e6, 1e6),
            name="stack",
        )(*parts)

    kv_even, kv_odd = gather_pairs(kv_sum, "var", stack)
    grad_agg_kv, grad_query, grad_agg_out, grad_gain = call(
        functools.partial(final_body, n_var, n_space, scale),
        [struct((width, kv_cols), F32), struct((1, cols), F32)] + [struct((width, cols), F32), struct((1, cols), F32)],
        grid=(1,),
        in_specs=[SMEM] + [vmem] * 3 + [pl.BlockSpec((width, width), lambda i: (0, 0))],
        limit=LIMITS["final"],
        cost_estimate=cost(2e8, 5e6),
        name="final",
    )(me, kv_even, kv_odd, query, agg_kv)

    def first_block(x):
        if x.ndim == 3:
            return pl.BlockSpec((1,) + x.shape[1:], lambda i: (0, 0, 0))
        return pl.BlockSpec(x.shape, lambda i: (0, 0))

    grad_embed, grad_var_embed = call(
        functools.partial(embed_final_body, len(mine0)),
        [struct((count, pixels, cols), F32), struct((count, cols), F32)],
        grid=(1,),
        in_specs=[first_block(x) for x in mine0 + mine1],
        limit=LIMITS["embed_final"],
        cost_estimate=cost(1e6, 1e6),
        name="embed_final",
    )(*mine0, *mine1)

    return (
        grad_embed,
        grad_var_embed,
        grad_query.reshape(cols),
        grad_agg_kv,
        grad_agg_out,
        grad_gain.reshape(cols),
        grad_qkv,
        grad_out,
    )


def solution(mesh):
    return jax.shard_map(
        shards,
        mesh=mesh,
        in_specs=(
            P("var", "space", None),
            P("var", None, None),
            P("var", None),
            P(),
            P(),
            P(),
            P(),
            P(None, "var"),
            P("var", None),
            P("space", None),
        ),
        out_specs=(
            P("var", None, "space"),
            P("var", "space"),
            P("space"),
            P(None, "space"),
            P(None, "space"),
            P("space"),
            P("space", "var"),
            P("var", "space"),
        ),
        check_vma=False,
    )
```
